32 devices in a mesh: seq: 4 (over y, core), fsdp: 8 (over z, x).
Axes of the slice: x: 2, y: 2, z: 4, core: 2. Of those that a mesh axis runs over, the one named last changes fastest.
Arguments:
- inputs: float32 [8, 1024, 2048], P('fsdp', 'seq'), may hold values from -9 to 9
- cotangent: float32 [8, 1024, 2048], P('fsdp', 'seq'), may hold values from -9 to 9
- lengths: int32 [8], P('fsdp'), may hold values from 0 to 1024, as said below
- positions: int32 [8, 1024], P('fsdp', 'seq'), may hold values from 0 to 1023, as said below
- query_key_value_weight: float32 [2048, 4096], P(('seq', 'fsdp')), may hold values from -0.0625 to 0.0625
- out_weight: float32 [2048, 2048], P(('seq', 'fsdp')), may hold values from -0.5 to 0.5
- gateup_weight: float32 [2048, 16384], P(('seq', 'fsdp')), may hold values from -0.09375 to 0.09375
- down_weight: float32 [2048, 8192], P(('seq', 'fsdp')), may hold values from -0.0625 to 0.0625
- norm_gains: float32 [2048, 2], P(('seq', 'fsdp')), may hold values from 0.8 to 6
- query_key_value_moment: float32 [2048, 4096], P(('seq', 'fsdp')), may hold values from -7.6293945e-05 to 7.6293945e-05
- output_weight_moment: float32 [2048, 2048], P(('seq', 'fsdp')), may hold values from -2.2888184e-05 to 2.2888184e-05
- gate_up_moment: float32 [2048, 16384], P(('seq', 'fsdp')), may hold values from -7.6293945e-05 to 7.6293945e-05
- down_weight_moment: float32 [2048, 8192], P(('seq', 'fsdp')), may hold values from -0.00010681152 to 0.00010681152
- norm_gains_moment: float32 [2048, 2], P(('seq', 'fsdp')), may hold values from -3.8146973e-05 to 3.8146973e-05
- query_key_value_variance: float32 [2048, 4096], P(('seq', 'fsdp')), may hold values from 3.0994415e-10 to 5.00679e-09
- out_second: float32 [2048, 2048], P(('seq', 'fsdp')), may hold values from 2.8014183e-11 to 4.5001508e-10
- gateup_second: float32 [2048, 16384], P(('seq', 'fsdp')), may hold values from 3.427267e-10 to 5.5134297e-09
- down_second: float32 [2048, 8192], P(('seq', 'fsdp')), may hold values from 7.4505807e-10 to 1.1920929e-08
- gains_second: float32 [2048, 2], P(('seq', 'fsdp')), may hold values from 7.748604e-11 to 1.2516975e-09
Outputs:
- layer_output: float32 [8, 1024, 2048], P('fsdp', 'seq')
- input_grad: float32 [8, 1024, 2048], P('fsdp', 'seq')
- grad_norm: float32 [], replicated
- qkv_next: float32 [2048, 4096], P(('seq', 'fsdp'))
- out_next: float32 [2048, 2048], P(('seq', 'fsdp'))
- gateup_next: float32 [2048, 16384], P(('seq', 'fsdp'))
- down_next: float32 [2048, 8192], P(('seq', 'fsdp'))
- gains_next: float32 [2048, 2], P(('seq', 'fsdp'))
- qkv_first_next: float32 [2048, 4096], P(('seq', 'fsdp'))
- out_first_next: float32 [2048, 2048], P(('seq', 'fsdp'))
- gateup_first_next: float32 [2048, 16384], P(('seq', 'fsdp'))
- down_first_next: float32 [2048, 8192], P(('seq', 'fsdp'))
- gains_first_next: float32 [2048, 2], P(('seq', 'fsdp'))
- qkv_second_next: float32 [2048, 4096], P(('seq', 'fsdp'))
- out_second_next: float32 [2048, 2048], P(('seq', 'fsdp'))
- gateup_second_next: float32 [2048, 16384], P(('seq', 'fsdp'))
- down_second_next: float32 [2048, 8192], P(('seq', 'fsdp'))
- gains_second_next: float32 [2048, 2], P(('seq', 'fsdp'))
The draws below stay inside these ranges and needn't reach their ends.
Inputs may be any that keep to these rules, and one draw needn't show every extreme that they name: `lengths`: exactly 2 sequences have length 0, all others 1024. Within a sequence, positions count up by one from 0 at its first token and restart at 0 at some tokens.
All inputs are finite; a program needn't handle non-finite values.
Results may differ from the reference program's by a relative error of at most 0.025.
Values may be sent and summed in bfloat16 or wider, within the bound.
A program may use at most 768 MiB of HBM per device.

```python
import math
import jax
import jax.numpy as jnp
from jax import lax

MODEL_WIDTH = 2048
QUERY_HEAD_COUNT = 8
KEY_VALUE_HEADS = 4
HEAD_SIZE = 256
FEED_UNITS = 8192
LENGTH = 1024
STEP = 10
SEQS = 8


def rising_profile(width, spread):
    index = jnp.arange(width)
    quarter = width // 4
    outer = index.astype(jnp.float32) / width
    inner = (index % quarter).astype(jnp.float32) / quarter
    return jnp.sqrt((1.0 + spread * outer) * (1.0 + spread * inner))


def draw_inputs(key, part):
    key = jax.random.fold_in(key, 3)
    first, second = jax.random.split(key)
    base = jax.random.truncated_normal(first, -3.0, 3.0, (SEQS, LENGTH, MODEL_WIDTH), jnp.float32)
    rows = jnp.exp(jax.random.uniform(second, (SEQS, LENGTH, 1), jnp.float32, math.log(0.3), math.log(3.0)))
    return base * rows


def draw_cotangent(key, part):
    key = jax.random.fold_in(key, 5)
    base = jax.random.truncated_normal(key, -3.0, 3.0, (SEQS, LENGTH, MODEL_WIDTH), jnp.float32)
    profile = rising_profile(MODEL_WIDTH, 2.0)
    return base * profile


def draw_norm_gains(key, part):
    key = jax.random.fold_in(key, 11)
    profile = rising_profile(MODEL_WIDTH, 2.0)
    noise = jax.random.uniform(key, (MODEL_WIDTH, 2), jnp.float32, 0.85, 1.15)
    return profile[:, None] * noise


def draw_lengths(key, part):
    key = jax.random.fold_in(key, 13)
    order = jax.random.permutation(key, SEQS)
    return jnp.where(order < SEQS // 4, 0, LENGTH).astype(jnp.int32)


def draw_positions(key, part):
    key = jax.random.fold_in(key, 17)
    first, second = jax.random.split(key)
    spot = jnp.arange(LENGTH, dtype=jnp.int32)
    starts = jax.random.randint(first, (SEQS, LENGTH), 0, LENGTH) < 4
    drawn = jax.random.permutation(second, SEQS) == 0
    starts = starts & jnp.logical_not(drawn)[:, None] | (spot[None, :] == 0)
    begin = lax.cummax(jnp.where(starts, spot[None, :], 0), axis=1)
    return (spot[None, :] - begin).astype(jnp.int32)


def levels(own_key, dims, cuts, least, top_value):
    factor_of, own = 1.0, jax.random.fold_in(own_key, 6)
    for dim, parts in cuts:
        draws = jnp.exp(jax.random.uniform(jax.random.fold_in(own, dim), (parts,), jnp.float32, least / len(cuts), top_value / len(cuts)))
        factor_of = factor_of * jnp.repeat(draws, dims[dim] // parts).reshape([-1 if axis == dim else 1 for axis in range(len(dims))])
    return factor_of


def normal_values(key, shape, scale, bound, pieces=(), held_as=jnp.bfloat16):
    values = jax.random.normal(key, shape, jnp.float32) * scale
    if len(pieces) > 0:
        values = levels(key, shape, pieces, -0.22, 0.18) * values
    return jnp.clip(values, min=-bound, max=bound).astype(held_as)


def setup_inputs(seed: int = 0) -> dict:
    arg_keys = jax.random.split(jax.random.key(seed), 20)
    inputs = draw_inputs(jax.random.fold_in(arg_keys[19], 71), 0)
    cotangent = draw_cotangent(jax.random.fold_in(arg_keys[19], 71), 0)
    lengths = draw_lengths(jax.random.fold_in(arg_keys[19], 71), 0)
    positions = draw_positions(jax.random.fold_in(arg_keys[19], 71), 0)
    query_key_value_weight = normal_values(arg_keys[4], (MODEL_WIDTH, (QUERY_HEAD_COUNT + 2 * KEY_VALUE_HEADS) * HEAD_SIZE), (4 * MODEL_WIDTH) ** -0.5, 0.0625, ((0, 32),), jnp.float32)
    out_weight = normal_values(arg_keys[5], (MODEL_WIDTH, QUERY_HEAD_COUNT * HEAD_SIZE), (QUERY_HEAD_COUNT * HEAD_SIZE // 16) ** -0.5, 0.5, ((0, 32),), jnp.float32)
    gateup_weight = normal_values(arg_keys[6], (MODEL_WIDTH, 2 * FEED_UNITS), (2 * MODEL_WIDTH) ** -0.5, 0.09375, ((0, 32),), jnp.float32)
    down_weight = normal_values(arg_keys[7], (MODEL_WIDTH, FEED_UNITS), FEED_UNITS ** -0.5, 0.0625, ((0, 32),), jnp.float32)
    norm_gains = draw_norm_gains(jax.random.fold_in(arg_keys[19], 71), 0)
    query_key_value_moment = normal_values(arg_keys[9], (MODEL_WIDTH, (QUERY_HEAD_COUNT + 2 * KEY_VALUE_HEADS) * HEAD_SIZE), (0.22 * (MODEL_WIDTH * (18 * FEED_UNITS + 4 * (QUERY_HEAD_COUNT + 2 * KEY_VALUE_HEADS) * HEAD_SIZE)) ** -0.5), 7.62939453125e-05, ((0, 32),), jnp.float32)
    output_weight_moment = normal_values(arg_keys[10], (MODEL_WIDTH, QUERY_HEAD_COUNT * HEAD_SIZE), (0.066 * (MODEL_WIDTH * (18 * FEED_UNITS + 4 * (QUERY_HEAD_COUNT + 2 * KEY_VALUE_HEADS) * HEAD_SIZE)) ** -0.5), 2.288818359375e-05, ((0, 32),), jnp.float32)
    gate_up_moment = normal_values(arg_keys[11], (MODEL_WIDTH, 2 * FEED_UNITS), (0.23 * (MODEL_WIDTH * (18 * FEED_UNITS + 4 * (QUERY_HEAD_COUNT + 2 * KEY_VALUE_HEADS) * HEAD_SIZE)) ** -0.5), 7.62939453125e-05, ((0, 32),), jnp.float32)
    down_weight_moment = normal_values(arg_keys[12], (MODEL_WIDTH, FEED_UNITS), (0.34 * (MODEL_WIDTH * (18 * FEED_UNITS + 4 * (QUERY_HEAD_COUNT + 2 * KEY_VALUE_HEADS) * HEAD_SIZE)) ** -0.5), 0.00010681152, ((0, 32),), jnp.float32)
    norm_gains_moment = normal_values(arg_keys[13], (MODEL_WIDTH, 2), (0.11 * (MODEL_WIDTH * (18 * FEED_UNITS + 4 * (QUERY_HEAD_COUNT + 2 * KEY_VALUE_HEADS) * HEAD_SIZE)) ** -0.5), 3.814697265625e-05, ((0, 32),), jnp.float32)
    query_key_value_variance = jnp.clip(jnp.exp(math.log(5.006790093631253e-09) - 2.7821582 * jax.random.uniform(arg_keys[14], (MODEL_WIDTH, (QUERY_HEAD_COUNT + 2 * KEY_VALUE_HEADS) * HEAD_SIZE), jnp.float32) ** levels(arg_keys[14], (MODEL_WIDTH, (QUERY_HEAD_COUNT + 2 * KEY_VALUE_HEADS) * HEAD_SIZE), ((0, 32),), -0.2, 0.2)), 3.0994415367580075e-10, 5.006790093631253e-09)
    out_second = jnp.clip(jnp.exp(math.log(4.500150807551506e-10) - 2.77657 * jax.random.uniform(arg_keys[15], (MODEL_WIDTH, QUERY_HEAD_COUNT * HEAD_SIZE), jnp.float32) ** levels(arg_keys[15], (MODEL_WIDTH, QUERY_HEAD_COUNT * HEAD_SIZE), ((0, 32),), -0.2, 0.2)), 2.8014182987257108e-11, 4.500150807551506e-10)
    gateup_second = jnp.clip(jnp.exp(math.log(5.513429712777906e-09) - 2.7780088 * jax.random.uniform(arg_keys[16], (MODEL_WIDTH, 2 * FEED_UNITS), jnp.float32) ** levels(arg_keys[16], (MODEL_WIDTH, 2 * FEED_UNITS), ((0, 32),), -0.2, 0.2)), 3.427267081246299e-10, 5.513429712777906e-09)
    down_second = jnp.clip(jnp.exp(math.log(1.1920929132713809e-08) - 2.7725887 * jax.random.uniform(arg_keys[17], (MODEL_WIDTH, FEED_UNITS), jnp.float32) ** levels(arg_keys[17], (MODEL_WIDTH, FEED_UNITS), ((0, 32),), -0.2, 0.2)), 7.450580707946131e-10, 1.1920929132713809e-08)
    gains_second = jnp.clip(jnp.exp(math.log(1.2516975234078132e-09) - 2.7821582 * jax.random.uniform(arg_keys[18], (MODEL_WIDTH, 2), jnp.float32) ** levels(arg_keys[18], (MODEL_WIDTH, 2), ((0, 32),), -0.2, 0.2)), 7.748603841895019e-11, 1.2516975234078132e-09)
    return {"inputs": inputs, "cotangent": cotangent, "lengths": lengths, "positions": positions, "query_key_value_weight": query_key_value_weight, "out_weight": out_weight, "gateup_weight": gateup_weight, "down_weight": down_weight, "norm_gains": norm_gains, "query_key_value_moment": query_key_value_moment, "output_weight_moment": output_weight_moment, "gate_up_moment": gate_up_moment, "down_weight_moment": down_weight_moment, "norm_gains_moment": norm_gains_moment, "query_key_value_variance": query_key_value_variance, "out_second": out_second, "gateup_second": gateup_second, "down_second": down_second, "gains_second": gains_second}


NORM_EPSILON = 1e-06
ROPE_BASE = 1000042.0
MASKED_SCORE = -1000000000.0
CLIP_NORM = 1.0
BETA_ONE = 0.9
BETA_TWO = 0.95
ADAM_EPSILON = 1e-08
DECAY_MATRIX = 0.1
RATE_MATRIX = 0.02
RATE_OUTPUT = 0.1
RATE_GAIN = 1.0
HIGHEST = lax.Precision.HIGHEST

@jax.custom_vjp
def reduced_precision(v):
    return lax.optimization_barrier(v.astype(jnp.bfloat16)).astype(jnp.float32)

@jax.custom_vjp
def reduced_backward(v):
    return v

def low_keep(v):
    return (reduced_precision(v), None)

def low_pass(kept, grad):
    return (grad,)

def back_keep(v):
    return (v, None)

def back_low(kept, grad):
    return (reduced_precision(grad),)
reduced_precision.defvjp(low_keep, low_pass)
reduced_backward.defvjp(back_keep, back_low)

def rotary_tables(positions, width):
    half = width // 2
    freqs = jnp.exp(-(jnp.arange(half, dtype=jnp.float32) * 2.0 / width) * math.log(ROPE_BASE))
    angles = positions.astype(jnp.float32)[..., None] * freqs
    angles = jnp.concatenate([angles, angles], -1)
    return (jnp.cos(angles)[..., None, :], jnp.sin(angles)[..., None, :])

def rotate_half(value_rows):
    half = value_rows.shape[-1] // 2
    return jnp.concatenate([-value_rows[..., half:], value_rows[..., :half]], -1)

def apply_rotary(value_rows, cosine_table, sine_table):
    return value_rows * cosine_table + rotate_half(value_rows) * sine_table

def rms_normalize(value_rows):
    return value_rows * lax.rsqrt(lax.optimization_barrier(jnp.mean(value_rows * value_rows, -1, keepdims=True)) + NORM_EPSILON)

def attend(item):
    query, key_rows, value_rows, limit = item
    token_length = query.shape[0]
    shard_portion = query.shape[1] // key_rows.shape[1]
    keys_all = jnp.repeat(key_rows, shard_portion, axis=1)
    values_all = jnp.repeat(value_rows, shard_portion, axis=1)
    spot = jnp.arange(token_length)
    visible = (spot[None, :] <= spot[:, None]) & (spot[None, :] < limit)
    scores = jnp.einsum('qhd,khd->hqk', query, keys_all, precision=HIGHEST) * (1.0 / math.sqrt(query.shape[2]))
    scores = reduced_backward(jnp.where(visible[None], scores, MASKED_SCORE))
    peak = lax.optimization_barrier(jnp.max(scores, -1, keepdims=True))
    expo = jnp.exp(scores - peak)
    probs = reduced_precision(expo / lax.optimization_barrier(jnp.sum(expo, -1, keepdims=True)))
    heads = jnp.einsum('hqk,khd->qhd', probs, values_all, precision=HIGHEST)
    heads = heads * (spot < limit).astype(heads.dtype)[:, None, None]
    return reduced_backward(reduced_precision(heads))

def layer_forward(inputs, query_key_value_weight, out_weight, gateup_weight, down_weight, norm_gains, limits, positions):
    qkv_low = reduced_precision(query_key_value_weight)
    out_low = reduced_precision(out_weight)
    gateup_low = reduced_precision(gateup_weight)
    down_low = reduced_precision(down_weight)
    gains_low = reduced_precision(norm_gains)
    sequence_batch, token_length, width = inputs.shape
    query_width = QUERY_HEAD_COUNT * HEAD_SIZE
    key_width = KEY_VALUE_HEADS * HEAD_SIZE
    first_normed = reduced_precision(rms_normalize(inputs) * gains_low[:, 0])
    merged_heads = reduced_backward(jnp.einsum('std,dc->stc', first_normed, qkv_low, precision=HIGHEST))
    cosine_table, sine_table = rotary_tables(positions, HEAD_SIZE)
    queries = reduced_backward(reduced_precision(apply_rotary(merged_heads[..., :query_width].reshape(sequence_batch, token_length, QUERY_HEAD_COUNT, HEAD_SIZE), cosine_table, sine_table)))
    key_rows = reduced_backward(reduced_precision(apply_rotary(merged_heads[..., query_width:query_width + key_width].reshape(sequence_batch, token_length, KEY_VALUE_HEADS, HEAD_SIZE), cosine_table, sine_table)))
    value_rows = reduced_backward(reduced_precision(merged_heads[..., query_width + key_width:].reshape(sequence_batch, token_length, KEY_VALUE_HEADS, HEAD_SIZE)))
    heads = lax.map(jax.checkpoint(attend), (queries, key_rows, value_rows, limits))
    attended = reduced_backward(jnp.einsum('stj,dj->std', heads.reshape(sequence_batch, token_length, query_width), out_low, precision=HIGHEST))
    residual_hidden = inputs + attended
    second_normed = reduced_precision(rms_normalize(residual_hidden) * gains_low[:, 1])
    gateup = reduced_backward(jnp.einsum('std,dc->stc', second_normed, gateup_low, precision=HIGHEST))
    act = reduced_precision(jax.nn.silu(gateup[..., :FEED_UNITS]) * gateup[..., FEED_UNITS:])
    return residual_hidden + reduced_backward(jnp.einsum('stf,df->std', act, down_low, precision=HIGHEST))

def adam_step(weight, grad, first, second, factor, rate, decay):
    clipped = grad * factor
    first_new = BETA_ONE * first + (1.0 - BETA_ONE) * clipped
    second_new = BETA_TWO * second + (1.0 - BETA_TWO) * clipped * clipped
    corr_one = 1.0 - BETA_ONE ** STEP
    corr_two = 1.0 - BETA_TWO ** STEP
    update = first_new / corr_one / (jnp.sqrt(second_new / corr_two) + ADAM_EPSILON)
    return (weight - rate * (update + decay * weight), first_new, second_new)

def reference(inputs, cotangent, lengths, positions, query_key_value_weight, out_weight, gateup_weight, down_weight, norm_gains, query_key_value_moment, output_weight_moment, gate_up_moment, down_weight_moment, norm_gains_moment, query_key_value_variance, out_second, gateup_second, down_second, gains_second):
    group = math.gcd(SEQS, max(1, 4096 // LENGTH))
    steps_count = SEQS // group

    def split(value_rows):
        return value_rows.reshape((steps_count, group) + value_rows.shape[1:])

    def one_group(carry, item):
        block_in, block_cot, block_len, block_pos = item

        def forward(x, wqkv, wout, wgu, wdown, wgain):
            return layer_forward(x, wqkv, wout, wgu, wdown, wgain, block_len, block_pos)
        result, pull = jax.vjp(forward, block_in, query_key_value_weight, out_weight, gateup_weight, down_weight, norm_gains)
        grads = pull(block_cot)
        summed = tuple((old + new for old, new in zip(carry, grads[1:])))
        return (summed, (result, grads[0]))
    start = (jnp.zeros(query_key_value_weight.shape, jnp.float32), jnp.zeros(out_weight.shape, jnp.float32), jnp.zeros(gateup_weight.shape, jnp.float32), jnp.zeros(down_weight.shape, jnp.float32), jnp.zeros(norm_gains.shape, jnp.float32))
    sums, (outputs, dinputs) = lax.scan(one_group, start, (split(inputs), split(cotangent), split(lengths), split(positions)))
    grad_qkv, grad_out, grad_gateup, grad_down, grad_gains = sums
    layer_output = outputs.reshape(inputs.shape)
    input_grad = dinputs.reshape(inputs.shape)
    squares = jnp.sum(grad_qkv * grad_qkv) + jnp.sum(grad_out * grad_out) + jnp.sum(grad_gateup * grad_gateup) + jnp.sum(grad_down * grad_down) + jnp.sum(grad_gains * grad_gains)
    grad_norm = jnp.sqrt(squares)
    factor = CLIP_NORM / jnp.maximum(grad_norm, CLIP_NORM)
    qkv_next, qkv_first_next, qkv_second_next = adam_step(query_key_value_weight, grad_qkv, query_key_value_moment, query_key_value_variance, factor, RATE_MATRIX, DECAY_MATRIX)
    out_next, out_first_next, out_second_next = adam_step(out_weight, grad_out, output_weight_moment, out_second, factor, RATE_OUTPUT, DECAY_MATRIX)
    gateup_next, gateup_first_next, gateup_second_next = adam_step(gateup_weight, grad_gateup, gate_up_moment, gateup_second, factor, RATE_MATRIX, DECAY_MATRIX)
    down_next, down_first_next, down_second_next = adam_step(down_weight, grad_down, down_weight_moment, down_second, factor, RATE_MATRIX, DECAY_MATRIX)
    gains_next, gains_first_next, gains_second_next = adam_step(norm_gains, grad_gains, norm_gains_moment, gains_second, factor, RATE_GAIN, 0.0)
    return (layer_output, input_grad, grad_norm, qkv_next, out_next, gateup_next, down_next, gains_next, qkv_first_next, out_first_next, gateup_first_next, down_first_next, gains_first_next, qkv_second_next, out_second_next, gateup_second_next, down_second_next, gains_second_next)
```

```python
import math

import jax
import jax.numpy as jnp
from jax import lax
from jax.sharding import Mesh, PartitionSpec as P

QUERY_HEAD_COUNT = 8
KEY_VALUE_HEADS = 4
HEAD_SIZE = 256
FEED_UNITS = 8192
STEP = 10

NORM_EPSILON = 1e-06
ROPE_BASE = 1000042.0
MASKED_SCORE = -1000000000.0
CLIP_NORM = 1.0
BETA_ONE = 0.9
BETA_TWO = 0.95
ADAM_EPSILON = 1e-08
DECAY_MATRIX = 0.1
RATE_MATRIX = 0.02
RATE_OUTPUT = 0.1
RATE_GAIN = 1.0

TP = ("seq", "near")
EVERY = ("seq", "far", "near")


def rotary_tables(positions, width):
    half = width // 2
    freqs = jnp.exp(-(jnp.arange(half, dtype=jnp.float32) * 2.0 / width) * math.log(ROPE_BASE))
    angles = positions.astype(jnp.float32)[..., None] * freqs
    angles = jnp.concatenate([angles, angles], -1)
    return (jnp.cos(angles)[..., None, :], jnp.sin(angles)[..., None, :])


def rotate_half(value_rows):
    half = value_rows.shape[-1] // 2
    return jnp.concatenate([-value_rows[..., half:], value_rows[..., :half]], -1)


def apply_rotary(value_rows, cosine_table, sine_table):
    return value_rows * cosine_table + rotate_half(value_rows) * sine_table


def rope_back(grads, cosine_table, sine_table):
    return grads * cosine_table - rotate_half(grads * sine_table)


def rms_normalize(value_rows):
    inverse_scale = lax.rsqrt(jnp.mean(value_rows * value_rows, -1, keepdims=True) + NORM_EPSILON)
    return (value_rows * inverse_scale, inverse_scale)


def norm_backward(normed_gradient, unit_input, inverse_scale, norm_gain_vector):
    unit_input_gradient = normed_gradient * norm_gain_vector
    backward_pass = inverse_scale * (
        unit_input_gradient
        - unit_input * jnp.mean(unit_input_gradient * unit_input, -1, keepdims=True)
    )
    gradient_term = jnp.sum((normed_gradient * unit_input).reshape(-1, unit_input.shape[-1]), 0)
    return (backward_pass, gradient_term)


def adam_step(weight, grad, first, second, factor, rate, decay):
    clipped = grad * factor
    first_new = BETA_ONE * first + (1.0 - BETA_ONE) * clipped
    second_new = BETA_TWO * second + (1.0 - BETA_TWO) * clipped * clipped
    corr_one = 1.0 - BETA_ONE**STEP
    corr_two = 1.0 - BETA_TWO**STEP
    update = first_new / corr_one / (jnp.sqrt(second_new / corr_two) + ADAM_EPSILON)
    return (weight - rate * (update + decay * weight), first_new, second_new)


def product(left, right, left_dim, right_dim):
    return lax.dot_general(
        left, right, (((left_dim,), (right_dim,)), ((), ())), preferred_element_type=jnp.float32
    )


def columns_out(pieces, group, over):
    parts, rows, columns = pieces.shape
    mine = lax.all_to_all(pieces, group, 0, 0, tiled=True)
    full = lax.all_gather(mine.reshape(-1, columns), over, axis=0, tiled=True)
    far = lax.axis_size(over)
    seq = lax.axis_size("seq")
    near = parts // seq
    full = full.reshape(far, seq, near, rows, columns).transpose(1, 0, 2, 3, 4)
    return full.reshape(-1, columns)


def columns_back(grad, group, over, rows):
    seq = lax.axis_size("seq")
    far = lax.axis_size(over)
    columns = grad.shape[1]
    near = grad.shape[0] // (seq * far * rows)
    terms = grad.astype(jnp.bfloat16).reshape(seq, far, near, rows, columns)
    terms = terms.transpose(1, 0, 2, 3, 4).reshape(-1, columns)
    mine = lax.psum_scatter(terms, over, scatter_dimension=0, tiled=True)
    return lax.all_to_all(mine.reshape(seq * near, rows, columns), group, 0, 0, tiled=True)


def shards(
    inputs,
    cotangent,
    lengths,
    positions,
    query_key_value_weight,
    out_weight,
    gateup_weight,
    down_weight,
    norm_gains,
    query_key_value_moment,
    output_weight_moment,
    gate_up_moment,
    down_weight_moment,
    norm_gains_moment,
    query_key_value_variance,
    out_second,
    gateup_second,
    down_second,
    gains_second,
):
    _, here, width = inputs.shape
    seq = lax.axis_size("seq")
    group = seq * lax.axis_size("near")
    rows = out_weight.shape[0]
    full = here * seq
    heads_here = QUERY_HEAD_COUNT // seq
    local_kv = KEY_VALUE_HEADS // seq
    per_kv = QUERY_HEAD_COUNT // KEY_VALUE_HEADS
    query_width = QUERY_HEAD_COUNT * HEAD_SIZE
    key_width = KEY_VALUE_HEADS * HEAD_SIZE
    mine_q, mine_k = query_width // seq, key_width // seq
    units = FEED_UNITS // group
    factor = 1.0 / math.sqrt(HEAD_SIZE)
    low = jnp.bfloat16

    inputs = inputs[0]
    cotangent = cotangent[0]
    length = lengths[0]

    qkv_low = query_key_value_weight.astype(low)
    qkv_pieces = jnp.concatenate(
        [
            qkv_low[:, :query_width].reshape(rows, seq, mine_q),
            qkv_low[:, query_width : query_width + key_width].reshape(rows, seq, mine_k),
            qkv_low[:, query_width + key_width :].reshape(rows, seq, mine_k),
        ],
        2,
    ).transpose(1, 0, 2)
    qkv = columns_out(qkv_pieces, "seq", ("far", "near"))
    out = columns_out(
        out_weight.astype(low).reshape(rows, seq, mine_q).transpose(1, 0, 2),
        "seq",
        ("far", "near"),
    )
    gains = lax.all_gather(norm_gains.astype(low), EVERY, axis=0, tiled=True).astype(jnp.float32)
    gain_one, gain_two = gains[:, 0], gains[:, 1]
    all_positions = lax.all_gather(positions[0], "seq", axis=0, tiled=True)

    unit_one, scale_one = rms_normalize(inputs)
    normed_one = lax.all_gather((unit_one * gain_one).astype(low), "seq", axis=0, tiled=True)
    cos, sin = rotary_tables(all_positions, HEAD_SIZE)
    merged = product(normed_one, qkv, 1, 0)
    queries = apply_rotary(merged[:, :mine_q].reshape(full, heads_here, HEAD_SIZE), cos, sin)
    queries = queries.astype(low).reshape(full, local_kv, per_kv, HEAD_SIZE)
    keys = apply_rotary(
        merged[:, mine_q : mine_q + mine_k].reshape(full, local_kv, HEAD_SIZE), cos, sin
    ).astype(low)
    values = merged[:, mine_q + mine_k :].reshape(full, local_kv, HEAD_SIZE).astype(low)

    gateup_pieces = gateup_weight.astype(low).reshape(rows, 2, group, units).transpose(2, 0, 1, 3)
    gateup_w = columns_out(gateup_pieces.reshape(group, rows, 2 * units), TP, "far")
    down_w = columns_out(
        down_weight.astype(low).reshape(rows, group, units).transpose(1, 0, 2), TP, "far"
    )
    dout = lax.all_gather(cotangent.astype(low), TP, axis=0, tiled=True)

    spot = jnp.arange(full)
    visible = (spot[None, :] <= spot[:, None]) & (spot < length)[None, :]
    live = (spot < length)[:, None, None, None]
    scores = jnp.einsum("qkgd,jkd->kgqj", queries, keys, preferred_element_type=jnp.float32)
    scores = jnp.where(visible, scores * factor, MASKED_SCORE)
    peak = jnp.max(scores, -1, keepdims=True)
    expo = jnp.exp(scores - peak)
    probs = expo / jnp.sum(expo, -1, keepdims=True)
    probs_low = probs.astype(low)
    heads = jnp.einsum("kgqj,jkd->qkgd", probs_low, values, preferred_element_type=jnp.float32)
    heads = (heads * live).astype(low).reshape(full, mine_q)
    attended = lax.psum_scatter(
        product(heads, out, 1, 1).astype(low), "seq", scatter_dimension=0, tiled=True
    )
    hidden = inputs + attended.astype(jnp.float32)
    unit_two, scale_two = rms_normalize(hidden)
    normed_two = lax.all_gather((unit_two * gain_two).astype(low), TP, axis=0, tiled=True)

    gate = product(normed_two, gateup_w[:, :units], 1, 0)
    upper = product(normed_two, gateup_w[:, units:], 1, 0)
    sig = jax.nn.sigmoid(gate)
    act = (gate * sig * upper).astype(low)
    dact = product(dout, down_w, 1, 0)
    dgate = dact * upper * sig * (1.0 + gate * (1.0 - sig))
    dupper = dact * gate * sig
    dgateup = jnp.concatenate([dgate.astype(low), dupper.astype(low)], 1)
    dnormed_two = lax.psum_scatter(
        product(dgateup, gateup_w, 1, 1).astype(low), TP, scatter_dimension=0, tiled=True
    ).astype(jnp.float32)
    grad_gateup = columns_back(product(normed_two, dgateup, 0, 0), TP, "far", rows)
    grad_down = columns_back(product(dout, act, 0, 0), TP, "far", rows)
    back_two, gain_term_two = norm_backward(dnormed_two, unit_two, scale_two, gain_two)
    dhidden = cotangent + back_two

    dattended = lax.all_gather(dhidden.astype(low), "seq", axis=0, tiled=True)
    dheads = product(dattended, out, 1, 0).astype(low).reshape(full, local_kv, per_kv, HEAD_SIZE)
    dheads = dheads * live.astype(low)
    grad_out = columns_back(product(dattended, heads, 0, 0), "seq", ("far", "near"), rows)
    dvalues = jnp.einsum("kgqj,qkgd->jkd", probs_low, dheads, preferred_element_type=jnp.float32)
    dprobs = jnp.einsum("qkgd,jkd->kgqj", dheads, values, preferred_element_type=jnp.float32)
    inner = jnp.sum(probs * dprobs, -1, keepdims=True)
    dscores = jnp.where(visible, (probs * (dprobs - inner)).astype(low), jnp.zeros((), low))
    dqueries = jnp.einsum("kgqj,jkd->qkgd", dscores, keys, preferred_element_type=jnp.float32)
    dkeys = jnp.einsum("kgqj,qkgd->jkd", dscores, queries, preferred_element_type=jnp.float32)
    dqueries = (dqueries * factor).astype(low).reshape(full, heads_here, HEAD_SIZE)
    dkeys = (dkeys * factor).astype(low)
    dfused = jnp.concatenate(
        [
            rope_back(dqueries.astype(jnp.float32), cos, sin).astype(low).reshape(full, mine_q),
            rope_back(dkeys.astype(jnp.float32), cos, sin).astype(low).reshape(full, mine_k),
            dvalues.astype(low).reshape(full, mine_k),
        ],
        1,
    )
    dnormed_one = lax.psum_scatter(
        product(dfused, qkv, 1, 1).astype(low), "seq", scatter_dimension=0, tiled=True
    ).astype(jnp.float32)
    grad_qkv = columns_back(product(normed_one, dfused, 0, 0), "seq", ("far", "near"), rows)
    back_one, gain_term_one = norm_backward(dnormed_one, unit_one, scale_one, gain_one)
    input_grad = dhidden + back_one
    layer_output = hidden + lax.psum_scatter(
        product(act, down_w, 1, 1).astype(low), TP, scatter_dimension=0, tiled=True
    ).astype(jnp.float32)

    gain_terms = jnp.stack([gain_term_one, gain_term_two], 1)
    grad_gains = lax.psum_scatter(gain_terms, EVERY, scatter_dimension=0, tiled=True)

    grad_qkv = grad_qkv.astype(jnp.float32)
    grad_qkv = jnp.concatenate(
        [
            grad_qkv[:, :, :mine_q].transpose(1, 0, 2).reshape(rows, query_width),
            grad_qkv[:, :, mine_q : mine_q + mine_k].transpose(1, 0, 2).reshape(rows, key_width),
            grad_qkv[:, :, mine_q + mine_k :].transpose(1, 0, 2).reshape(rows, key_width),
        ],
        1,
    )
    grad_out = grad_out.astype(jnp.float32).transpose(1, 0, 2).reshape(rows, query_width)
    grad_gateup = grad_gateup.astype(jnp.float32).reshape(group, rows, 2, units)
    grad_gateup = grad_gateup.transpose(1, 2, 0, 3).reshape(rows, 2 * FEED_UNITS)
    grad_down = grad_down.astype(jnp.float32).transpose(1, 0, 2).reshape(rows, FEED_UNITS)

    local_squares = (
        jnp.sum(grad_qkv * grad_qkv)
        + jnp.sum(grad_out * grad_out)
        + jnp.sum(grad_gateup * grad_gateup)
        + jnp.sum(grad_down * grad_down)
        + jnp.sum(grad_gains * grad_gains)
    )
    grad_norm = jnp.sqrt(lax.psum(local_squares, EVERY))
    clip = CLIP_NORM / jnp.maximum(grad_norm, CLIP_NORM)
    steps = (
        (query_key_value_weight, grad_qkv, query_key_value_moment, query_key_value_variance, RATE_MATRIX, DECAY_MATRIX),
        (out_weight, grad_out, output_weight_moment, out_second, RATE_OUTPUT, DECAY_MATRIX),
        (gateup_weight, grad_gateup, gate_up_moment, gateup_second, RATE_MATRIX, DECAY_MATRIX),
        (down_weight, grad_down, down_weight_moment, down_second, RATE_MATRIX, DECAY_MATRIX),
        (norm_gains, grad_gains, norm_gains_moment, gains_second, RATE_GAIN, 0.0),
    )
    stepped = [adam_step(w, g, m, v, clip, rate, decay) for w, g, m, v, rate, decay in steps]
    nexts, firsts, seconds = zip(*stepped)
    return (layer_output[None], input_grad[None], grad_norm, *nexts, *firsts, *seconds)


def solution(mesh):
    seq, fsdp = mesh.shape["seq"], mesh.shape["fsdp"]
    cut = Mesh(mesh.devices.reshape(seq, fsdp // 2, 2), EVERY)
    tokens = P(("far", "near"), "seq", None)
    matrix = P(EVERY, None)
    return jax.shard_map(
        shards,
        mesh=cut,
        in_specs=(tokens, tokens, P(("far", "near")), P(("far", "near"), "seq")) + (matrix,) * 15,
        out_specs=(tokens, tokens, P()) + (matrix,) * 15,
        check_vma=False,
    )
```

```python
import functools
import math

import jax
import jax.numpy as jnp
from jax import lax
from jax.experimental import pallas as pl
from jax.experimental.pallas import tpu as pltpu
from jax.sharding import Mesh, PartitionSpec as P

QUERY_HEAD_COUNT = 8
KEY_VALUE_HEADS = 4
HEAD_SIZE = 256
FEED_UNITS = 8192
STEP = 10

NORM_EPSILON = 1e-06
ROPE_BASE = 1000042.0
MASKED_SCORE = -1000000000.0
CLIP_NORM = 1.0
BETA_ONE = 0.9
BETA_TWO = 0.95
ADAM_EPSILON = 1e-08
DECAY_MATRIX = 0.1
RATE_MATRIX = 0.02
RATE_OUTPUT = 0.1
RATE_GAIN = 1.0

EVERY = ("seq", "far", "near")


MESH_IDS = pl.DeviceIdType.MESH
ANYWHERE = pl.BlockSpec(memory_space=pl.ANY)
IN_VMEM = pl.BlockSpec(memory_space=pltpu.VMEM)
VMEM_LIMIT = 60 * 1024 * 1024


def places():
    s, n = lax.axis_index("seq"), lax.axis_index("near")
    return s, n, s + 1 - 2 * (s % 2), (s + 2) % 4, 1 - n


def meet(*others):
    barrier = pltpu.get_barrier_semaphore()
    for other in others:
        pl.semaphore_signal(barrier, inc=1, device_id=other, device_id_type=MESH_IDS)
    pl.semaphore_wait(barrier, len(others))


def sender(send_sems, recv_sems):
    copies = {}

    def send(key, source, target, device):
        at = len(copies)
        copies[key] = pltpu.make_async_remote_copy(
            src_ref=source,
            dst_ref=target,
            send_sem=send_sems.at[at],
            recv_sem=recv_sems.at[at],
            device_id=device,
            device_id_type=MESH_IDS,
        )
        copies[key].start()

    return copies, send


def gather_plane_kernel(rows, x_ref, o_ref, local_sem, send_sems, recv_sems):
    s, n, core, across, beside = places()
    half = rows // 2
    to_core, to_y, to_x = {"seq": core}, {"seq": across}, {"near": beside}

    def block(seq, near, part):
        return o_ref.at[pl.ds((seq * 2 + near) * rows + part * half, half)]

    def own(part):
        return x_ref.at[pl.ds(part * half, half)]

    meet(to_core, to_y, to_x)
    local = pltpu.make_async_copy(x_ref, o_ref.at[pl.ds((s * 2 + n) * rows, rows)], local_sem)
    local.start()
    copies, send = sender(send_sems, recv_sems)
    send("y0", own(0), block(s, n, 0), to_y)
    send("x1", own(1), block(s, n, 1), to_x)
    send("y1", own(1), block(s, n, 1), to_y)
    send("x0", own(0), block(s, n, 0), to_x)
    send("c0", own(0), block(s, n, 0), to_core)
    send("c1", own(1), block(s, n, 1), to_core)
    copies["y0"].wait_recv()
    send("yx", block(across, n, 0), block(across, n, 0), to_x)
    send("yc0", block(across, n, 0), block(across, n, 0), to_core)
    copies["x1"].wait_recv()
    send("xy", block(s, beside, 1), block(s, beside, 1), to_y)
    send("xc1", block(s, beside, 1), block(s, beside, 1), to_core)
    copies["y1"].wait_recv()
    send("yc1", block(across, n, 1), block(across, n, 1), to_core)
    copies["x0"].wait_recv()
    send("xc0", block(s, beside, 0), block(s, beside, 0), to_core)
    copies["yx"].wait_recv()
    send("dc0", block(across, beside, 0), block(across, beside, 0), to_core)
    copies["xy"].wait_recv()
    send("dc1", block(across, beside, 1), block(across, beside, 1), to_core)
    for key in ("c0", "c1", "yc0", "yc1", "xc0", "xc1", "dc0", "dc1"):
        copies[key].wait_recv()
    for copy in copies.values():
        copy.wait_send()
    local.wait()


def gather_plane(x, collective_id):
    rows, columns = x.shape
    return pl.pallas_call(
        functools.partial(gather_plane_kernel, rows),
        out_shape=jax.ShapeDtypeStruct((8 * rows, columns), x.dtype),
        in_specs=[ANYWHERE],
        out_specs=ANYWHERE,
        scratch_shapes=[
            pltpu.SemaphoreType.DMA,
            pltpu.SemaphoreType.DMA((14,)),
            pltpu.SemaphoreType.DMA((14,)),
        ],
        compiler_params=pltpu.CompilerParams(collective_id=collective_id, has_side_effects=True),
    )(x)


def gather_seq_kernel(rows, x_ref, o_ref, local_sem, send_sems, recv_sems):
    s, _, core, across, _ = places()
    half = rows // 2
    to_core, to_y = {"seq": core}, {"seq": across}

    def block(seq, part):
        return o_ref.at[pl.ds(seq * rows + part * half, half)]

    def own(part):
        return x_ref.at[pl.ds(part * half, half)]

    meet(to_core, to_y)
    local = pltpu.make_async_copy(x_ref, o_ref.at[pl.ds(s * rows, rows)], local_sem)
    local.start()
    copies, send = sender(send_sems, recv_sems)
    for part in range(2):
        send(("y", part), own(part), block(s, part), to_y)
    for part in range(2):
        send(("c", part), own(part), block(s, part), to_core)
    for part in range(2):
        copies["y", part].wait_recv()
        send(("yc", part), block(across, part), block(across, part), to_core)
    for part in range(2):
        copies["c", part].wait_recv()
        copies["yc", part].wait_recv()
    for copy in copies.values():
        copy.wait_send()
    local.wait()


def gather_seq(x, collective_id):
    rows, columns = x.shape
    return pl.pallas_call(
        functools.partial(gather_seq_kernel, rows),
        out_shape=jax.ShapeDtypeStruct((4 * rows, columns), x.dtype),
        in_specs=[ANYWHERE],
        out_specs=ANYWHERE,
        scratch_shapes=[
            pltpu.SemaphoreType.DMA,
            pltpu.SemaphoreType.DMA((6,)),
            pltpu.SemaphoreType.DMA((6,)),
        ],
        compiler_params=pltpu.CompilerParams(collective_id=collective_id, has_side_effects=True),
    )(x)


def add_rows(target, first, second, third=None, step=64):
    rows = target.shape[0]

    def body(i, carry):
        at = pl.ds(pl.multiple_of(i * step, step), step)
        total = first[at, :].astype(jnp.float32) + second[at, :].astype(jnp.float32)
        if third is not None:
            total = total + third[at, :].astype(jnp.float32)
        target[at, :] = total.astype(target.dtype)
        return carry

    lax.fori_loop(0, rows // step, body, 0)


def scatter_plane_kernel(rows, p_ref, o_ref, mine, far, hop_x, hop_y, last_x, last_y, local_sems, send_sems, recv_sems):
    s, n, core, across, beside = places()
    half = rows // 2
    to_core, to_y, to_x = {"seq": core}, {"seq": across}, {"near": beside}

    def block(seq, near):
        return p_ref.at[pl.ds((seq * 2 + near) * rows, rows)]

    def part(ref, at, p):
        return ref.at[at, pl.ds(p * half, half)]

    meet(to_core, to_y, to_x)
    copies, send = sender(send_sems, recv_sems)
    other = (core + 2) % 4
    given = [block(other, beside), block(other, n), block(core, beside), block(core, n)]
    kept = [block(across, beside), block(across, n), block(s, beside), block(s, n)]
    locals_ = []
    for k in range(4):
        send(k, given[k], far.at[k], to_core)
        locals_.append(pltpu.make_async_copy(kept[k], mine.at[k], local_sems.at[k]))
        locals_[k].start()
    for k in range(3):
        locals_[k].wait()
        copies[k].wait_recv()
        add_rows(mine.at[k], mine.at[k], far.at[k])
        if k == 0:
            send("hx", part(mine, 0, 0), hop_x, to_x)
            send("hy", part(mine, 0, 1), hop_y, to_y)
        elif k == 1:
            send("y1", part(mine, 1, 1), part(last_y, 0, 1), to_y)
        else:
            send("x0", part(mine, 2, 0), part(last_x, 0, 0), to_x)
    copies["hx"].wait_recv()
    add_rows(part(mine, 1, 0), part(mine, 1, 0), hop_x)
    send("y0", part(mine, 1, 0), part(last_y, 0, 0), to_y)
    copies["hy"].wait_recv()
    add_rows(part(mine, 2, 1), part(mine, 2, 1), hop_y)
    send("x1", part(mine, 2, 1), part(last_x, 0, 1), to_x)
    locals_[3].wait()
    copies[3].wait_recv()
    add_rows(o_ref, mine.at[3], far.at[3])
    for p, first, second in ((1, "y1", "x1"), (0, "x0", "y0")):
        copies[first].wait_recv()
        copies[second].wait_recv()
        here = o_ref.at[pl.ds(p * half, half)]
        add_rows(here, here, part(last_x, 0, p), part(last_y, 0, p))
    for copy in copies.values():
        copy.wait_send()


def scatter_plane(p, collective_id):
    rows, columns = p.shape[0] // 8, p.shape[1]
    low = jnp.bfloat16
    return pl.pallas_call(
        functools.partial(scatter_plane_kernel, rows),
        out_shape=jax.ShapeDtypeStruct((rows, columns), jnp.float32),
        in_specs=[ANYWHERE],
        out_specs=IN_VMEM,
        scratch_shapes=[
            pltpu.VMEM((4, rows, columns), low),
            pltpu.VMEM((4, rows, columns), low),
            pltpu.VMEM((rows // 2, columns), low),
            pltpu.VMEM((rows // 2, columns), low),
            pltpu.VMEM((1, rows, columns), low),
            pltpu.VMEM((1, rows, columns), low),
            pltpu.SemaphoreType.DMA((4,)),
            pltpu.SemaphoreType.DMA((10,)),
            pltpu.SemaphoreType.DMA((10,)),
        ],
        compiler_params=pltpu.CompilerParams(
            collective_id=collective_id, has_side_effects=True, vmem_limit_bytes=VMEM_LIMIT
        ),
    )(p)


def scatter_seq_kernel(rows, p_ref, o_ref, mine, far, last, local_sems, send_sems, recv_sems):
    s, _, core, across, _ = places()
    half = rows // 2
    to_core, to_y = {"seq": core}, {"seq": across}

    def block(seq):
        return p_ref.at[pl.ds(seq * rows, rows)]

    meet(to_core, to_y)
    copies, send = sender(send_sems, recv_sems)
    given = [block((core + 2) % 4), block(core)]
    kept = [block(across), block(s)]
    locals_ = []
    for k in range(2):
        send(k, given[k], far.at[k], to_core)
        locals_.append(pltpu.make_async_copy(kept[k], mine.at[k], local_sems.at[k]))
        locals_[k].start()
    locals_[0].wait()
    copies[0].wait_recv()
    for p in range(2):
        at = pl.ds(p * half, half)
        add_rows(mine.at[0, at], mine.at[0, at], far.at[0, at])
        send(("y", p), mine.at[0, at], last.at[at], to_y)
    locals_[1].wait()
    copies[1].wait_recv()
    add_rows(o_ref, mine.at[1], far.at[1])
    for p in range(2):
        at = pl.ds(p * half, half)
        copies["y", p].wait_recv()
        add_rows(o_ref.at[at], o_ref.at[at], last.at[at])
    for copy in copies.values():
        copy.wait_send()


def scatter_seq(p, collective_id):
    rows, columns = p.shape[0] // 4, p.shape[1]
    low = jnp.bfloat16
    return pl.pallas_call(
        functools.partial(scatter_seq_kernel, rows),
        out_shape=jax.ShapeDtypeStruct((rows, columns), jnp.float32),
        in_specs=[ANYWHERE],
        out_specs=IN_VMEM,
        scratch_shapes=[
            pltpu.VMEM((2, rows, columns), low),
            pltpu.VMEM((2, rows, columns), low),
            pltpu.VMEM((rows, columns), low),
            pltpu.SemaphoreType.DMA((2,)),
            pltpu.SemaphoreType.DMA((4,)),
            pltpu.SemaphoreType.DMA((4,)),
        ],
        compiler_params=pltpu.CompilerParams(
            collective_id=collective_id, has_side_effects=True, vmem_limit_bytes=VMEM_LIMIT
        ),
    )(p)


def exchange_plane_kernel(rows, x_ref, o_ref, local_sem, send_sems, recv_sems):
    s, n, core, across, beside = places()
    diagonal = (core + 2) % 4
    mine = s * 2 + n
    others = [
        (seq, near)
        for near in (beside, n)
        for seq in (diagonal, across, core, s)
    ][:-1]

    def at(p):
        return pl.ds(p * rows, rows)

    meet(*[{"seq": seq, "near": near} for seq, near in others])
    copies, send = sender(send_sems, recv_sems)
    for seq, near in others:
        send((len(copies),), x_ref.at[at(seq * 2 + near)], o_ref.at[at(mine)], {"seq": seq, "near": near})
    local = pltpu.make_async_copy(x_ref.at[at(mine)], o_ref.at[at(mine)], local_sem)
    local.start()
    for copy in copies.values():
        copy.wait_recv()
    for copy in copies.values():
        copy.wait_send()
    local.wait()


def exchange_plane(x, collective_id):
    return pl.pallas_call(
        functools.partial(exchange_plane_kernel, x.shape[0] // 8),
        out_shape=jax.ShapeDtypeStruct(x.shape, x.dtype),
        in_specs=[ANYWHERE],
        out_specs=ANYWHERE,
        scratch_shapes=[
            pltpu.SemaphoreType.DMA,
            pltpu.SemaphoreType.DMA((7,)),
            pltpu.SemaphoreType.DMA((7,)),
        ],
        compiler_params=pltpu.CompilerParams(collective_id=collective_id, has_side_effects=True),
    )(x)


def gather_heads_kernel(far_size, w_ref, x_ref, i_ref, o_ref, ox_ref, oi_ref, local_sems, send_sems, recv_sems):
    s, n, core, across, beside = places()
    diagonal = (core + 2) % 4
    f = lax.axis_index("far")
    half = x_ref.shape[0] // 2
    to_core, to_y, to_x = {"seq": core}, {"seq": across}, {"near": beside}
    right, left = {"far": (f + 1) % far_size}, {"far": (f + far_size - 1) % far_size}

    meet(to_core, to_y, {"seq": diagonal}, to_x, right, left)
    copies, send = sender(send_sems, recv_sems)
    keep = pltpu.make_async_copy(w_ref.at[s], o_ref.at[s, f, n], local_sems.at[0])
    keep.start()
    keep_x = pltpu.make_async_copy(x_ref, ox_ref.at[s], local_sems.at[1])
    keep_x.start()
    keep_i = pltpu.make_async_copy(i_ref, oi_ref.at[s], local_sems.at[2])
    keep_i.start()
    for k, seq in enumerate((diagonal, across, core)):
        send(("w", k), w_ref.at[seq], o_ref.at[s, f, n], {"seq": seq})
        send(("i", k), i_ref, oi_ref.at[s], {"seq": seq})
    for p in range(2):
        at = pl.ds(p * half, half)
        send(("y", p), x_ref.at[at], ox_ref.at[s, at], to_y)
        send(("c", p), x_ref.at[at], ox_ref.at[s, at], to_core)
    keep.wait()
    for k in range(3):
        copies["w", k].wait_recv()

    def group(far, near):
        return o_ref.at[:, far, near]

    def along(key, far, device, sem):
        return pltpu.make_async_remote_copy(
            src_ref=group(far, n),
            dst_ref=group(far, n),
            send_sem=send_sems.at[sem],
            recv_sem=recv_sems.at[sem],
            device_id=device,
            device_id_type=MESH_IDS,
        )

    base = 12

    def beside_copy(far, sem):
        return along("x", far, to_x, sem)

    def to_right(k):
        return along("r", (f + far_size - k) % far_size, right, base + k)

    def to_left(k):
        return along("l", (f + k) % far_size, left, base + far_size + k)

    def x_from_left(k):
        return beside_copy((f + far_size - k) % far_size, base + 2 * far_size + k)

    def x_from_right(k):
        return beside_copy((f + k) % far_size, base + 3 * far_size + k)

    for k in range(far_size):
        if k > 0:

            @pl.when(f >= k)
            def _():
                to_right(k - 1).wait_recv()

        @pl.when((f >= k) & (f < far_size - 1))
        def _():
            to_right(k).start()

        if k > 0:

            @pl.when(f + k < far_size)
            def _():
                to_left(k - 1).wait_recv()

        @pl.when((f + k < far_size) & (f > 0))
        def _():
            to_left(k).start()

        if k == 0:
            x_from_left(0).start()
        else:

            @pl.when(f >= k)
            def _():
                x_from_left(k).start()

            @pl.when(f + k < far_size)
            def _():
                x_from_right(k).start()

        if k == 0:
            for p in range(2):
                at = pl.ds(p * half, half)
                copies["y", p].wait_recv()
                send(("yc", p), ox_ref.at[across, at], ox_ref.at[across, at], to_core)
    for p in range(2):
        copies["c", p].wait_recv()
        copies["yc", p].wait_recv()
    for k in range(3):
        copies["i", k].wait_recv()
    for k in range(far_size):

        @pl.when((f >= k) & (f < far_size - 1))
        def _():
            to_right(k).wait_send()

        @pl.when((f + k < far_size) & (f > 0))
        def _():
            to_left(k).wait_send()

        @pl.when(f >= k)
        def _():
            x_from_left(k).wait_recv()
            x_from_left(k).wait_send()

        if k > 0:

            @pl.when(f + k < far_size)
            def _():
                x_from_right(k).wait_recv()
                x_from_right(k).wait_send()

    for copy in copies.values():
        copy.wait_send()
    keep_x.wait()
    keep_i.wait()


def gather_heads(w, x, i, collective_id):
    far_size = lax.axis_size("far")
    _, rows, columns = w.shape
    tokens, width = x.shape
    sems = 12 + 4 * far_size
    full, all_x, all_i = pl.pallas_call(
        functools.partial(gather_heads_kernel, far_size),
        out_shape=[
            jax.ShapeDtypeStruct((4, far_size, 2, rows, columns), w.dtype),
            jax.ShapeDtypeStruct((4, tokens, width), x.dtype),
            jax.ShapeDtypeStruct((4, *i.shape), i.dtype),
        ],
        in_specs=[ANYWHERE] * 3,
        out_specs=[ANYWHERE] * 3,
        scratch_shapes=[
            pltpu.SemaphoreType.DMA((3,)),
            pltpu.SemaphoreType.DMA((sems,)),
            pltpu.SemaphoreType.DMA((sems,)),
        ],
        compiler_params=pltpu.CompilerParams(collective_id=collective_id, has_side_effects=True),
    )(w, x, i)
    return full.reshape(-1, columns), all_x.reshape(-1, width), all_i


def rotary_tables(positions, width):
    half = width // 2
    freqs = jnp.exp(-(jnp.arange(half, dtype=jnp.float32) * 2.0 / width) * math.log(ROPE_BASE))
    angles = positions.astype(jnp.float32)[..., None] * freqs
    angles = jnp.concatenate([angles, angles], -1)
    return (jnp.cos(angles)[..., None, :], jnp.sin(angles)[..., None, :])


def rotate_half(value_rows):
    half = value_rows.shape[-1] // 2
    return jnp.concatenate([-value_rows[..., half:], value_rows[..., :half]], -1)


def apply_rotary(value_rows, cosine_table, sine_table):
    return value_rows * cosine_table + rotate_half(value_rows) * sine_table


def rope_back(grads, cosine_table, sine_table):
    return grads * cosine_table - rotate_half(grads * sine_table)


def rms_normalize(value_rows):
    inverse_scale = lax.rsqrt(jnp.mean(value_rows * value_rows, -1, keepdims=True) + NORM_EPSILON)
    return (value_rows * inverse_scale, inverse_scale)


def norm_backward(unit_gradient, unit_input, inverse_scale):
    return inverse_scale * (
        unit_gradient - unit_input * jnp.mean(unit_gradient * unit_input, -1, keepdims=True)
    )


def adam_step(weight, grad, first, second, factor, rate, decay):
    clipped = grad * factor
    first_new = BETA_ONE * first + (1.0 - BETA_ONE) * clipped
    second_new = BETA_TWO * second + (1.0 - BETA_TWO) * clipped * clipped
    corr_one = 1.0 - BETA_ONE**STEP
    corr_two = 1.0 - BETA_TWO**STEP
    update = first_new / corr_one / (jnp.sqrt(second_new / corr_two) + ADAM_EPSILON)
    return (weight - rate * (update + decay * weight), first_new, second_new)


def product(left, right, left_dim, right_dim):
    return lax.dot_general(
        left, right, (((left_dim,), (right_dim,)), ((), ())), preferred_element_type=jnp.float32
    )


CHUNKS = 2


def shards(
    inputs,
    cotangent,
    lengths,
    positions,
    query_key_value_weight,
    out_weight,
    gateup_weight,
    down_weight,
    norm_gains,
    query_key_value_moment,
    output_weight_moment,
    gate_up_moment,
    down_weight_moment,
    norm_gains_moment,
    query_key_value_variance,
    out_second,
    gateup_second,
    down_second,
    gains_second,
):
    _, here, width = inputs.shape
    seq = lax.axis_size("seq")
    far = lax.axis_size("far")
    group = seq * 2
    rows = out_weight.shape[0]
    full = here * seq
    heads_here = QUERY_HEAD_COUNT // seq
    local_kv = KEY_VALUE_HEADS // seq
    per_kv = QUERY_HEAD_COUNT // KEY_VALUE_HEADS
    query_width = QUERY_HEAD_COUNT * HEAD_SIZE
    key_width = KEY_VALUE_HEADS * HEAD_SIZE
    mine_q, mine_k = query_width // seq, key_width // seq
    mine_qkv = mine_q + 2 * mine_k
    units = FEED_UNITS // group
    part = units // CHUNKS
    factor = 1.0 / math.sqrt(HEAD_SIZE)
    low = jnp.bfloat16

    inputs = inputs[0]
    cotangent = cotangent[0]
    length = lengths[0]
    gains = norm_gains.astype(low).astype(jnp.float32)
    gain_one, gain_two = gains[:, :1], gains[:, 1:]

    def rounded(weight, gain=None):
        weight = weight.astype(low)
        return weight if gain is None else (weight.astype(jnp.float32) * gain).astype(low)

    def far_first(x):
        x = x.reshape(-1, seq, far, 2 * rows).transpose(0, 2, 1, 3)
        return x.reshape(-1, width)

    def far_last(x):
        return x.reshape(-1, far, seq, 2 * rows).transpose(0, 2, 1, 3).reshape(-1, width)

    gateup_low = rounded(gateup_weight, gain_two).reshape(rows, 2, group, CHUNKS, part)
    down_low = rounded(down_weight).reshape(rows, 1, group, CHUNKS, part)
    feed_pieces = jnp.concatenate([gateup_low, down_low], 1).transpose(3, 2, 0, 1, 4)
    feed_pieces = feed_pieces.reshape(CHUNKS, group * rows, 3 * part)
    feed = []
    for c in range(CHUNKS):
        piece = exchange_plane(feed_pieces[c], 1)
        feed.append(lax.all_gather(piece, "far", axis=0, tiled=True))

    qkv_low = rounded(query_key_value_weight, gain_one)
    head_pieces = jnp.concatenate(
        [
            qkv_low[:, :query_width].reshape(rows, seq, mine_q),
            qkv_low[:, query_width : query_width + key_width].reshape(rows, seq, mine_k),
            qkv_low[:, query_width + key_width :].reshape(rows, seq, mine_k),
            rounded(out_weight).reshape(rows, seq, mine_q),
        ],
        2,
    ).transpose(1, 0, 2)
    unit_one, scale_one = rms_normalize(inputs)
    spots = jnp.pad(positions.reshape(-1, 128), ((0, 8 - here // 128), (0, 0)))
    head_w, normed_one, all_spots = gather_heads(head_pieces, unit_one.astype(low), spots, 2)
    qkv, out = head_w[:, :mine_qkv], head_w[:, mine_qkv:]
    all_positions = all_spots[:, : here // 128].reshape(full)

    cos, sin = rotary_tables(all_positions, HEAD_SIZE)
    merged = product(normed_one, qkv, 1, 0)
    queries = apply_rotary(merged[:, :mine_q].reshape(full, heads_here, HEAD_SIZE), cos, sin)
    queries = queries.astype(low).reshape(full, local_kv, per_kv, HEAD_SIZE)
    keys = apply_rotary(
        merged[:, mine_q : mine_q + mine_k].reshape(full, local_kv, HEAD_SIZE), cos, sin
    ).astype(low)
    values = merged[:, mine_q + mine_k :].reshape(full, local_kv, HEAD_SIZE).astype(low)

    spot = jnp.arange(full)
    visible = (spot[None, :] <= spot[:, None]) & (spot < length)[None, :]
    live = (spot < length)[:, None, None, None]
    scores = jnp.einsum("qkgd,jkd->kgqj", queries, keys, preferred_element_type=jnp.float32)
    scores = jnp.where(visible, scores * factor, MASKED_SCORE)
    peak = jnp.max(scores, -1, keepdims=True)
    expo = jnp.exp(scores - peak)
    probs = expo / jnp.sum(expo, -1, keepdims=True)
    probs_low = probs.astype(low)
    heads = jnp.einsum("kgqj,jkd->qkgd", probs_low, values, preferred_element_type=jnp.float32)
    heads = (heads * live).astype(low).reshape(full, mine_q)
    hidden = inputs + scatter_seq(product(heads, out, 1, 1).astype(low), 3)
    unit_two, scale_two = rms_normalize(hidden)
    normed_two = gather_plane(far_first(unit_two.astype(low)), 4)
    dout = gather_plane(far_first(cotangent.astype(low)), 4)

    dnormed_two, output_terms, feed_grads = 0.0, 0.0, []
    for w in feed:
        gateup_w, down_w = w[:, : 2 * part], w[:, 2 * part :]
        gate = product(normed_two, gateup_w[:, :part], 1, 0)
        upper = product(normed_two, gateup_w[:, part:], 1, 0)
        sig = jax.nn.sigmoid(gate)
        act = (gate * sig * upper).astype(low)
        dact = product(dout, down_w, 1, 0)
        dgate = dact * upper * sig * (1.0 + gate * (1.0 - sig))
        dupper = dact * gate * sig
        dgateup = jnp.concatenate([dgate.astype(low), dupper.astype(low)], 1)
        terms = jnp.concatenate(
            [
                product(normed_two, dgateup, 0, 0).astype(low),
                product(dout, act, 0, 0).astype(low),
            ],
            1,
        )
        feed_grads.append(lax.psum_scatter(terms, "far", scatter_dimension=0, tiled=True))
        dnormed_two = dnormed_two + product(dgateup, gateup_w, 1, 1)
        output_terms = output_terms + product(act, down_w, 1, 1)
    dnormed_two = far_last(scatter_plane(dnormed_two.astype(low), 5))
    back_two = norm_backward(dnormed_two, unit_two, scale_two)
    dhidden = cotangent + back_two

    dattended = gather_seq(dhidden.astype(low), 6)
    dheads = product(dattended, out, 1, 0).astype(low).reshape(full, local_kv, per_kv, HEAD_SIZE)
    dheads = dheads * live.astype(low)
    dvalues = jnp.einsum("kgqj,qkgd->jkd", probs_low, dheads, preferred_element_type=jnp.float32)
    dprobs = jnp.einsum("qkgd,jkd->kgqj", dheads, values, preferred_element_type=jnp.float32)
    inner = jnp.sum(probs * dprobs, -1, keepdims=True)
    dscores = jnp.where(visible, (probs * (dprobs - inner)).astype(low), jnp.zeros((), low))
    dqueries = jnp.einsum("kgqj,jkd->qkgd", dscores, keys, preferred_element_type=jnp.float32)
    dkeys = jnp.einsum("kgqj,qkgd->jkd", dscores, queries, preferred_element_type=jnp.float32)
    dqueries = (dqueries * factor).astype(low).reshape(full, heads_here, HEAD_SIZE)
    dkeys = (dkeys * factor).astype(low)
    dfused = jnp.concatenate(
        [
            rope_back(dqueries.astype(jnp.float32), cos, sin).astype(low).reshape(full, mine_q),
            rope_back(dkeys.astype(jnp.float32), cos, sin).astype(low).reshape(full, mine_k),
            dvalues.astype(low).reshape(full, mine_k),
        ],
        1,
    )
    head_terms = jnp.concatenate(
        [
            product(normed_one, dfused, 0, 0).astype(low),
            product(dattended, heads, 0, 0).astype(low),
        ],
        1,
    )
    head_terms = head_terms.reshape(seq, far * 2, rows, -1).transpose(1, 0, 2, 3)
    head_terms = lax.psum_scatter(
        head_terms.reshape(width, -1), ("far", "near"), scatter_dimension=0, tiled=True
    )
    dnormed_one = scatter_seq(product(dfused, qkv, 1, 1).astype(low), 3)
    back_one = norm_backward(dnormed_one, unit_one, scale_one)
    input_grad = dhidden + back_one
    layer_output = hidden + far_last(scatter_plane(output_terms.astype(low), 5))

    head_grads = lax.all_to_all(head_terms.reshape(seq, rows, -1), "seq", 0, 0, tiled=True)
    head_grads = head_grads.astype(jnp.float32)

    def head_rows(start, size):
        return head_grads[:, :, start : start + size].transpose(1, 0, 2).reshape(rows, -1)

    grad_qkv = jnp.concatenate(
        [head_rows(0, mine_q), head_rows(mine_q, mine_k), head_rows(mine_q + mine_k, mine_k)], 1
    )
    grad_out = head_rows(mine_qkv, mine_q)
    feed_grads = jnp.stack(
        [exchange_plane(grads, 1).reshape(group, rows, 3, part) for grads in feed_grads], 3
    ).astype(jnp.float32)
    feed_grads = feed_grads.transpose(1, 2, 0, 3, 4)
    grad_gateup = feed_grads[:, :2].reshape(rows, 2 * FEED_UNITS)
    grad_down = feed_grads[:, 2].reshape(rows, FEED_UNITS)

    gain_term_one = jnp.sum(rounded(query_key_value_weight) * grad_qkv, 1, keepdims=True)
    gain_term_two = jnp.sum(rounded(gateup_weight) * grad_gateup, 1, keepdims=True)
    grad_gains = jnp.concatenate([gain_term_one, gain_term_two], 1)
    grad_qkv = grad_qkv * gain_one
    grad_gateup = grad_gateup * gain_two

    local_squares = (
        jnp.sum(grad_qkv * grad_qkv)
        + jnp.sum(grad_out * grad_out)
        + jnp.sum(grad_gateup * grad_gateup)
        + jnp.sum(grad_down * grad_down)
        + jnp.sum(grad_gains * grad_gains)
    )
    grad_norm = jnp.sqrt(lax.psum(local_squares, EVERY))
    clip = CLIP_NORM / jnp.maximum(grad_norm, CLIP_NORM)
    steps = (
        (query_key_value_weight, grad_qkv, query_key_value_moment, query_key_value_variance, RATE_MATRIX, DECAY_MATRIX),
        (out_weight, grad_out, output_weight_moment, out_second, RATE_OUTPUT, DECAY_MATRIX),
        (gateup_weight, grad_gateup, gate_up_moment, gateup_second, RATE_MATRIX, DECAY_MATRIX),
        (down_weight, grad_down, down_weight_moment, down_second, RATE_MATRIX, DECAY_MATRIX),
        (norm_gains, grad_gains, norm_gains_moment, gains_second, RATE_GAIN, 0.0),
    )
    stepped = [adam_step(w, g, m, v, clip, rate, decay) for w, g, m, v, rate, decay in steps]
    nexts, firsts, seconds = zip(*stepped)
    return (layer_output[None], input_grad[None], grad_norm, *nexts, *firsts, *seconds)


def solution(mesh):
    seq, fsdp = mesh.shape["seq"], mesh.shape["fsdp"]
    cut = Mesh(mesh.devices.reshape(seq, fsdp // 2, 2), EVERY)
    tokens = P(("far", "near"), "seq", None)
    matrix = P(EVERY, None)
    return jax.shard_map(
        shards,
        mesh=cut,
        in_specs=(tokens, tokens, P(("far", "near")), P(("far", "near"), "seq")) + (matrix,) * 15,
        out_specs=(tokens, tokens, P()) + (matrix,) * 15,
        check_vma=False,
    )
```

```python
import functools
import math

import jax
import jax.numpy as jnp
from jax import lax
from jax.experimental import pallas as pl
from jax.experimental.pallas import tpu as pltpu
from jax.sharding import Mesh, PartitionSpec as P

QUERY_HEAD_COUNT = 8
KEY_VALUE_HEADS = 4
HEAD_SIZE = 256
FEED_UNITS = 8192
STEP = 10

NORM_EPSILON = 1e-06
ROPE_BASE = 1000042.0
MASKED_SCORE = -1000000000.0
CLIP_NORM = 1.0
BETA_ONE = 0.9
BETA_TWO = 0.95
ADAM_EPSILON = 1e-08
DECAY_MATRIX = 0.1
RATE_MATRIX = 0.02
RATE_OUTPUT = 0.1
RATE_GAIN = 1.0

EVERY = ("seq", "far", "near")
TP = ("seq", "near")


MESH_IDS = pl.DeviceIdType.MESH
ANYWHERE = pl.BlockSpec(memory_space=pl.ANY)
IN_VMEM = pl.BlockSpec(memory_space=pltpu.VMEM)
VMEM_LIMIT = 60 * 1024 * 1024


def places():
    s, n = lax.axis_index("seq"), lax.axis_index("near")
    return s, n, s + 1 - 2 * (s % 2), (s + 2) % 4, 1 - n


def meet(*others):
    barrier = pltpu.get_barrier_semaphore()
    for other in others:
        pl.semaphore_signal(barrier, inc=1, device_id=other, device_id_type=MESH_IDS)
    pl.semaphore_wait(barrier, len(others))


def sender(send_sems, recv_sems):
    copies = {}

    def send(key, source, target, device):
        at = len(copies)
        copies[key] = pltpu.make_async_remote_copy(
            src_ref=source,
            dst_ref=target,
            send_sem=send_sems.at[at],
            recv_sem=recv_sems.at[at],
            device_id=device,
            device_id_type=MESH_IDS,
        )
        copies[key].start()

    return copies, send


def gather_plane_kernel(rows, x_ref, o_ref, local_sem, send_sems, recv_sems):
    s, n, core, across, beside = places()
    half = rows // 2
    to_core, to_y, to_x = {"seq": core}, {"seq": across}, {"near": beside}

    def block(seq, near, part):
        return o_ref.at[pl.ds((seq * 2 + near) * rows + part * half, half)]

    def own(part):
        return x_ref.at[pl.ds(part * half, half)]

    meet(to_core, to_y, to_x)
    local = pltpu.make_async_copy(x_ref, o_ref.at[pl.ds((s * 2 + n) * rows, rows)], local_sem)
    local.start()
    copies, send = sender(send_sems, recv_sems)
    send("y0", own(0), block(s, n, 0), to_y)
    send("x1", own(1), block(s, n, 1), to_x)
    send("y1", own(1), block(s, n, 1), to_y)
    send("x0", own(0), block(s, n, 0), to_x)
    send("c0", own(0), block(s, n, 0), to_core)
    send("c1", own(1), block(s, n, 1), to_core)
    copies["y0"].wait_recv()
    send("yx", block(across, n, 0), block(across, n, 0), to_x)
    send("yc0", block(across, n, 0), block(across, n, 0), to_core)
    copies["x1"].wait_recv()
    send("xy", block(s, beside, 1), block(s, beside, 1), to_y)
    send("xc1", block(s, beside, 1), block(s, beside, 1), to_core)
    copies["y1"].wait_recv()
    send("yc1", block(across, n, 1), block(across, n, 1), to_core)
    copies["x0"].wait_recv()
    send("xc0", block(s, beside, 0), block(s, beside, 0), to_core)
    copies["yx"].wait_recv()
    send("dc0", block(across, beside, 0), block(across, beside, 0), to_core)
    copies["xy"].wait_recv()
    send("dc1", block(across, beside, 1), block(across, beside, 1), to_core)
    for key in ("c0", "c1", "yc0", "yc1", "xc0", "xc1", "dc0", "dc1"):
        copies[key].wait_recv()
    for copy in copies.values():
        copy.wait_send()
    local.wait()


def gather_plane(x, collective_id):
    rows, columns = x.shape
    return pl.pallas_call(
        functools.partial(gather_plane_kernel, rows),
        out_shape=jax.ShapeDtypeStruct((8 * rows, columns), x.dtype),
        in_specs=[ANYWHERE],
        out_specs=ANYWHERE,
        scratch_shapes=[
            pltpu.SemaphoreType.DMA,
            pltpu.SemaphoreType.DMA((14,)),
            pltpu.SemaphoreType.DMA((14,)),
        ],
        compiler_params=pltpu.CompilerParams(collective_id=collective_id, has_side_effects=True),
    )(x)


def gather_seq_kernel(rows, x_ref, o_ref, local_sem, send_sems, recv_sems):
    s, _, core, across, _ = places()
    half = rows // 2
    to_core, to_y = {"seq": core}, {"seq": across}

    def block(seq, part):
        return o_ref.at[pl.ds(seq * rows + part * half, half)]

    def own(part):
        return x_ref.at[pl.ds(part * half, half)]

    meet(to_core, to_y)
    local = pltpu.make_async_copy(x_ref, o_ref.at[pl.ds(s * rows, rows)], local_sem)
    local.start()
    copies, send = sender(send_sems, recv_sems)
    for part in range(2):
        send(("y", part), own(part), block(s, part), to_y)
    for part in range(2):
        send(("c", part), own(part), block(s, part), to_core)
    for part in range(2):
        copies["y", part].wait_recv()
        send(("yc", part), block(across, part), block(across, part), to_core)
    for part in range(2):
        copies["c", part].wait_recv()
        copies["yc", part].wait_recv()
    for copy in copies.values():
        copy.wait_send()
    local.wait()


def gather_seq(x, collective_id):
    rows, columns = x.shape
    return pl.pallas_call(
        functools.partial(gather_seq_kernel, rows),
        out_shape=jax.ShapeDtypeStruct((4 * rows, columns), x.dtype),
        in_specs=[ANYWHERE],
        out_specs=ANYWHERE,
        scratch_shapes=[
            pltpu.SemaphoreType.DMA,
            pltpu.SemaphoreType.DMA((6,)),
            pltpu.SemaphoreType.DMA((6,)),
        ],
        compiler_params=pltpu.CompilerParams(collective_id=collective_id, has_side_effects=True),
    )(x)


def add_rows(target, first, second, third=None, step=64):
    rows = target.shape[0]

    def body(i, carry):
        at = pl.ds(pl.multiple_of(i * step, step), step)
        total = first[at, :].astype(jnp.float32) + second[at, :].astype(jnp.float32)
        if third is not None:
            total = total + third[at, :].astype(jnp.float32)
        target[at, :] = total.astype(target.dtype)
        return carry

    lax.fori_loop(0, rows // step, body, 0)


def scatter_plane_kernel(rows, p_ref, o_ref, mine, far, hop_x, hop_y, last_x, last_y, local_sems, send_sems, recv_sems):
    s, n, core, across, beside = places()
    half = rows // 2
    to_core, to_y, to_x = {"seq": core}, {"seq": across}, {"near": beside}

    def block(seq, near):
        return p_ref.at[pl.ds((seq * 2 + near) * rows, rows)]

    def part(ref, at, p):
        return ref.at[at, pl.ds(p * half, half)]

    meet(to_core, to_y, to_x)
    copies, send = sender(send_sems, recv_sems)
    other = (core + 2) % 4
    given = [block(other, beside), block(other, n), block(core, beside), block(core, n)]
    kept = [block(across, beside), block(across, n), block(s, beside), block(s, n)]
    locals_ = []
    for k in range(4):
        send(k, given[k], far.at[k], to_core)
        locals_.append(pltpu.make_async_copy(kept[k], mine.at[k], local_sems.at[k]))
        locals_[k].start()
    for k in range(3):
        locals_[k].wait()
        copies[k].wait_recv()
        add_rows(mine.at[k], mine.at[k], far.at[k])
        if k == 0:
            send("hx", part(mine, 0, 0), hop_x, to_x)
            send("hy", part(mine, 0, 1), hop_y, to_y)
        elif k == 1:
            send("y1", part(mine, 1, 1), part(last_y, 0, 1), to_y)
        else:
            send("x0", part(mine, 2, 0), part(last_x, 0, 0), to_x)
    copies["hx"].wait_recv()
    add_rows(part(mine, 1, 0), part(mine, 1, 0), hop_x)
    send("y0", part(mine, 1, 0), part(last_y, 0, 0), to_y)
    copies["hy"].wait_recv()
    add_rows(part(mine, 2, 1), part(mine, 2, 1), hop_y)
    send("x1", part(mine, 2, 1), part(last_x, 0, 1), to_x)
    locals_[3].wait()
    copies[3].wait_recv()
    add_rows(o_ref, mine.at[3], far.at[3])
    for p, first, second in ((1, "y1", "x1"), (0, "x0", "y0")):
        copies[first].wait_recv()
        copies[second].wait_recv()
        here = o_ref.at[pl.ds(p * half, half)]
        add_rows(here, here, part(last_x, 0, p), part(last_y, 0, p))
    for copy in copies.values():
        copy.wait_send()


def scatter_plane(p, collective_id):
    rows, columns = p.shape[0] // 8, p.shape[1]
    low = jnp.bfloat16
    return pl.pallas_call(
        functools.partial(scatter_plane_kernel, rows),
        out_shape=jax.ShapeDtypeStruct((rows, columns), jnp.float32),
        in_specs=[ANYWHERE],
        out_specs=IN_VMEM,
        scratch_shapes=[
            pltpu.VMEM((4, rows, columns), low),
            pltpu.VMEM((4, rows, columns), low),
            pltpu.VMEM((rows // 2, columns), low),
            pltpu.VMEM((rows // 2, columns), low),
            pltpu.VMEM((1, rows, columns), low),
            pltpu.VMEM((1, rows, columns), low),
            pltpu.SemaphoreType.DMA((4,)),
            pltpu.SemaphoreType.DMA((10,)),
            pltpu.SemaphoreType.DMA((10,)),
        ],
        compiler_params=pltpu.CompilerParams(
            collective_id=collective_id, has_side_effects=True, vmem_limit_bytes=VMEM_LIMIT
        ),
    )(p)


def scatter_seq_kernel(rows, p_ref, o_ref, mine, far, last, local_sems, send_sems, recv_sems):
    s, _, core, across, _ = places()
    half = rows // 2
    to_core, to_y = {"seq": core}, {"seq": across}

    def block(seq):
        return p_ref.at[pl.ds(seq * rows, rows)]

    meet(to_core, to_y)
    copies, send = sender(send_sems, recv_sems)
    given = [block((core + 2) % 4), block(core)]
    kept = [block(across), block(s)]
    locals_ = []
    for k in range(2):
        send(k, given[k], far.at[k], to_core)
        locals_.append(pltpu.make_async_copy(kept[k], mine.at[k], local_sems.at[k]))
        locals_[k].start()
    locals_[0].wait()
    copies[0].wait_recv()
    for p in range(2):
        at = pl.ds(p * half, half)
        add_rows(mine.at[0, at], mine.at[0, at], far.at[0, at])
        send(("y", p), mine.at[0, at], last.at[at], to_y)
    locals_[1].wait()
    copies[1].wait_recv()
    add_rows(o_ref, mine.at[1], far.at[1])
    for p in range(2):
        at = pl.ds(p * half, half)
        copies["y", p].wait_recv()
        add_rows(o_ref.at[at], o_ref.at[at], last.at[at])
    for copy in copies.values():
        copy.wait_send()


def scatter_seq(p, collective_id):
    rows, columns = p.shape[0] // 4, p.shape[1]
    low = jnp.bfloat16
    return pl.pallas_call(
        functools.partial(scatter_seq_kernel, rows),
        out_shape=jax.ShapeDtypeStruct((rows, columns), jnp.float32),
        in_specs=[ANYWHERE],
        out_specs=IN_VMEM,
        scratch_shapes=[
            pltpu.VMEM((2, rows, columns), low),
            pltpu.VMEM((2, rows, columns), low),
            pltpu.VMEM((rows, columns), low),
            pltpu.SemaphoreType.DMA((2,)),
            pltpu.SemaphoreType.DMA((4,)),
            pltpu.SemaphoreType.DMA((4,)),
        ],
        compiler_params=pltpu.CompilerParams(
            collective_id=collective_id, has_side_effects=True, vmem_limit_bytes=VMEM_LIMIT
        ),
    )(p)


def exchange_plane_kernel(count, *refs):
    x_refs, o_refs = refs[:count], refs[count : 2 * count]
    local_sems, send_sems, recv_sems = refs[2 * count :]
    s, n, core, across, beside = places()
    diagonal = (core + 2) % 4
    mine = s * 2 + n
    others = [(seq, near) for near in (beside, n) for seq in (diagonal, across, core, s)][:-1]

    meet(*[{"seq": seq, "near": near} for seq, near in others])
    copies, send = sender(send_sems, recv_sems)
    locals_ = []
    for k, (x_ref, o_ref) in enumerate(zip(x_refs, o_refs)):
        rows = x_ref.shape[0] // 8

        def at(p):
            return pl.ds(p * rows, rows)

        for seq, near in others:
            target = {"seq": seq, "near": near}
            send(len(copies), x_ref.at[at(seq * 2 + near)], o_ref.at[at(mine)], target)
        locals_.append(pltpu.make_async_copy(x_ref.at[at(mine)], o_ref.at[at(mine)], local_sems.at[k]))
        locals_[k].start()
    for copy in copies.values():
        copy.wait_recv()
    for copy in copies.values():
        copy.wait_send()
    for copy in locals_:
        copy.wait()


def exchange_plane(arrays, collective_id):
    count = len(arrays)
    return pl.pallas_call(
        functools.partial(exchange_plane_kernel, count),
        out_shape=[jax.ShapeDtypeStruct(x.shape, x.dtype) for x in arrays],
        in_specs=[ANYWHERE] * count,
        out_specs=[ANYWHERE] * count,
        scratch_shapes=[
            pltpu.SemaphoreType.DMA((count,)),
            pltpu.SemaphoreType.DMA((7 * count,)),
            pltpu.SemaphoreType.DMA((7 * count,)),
        ],
        compiler_params=pltpu.CompilerParams(collective_id=collective_id, has_side_effects=True),
    )(*arrays)


def scatter_near_kernel(p_ref, o_ref, mine, theirs, local_sems, out_sems, send_sems, recv_sems):
    _, n, _, _, beside = places()
    to_x = {"near": beside}
    far_size = p_ref.shape[1]
    meet(to_x)
    copies, send = sender(send_sems, recv_sems)
    locals_, outs = [], []
    for f in range(far_size):
        send(f, p_ref.at[:, f, beside], theirs.at[f], to_x)
        locals_.append(pltpu.make_async_copy(p_ref.at[:, f, n], mine.at[f], local_sems.at[f]))
        locals_[f].start()
    for f in range(far_size):
        locals_[f].wait()
        copies[f].wait_recv()
        for q in range(4):
            add_rows(mine.at[f, q], mine.at[f, q], theirs.at[f, q], step=16)
        outs.append(pltpu.make_async_copy(mine.at[f], o_ref.at[f], out_sems.at[f]))
        outs[f].start()
    for f in range(far_size):
        outs[f].wait()
        copies[f].wait_send()


def scatter_near(p, collective_id):
    seq, far_size, _, rows, columns = p.shape
    return pl.pallas_call(
        scatter_near_kernel,
        out_shape=jax.ShapeDtypeStruct((far_size, seq, rows, columns), p.dtype),
        in_specs=[ANYWHERE],
        out_specs=ANYWHERE,
        scratch_shapes=[
            pltpu.VMEM((far_size, seq, rows, columns), p.dtype),
            pltpu.VMEM((far_size, seq, rows, columns), p.dtype),
            pltpu.SemaphoreType.DMA((far_size,)),
            pltpu.SemaphoreType.DMA((far_size,)),
            pltpu.SemaphoreType.DMA((far_size,)),
            pltpu.SemaphoreType.DMA((far_size,)),
        ],
        compiler_params=pltpu.CompilerParams(
            collective_id=collective_id, has_side_effects=True, vmem_limit_bytes=VMEM_LIMIT
        ),
    )(p)


def gather_heads_kernel(
    far_size,
    w_ref,
    x_ref,
    i_ref,
    d_ref,
    e_ref,
    o_ref,
    ox_ref,
    oi_ref,
    od_ref,
    oe_ref,
    local_sems,
    send_sems,
    recv_sems,
):
    s, n, core, across, beside = places()
    diagonal = (core + 2) % 4
    f = lax.axis_index("far")
    half = x_ref.shape[0] // 2
    to_core, to_y, to_x = {"seq": core}, {"seq": across}, {"near": beside}
    right, left = {"far": (f + 1) % far_size}, {"far": (f + far_size - 1) % far_size}

    others = [(seq, near) for near in (beside, n) for seq in (diagonal, across, core, s)][:-1]
    meet(*[{"seq": seq, "near": near} for seq, near in others], right, left)
    copies, send = sender(send_sems, recv_sems)
    keep = pltpu.make_async_copy(w_ref.at[s], o_ref.at[s, f, n], local_sems.at[0])
    keep.start()
    keep_x = pltpu.make_async_copy(x_ref, ox_ref.at[s], local_sems.at[1])
    keep_x.start()
    keep_i = pltpu.make_async_copy(i_ref, oi_ref.at[s], local_sems.at[2])
    keep_i.start()
    for k, seq in enumerate((diagonal, across, core)):
        send(("w", k), w_ref.at[seq], o_ref.at[s, f, n], {"seq": seq})
        send(("i", k), i_ref, oi_ref.at[s], {"seq": seq})
    for p in range(2):
        at = pl.ds(p * half, half)
        send(("y", p), x_ref.at[at], ox_ref.at[s, at], to_y)
        send(("c", p), x_ref.at[at], ox_ref.at[s, at], to_core)

    def block(seq, near, p):
        return od_ref.at[seq * 2 + near, pl.ds(p * half, half)]

    def own(p):
        return d_ref.at[pl.ds(p * half, half)]

    keep_d = pltpu.make_async_copy(d_ref, od_ref.at[s * 2 + n], local_sems.at[3])
    keep_d.start()
    send("y0", own(0), block(s, n, 0), to_y)
    send("x1", own(1), block(s, n, 1), to_x)
    send("y1", own(1), block(s, n, 1), to_y)
    send("x0", own(0), block(s, n, 0), to_x)
    send("c0", own(0), block(s, n, 0), to_core)
    send("c1", own(1), block(s, n, 1), to_core)
    keep_e = pltpu.make_async_copy(e_ref.at[s * 2 + n], oe_ref.at[s * 2 + n], local_sems.at[4])
    keep_e.start()
    for k, (seq, near) in enumerate(others):
        target = {"seq": seq, "near": near}
        send(("e", k), e_ref.at[seq * 2 + near], oe_ref.at[s * 2 + n], target)
    keep.wait()
    for k in range(3):
        copies["w", k].wait_recv()

    def group(far, near):
        return o_ref.at[:, far, near]

    def along(key, far, device, sem):
        return pltpu.make_async_remote_copy(
            src_ref=group(far, n),
            dst_ref=group(far, n),
            send_sem=send_sems.at[sem],
            recv_sem=recv_sems.at[sem],
            device_id=device,
            device_id_type=MESH_IDS,
        )

    base = 33

    def beside_copy(far, sem):
        return along("x", far, to_x, sem)

    def to_right(k):
        return along("r", (f + far_size - k) % far_size, right, base + k)

    def to_left(k):
        return along("l", (f + k) % far_size, left, base + far_size + k)

    def x_from_left(k):
        return beside_copy((f + far_size - k) % far_size, base + 2 * far_size + k)

    def x_from_right(k):
        return beside_copy((f + k) % far_size, base + 3 * far_size + k)

    for k in range(far_size):
        if k > 0:

            @pl.when(f >= k)
            def _():
                to_right(k - 1).wait_recv()

        @pl.when((f >= k) & (f < far_size - 1))
        def _():
            to_right(k).start()

        if k > 0:

            @pl.when(f + k < far_size)
            def _():
                to_left(k - 1).wait_recv()

        @pl.when((f + k < far_size) & (f > 0))
        def _():
            to_left(k).start()

        if k == 0:
            x_from_left(0).start()
        else:

            @pl.when(f >= k)
            def _():
                x_from_left(k).start()

            @pl.when(f + k < far_size)
            def _():
                x_from_right(k).start()

        if k == 0:
            for p in range(2):
                at = pl.ds(p * half, half)
                copies["y", p].wait_recv()
                send(("yc", p), ox_ref.at[across, at], ox_ref.at[across, at], to_core)
        if k == 1:
            copies["y0"].wait_recv()
            send("yx", block(across, n, 0), block(across, n, 0), to_x)
            send("yc0", block(across, n, 0), block(across, n, 0), to_core)
            copies["x1"].wait_recv()
            send("xy", block(s, beside, 1), block(s, beside, 1), to_y)
            send("xc1", block(s, beside, 1), block(s, beside, 1), to_core)
            copies["y1"].wait_recv()
            send("yc1", block(across, n, 1), block(across, n, 1), to_core)
            copies["x0"].wait_recv()
            send("xc0", block(s, beside, 0), block(s, beside, 0), to_core)
        if k == min(2, far_size - 1):
            copies["yx"].wait_recv()
            send("dc0", block(across, beside, 0), block(across, beside, 0), to_core)
            copies["xy"].wait_recv()
            send("dc1", block(across, beside, 1), block(across, beside, 1), to_core)
    for key in ("c0", "c1", "yc0", "yc1", "xc0", "xc1", "dc0", "dc1"):
        copies[key].wait_recv()
    for p in range(2):
        copies["c", p].wait_recv()
        copies["yc", p].wait_recv()
    for k in range(3):
        copies["i", k].wait_recv()
    for k in range(7):
        copies["e", k].wait_recv()
    for k in range(far_size):

        @pl.when((f >= k) & (f < far_size - 1))
        def _():
            to_right(k).wait_send()

        @pl.when((f + k < far_size) & (f > 0))
        def _():
            to_left(k).wait_send()

        @pl.when(f >= k)
        def _():
            x_from_left(k).wait_recv()
            x_from_left(k).wait_send()

        if k > 0:

            @pl.when(f + k < far_size)
            def _():
                x_from_right(k).wait_recv()
                x_from_right(k).wait_send()

    for copy in copies.values():
        copy.wait_send()
    keep_x.wait()
    keep_i.wait()
    keep_d.wait()
    keep_e.wait()


def gather_heads(w, x, i, d, e, collective_id):
    far_size = lax.axis_size("far")
    _, rows, columns = w.shape
    tokens, width = x.shape
    sems = 33 + 4 * far_size
    full, all_x, all_i, all_d, mine_e = pl.pallas_call(
        functools.partial(gather_heads_kernel, far_size),
        out_shape=[
            jax.ShapeDtypeStruct((4, far_size, 2, rows, columns), w.dtype),
            jax.ShapeDtypeStruct((4, tokens, width), x.dtype),
            jax.ShapeDtypeStruct((4, *i.shape), i.dtype),
            jax.ShapeDtypeStruct((8, *d.shape), d.dtype),
            jax.ShapeDtypeStruct(e.shape, e.dtype),
        ],
        in_specs=[ANYWHERE] * 5,
        out_specs=[ANYWHERE] * 5,
        scratch_shapes=[
            pltpu.SemaphoreType.DMA((5,)),
            pltpu.SemaphoreType.DMA((sems,)),
            pltpu.SemaphoreType.DMA((sems,)),
        ],
        compiler_params=pltpu.CompilerParams(collective_id=collective_id, has_side_effects=True),
    )(w, x, i, d, e)
    all_x, all_d = all_x.reshape(-1, width), all_d.reshape(-1, d.shape[1])
    return full.reshape(-1, columns), all_x, all_i, all_d, mine_e


def feed_kernel(x_ref, d_ref, w_ref, *refs):
    before, (act_ref, dgu_ref, y_ref, dx_ref) = refs[:-4], refs[-4:]
    part = w_ref.shape[1] // 3
    low = jnp.bfloat16
    x = x_ref[...]
    gate = product(x, w_ref[:, :part], 1, 0)
    upper = product(x, w_ref[:, part : 2 * part], 1, 0)
    dact = product(d_ref[...], w_ref[:, 2 * part :], 1, 0)
    sig = 1.0 / (1.0 + jnp.exp(-gate))
    silu = gate * sig
    act = (silu * upper).astype(low)
    act_ref[...] = act
    dgu_ref[:, :part] = (dact * upper * (sig + silu * (1.0 - sig))).astype(low)
    dgu_ref[:, part:] = (dact * silu).astype(low)
    y = product(act, w_ref[:, 2 * part :], 1, 1)
    dx = product(dgu_ref[...], w_ref[:, : 2 * part], 1, 1)
    if before:
        y = y + before[0][...].astype(jnp.float32)
        dx = dx + before[1][...].astype(jnp.float32)
    y_ref[...] = y.astype(low)
    dx_ref[...] = dx.astype(low)


def feed(x, d, w, before, tile=512):
    tokens, width = x.shape
    part = w.shape[1] // 3
    low = jnp.bfloat16

    def tokens_of(columns):
        return pl.BlockSpec((tile, columns), lambda t: (t, 0))

    whole = pl.BlockSpec(w.shape, lambda t: (0, 0), pipeline_mode=pl.Buffered(1))
    sizes = (part, 2 * part, width, width)
    return pl.pallas_call(
        feed_kernel,
        grid=(tokens // tile,),
        out_shape=[jax.ShapeDtypeStruct((tokens, columns), low) for columns in sizes],
        in_specs=[tokens_of(width), tokens_of(width), whole] + [tokens_of(width)] * len(before),
        out_specs=[tokens_of(columns) for columns in sizes],
        compiler_params=pltpu.CompilerParams(vmem_limit_bytes=VMEM_LIMIT),
        cost_estimate=pl.CostEstimate(flops=12 * tokens * width * part, bytes_accessed=60_000_000, transcendentals=0),
    )(x, d, w, *before)


def feed_grads_kernel(x_ref, d_ref, dgu_ref, act_ref, o_ref):
    split = dgu_ref.shape[1]
    o_ref[:, :split] = product(x_ref[...], dgu_ref[...], 0, 0).astype(o_ref.dtype)
    o_ref[:, split:] = product(d_ref[...], act_ref[...], 0, 0).astype(o_ref.dtype)

def feed_grads(x, d, dgu, act, tile=256):
    tokens, width = x.shape
    columns = dgu.shape[1] + act.shape[1]
    some = pl.BlockSpec((tokens, tile), lambda t: (0, t))

    def whole(array):
        return pl.BlockSpec(array.shape, lambda t: (0, 0), pipeline_mode=pl.Buffered(1))

    return pl.pallas_call(
        feed_grads_kernel,
        grid=(width // tile,),
        out_shape=jax.ShapeDtypeStruct((width, columns), x.dtype),
        in_specs=[some, some, whole(dgu), whole(act)],
        out_specs=pl.BlockSpec((tile, columns), lambda t: (t, 0)),
        compiler_params=pltpu.CompilerParams(vmem_limit_bytes=VMEM_LIMIT),
        cost_estimate=pl.CostEstimate(flops=2 * tokens * width * columns, bytes_accessed=40_000_000, transcendentals=0),
    )(x, d, dgu, act)


def rotary_tables(positions, width):
    half = width // 2
    freqs = jnp.exp(-(jnp.arange(half, dtype=jnp.float32) * 2.0 / width) * math.log(ROPE_BASE))
    angles = positions.astype(jnp.float32)[..., None] * freqs
    angles = jnp.concatenate([angles, angles], -1)
    return (jnp.cos(angles)[..., None, :], jnp.sin(angles)[..., None, :])


def rotate_half(value_rows):
    half = value_rows.shape[-1] // 2
    return jnp.concatenate([-value_rows[..., half:], value_rows[..., :half]], -1)


def apply_rotary(value_rows, cosine_table, sine_table):
    return value_rows * cosine_table + rotate_half(value_rows) * sine_table


def rope_back(grads, cosine_table, sine_table):
    return grads * cosine_table - rotate_half(grads * sine_table)


def rms_normalize(value_rows):
    inverse_scale = lax.rsqrt(jnp.mean(value_rows * value_rows, -1, keepdims=True) + NORM_EPSILON)
    return (value_rows * inverse_scale, inverse_scale)


def norm_backward(unit_gradient, unit_input, inverse_scale):
    return inverse_scale * (
        unit_gradient - unit_input * jnp.mean(unit_gradient * unit_input, -1, keepdims=True)
    )


def adam_step(weight, grad, first, second, rate, decay):
    first_new = BETA_ONE * first + (1.0 - BETA_ONE) * grad
    second_new = BETA_TWO * second + (1.0 - BETA_TWO) * grad * grad
    corr_one = 1.0 - BETA_ONE**STEP
    corr_two = 1.0 - BETA_TWO**STEP
    update = (first_new * (1.0 / corr_one)) / (jnp.sqrt(second_new * (1.0 / corr_two)) + ADAM_EPSILON)
    return (weight - rate * (update + decay * weight), first_new, second_new)


def feed_pieces(part):
    gateup, down = [], []
    for half in range(2):
        for device in range(8):
            start = (half * 8 + device) * part
            gateup.append((half, device, 0, start))
            gateup.append((half, device, part, FEED_UNITS + start))
            down.append((half, device, 2 * part, start))
    return gateup, down


def head_pieces_of(columns):
    key = columns // 6
    query = 2 * key
    qkv, out = [], []
    for device in range(4):
        qkv.append((device, 0, device * query, query))
        qkv.append((device, query, 4 * query + device * key, key))
        qkv.append((device, query + key, 4 * (query + key) + device * key, key))
        out.append((device, query + 2 * key, device * query, query))
    return qkv, out


def norm_kernel(zero_ref, one_ref, head_ref, qkv_ref, gateup_ref, gains_ref, square_ref, gain_grads_ref):
    halves = (zero_ref, one_ref)
    part = zero_ref.shape[2] // 3
    gateup, down = feed_pieces(part)
    qkv, out = head_pieces_of(head_ref.shape[2])
    gains = gains_ref[...].astype(jnp.bfloat16).astype(jnp.float32)

    def low(x):
        return x.astype(jnp.bfloat16).astype(jnp.float32)

    def over(x):
        return jnp.sum(x, 1, keepdims=True)

    two_squares = two_terms = down_squares = 0.0
    for half, device, at, column in gateup:
        grad = halves[half][device, :, at : at + part].astype(jnp.float32)
        two_squares = two_squares + grad * grad
        two_terms = two_terms + grad * low(gateup_ref[:, column : column + part])
    for half, device, at, column in down:
        grad = halves[half][device, :, at : at + part].astype(jnp.float32)
        down_squares = down_squares + grad * grad
    one_squares = one_terms = out_squares = 0.0
    for device, at, column, size in qkv:
        grad = head_ref[device, :, at : at + size].astype(jnp.float32)
        one_squares = one_squares + over(grad * grad)
        one_terms = one_terms + over(grad * low(qkv_ref[:, column : column + size]))
    for device, at, column, size in out:
        grad = head_ref[device, :, at : at + size].astype(jnp.float32)
        out_squares = out_squares + over(grad * grad)
    two_terms = over(two_terms)
    gain_grads_ref[:, 0:1] = one_terms
    gain_grads_ref[:, 1:2] = two_terms
    one, two = gains[:, 0:1], gains[:, 1:2]
    rows = (
        one * one * one_squares
        + two * two * over(two_squares)
        + over(down_squares)
        + out_squares
        + one_terms * one_terms
        + two_terms * two_terms
    )
    total = jnp.sum(rows)

    @pl.when(pl.program_id(0) == 0)
    def _():
        square_ref[0, 0] = total

    @pl.when(pl.program_id(0) > 0)
    def _():
        square_ref[0, 0] = square_ref[0, 0] + total


ROWS = 16


def rows_of(array):
    if array.ndim == 3:
        return pl.BlockSpec((array.shape[0], ROWS, array.shape[2]), lambda r: (0, r, 0))
    return pl.BlockSpec((ROWS, array.shape[1]), lambda r: (r, 0))


def gradient_norm(zero, one, head, qkv, gateup, gains):
    arrays = (zero, one, head, qkv, gateup, gains)
    return pl.pallas_call(
        norm_kernel,
        grid=(gains.shape[0] // ROWS,),
        out_shape=[jax.ShapeDtypeStruct((1, 1), jnp.float32), jax.ShapeDtypeStruct(gains.shape, jnp.float32)],
        in_specs=[rows_of(x) for x in arrays],
        out_specs=[pl.BlockSpec(memory_space=pltpu.SMEM), rows_of(gains)],
        compiler_params=pltpu.CompilerParams(vmem_limit_bytes=VMEM_LIMIT),
    )(*arrays)


def adam_kernel(clip_ref, zero_ref, one_ref, head_ref, gain_grads_ref, *refs):
    weights, firsts, seconds = refs[0:5], refs[5:10], refs[10:15]
    weights_out, firsts_out, seconds_out = refs[15:20], refs[20:25], refs[25:30]
    halves = (zero_ref, one_ref)
    part = zero_ref.shape[2] // 3
    gateup, down = feed_pieces(part)
    qkv, out = head_pieces_of(head_ref.shape[2])
    clip = clip_ref[0, 0]
    gains = weights[4][...].astype(jnp.bfloat16).astype(jnp.float32) * clip
    one, two = gains[:, 0:1], gains[:, 1:2]

    def step(which, columns, grad, rate, decay):
        new = adam_step(
            weights[which][:, columns], grad, firsts[which][:, columns], seconds[which][:, columns], rate, decay
        )
        weights_out[which][:, columns] = new[0]
        firsts_out[which][:, columns] = new[1]
        seconds_out[which][:, columns] = new[2]

    for pieces, which, scale, rate in ((qkv, 0, one, RATE_MATRIX), (out, 1, clip, RATE_OUTPUT)):
        for device, at, column, size in pieces:
            grad = head_ref[device, :, at : at + size].astype(jnp.float32) * scale
            step(which, slice(column, column + size), grad, rate, DECAY_MATRIX)
    for pieces, which, scale in ((gateup, 2, two), (down, 3, clip)):
        for half, device, at, column in pieces:
            grad = halves[half][device, :, at : at + part].astype(jnp.float32) * scale
            step(which, slice(column, column + part), grad, RATE_MATRIX, DECAY_MATRIX)
    step(4, slice(0, 2), gain_grads_ref[...] * clip, RATE_GAIN, 0.0)


def adam(clip, zero, one, head, gain_grads, weights, firsts, seconds):
    state = (*weights, *firsts, *seconds)
    arrays = (zero, one, head, gain_grads, *state)
    return pl.pallas_call(
        adam_kernel,
        grid=(gain_grads.shape[0] // ROWS,),
        out_shape=[jax.ShapeDtypeStruct(x.shape, x.dtype) for x in state],
        in_specs=[pl.BlockSpec(memory_space=pltpu.SMEM)] + [rows_of(x) for x in arrays],
        out_specs=[rows_of(x) for x in state],
        compiler_params=pltpu.CompilerParams(vmem_limit_bytes=VMEM_LIMIT),
    )(clip, *arrays)


def product(left, right, left_dim, right_dim):
    return lax.dot_general(
        left, right, (((left_dim,), (right_dim,)), ((), ())), preferred_element_type=jnp.float32
    )


def shards(
    inputs,
    cotangent,
    lengths,
    positions,
    query_key_value_weight,
    out_weight,
    gateup_weight,
    down_weight,
    norm_gains,
    query_key_value_moment,
    output_weight_moment,
    gate_up_moment,
    down_weight_moment,
    norm_gains_moment,
    query_key_value_variance,
    out_second,
    gateup_second,
    down_second,
    gains_second,
):
    _, here, width = inputs.shape
    seq = lax.axis_size("seq")
    far = lax.axis_size("far")
    group = seq * 2
    rows = out_weight.shape[0]
    full = here * seq
    heads_here = QUERY_HEAD_COUNT // seq
    local_kv = KEY_VALUE_HEADS // seq
    per_kv = QUERY_HEAD_COUNT // KEY_VALUE_HEADS
    query_width = QUERY_HEAD_COUNT * HEAD_SIZE
    key_width = KEY_VALUE_HEADS * HEAD_SIZE
    mine_q, mine_k = query_width // seq, key_width // seq
    mine_qkv = mine_q + 2 * mine_k
    units = FEED_UNITS // group
    part = units // 2
    factor = 1.0 / math.sqrt(HEAD_SIZE)
    low = jnp.bfloat16

    inputs = inputs[0]
    cotangent = cotangent[0]
    length = lengths[0]
    gains = norm_gains.astype(low).astype(jnp.float32)
    gain_one, gain_two = gains[:, :1], gains[:, 1:]

    def after(x, *others):
        return lax.optimization_barrier((x, *others))[0]

    def rounded(weight, gain=None):
        weight = weight.astype(low)
        return weight if gain is None else (weight.astype(jnp.float32) * gain).astype(low)

    def far_first(x):
        x = x.reshape(-1, seq, far, 2 * rows).transpose(0, 2, 1, 3)
        return x.reshape(-1, width)

    def far_last(x):
        return x.reshape(-1, far, seq, 2 * rows).transpose(0, 2, 1, 3).reshape(-1, width)

    def feed_piece(half):
        start, size = half * FEED_UNITS // 2, FEED_UNITS // 2
        columns = [
            rounded(gateup_weight[:, start : start + size], gain_two),
            rounded(gateup_weight[:, FEED_UNITS + start : FEED_UNITS + start + size], gain_two),
            rounded(down_weight[:, start : start + size]),
        ]
        columns = [x.reshape(rows, group, part).transpose(1, 0, 2) for x in columns]
        return jnp.concatenate(columns, 2)

    (piece,) = exchange_plane([feed_piece(0).reshape(group * rows, 3 * part)], 1)
    feed_zero = lax.all_gather(piece, "far", axis=0, tiled=True)

    qkv_low = rounded(query_key_value_weight, gain_one)
    head_pieces = jnp.concatenate(
        [
            qkv_low[:, :query_width].reshape(rows, seq, mine_q),
            qkv_low[:, query_width : query_width + key_width].reshape(rows, seq, mine_k),
            qkv_low[:, query_width + key_width :].reshape(rows, seq, mine_k),
            rounded(out_weight).reshape(rows, seq, mine_q),
        ],
        2,
    ).transpose(1, 0, 2)
    unit_one, scale_one = rms_normalize(inputs)
    spots = jnp.pad(positions.reshape(-1, 128), ((0, 8 - here // 128), (0, 0)))
    dout_here = far_first(cotangent.astype(low))
    head_pieces = after(head_pieces, piece)
    head_w, normed_one, all_spots, dout, piece = gather_heads(
        head_pieces, unit_one.astype(low), spots, dout_here, feed_piece(1), 2
    )
    feed_one = lax.all_gather(piece.reshape(group * rows, -1), "far", axis=0, tiled=True)
    qkv, out = head_w[:, :mine_qkv], head_w[:, mine_qkv:]
    all_positions = all_spots[:, : here // 128].reshape(full)

    cos, sin = rotary_tables(all_positions, HEAD_SIZE)
    merged = product(normed_one, qkv, 1, 0)
    queries = apply_rotary(merged[:, :mine_q].reshape(full, heads_here, HEAD_SIZE), cos, sin)
    queries = queries.astype(low).reshape(full, local_kv, per_kv, HEAD_SIZE)
    keys = apply_rotary(
        merged[:, mine_q : mine_q + mine_k].reshape(full, local_kv, HEAD_SIZE), cos, sin
    ).astype(low)
    values = merged[:, mine_q + mine_k :].reshape(full, local_kv, HEAD_SIZE).astype(low)

    spot = jnp.arange(full)
    visible = (spot[None, :] <= spot[:, None]) & (spot < length)[None, :]
    live = (spot < length)[:, None, None, None]
    scores = jnp.einsum("qkgd,jkd->kgqj", queries, keys, preferred_element_type=jnp.float32)
    scores = jnp.where(visible, scores * factor, MASKED_SCORE)
    peak = jnp.max(scores, -1, keepdims=True)
    expo = jnp.exp(scores - peak)
    probs = expo / jnp.sum(expo, -1, keepdims=True)
    probs_low = probs.astype(low)
    heads = jnp.einsum("kgqj,jkd->qkgd", probs_low, values, preferred_element_type=jnp.float32)
    heads = (heads * live).astype(low).reshape(full, mine_q)
    hidden = inputs + scatter_seq(product(heads, out, 1, 1).astype(low), 3)
    unit_two, scale_two = rms_normalize(hidden)
    normed_two = gather_plane(far_first(unit_two.astype(low)), 4)
    act_zero, dgateup_zero, *sums = feed(normed_two, dout, feed_zero, ())
    terms_zero = feed_grads(normed_two, dout, dgateup_zero, act_zero)
    feed_one = after(feed_one, terms_zero)
    act_one, dgateup_one, output_terms, dnormed_two = feed(normed_two, dout, feed_one, sums)
    dnormed_two = scatter_plane(dnormed_two, 5)
    dgateup_one = after(dgateup_one, dnormed_two)
    terms_one = feed_grads(normed_two, dout, dgateup_one, act_one)
    dnormed_two = far_last(dnormed_two)
    grads_zero = lax.psum_scatter(terms_zero, "far", scatter_dimension=0, tiled=True)
    grads_one = lax.psum_scatter(
        after(terms_one, grads_zero), "far", scatter_dimension=0, tiled=True
    )
    back_two = norm_backward(dnormed_two, unit_two, scale_two)
    dhidden = cotangent + back_two

    dattended = gather_seq(after(dhidden.astype(low), terms_one), 6)
    dheads = product(dattended, out, 1, 0).astype(low).reshape(full, local_kv, per_kv, HEAD_SIZE)
    dheads = dheads * live.astype(low)
    dvalues = jnp.einsum("kgqj,qkgd->jkd", probs_low, dheads, preferred_element_type=jnp.float32)
    dprobs = jnp.einsum("qkgd,jkd->kgqj", dheads, values, preferred_element_type=jnp.float32)
    inner = jnp.sum(probs * dprobs, -1, keepdims=True)
    dscores = jnp.where(visible, (probs * (dprobs - inner)).astype(low), jnp.zeros((), low))
    dqueries = jnp.einsum("kgqj,jkd->qkgd", dscores, keys, preferred_element_type=jnp.float32)
    dkeys = jnp.einsum("kgqj,qkgd->jkd", dscores, queries, preferred_element_type=jnp.float32)
    dqueries = (dqueries * factor).astype(low).reshape(full, heads_here, HEAD_SIZE)
    dkeys = (dkeys * factor).astype(low)
    dfused = jnp.concatenate(
        [
            rope_back(dqueries.astype(jnp.float32), cos, sin).astype(low).reshape(full, mine_q),
            rope_back(dkeys.astype(jnp.float32), cos, sin).astype(low).reshape(full, mine_k),
            dvalues.astype(low).reshape(full, mine_k),
        ],
        1,
    )
    head_terms = jnp.concatenate(
        [
            product(normed_one, dfused, 0, 0).astype(low),
            product(dattended, heads, 0, 0).astype(low),
        ],
        1,
    )
    head_terms = scatter_near(head_terms.reshape(seq, far, 2, rows, -1), 8)
    head_terms = after(head_terms, grads_zero, grads_one)
    head_terms = lax.psum_scatter(
        head_terms.reshape(far * seq * rows, -1), "far", scatter_dimension=0, tiled=True
    )
    dnormed_one = scatter_seq(product(dfused, qkv, 1, 1).astype(low), 3)
    back_one = norm_backward(dnormed_one, unit_one, scale_one)
    input_grad = dhidden + back_one
    output_terms = scatter_plane(after(output_terms, dnormed_one), 5)
    layer_output = hidden + far_last(output_terms)

    halves = exchange_plane([grads_zero, grads_one], 7)
    head_terms = after(head_terms, output_terms, halves[0])
    halves = [x.reshape(group, rows, 3 * part) for x in halves]
    head_grads = lax.all_to_all(head_terms.reshape(seq, rows, -1), "seq", 0, 0, tiled=True)

    weights = (query_key_value_weight, out_weight, gateup_weight, down_weight, norm_gains)
    firsts = (query_key_value_moment, output_weight_moment, gate_up_moment, down_weight_moment, norm_gains_moment)
    seconds = (query_key_value_variance, out_second, gateup_second, down_second, gains_second)
    squares, gain_grads = gradient_norm(
        *halves, head_grads, query_key_value_weight, gateup_weight, norm_gains
    )
    squares = lax.psum(lax.psum(lax.psum(squares[0, 0], "seq"), "near"), "far")
    grad_norm = jnp.sqrt(squares)
    clip = CLIP_NORM / jnp.maximum(grad_norm, CLIP_NORM)
    stepped = adam(clip.reshape(1, 1), *halves, head_grads, gain_grads, weights, firsts, seconds)
    return (layer_output[None], input_grad[None], grad_norm, *stepped)


def solution(mesh):
    seq, fsdp = mesh.shape["seq"], mesh.shape["fsdp"]
    cut = Mesh(mesh.devices.reshape(seq, fsdp // 2, 2), EVERY)
    tokens = P(("far", "near"), "seq", None)
    matrix = P(EVERY, None)
    return jax.shard_map(
        shards,
        mesh=cut,
        in_specs=(tokens, tokens, P(("far", "near")), P(("far", "near"), "seq")) + (matrix,) * 15,
        out_specs=(tokens, tokens, P()) + (matrix,) * 15,
        check_vma=False,
    )
```

```python
import functools
import math

import jax
import jax.numpy as jnp
from jax import lax
from jax.experimental import pallas as pl
from jax.experimental.pallas import tpu as pltpu
from jax.sharding import Mesh, PartitionSpec as P

QUERY_HEAD_COUNT = 8
KEY_VALUE_HEADS = 4
HEAD_SIZE = 256
FEED_UNITS = 8192
STEP = 10

NORM_EPSILON = 1e-06
ROPE_BASE = 1000042.0
MASKED_SCORE = -1000000000.0
CLIP_NORM = 1.0
BETA_ONE = 0.9
BETA_TWO = 0.95
ADAM_EPSILON = 1e-08
DECAY_MATRIX = 0.1
RATE_MATRIX = 0.02
RATE_OUTPUT = 0.1
RATE_GAIN = 1.0

EVERY = ("seq", "far", "near")
TP = ("seq", "near")


MESH_IDS = pl.DeviceIdType.MESH
ANYWHERE = pl.BlockSpec(memory_space=pl.ANY)
IN_VMEM = pl.BlockSpec(memory_space=pltpu.VMEM)
VMEM_LIMIT = 60 * 1024 * 1024


def places():
    s, n = lax.axis_index("seq"), lax.axis_index("near")
    return s, n, s + 1 - 2 * (s % 2), (s + 2) % 4, 1 - n


def meet(*others):
    barrier = pltpu.get_barrier_semaphore()
    for other in others:
        pl.semaphore_signal(barrier, inc=1, device_id=other, device_id_type=MESH_IDS)
    pl.semaphore_wait(barrier, len(others))


def sender(send_sems, recv_sems):
    copies = {}

    def send(key, source, target, device):
        at = len(copies)
        copies[key] = pltpu.make_async_remote_copy(
            src_ref=source,
            dst_ref=target,
            send_sem=send_sems.at[at],
            recv_sem=recv_sems.at[at],
            device_id=device,
            device_id_type=MESH_IDS,
        )
        copies[key].start()

    return copies, send


def gather_plane_kernel(rows, x_ref, o_ref, local_sem, send_sems, recv_sems):
    s, n, core, across, beside = places()
    half = rows // 2
    to_core, to_y, to_x = {"seq": core}, {"seq": across}, {"near": beside}

    def block(seq, near, part):
        return o_ref.at[pl.ds((seq * 2 + near) * rows + part * half, half)]

    def own(part):
        return x_ref.at[pl.ds(part * half, half)]

    meet(to_core, to_y, to_x)
    local = pltpu.make_async_copy(x_ref, o_ref.at[pl.ds((s * 2 + n) * rows, rows)], local_sem)
    local.start()
    copies, send = sender(send_sems, recv_sems)
    send("y0", own(0), block(s, n, 0), to_y)
    send("x1", own(1), block(s, n, 1), to_x)
    send("y1", own(1), block(s, n, 1), to_y)
    send("x0", own(0), block(s, n, 0), to_x)
    send("c0", own(0), block(s, n, 0), to_core)
    send("c1", own(1), block(s, n, 1), to_core)
    copies["y0"].wait_recv()
    send("yx", block(across, n, 0), block(across, n, 0), to_x)
    send("yc0", block(across, n, 0), block(across, n, 0), to_core)
    copies["x1"].wait_recv()
    send("xy", block(s, beside, 1), block(s, beside, 1), to_y)
    send("xc1", block(s, beside, 1), block(s, beside, 1), to_core)
    copies["y1"].wait_recv()
    send("yc1", block(across, n, 1), block(across, n, 1), to_core)
    copies["x0"].wait_recv()
    send("xc0", block(s, beside, 0), block(s, beside, 0), to_core)
    copies["yx"].wait_recv()
    send("dc0", block(across, beside, 0), block(across, beside, 0), to_core)
    copies["xy"].wait_recv()
    send("dc1", block(across, beside, 1), block(across, beside, 1), to_core)
    for key in ("c0", "c1", "yc0", "yc1", "xc0", "xc1", "dc0", "dc1"):
        copies[key].wait_recv()
    for copy in copies.values():
        copy.wait_send()
    local.wait()


def gather_plane(x, collective_id):
    rows, columns = x.shape
    return pl.pallas_call(
        functools.partial(gather_plane_kernel, rows),
        out_shape=jax.ShapeDtypeStruct((8 * rows, columns), x.dtype),
        in_specs=[ANYWHERE],
        out_specs=ANYWHERE,
        scratch_shapes=[
            pltpu.SemaphoreType.DMA,
            pltpu.SemaphoreType.DMA((14,)),
            pltpu.SemaphoreType.DMA((14,)),
        ],
        compiler_params=pltpu.CompilerParams(collective_id=collective_id, has_side_effects=True),
    )(x)


def add_rows(target, first, second, third=None, step=64):
    rows = target.shape[0]

    def body(i, carry):
        at = pl.ds(pl.multiple_of(i * step, step), step)
        total = first[at, :].astype(jnp.float32) + second[at, :].astype(jnp.float32)
        if third is not None:
            total = total + third[at, :].astype(jnp.float32)
        target[at, :] = total.astype(target.dtype)
        return carry

    lax.fori_loop(0, rows // step, body, 0)


def scatter_plane_kernel(rows, p_ref, o_ref, mine, far, hop_x, hop_y, last_x, last_y, local_sems, send_sems, recv_sems):
    s, n, core, across, beside = places()
    half = rows // 2
    to_core, to_y, to_x = {"seq": core}, {"seq": across}, {"near": beside}

    def block(seq, near):
        return p_ref.at[pl.ds((seq * 2 + near) * rows, rows)]

    def part(ref, at, p):
        return ref.at[at, pl.ds(p * half, half)]

    meet(to_core, to_y, to_x)
    copies, send = sender(send_sems, recv_sems)
    other = (core + 2) % 4
    given = [block(other, beside), block(other, n), block(core, beside), block(core, n)]
    kept = [block(across, beside), block(across, n), block(s, beside), block(s, n)]
    locals_ = []
    for k in range(4):
        send(k, given[k], far.at[k], to_core)
        locals_.append(pltpu.make_async_copy(kept[k], mine.at[k], local_sems.at[k]))
        locals_[k].start()
    for k in range(3):
        locals_[k].wait()
        copies[k].wait_recv()
        add_rows(mine.at[k], mine.at[k], far.at[k])
        if k == 0:
            send("hx", part(mine, 0, 0), hop_x, to_x)
            send("hy", part(mine, 0, 1), hop_y, to_y)
        elif k == 1:
            send("y1", part(mine, 1, 1), part(last_y, 0, 1), to_y)
        else:
            send("x0", part(mine, 2, 0), part(last_x, 0, 0), to_x)
    copies["hx"].wait_recv()
    add_rows(part(mine, 1, 0), part(mine, 1, 0), hop_x)
    send("y0", part(mine, 1, 0), part(last_y, 0, 0), to_y)
    copies["hy"].wait_recv()
    add_rows(part(mine, 2, 1), part(mine, 2, 1), hop_y)
    send("x1", part(mine, 2, 1), part(last_x, 0, 1), to_x)
    locals_[3].wait()
    copies[3].wait_recv()
    add_rows(o_ref, mine.at[3], far.at[3])
    for p, first, second in ((1, "y1", "x1"), (0, "x0", "y0")):
        copies[first].wait_recv()
        copies[second].wait_recv()
        here = o_ref.at[pl.ds(p * half, half)]
        add_rows(here, here, part(last_x, 0, p), part(last_y, 0, p))
    for copy in copies.values():
        copy.wait_send()


def scatter_plane(p, collective_id):
    rows, columns = p.shape[0] // 8, p.shape[1]
    low = jnp.bfloat16
    return pl.pallas_call(
        functools.partial(scatter_plane_kernel, rows),
        out_shape=jax.ShapeDtypeStruct((rows, columns), jnp.float32),
        in_specs=[ANYWHERE],
        out_specs=IN_VMEM,
        scratch_shapes=[
            pltpu.VMEM((4, rows, columns), low),
            pltpu.VMEM((4, rows, columns), low),
            pltpu.VMEM((rows // 2, columns), low),
            pltpu.VMEM((rows // 2, columns), low),
            pltpu.VMEM((1, rows, columns), low),
            pltpu.VMEM((1, rows, columns), low),
            pltpu.SemaphoreType.DMA((4,)),
            pltpu.SemaphoreType.DMA((10,)),
            pltpu.SemaphoreType.DMA((10,)),
        ],
        compiler_params=pltpu.CompilerParams(
            collective_id=collective_id, has_side_effects=True, vmem_limit_bytes=VMEM_LIMIT
        ),
    )(p)


def scatter_seq_kernel(rows, p_ref, o_ref, mine, far, last, local_sems, send_sems, recv_sems):
    s, _, core, across, _ = places()
    half = rows // 2
    to_core, to_y = {"seq": core}, {"seq": across}

    def block(seq):
        return p_ref.at[pl.ds(seq * rows, rows)]

    meet(to_core, to_y)
    copies, send = sender(send_sems, recv_sems)
    given = [block((core + 2) % 4), block(core)]
    kept = [block(across), block(s)]
    locals_ = []
    for k in range(2):
        send(k, given[k], far.at[k], to_core)
        locals_.append(pltpu.make_async_copy(kept[k], mine.at[k], local_sems.at[k]))
        locals_[k].start()
    locals_[0].wait()
    copies[0].wait_recv()
    for p in range(2):
        at = pl.ds(p * half, half)
        add_rows(mine.at[0, at], mine.at[0, at], far.at[0, at])
        send(("y", p), mine.at[0, at], last.at[at], to_y)
    locals_[1].wait()
    copies[1].wait_recv()
    add_rows(o_ref, mine.at[1], far.at[1])
    for p in range(2):
        at = pl.ds(p * half, half)
        copies["y", p].wait_recv()
        add_rows(o_ref.at[at], o_ref.at[at], last.at[at])
    for copy in copies.values():
        copy.wait_send()


def scatter_seq(p, collective_id):
    rows, columns = p.shape[0] // 4, p.shape[1]
    low = jnp.bfloat16
    return pl.pallas_call(
        functools.partial(scatter_seq_kernel, rows),
        out_shape=jax.ShapeDtypeStruct((rows, columns), jnp.float32),
        in_specs=[ANYWHERE],
        out_specs=IN_VMEM,
        scratch_shapes=[
            pltpu.VMEM((2, rows, columns), low),
            pltpu.VMEM((2, rows, columns), low),
            pltpu.VMEM((rows, columns), low),
            pltpu.SemaphoreType.DMA((2,)),
            pltpu.SemaphoreType.DMA((4,)),
            pltpu.SemaphoreType.DMA((4,)),
        ],
        compiler_params=pltpu.CompilerParams(
            collective_id=collective_id, has_side_effects=True, vmem_limit_bytes=VMEM_LIMIT
        ),
    )(p)


def exchange_plane_kernel(count, *refs):
    x_refs, o_refs = refs[:count], refs[count : 2 * count]
    local_sems, send_sems, recv_sems = refs[2 * count :]
    s, n, core, across, beside = places()
    diagonal = (core + 2) % 4
    mine = s * 2 + n
    others = [(seq, near) for near in (beside, n) for seq in (diagonal, across, core, s)][:-1]

    meet(*[{"seq": seq, "near": near} for seq, near in others])
    copies, send = sender(send_sems, recv_sems)
    locals_ = []
    for k, (x_ref, o_ref) in enumerate(zip(x_refs, o_refs)):
        rows = x_ref.shape[0] // 8

        def at(p):
            return pl.ds(p * rows, rows)

        for seq, near in others:
            target = {"seq": seq, "near": near}
            send(len(copies), x_ref.at[at(seq * 2 + near)], o_ref.at[at(mine)], target)
        locals_.append(pltpu.make_async_copy(x_ref.at[at(mine)], o_ref.at[at(mine)], local_sems.at[k]))
        locals_[k].start()
    for copy in copies.values():
        copy.wait_recv()
    for copy in copies.values():
        copy.wait_send()
    for copy in locals_:
        copy.wait()


def exchange_plane(arrays, collective_id):
    count = len(arrays)
    return pl.pallas_call(
        functools.partial(exchange_plane_kernel, count),
        out_shape=[jax.ShapeDtypeStruct(x.shape, x.dtype) for x in arrays],
        in_specs=[ANYWHERE] * count,
        out_specs=[ANYWHERE] * count,
        scratch_shapes=[
            pltpu.SemaphoreType.DMA((count,)),
            pltpu.SemaphoreType.DMA((7 * count,)),
            pltpu.SemaphoreType.DMA((7 * count,)),
        ],
        compiler_params=pltpu.CompilerParams(collective_id=collective_id, has_side_effects=True),
    )(*arrays)


def gather_heads_kernel(
    far_size,
    w_ref,
    x_ref,
    i_ref,
    d_ref,
    e_ref,
    o_ref,
    ox_ref,
    oi_ref,
    od_ref,
    oe_ref,
    local_sems,
    send_sems,
    recv_sems,
):
    s, n, core, across, beside = places()
    diagonal = (core + 2) % 4
    f = lax.axis_index("far")
    half = x_ref.shape[0] // 2
    to_core, to_y, to_x = {"seq": core}, {"seq": across}, {"near": beside}
    right, left = {"far": (f + 1) % far_size}, {"far": (f + far_size - 1) % far_size}

    others = [(seq, near) for near in (beside, n) for seq in (diagonal, across, core, s)][:-1]
    meet(*[{"seq": seq, "near": near} for seq, near in others], right, left)
    copies, send = sender(send_sems, recv_sems)
    keep = pltpu.make_async_copy(w_ref.at[s], o_ref.at[s, f, n], local_sems.at[0])
    keep.start()
    keep_x = pltpu.make_async_copy(x_ref, ox_ref.at[s], local_sems.at[1])
    keep_x.start()
    keep_i = pltpu.make_async_copy(i_ref, oi_ref.at[s], local_sems.at[2])
    keep_i.start()
    for k, seq in enumerate((diagonal, across, core)):
        send(("w", k), w_ref.at[seq], o_ref.at[s, f, n], {"seq": seq})
        send(("i", k), i_ref, oi_ref.at[s], {"seq": seq})
    for p in range(2):
        at = pl.ds(p * half, half)
        send(("y", p), x_ref.at[at], ox_ref.at[s, at], to_y)
        send(("c", p), x_ref.at[at], ox_ref.at[s, at], to_core)

    def block(seq, near, p):
        return od_ref.at[seq * 2 + near, pl.ds(p * half, half)]

    def own(p):
        return d_ref.at[pl.ds(p * half, half)]

    keep_d = pltpu.make_async_copy(d_ref, od_ref.at[s * 2 + n], local_sems.at[3])
    keep_d.start()
    send("y0", own(0), block(s, n, 0), to_y)
    send("x1", own(1), block(s, n, 1), to_x)
    send("y1", own(1), block(s, n, 1), to_y)
    send("x0", own(0), block(s, n, 0), to_x)
    send("c0", own(0), block(s, n, 0), to_core)
    send("c1", own(1), block(s, n, 1), to_core)
    keep_e = pltpu.make_async_copy(e_ref.at[s * 2 + n], oe_ref.at[s * 2 + n], local_sems.at[4])
    keep_e.start()
    for k, (seq, near) in enumerate(others):
        target = {"seq": seq, "near": near}
        send(("e", k), e_ref.at[seq * 2 + near], oe_ref.at[s * 2 + n], target)
    keep.wait()
    for k in range(3):
        copies["w", k].wait_recv()

    def group(far, near):
        return o_ref.at[:, far, near]

    def along(key, far, device, sem):
        return pltpu.make_async_remote_copy(
            src_ref=group(far, n),
            dst_ref=group(far, n),
            send_sem=send_sems.at[sem],
            recv_sem=recv_sems.at[sem],
            device_id=device,
            device_id_type=MESH_IDS,
        )

    base = 33

    def beside_copy(far, sem):
        return along("x", far, to_x, sem)

    def to_right(k):
        return along("r", (f + far_size - k) % far_size, right, base + k)

    def to_left(k):
        return along("l", (f + k) % far_size, left, base + far_size + k)

    def x_from_left(k):
        return beside_copy((f + far_size - k) % far_size, base + 2 * far_size + k)

    def x_from_right(k):
        return beside_copy((f + k) % far_size, base + 3 * far_size + k)

    for k in range(far_size):
        if k > 0:

            @pl.when(f >= k)
            def _():
                to_right(k - 1).wait_recv()

        @pl.when((f >= k) & (f < far_size - 1))
        def _():
            to_right(k).start()

        if k > 0:

            @pl.when(f + k < far_size)
            def _():
                to_left(k - 1).wait_recv()

        @pl.when((f + k < far_size) & (f > 0))
        def _():
            to_left(k).start()

        if k == 0:
            x_from_left(0).start()
        else:

            @pl.when(f >= k)
            def _():
                x_from_left(k).start()

            @pl.when(f + k < far_size)
            def _():
                x_from_right(k).start()

        if k == 0:
            for p in range(2):
                at = pl.ds(p * half, half)
                copies["y", p].wait_recv()
                send(("yc", p), ox_ref.at[across, at], ox_ref.at[across, at], to_core)
        if k == 1:
            copies["y0"].wait_recv()
            send("yx", block(across, n, 0), block(across, n, 0), to_x)
            send("yc0", block(across, n, 0), block(across, n, 0), to_core)
            copies["x1"].wait_recv()
            send("xy", block(s, beside, 1), block(s, beside, 1), to_y)
            send("xc1", block(s, beside, 1), block(s, beside, 1), to_core)
            copies["y1"].wait_recv()
            send("yc1", block(across, n, 1), block(across, n, 1), to_core)
            copies["x0"].wait_recv()
            send("xc0", block(s, beside, 0), block(s, beside, 0), to_core)
        if k == min(2, far_size - 1):
            copies["yx"].wait_recv()
            send("dc0", block(across, beside, 0), block(across, beside, 0), to_core)
            copies["xy"].wait_recv()
            send("dc1", block(across, beside, 1), block(across, beside, 1), to_core)
    for key in ("c0", "c1", "yc0", "yc1", "xc0", "xc1", "dc0", "dc1"):
        copies[key].wait_recv()
    for p in range(2):
        copies["c", p].wait_recv()
        copies["yc", p].wait_recv()
    for k in range(3):
        copies["i", k].wait_recv()
    for k in range(7):
        copies["e", k].wait_recv()
    for k in range(far_size):

        @pl.when((f >= k) & (f < far_size - 1))
        def _():
            to_right(k).wait_send()

        @pl.when((f + k < far_size) & (f > 0))
        def _():
            to_left(k).wait_send()

        @pl.when(f >= k)
        def _():
            x_from_left(k).wait_recv()
            x_from_left(k).wait_send()

        if k > 0:

            @pl.when(f + k < far_size)
            def _():
                x_from_right(k).wait_recv()
                x_from_right(k).wait_send()

    for copy in copies.values():
        copy.wait_send()
    keep_x.wait()
    keep_i.wait()
    keep_d.wait()
    keep_e.wait()


def gather_heads(w, x, i, d, e, collective_id):
    far_size = lax.axis_size("far")
    _, rows, columns = w.shape
    tokens, width = x.shape
    sems = 33 + 4 * far_size
    full, all_x, all_i, all_d, mine_e = pl.pallas_call(
        functools.partial(gather_heads_kernel, far_size),
        out_shape=[
            jax.ShapeDtypeStruct((4, far_size, 2, rows, columns), w.dtype),
            jax.ShapeDtypeStruct((4, tokens, width), x.dtype),
            jax.ShapeDtypeStruct((4, *i.shape), i.dtype),
            jax.ShapeDtypeStruct((8, *d.shape), d.dtype),
            jax.ShapeDtypeStruct(e.shape, e.dtype),
        ],
        in_specs=[ANYWHERE] * 5,
        out_specs=[ANYWHERE] * 5,
        scratch_shapes=[
            pltpu.SemaphoreType.DMA((5,)),
            pltpu.SemaphoreType.DMA((sems,)),
            pltpu.SemaphoreType.DMA((sems,)),
        ],
        compiler_params=pltpu.CompilerParams(collective_id=collective_id, has_side_effects=True),
    )(w, x, i, d, e)
    all_x, all_d = all_x.reshape(-1, width), all_d.reshape(-1, d.shape[1])
    return full.reshape(-1, columns), all_x, all_i, all_d, mine_e


def tile_at(tile, rows):
    return pl.ds(pl.multiple_of(tile * rows, rows), rows)


def stacked(pair):
    half = pair.shape[1] // 2
    return jnp.concatenate([pair[:, :half], pair[:, half:]], 0)


def turned(value, cos, sin):
    half = value.shape[1] // 2
    first, second = value[:, :half], value[:, half:]
    return first * cos - second * sin, second * cos + first * sin


def visible_keys(tile, rows, keys, length):
    shape = (2 * rows, keys)
    row = lax.broadcasted_iota(jnp.int32, shape, 0)
    row = jnp.where(row >= rows, row - rows, row) + tile * rows
    column = lax.broadcasted_iota(jnp.int32, shape, 1)
    return (column <= row) & (column < length)


def attention_kernel(length_ref, x_ref, w_ref, turn_ref, q_ref, k_ref, v_ref, heads_ref, lse_ref, p_ref):
    rows = x_ref.shape[0] // 4
    size = k_ref.shape[1]
    low = jnp.bfloat16
    length = length_ref[0]

    def project(tile, carry):
        at = tile_at(tile, rows)
        merged = product(x_ref[at, :], w_ref[:, : 4 * size], 1, 0)
        cos, sin = turn_ref[at, : size // 2], turn_ref[at, size // 2 :]
        for ref, start, column, scale in (
            (q_ref, 0, 0, size**-0.5),
            (q_ref, size, size, size**-0.5),
            (k_ref, 2 * size, 0, 1.0),
        ):
            first, second = turned(merged[:, start : start + size], cos, sin)
            ref[at, column : column + size // 2] = (first * scale).astype(low)
            ref[at, column + size // 2 : column + size] = (second * scale).astype(low)
        v_ref[at, :] = merged[:, 3 * size :].astype(low)
        return carry

    lax.fori_loop(0, 4, project, 0)
    for tile in range(4):
        at = pl.ds(tile * rows, rows)
        keys = (tile + 1) * rows
        scores = product(stacked(q_ref[at, :]), k_ref[:keys, :], 1, 1)
        scores = jnp.where(visible_keys(tile, rows, keys, length), scores, MASKED_SCORE)
        peak = jnp.max(scores, 1, keepdims=True)
        expo = jnp.exp(scores - peak)
        total = jnp.sum(expo, 1, keepdims=True)
        result = product((expo * (1.0 / total)).astype(low), v_ref[:keys, :], 1, 0)
        live = lax.broadcasted_iota(jnp.int32, (rows, 1), 0) + tile * rows < length
        lse = peak + jnp.log(total)
        for head in range(2):
            mine = slice(head * rows, (head + 1) * rows)
            heads_ref[at, head * size : (head + 1) * size] = jnp.where(live, result[mine], 0.0).astype(low)
            lse_ref[at, head : head + 1] = lse[mine]

    def out(tile, carry):
        at = tile_at(tile, rows)
        p_ref[at, :] = product(heads_ref[at, :], w_ref[:, 4 * size :], 1, 1).astype(low)
        return carry

    lax.fori_loop(0, 4, out, 0)


def attention(length, x, w, turns):
    tokens, width = x.shape
    size = w.shape[1] // 6
    low = jnp.bfloat16
    shapes = [(tokens, 2 * size), (tokens, size), (tokens, size), (tokens, 2 * size)]
    return pl.pallas_call(
        attention_kernel,
        out_shape=[jax.ShapeDtypeStruct(shape, low) for shape in shapes]
        + [jax.ShapeDtypeStruct((tokens, 128), jnp.float32), jax.ShapeDtypeStruct((tokens, width), low)],
        in_specs=[pl.BlockSpec(memory_space=pltpu.SMEM)] + [IN_VMEM] * 3,
        out_specs=[IN_VMEM] * 6,
        compiler_params=pltpu.CompilerParams(vmem_limit_bytes=VMEM_LIMIT),
        cost_estimate=pl.CostEstimate(flops=10_000_000_000, bytes_accessed=20_000_000, transcendentals=0),
    )(length, x, w, turns)


def attention_back_kernel(
    length_ref,
    q_ref,
    k_ref,
    v_ref,
    heads_ref,
    lse_ref,
    turn_ref,
    g_ref,
    y_ref,
    w_ref,
    x_ref,
    terms_ref,
    dx_ref,
    sum_ref,
    weights,
    tokens,
    dheads,
    dfused,
    dk,
    dv,
    mine,
    far,
    hop_x,
    hop_y,
    last_x,
    last_y,
    far_d,
    last_d,
    out_grad,
    qkv_grad,
    out_there,
    qkv_there,
    local_sems,
    send_sems,
    recv_sems,
):
    s, n, core, across, beside = places()
    other = (core + 2) % 4
    to_core, to_y, to_x = {"seq": core}, {"seq": across}, {"near": beside}
    rows = g_ref.shape[0]
    half = rows // 2
    size = k_ref.shape[1]
    low = jnp.bfloat16
    length = length_ref[0]
    far_size = terms_ref.shape[0]

    def local(source, target, at):
        copy = pltpu.make_async_copy(source, target, local_sems.at[at])
        copy.start()
        return copy

    def part(ref, p):
        return ref.at[pl.ds(p * half, half)]

    def token_rows(seq, p):
        return tokens.at[pl.ds(seq * rows + p * half, half)]

    def block(seq, near):
        return y_ref.at[pl.ds((seq * 2 + near) * rows, rows)]

    meet(to_core, to_y, to_x)
    copies, send = sender(send_sems, recv_sems)
    keep = local(g_ref, tokens.at[pl.ds(s * rows, rows)], 0)
    for p in range(2):
        send(("gy", p), part(g_ref, p), token_rows(s, p), to_y)
    for p in range(2):
        send(("gc", p), part(g_ref, p), token_rows(s, p), to_core)
    given = [block(other, beside), block(other, n), block(core, beside), block(core, n)]
    kept = [block(across, beside), block(across, n), block(s, beside), block(s, n)]
    loads = []
    for k in range(4):
        send(k, given[k], far.at[k], to_core)
        loads.append(local(kept[k], mine.at[k], 1 + k))
    load_w = local(w_ref, weights, 5)
    for k in range(3):
        loads[k].wait()
        copies[k].wait_recv()
        add_rows(mine.at[k], mine.at[k], far.at[k])
        if k == 0:
            send("hx", part(mine.at[0], 0), hop_x, to_x)
    send("x0", part(mine.at[2], 0), part(last_x, 0), to_x)
    for p in range(2):
        copies["gy", p].wait_recv()
        send(("gyc", p), token_rows(across, p), token_rows(across, p), to_core)
    send("hy", part(mine.at[0], 1), hop_y, to_y)
    send("y1", part(mine.at[1], 1), part(last_y, 1), to_y)
    loads[3].wait()
    copies[3].wait_recv()
    add_rows(sum_ref, mine.at[3], far.at[3])
    keep.wait()
    load_w.wait()
    for p in range(2):
        copies["gc", p].wait_recv()
        copies["gyc", p].wait_recv()

    def dheads_of(tile, carry):
        at = tile_at(tile, rows)
        live = lax.broadcasted_iota(jnp.int32, (rows, 1), 0) + tile * rows < length
        value = product(tokens[at, :], weights[:, 4 * size :], 1, 0)
        dheads[at, :] = jnp.where(live, value, 0.0).astype(low)
        return carry

    def by_rows(value):
        return value.astype(low).reshape(far_size, 2, -1, value.shape[1])

    width = tokens.shape[1]
    quarter = width // 4
    for q in range(4):
        out_grad[q] = by_rows(product(tokens[:, q * quarter : (q + 1) * quarter], heads_ref[...], 0, 0))
    send("out", out_grad.at[:, :, beside], out_there, to_x)
    lax.fori_loop(0, 4, dheads_of, 0)
    for copy in ("gyc", "gy", "gc"):
        for p in range(2):
            copies[copy, p].wait_send()
    load_x = local(x_ref, tokens, 0)
    copies["hx"].wait_recv()
    add_rows(part(mine.at[1], 0), part(mine.at[1], 0), hop_x)
    send("y0", part(mine.at[1], 0), part(last_y, 0), to_y)
    copies["hy"].wait_recv()
    add_rows(part(mine.at[2], 1), part(mine.at[2], 1), hop_y)
    send("x1", part(mine.at[2], 1), part(last_x, 1), to_x)

    dk[...] = jnp.zeros_like(dk)
    dv[...] = jnp.zeros_like(dv)
    for tile in range(4):
        at = pl.ds(tile * rows, rows)
        keys = (tile + 1) * rows
        query = stacked(q_ref[at, :])
        dhead = stacked(dheads[at, :])
        scores = product(query, k_ref[:keys, :], 1, 1)
        lse = jnp.concatenate([lse_ref[at, 0:1], lse_ref[at, 1:2]], 0)
        probs = jnp.where(visible_keys(tile, rows, keys, length), jnp.exp(scores - lse), 0.0)
        dprobs = product(dhead, v_ref[:keys, :], 1, 1)
        inner = jnp.sum(probs * dprobs, 1, keepdims=True)
        dscores = (probs * (dprobs - inner)).astype(low)
        dv[:keys, :] += product(probs.astype(low), dhead, 0, 0)
        dk[:keys, :] += product(dscores, query, 0, 0)
        dquery = product(dscores, k_ref[:keys, :], 1, 0) * size**-0.5
        cos, sin = turn_ref[at, : size // 2], turn_ref[at, size // 2 :]
        for head in range(2):
            rounded = dquery[head * rows : (head + 1) * rows].astype(low).astype(jnp.float32)
            first, second = turned(rounded, cos, -sin)
            dfused[at, head * size : head * size + size // 2] = first.astype(low)
            dfused[at, head * size + size // 2 : (head + 1) * size] = second.astype(low)
    first, second = turned(
        dk[...].astype(low).astype(jnp.float32), turn_ref[:, : size // 2], -turn_ref[:, size // 2 :]
    )
    dfused[:, 2 * size : 2 * size + size // 2] = first.astype(low)
    dfused[:, 2 * size + size // 2 : 3 * size] = second.astype(low)
    dfused[:, 3 * size :] = dv[...].astype(low)

    load_x.wait()
    for q in range(4):
        qkv_grad[q] = by_rows(product(tokens[:, q * quarter : (q + 1) * quarter], dfused[...], 0, 0))
        send(("qkv", q), qkv_grad.at[q, :, beside], qkv_there.at[q], to_x)

    for p, first, second in ((1, "y1", "x1"), (0, "x0", "y0")):
        copies[first].wait_recv()
        copies[second].wait_recv()
        add_rows(part(sum_ref, p), part(sum_ref, p), part(last_x, p), part(last_y, p))
    for key in ("hx", "hy", "y0", "y1", "x0", "x1"):
        copies[key].wait_send()

    def dx_of(k, tile):
        mine[k] = product(dfused[tile_at(tile, rows), :], weights[:, : 4 * size], 1, 1).astype(low)

    dx_of(0, other)
    send("d0", mine.at[0], far_d.at[0], to_core)
    dx_of(1, core)
    send("d1", mine.at[1], far_d.at[1], to_core)
    dx_of(2, across)
    copies["d0"].wait_recv()
    for p in range(2):
        add_rows(part(mine.at[2], p), part(mine.at[2], p), part(far_d.at[0], p))
        send(("dy", p), part(mine.at[2], p), part(last_d, p), to_y)
    dx_of(3, s)
    copies["d1"].wait_recv()
    add_rows(dx_ref, mine.at[3], far_d.at[1])
    outs = []
    copies["out"].wait_recv()
    for q in range(4):
        for f in range(far_size):
            out_there[q, f] = (
                out_there[q, f].astype(jnp.float32) + out_grad[q, f, n].astype(jnp.float32)
            ).astype(low)
    for p in range(2):
        copies["dy", p].wait_recv()
        add_rows(part(dx_ref, p), part(dx_ref, p), part(last_d, p))
    for q in range(4):
        copies["qkv", q].wait_recv()
        for f in range(far_size):
            qkv_there[q, f] = (
                qkv_there[q, f].astype(jnp.float32) + qkv_grad[q, f, n].astype(jnp.float32)
            ).astype(low)
        outs.append(local(out_there.at[q], terms_ref.at[:, q, :, 4 * size :], q))
        outs.append(local(qkv_there.at[q], terms_ref.at[:, q, :, : 4 * size], 4 + q))
    for copy in outs:
        copy.wait()
    waited = {"hx", "hy", "y0", "y1", "x0", "x1"}
    for key, copy in copies.items():
        if key not in waited and not (isinstance(key, tuple) and key[0] in ("gyc", "gy", "gc")):
            copy.wait_send()


def attention_back(length, saved, turns, g, y, w, x, collective_id):
    q, k, v, heads, lse = saved
    tokens, width = x.shape
    size = k.shape[1]
    rows = tokens // 4
    far_size = lax.axis_size("far")
    weight_rows = width // (8 * far_size)
    low = jnp.bfloat16
    block = pltpu.VMEM((rows, width), low)
    half_block = pltpu.VMEM((rows // 2, width), low)
    return pl.pallas_call(
        attention_back_kernel,
        out_shape=[
            jax.ShapeDtypeStruct((far_size, 4, weight_rows, 6 * size), low),
            jax.ShapeDtypeStruct((rows, width), jnp.float32),
            jax.ShapeDtypeStruct((rows, width), jnp.float32),
        ],
        in_specs=[pl.BlockSpec(memory_space=pltpu.SMEM)] + [IN_VMEM] * 6 + [ANYWHERE] * 4,
        out_specs=[ANYWHERE, IN_VMEM, IN_VMEM],
        scratch_shapes=[
            pltpu.VMEM(w.shape, low),
            pltpu.VMEM((tokens, width), low),
            pltpu.VMEM((tokens, 2 * size), low),
            pltpu.VMEM((tokens, 4 * size), low),
            pltpu.VMEM((tokens, size), jnp.float32),
            pltpu.VMEM((tokens, size), jnp.float32),
            pltpu.VMEM((4, rows, width), low),
            pltpu.VMEM((4, rows, width), low),
            half_block,
            half_block,
            block,
            block,
            pltpu.VMEM((2, rows, width), low),
            block,
            pltpu.VMEM((4, far_size, 2, weight_rows, 2 * size), low),
            pltpu.VMEM((4, far_size, 2, weight_rows, 4 * size), low),
            pltpu.VMEM((4, far_size, weight_rows, 2 * size), low),
            pltpu.VMEM((4, far_size, weight_rows, 4 * size), low),
            pltpu.SemaphoreType.DMA((8,)),
            pltpu.SemaphoreType.DMA((25,)),
            pltpu.SemaphoreType.DMA((25,)),
        ],
        compiler_params=pltpu.CompilerParams(
            collective_id=collective_id, has_side_effects=True, vmem_limit_bytes=VMEM_LIMIT
        ),
        cost_estimate=pl.CostEstimate(flops=20_000_000_000, bytes_accessed=40_000_000, transcendentals=0),
    )(length, q, k, v, heads, lse, turns, g, y, w, x)


def feed_kernel(x_ref, d_ref, w_ref, *refs):
    before, (act_ref, dgu_ref, y_ref, dx_ref) = refs[:-4], refs[-4:]
    part = w_ref.shape[1] // 3
    low = jnp.bfloat16
    x = x_ref[...]
    gate = product(x, w_ref[:, :part], 1, 0)
    upper = product(x, w_ref[:, part : 2 * part], 1, 0)
    dact = product(d_ref[...], w_ref[:, 2 * part :], 1, 0)
    sig = 1.0 / (1.0 + jnp.exp(-gate))
    silu = gate * sig
    act = (silu * upper).astype(low)
    act_ref[...] = act
    dgu_ref[:, :part] = (dact * upper * (sig + silu * (1.0 - sig))).astype(low)
    dgu_ref[:, part:] = (dact * silu).astype(low)
    y = product(act, w_ref[:, 2 * part :], 1, 1)
    dx = product(dgu_ref[...], w_ref[:, : 2 * part], 1, 1)
    if before:
        y = y + before[0][...].astype(jnp.float32)
        dx = dx + before[1][...].astype(jnp.float32)
    y_ref[...] = y.astype(low)
    dx_ref[...] = dx.astype(low)


def feed(x, d, w, before, tile=512):
    tokens, width = x.shape
    part = w.shape[1] // 3
    low = jnp.bfloat16

    def tokens_of(columns):
        return pl.BlockSpec((tile, columns), lambda t: (t, 0))

    whole = pl.BlockSpec(w.shape, lambda t: (0, 0), pipeline_mode=pl.Buffered(1))
    sizes = (part, 2 * part, width, width)
    return pl.pallas_call(
        feed_kernel,
        grid=(tokens // tile,),
        out_shape=[jax.ShapeDtypeStruct((tokens, columns), low) for columns in sizes],
        in_specs=[tokens_of(width), tokens_of(width), whole] + [tokens_of(width)] * len(before),
        out_specs=[tokens_of(columns) for columns in sizes],
        compiler_params=pltpu.CompilerParams(vmem_limit_bytes=VMEM_LIMIT),
        cost_estimate=pl.CostEstimate(flops=12 * tokens * width * part, bytes_accessed=60_000_000, transcendentals=0),
    )(x, d, w, *before)


def feed_grads_kernel(x_ref, d_ref, dgu_ref, act_ref, o_ref):
    split = dgu_ref.shape[1]
    o_ref[:, :split] = product(x_ref[...], dgu_ref[...], 0, 0).astype(o_ref.dtype)
    o_ref[:, split:] = product(d_ref[...], act_ref[...], 0, 0).astype(o_ref.dtype)

def feed_grads(x, d, dgu, act, tile=256):
    tokens, width = x.shape
    columns = dgu.shape[1] + act.shape[1]
    some = pl.BlockSpec((tokens, tile), lambda t: (0, t))

    def whole(array):
        return pl.BlockSpec(array.shape, lambda t: (0, 0), pipeline_mode=pl.Buffered(1))

    return pl.pallas_call(
        feed_grads_kernel,
        grid=(width // tile,),
        out_shape=jax.ShapeDtypeStruct((width, columns), x.dtype),
        in_specs=[some, some, whole(dgu), whole(act)],
        out_specs=pl.BlockSpec((tile, columns), lambda t: (t, 0)),
        compiler_params=pltpu.CompilerParams(vmem_limit_bytes=VMEM_LIMIT),
        cost_estimate=pl.CostEstimate(flops=2 * tokens * width * columns, bytes_accessed=40_000_000, transcendentals=0),
    )(x, d, dgu, act)


def rotary_tables(positions, width):
    half = width // 2
    freqs = jnp.exp(-(jnp.arange(half, dtype=jnp.float32) * 2.0 / width) * math.log(ROPE_BASE))
    angles = positions.astype(jnp.float32)[:, None] * freqs
    return jnp.concatenate([jnp.cos(angles), jnp.sin(angles)], -1)


def rms_normalize(value_rows):
    inverse_scale = lax.rsqrt(jnp.mean(value_rows * value_rows, -1, keepdims=True) + NORM_EPSILON)
    return (value_rows * inverse_scale, inverse_scale)


def norm_backward(unit_gradient, unit_input, inverse_scale):
    return inverse_scale * (
        unit_gradient - unit_input * jnp.mean(unit_gradient * unit_input, -1, keepdims=True)
    )


def adam_step(weight, grad, first, second, rate, decay):
    first_new = BETA_ONE * first + (1.0 - BETA_ONE) * grad
    second_new = BETA_TWO * second + (1.0 - BETA_TWO) * grad * grad
    corr_one = 1.0 - BETA_ONE**STEP
    corr_two = 1.0 - BETA_TWO**STEP
    update = (first_new * (1.0 / corr_one)) / (jnp.sqrt(second_new * (1.0 / corr_two)) + ADAM_EPSILON)
    return (weight - rate * (update + decay * weight), first_new, second_new)


def feed_pieces(part):
    gateup, down = [], []
    for half in range(2):
        for device in range(8):
            start = (half * 8 + device) * part
            gateup.append((half, device, 0, start))
            gateup.append((half, device, part, FEED_UNITS + start))
            down.append((half, device, 2 * part, start))
    return gateup, down


def head_pieces_of(columns):
    key = columns // 6
    query = 2 * key
    qkv, out = [], []
    for device in range(4):
        qkv.append((device, 0, device * query, query))
        qkv.append((device, query, 4 * query + device * key, key))
        qkv.append((device, query + key, 4 * (query + key) + device * key, key))
        out.append((device, query + 2 * key, device * query, query))
    return qkv, out


def norm_kernel(zero_ref, one_ref, head_ref, qkv_ref, gateup_ref, gains_ref, square_ref, gain_grads_ref):
    halves = (zero_ref, one_ref)
    part = zero_ref.shape[2] // 3
    gateup, down = feed_pieces(part)
    qkv, out = head_pieces_of(head_ref.shape[2])
    gains = gains_ref[...].astype(jnp.bfloat16).astype(jnp.float32)

    def low(x):
        return x.astype(jnp.bfloat16).astype(jnp.float32)

    def over(x):
        return jnp.sum(x, 1, keepdims=True)

    two_squares = two_terms = down_squares = 0.0
    for half, device, at, column in gateup:
        grad = halves[half][device, :, at : at + part].astype(jnp.float32)
        two_squares = two_squares + grad * grad
        two_terms = two_terms + grad * low(gateup_ref[:, column : column + part])
    for half, device, at, column in down:
        grad = halves[half][device, :, at : at + part].astype(jnp.float32)
        down_squares = down_squares + grad * grad
    one_squares = one_terms = out_squares = 0.0
    for device, at, column, size in qkv:
        grad = head_ref[device, :, at : at + size].astype(jnp.float32)
        one_squares = one_squares + over(grad * grad)
        one_terms = one_terms + over(grad * low(qkv_ref[:, column : column + size]))
    for device, at, column, size in out:
        grad = head_ref[device, :, at : at + size].astype(jnp.float32)
        out_squares = out_squares + over(grad * grad)
    two_terms = over(two_terms)
    gain_grads_ref[:, 0:1] = one_terms
    gain_grads_ref[:, 1:2] = two_terms
    one, two = gains[:, 0:1], gains[:, 1:2]
    rows = (
        one * one * one_squares
        + two * two * over(two_squares)
        + over(down_squares)
        + out_squares
        + one_terms * one_terms
        + two_terms * two_terms
    )
    total = jnp.sum(rows)

    @pl.when(pl.program_id(0) == 0)
    def _():
        square_ref[0, 0] = total

    @pl.when(pl.program_id(0) > 0)
    def _():
        square_ref[0, 0] = square_ref[0, 0] + total


ROWS = 16


def rows_of(array):
    if array.ndim == 3:
        return pl.BlockSpec((array.shape[0], ROWS, array.shape[2]), lambda r: (0, r, 0))
    return pl.BlockSpec((ROWS, array.shape[1]), lambda r: (r, 0))


def gradient_norm(zero, one, head, qkv, gateup, gains):
    arrays = (zero, one, head, qkv, gateup, gains)
    return pl.pallas_call(
        norm_kernel,
        grid=(gains.shape[0] // ROWS,),
        out_shape=[jax.ShapeDtypeStruct((1, 1), jnp.float32), jax.ShapeDtypeStruct(gains.shape, jnp.float32)],
        in_specs=[rows_of(x) for x in arrays],
        out_specs=[pl.BlockSpec(memory_space=pltpu.SMEM), rows_of(gains)],
        compiler_params=pltpu.CompilerParams(vmem_limit_bytes=VMEM_LIMIT),
    )(*arrays)


def adam_kernel(clip_ref, zero_ref, one_ref, head_ref, gain_grads_ref, *refs):
    weights, firsts, seconds = refs[0:5], refs[5:10], refs[10:15]
    weights_out, firsts_out, seconds_out = refs[15:20], refs[20:25], refs[25:30]
    halves = (zero_ref, one_ref)
    part = zero_ref.shape[2] // 3
    gateup, down = feed_pieces(part)
    qkv, out = head_pieces_of(head_ref.shape[2])
    clip = clip_ref[0, 0]
    gains = weights[4][...].astype(jnp.bfloat16).astype(jnp.float32) * clip
    one, two = gains[:, 0:1], gains[:, 1:2]

    def step(which, columns, grad, rate, decay):
        new = adam_step(
            weights[which][:, columns], grad, firsts[which][:, columns], seconds[which][:, columns], rate, decay
        )
        weights_out[which][:, columns] = new[0]
        firsts_out[which][:, columns] = new[1]
        seconds_out[which][:, columns] = new[2]

    for pieces, which, scale, rate in ((qkv, 0, one, RATE_MATRIX), (out, 1, clip, RATE_OUTPUT)):
        for device, at, column, size in pieces:
            grad = head_ref[device, :, at : at + size].astype(jnp.float32) * scale
            step(which, slice(column, column + size), grad, rate, DECAY_MATRIX)
    for pieces, which, scale in ((gateup, 2, two), (down, 3, clip)):
        for half, device, at, column in pieces:
            grad = halves[half][device, :, at : at + part].astype(jnp.float32) * scale
            step(which, slice(column, column + part), grad, RATE_MATRIX, DECAY_MATRIX)
    step(4, slice(0, 2), gain_grads_ref[...] * clip, RATE_GAIN, 0.0)


def adam(clip, zero, one, head, gain_grads, weights, firsts, seconds):
    state = (*weights, *firsts, *seconds)
    arrays = (zero, one, head, gain_grads, *state)
    return pl.pallas_call(
        adam_kernel,
        grid=(gain_grads.shape[0] // ROWS,),
        out_shape=[jax.ShapeDtypeStruct(x.shape, x.dtype) for x in state],
        in_specs=[pl.BlockSpec(memory_space=pltpu.SMEM)] + [rows_of(x) for x in arrays],
        out_specs=[rows_of(x) for x in state],
        compiler_params=pltpu.CompilerParams(vmem_limit_bytes=VMEM_LIMIT),
    )(clip, *arrays)


def product(left, right, left_dim, right_dim):
    return lax.dot_general(
        left, right, (((left_dim,), (right_dim,)), ((), ())), preferred_element_type=jnp.float32
    )


def shards(
    inputs,
    cotangent,
    lengths,
    positions,
    query_key_value_weight,
    out_weight,
    gateup_weight,
    down_weight,
    norm_gains,
    query_key_value_moment,
    output_weight_moment,
    gate_up_moment,
    down_weight_moment,
    norm_gains_moment,
    query_key_value_variance,
    out_second,
    gateup_second,
    down_second,
    gains_second,
):
    width = inputs.shape[2]
    seq = lax.axis_size("seq")
    far = lax.axis_size("far")
    group = seq * 2
    rows = out_weight.shape[0]
    query_width = QUERY_HEAD_COUNT * HEAD_SIZE
    key_width = KEY_VALUE_HEADS * HEAD_SIZE
    mine_q, mine_k = query_width // seq, key_width // seq
    units = FEED_UNITS // group
    part = units // 2
    low = jnp.bfloat16

    inputs = inputs[0]
    cotangent = cotangent[0]
    gains = norm_gains.astype(low).astype(jnp.float32)
    gain_one, gain_two = gains[:, :1], gains[:, 1:]

    def after(x, *others):
        return lax.optimization_barrier((x, *others))[0]

    def rounded(weight, gain=None):
        weight = weight.astype(low)
        return weight if gain is None else (weight.astype(jnp.float32) * gain).astype(low)

    def far_first(x):
        x = x.reshape(-1, seq, far, 2 * rows).transpose(0, 2, 1, 3)
        return x.reshape(-1, width)

    def far_last(x):
        return x.reshape(-1, far, seq, 2 * rows).transpose(0, 2, 1, 3).reshape(-1, width)

    def feed_piece(half):
        start, size = half * FEED_UNITS // 2, FEED_UNITS // 2
        columns = [
            rounded(gateup_weight[:, start : start + size], gain_two),
            rounded(gateup_weight[:, FEED_UNITS + start : FEED_UNITS + start + size], gain_two),
            rounded(down_weight[:, start : start + size]),
        ]
        columns = [x.reshape(rows, group, part).transpose(1, 0, 2) for x in columns]
        return jnp.concatenate(columns, 2)

    (piece,) = exchange_plane([feed_piece(0).reshape(group * rows, 3 * part)], 1)
    feed_zero = lax.all_gather(piece, "far", axis=0, tiled=True)

    qkv_low = rounded(query_key_value_weight, gain_one)
    head_pieces = jnp.concatenate(
        [
            qkv_low[:, :query_width].reshape(rows, seq, mine_q),
            qkv_low[:, query_width : query_width + key_width].reshape(rows, seq, mine_k),
            qkv_low[:, query_width + key_width :].reshape(rows, seq, mine_k),
            rounded(out_weight).reshape(rows, seq, mine_q),
        ],
        2,
    ).transpose(1, 0, 2)
    unit_one, scale_one = rms_normalize(inputs)
    turns = rotary_tables(positions.reshape(-1), HEAD_SIZE)
    dout_here = far_first(cotangent.astype(low))
    head_pieces = after(head_pieces, piece)
    head_w, normed_one, all_turns, dout, piece = gather_heads(
        head_pieces, unit_one.astype(low), turns, dout_here, feed_piece(1), 2
    )
    feed_one = lax.all_gather(piece.reshape(group * rows, -1), "far", axis=0, tiled=True)
    all_turns = all_turns.reshape(-1, HEAD_SIZE)
    *saved, attended = attention(lengths, normed_one, head_w, all_turns)
    hidden = inputs + scatter_seq(attended, 3)
    unit_two, scale_two = rms_normalize(hidden)
    normed_two = gather_plane(far_first(unit_two.astype(low)), 4)
    act_zero, dgateup_zero, *sums = feed(normed_two, dout, feed_zero, ())
    terms_zero = feed_grads(normed_two, dout, dgateup_zero, act_zero)
    feed_one = after(feed_one, terms_zero)
    act_one, dgateup_one, output_terms, dnormed_two = feed(normed_two, dout, feed_one, sums)
    dnormed_two = scatter_plane(dnormed_two, 5)
    dgateup_one = after(dgateup_one, dnormed_two)
    terms_one = feed_grads(normed_two, dout, dgateup_one, act_one)
    dnormed_two = far_last(dnormed_two)
    grads_zero = lax.psum_scatter(terms_zero, "far", scatter_dimension=0, tiled=True)
    grads_one = lax.psum_scatter(
        after(terms_one, grads_zero), "far", scatter_dimension=0, tiled=True
    )
    back_two = norm_backward(dnormed_two, unit_two, scale_two)
    dhidden = cotangent + back_two

    dattended = after(dhidden.astype(low), terms_one)
    head_terms, dnormed_one, output_terms = attention_back(
        lengths, saved, all_turns, dattended, output_terms, head_w, normed_one, 6
    )
    head_terms = after(head_terms, grads_zero, grads_one)
    head_terms = lax.psum_scatter(
        head_terms.reshape(far * seq * rows, -1), "far", scatter_dimension=0, tiled=True
    )
    input_grad = dhidden + norm_backward(dnormed_one, unit_one, scale_one)
    layer_output = hidden + far_last(output_terms)

    halves = exchange_plane([grads_zero, grads_one], 7)
    head_terms = after(head_terms, halves[0])
    halves = [x.reshape(group, rows, 3 * part) for x in halves]
    head_grads = lax.all_to_all(head_terms.reshape(seq, rows, -1), "seq", 0, 0, tiled=True)

    weights = (query_key_value_weight, out_weight, gateup_weight, down_weight, norm_gains)
    firsts = (query_key_value_moment, output_weight_moment, gate_up_moment, down_weight_moment, norm_gains_moment)
    seconds = (query_key_value_variance, out_second, gateup_second, down_second, gains_second)
    squares, gain_grads = gradient_norm(
        *halves, head_grads, query_key_value_weight, gateup_weight, norm_gains
    )
    squares = lax.psum(lax.psum(lax.psum(squares[0, 0], "seq"), "near"), "far")
    grad_norm = jnp.sqrt(squares)
    clip = CLIP_NORM / jnp.maximum(grad_norm, CLIP_NORM)
    stepped = adam(clip.reshape(1, 1), *halves, head_grads, gain_grads, weights, firsts, seconds)
    return (layer_output[None], input_grad[None], grad_norm, *stepped)


def solution(mesh):
    seq, fsdp = mesh.shape["seq"], mesh.shape["fsdp"]
    cut = Mesh(mesh.devices.reshape(seq, fsdp // 2, 2), EVERY)
    tokens = P(("far", "near"), "seq", None)
    matrix = P(EVERY, None)
    return jax.shard_map(
        shards,
        mesh=cut,
        in_specs=(tokens, tokens, P(("far", "near")), P(("far", "near"), "seq")) + (matrix,) * 15,
        out_specs=(tokens, tokens, P()) + (matrix,) * 15,
        check_vma=False,
    )
```

```python
import functools
import math

import jax
import jax.numpy as jnp
from jax import lax
from jax.experimental import pallas as pl
from jax.experimental.pallas import tpu as pltpu
from jax.sharding import Mesh, PartitionSpec as P

QUERY_HEAD_COUNT = 8
KEY_VALUE_HEADS = 4
HEAD_SIZE = 256
FEED_UNITS = 8192
STEP = 10

NORM_EPSILON = 1e-06
ROPE_BASE = 1000042.0
MASKED_SCORE = -1000000000.0
CLIP_NORM = 1.0
BETA_ONE = 0.9
BETA_TWO = 0.95
ADAM_EPSILON = 1e-08
DECAY_MATRIX = 0.1
RATE_MATRIX = 0.02
RATE_OUTPUT = 0.1
RATE_GAIN = 1.0

EVERY = ("seq", "far", "near")


MESH_IDS = pl.DeviceIdType.MESH
ANYWHERE = pl.BlockSpec(memory_space=pl.ANY)
IN_VMEM = pl.BlockSpec(memory_space=pltpu.VMEM)
VMEM_LIMIT = 60 * 1024 * 1024


def places():
    s, n = lax.axis_index("seq"), lax.axis_index("near")
    return s, n, s + 1 - 2 * (s % 2), (s + 2) % 4, 1 - n


def meet(*others):
    barrier = pltpu.get_barrier_semaphore()
    for other in others:
        pl.semaphore_signal(barrier, inc=1, device_id=other, device_id_type=MESH_IDS)
    pl.semaphore_wait(barrier, len(others))


def sender(send_sems, recv_sems):
    copies = {}

    def send(key, source, target, device):
        at = len(copies)
        copies[key] = pltpu.make_async_remote_copy(
            src_ref=source,
            dst_ref=target,
            send_sem=send_sems.at[at],
            recv_sem=recv_sems.at[at],
            device_id=device,
            device_id_type=MESH_IDS,
        )
        copies[key].start()

    return copies, send


def add_rows(target, first, second, third=None, step=64):
    rows = target.shape[0]

    def body(i, carry):
        at = pl.ds(pl.multiple_of(i * step, step), step)
        total = first[at, :].astype(jnp.float32) + second[at, :].astype(jnp.float32)
        if third is not None:
            total = total + third[at, :].astype(jnp.float32)
        target[at, :] = total.astype(target.dtype)
        return carry

    lax.fori_loop(0, rows // step, body, 0)


def scatter_seq_kernel(rows, p_ref, o_ref, mine, far, last, local_sems, send_sems, recv_sems):
    s, _, core, across, _ = places()
    half = rows // 2
    to_core, to_y = {"seq": core}, {"seq": across}

    def block(seq):
        return p_ref.at[pl.ds(seq * rows, rows)]

    meet(to_core, to_y)
    copies, send = sender(send_sems, recv_sems)
    given = [block((core + 2) % 4), block(core)]
    kept = [block(across), block(s)]
    locals_ = []
    for k in range(2):
        send(k, given[k], far.at[k], to_core)
        locals_.append(pltpu.make_async_copy(kept[k], mine.at[k], local_sems.at[k]))
        locals_[k].start()
    locals_[0].wait()
    copies[0].wait_recv()
    for p in range(2):
        at = pl.ds(p * half, half)
        add_rows(mine.at[0, at], mine.at[0, at], far.at[0, at])
        send(("y", p), mine.at[0, at], last.at[at], to_y)
    locals_[1].wait()
    copies[1].wait_recv()
    add_rows(o_ref, mine.at[1], far.at[1])
    for p in range(2):
        at = pl.ds(p * half, half)
        copies["y", p].wait_recv()
        add_rows(o_ref.at[at], o_ref.at[at], last.at[at])
    for copy in copies.values():
        copy.wait_send()


def scatter_seq(p, collective_id):
    rows, columns = p.shape[0] // 4, p.shape[1]
    low = jnp.bfloat16
    return pl.pallas_call(
        functools.partial(scatter_seq_kernel, rows),
        out_shape=jax.ShapeDtypeStruct((rows, columns), jnp.float32),
        in_specs=[ANYWHERE],
        out_specs=IN_VMEM,
        scratch_shapes=[
            pltpu.VMEM((2, rows, columns), low),
            pltpu.VMEM((2, rows, columns), low),
            pltpu.VMEM((rows, columns), low),
            pltpu.SemaphoreType.DMA((2,)),
            pltpu.SemaphoreType.DMA((4,)),
            pltpu.SemaphoreType.DMA((4,)),
        ],
        compiler_params=pltpu.CompilerParams(
            collective_id=collective_id, has_side_effects=True, vmem_limit_bytes=VMEM_LIMIT
        ),
    )(p)


def exchange_plane_kernel(count, *refs):
    x_refs, o_refs = refs[:count], refs[count : 2 * count]
    local_sems, send_sems, recv_sems = refs[2 * count :]
    s, n, core, across, beside = places()
    diagonal = (core + 2) % 4
    mine = s * 2 + n
    others = [(seq, near) for near in (beside, n) for seq in (diagonal, across, core, s)][:-1]

    meet(*[{"seq": seq, "near": near} for seq, near in others])
    copies, send = sender(send_sems, recv_sems)
    locals_ = []
    for k, (x_ref, o_ref) in enumerate(zip(x_refs, o_refs)):
        rows = x_ref.shape[0] // 8

        def at(p):
            return pl.ds(p * rows, rows)

        for seq, near in others:
            target = {"seq": seq, "near": near}
            send(len(copies), x_ref.at[at(seq * 2 + near)], o_ref.at[at(mine)], target)
        locals_.append(pltpu.make_async_copy(x_ref.at[at(mine)], o_ref.at[at(mine)], local_sems.at[k]))
        locals_[k].start()
    for copy in copies.values():
        copy.wait_recv()
    for copy in copies.values():
        copy.wait_send()
    for copy in locals_:
        copy.wait()


def exchange_plane(arrays, collective_id):
    count = len(arrays)
    return pl.pallas_call(
        functools.partial(exchange_plane_kernel, count),
        out_shape=[jax.ShapeDtypeStruct(x.shape, x.dtype) for x in arrays],
        in_specs=[ANYWHERE] * count,
        out_specs=[ANYWHERE] * count,
        scratch_shapes=[
            pltpu.SemaphoreType.DMA((count,)),
            pltpu.SemaphoreType.DMA((7 * count,)),
            pltpu.SemaphoreType.DMA((7 * count,)),
        ],
        compiler_params=pltpu.CompilerParams(collective_id=collective_id, has_side_effects=True),
    )(*arrays)


def gather_heads_kernel(
    far_size,
    w_ref,
    x_ref,
    i_ref,
    d_ref,
    e_ref,
    o_ref,
    ox_ref,
    oi_ref,
    od_ref,
    oe_ref,
    local_sems,
    send_sems,
    recv_sems,
):
    s, n, core, across, beside = places()
    diagonal = (core + 2) % 4
    f = lax.axis_index("far")
    half = x_ref.shape[0] // 2
    to_core, to_y, to_x = {"seq": core}, {"seq": across}, {"near": beside}
    right, left = {"far": (f + 1) % far_size}, {"far": (f + far_size - 1) % far_size}

    others = [(seq, near) for near in (beside, n) for seq in (diagonal, across, core, s)][:-1]
    meet(*[{"seq": seq, "near": near} for seq, near in others], right, left)
    copies, send = sender(send_sems, recv_sems)
    keep = pltpu.make_async_copy(w_ref.at[s], o_ref.at[s, f, n], local_sems.at[0])
    keep.start()
    keep_x = pltpu.make_async_copy(x_ref, ox_ref.at[s], local_sems.at[1])
    keep_x.start()
    keep_i = pltpu.make_async_copy(i_ref, oi_ref.at[s], local_sems.at[2])
    keep_i.start()
    for k, seq in enumerate((diagonal, across, core)):
        send(("w", k), w_ref.at[seq], o_ref.at[s, f, n], {"seq": seq})
        send(("i", k), i_ref, oi_ref.at[s], {"seq": seq})
    for p in range(2):
        at = pl.ds(p * half, half)
        send(("y", p), x_ref.at[at], ox_ref.at[s, at], to_y)
        send(("c", p), x_ref.at[at], ox_ref.at[s, at], to_core)

    def block(seq, near, p):
        return od_ref.at[seq * 2 + near, pl.ds(p * half, half)]

    def own(p):
        return d_ref.at[pl.ds(p * half, half)]

    keep_d = pltpu.make_async_copy(d_ref, od_ref.at[s * 2 + n], local_sems.at[3])
    keep_d.start()
    send("y0", own(0), block(s, n, 0), to_y)
    send("x1", own(1), block(s, n, 1), to_x)
    send("y1", own(1), block(s, n, 1), to_y)
    send("x0", own(0), block(s, n, 0), to_x)
    send("c0", own(0), block(s, n, 0), to_core)
    send("c1", own(1), block(s, n, 1), to_core)
    keep_e = pltpu.make_async_copy(e_ref.at[s * 2 + n], oe_ref.at[s * 2 + n], local_sems.at[4])
    keep_e.start()
    for k, (seq, near) in enumerate(others):
        target = {"seq": seq, "near": near}
        send(("e", k), e_ref.at[seq * 2 + near], oe_ref.at[s * 2 + n], target)
    keep.wait()
    for k in range(3):
        copies["w", k].wait_recv()

    def along(far, p, device, sem):
        piece = o_ref.at[p, far, n]
        return pltpu.make_async_remote_copy(
            src_ref=piece,
            dst_ref=piece,
            send_sem=send_sems.at[base + 4 * sem + p],
            recv_sem=recv_sems.at[base + 4 * sem + p],
            device_id=device,
            device_id_type=MESH_IDS,
        )

    base = 33

    def to_right(k, p):
        return along((f + far_size - k) % far_size, p, right, k)

    def to_left(k, p):
        return along((f + k) % far_size, p, left, far_size + k)

    def x_from_left(k, p):
        return along((f + far_size - k) % far_size, p, to_x, 2 * far_size + k)

    def x_from_right(k, p):
        return along((f + k) % far_size, p, to_x, 3 * far_size + k)

    for k in range(far_size):
        for p in range(4):
            if k > 0:

                @pl.when(f >= k)
                def _():
                    to_right(k - 1, p).wait_recv()

            @pl.when((f >= k) & (f < far_size - 1))
            def _():
                to_right(k, p).start()

            if k > 0:

                @pl.when(f + k < far_size)
                def _():
                    to_left(k - 1, p).wait_recv()

            @pl.when((f + k < far_size) & (f > 0))
            def _():
                to_left(k, p).start()

            if k == 0:
                x_from_left(0, p).start()
            else:

                @pl.when(f >= k)
                def _():
                    x_from_left(k, p).start()

                @pl.when(f + k < far_size)
                def _():
                    x_from_right(k, p).start()

        if k == min(1, far_size - 1):
            for p in range(2):
                at = pl.ds(p * half, half)
                copies["y", p].wait_recv()
                send(("yc", p), ox_ref.at[across, at], ox_ref.at[across, at], to_core)
        if k == max(far_size - 2, 0):
            copies["y0"].wait_recv()
            send("yx", block(across, n, 0), block(across, n, 0), to_x)
            send("yc0", block(across, n, 0), block(across, n, 0), to_core)
            copies["x1"].wait_recv()
            send("xy", block(s, beside, 1), block(s, beside, 1), to_y)
            send("xc1", block(s, beside, 1), block(s, beside, 1), to_core)
            copies["y1"].wait_recv()
            send("yc1", block(across, n, 1), block(across, n, 1), to_core)
            copies["x0"].wait_recv()
            send("xc0", block(s, beside, 0), block(s, beside, 0), to_core)
    copies["yx"].wait_recv()
    send("dc0", block(across, beside, 0), block(across, beside, 0), to_core)
    copies["xy"].wait_recv()
    send("dc1", block(across, beside, 1), block(across, beside, 1), to_core)
    for key in ("c0", "c1", "yc0", "yc1", "xc0", "xc1", "dc0", "dc1"):
        copies[key].wait_recv()
    for p in range(2):
        copies["c", p].wait_recv()
        copies["yc", p].wait_recv()
    for k in range(3):
        copies["i", k].wait_recv()
    for k in range(7):
        copies["e", k].wait_recv()
    for k in range(far_size):
        for p in range(4):

            @pl.when((f >= k) & (f < far_size - 1))
            def _():
                to_right(k, p).wait_send()

            @pl.when((f + k < far_size) & (f > 0))
            def _():
                to_left(k, p).wait_send()

            @pl.when(f >= k)
            def _():
                x_from_left(k, p).wait_recv()
                x_from_left(k, p).wait_send()

            if k > 0:

                @pl.when(f + k < far_size)
                def _():
                    x_from_right(k, p).wait_recv()
                    x_from_right(k, p).wait_send()

    for copy in copies.values():
        copy.wait_send()
    keep_x.wait()
    keep_i.wait()
    keep_d.wait()
    keep_e.wait()


def gather_heads(w, x, i, d, e, collective_id):
    far_size = lax.axis_size("far")
    _, rows, columns = w.shape
    tokens, width = x.shape
    sems = 33 + 16 * far_size
    full, all_x, all_i, all_d, mine_e = pl.pallas_call(
        functools.partial(gather_heads_kernel, far_size),
        out_shape=[
            jax.ShapeDtypeStruct((4, far_size, 2, rows, columns), w.dtype),
            jax.ShapeDtypeStruct((4, tokens, width), x.dtype),
            jax.ShapeDtypeStruct((4, *i.shape), i.dtype),
            jax.ShapeDtypeStruct((8, *d.shape), d.dtype),
            jax.ShapeDtypeStruct(e.shape, e.dtype),
        ],
        in_specs=[ANYWHERE] * 5,
        out_specs=[ANYWHERE] * 5,
        scratch_shapes=[
            pltpu.SemaphoreType.DMA((5,)),
            pltpu.SemaphoreType.DMA((sems,)),
            pltpu.SemaphoreType.DMA((sems,)),
        ],
        compiler_params=pltpu.CompilerParams(collective_id=collective_id, has_side_effects=True),
    )(w, x, i, d, e)
    all_x, all_d = all_x.reshape(-1, width), all_d.reshape(-1, d.shape[1])
    return full.reshape(-1, columns), all_x, all_i, all_d, mine_e


def tile_at(tile, rows):
    return pl.ds(pl.multiple_of(tile * rows, rows), rows)


def stacked(pair):
    half = pair.shape[1] // 2
    return jnp.concatenate([pair[:, :half], pair[:, half:]], 0)


def turned(value, cos, sin):
    half = value.shape[1] // 2
    first, second = value[:, :half], value[:, half:]
    return first * cos - second * sin, second * cos + first * sin


def visible_keys(tile, rows, keys, length):
    shape = (2 * rows, keys)
    row = lax.broadcasted_iota(jnp.int32, shape, 0)
    row = jnp.where(row >= rows, row - rows, row) + tile * rows
    column = lax.broadcasted_iota(jnp.int32, shape, 1)
    return (column <= row) & (column < length)


def attention_kernel(length_ref, x_ref, w_ref, turn_ref, q_ref, k_ref, v_ref, heads_ref, lse_ref, p_ref):
    rows = x_ref.shape[0] // 4
    size = k_ref.shape[1]
    low = jnp.bfloat16
    length = length_ref[0]

    def project(tile, carry):
        at = tile_at(tile, rows)
        merged = product(x_ref[at, :], w_ref[:, : 4 * size], 1, 0)
        cos, sin = turn_ref[at, : size // 2], turn_ref[at, size // 2 :]
        for ref, start, column, scale in (
            (q_ref, 0, 0, size**-0.5),
            (q_ref, size, size, size**-0.5),
            (k_ref, 2 * size, 0, 1.0),
        ):
            first, second = turned(merged[:, start : start + size], cos, sin)
            ref[at, column : column + size // 2] = (first * scale).astype(low)
            ref[at, column + size // 2 : column + size] = (second * scale).astype(low)
        v_ref[at, :] = merged[:, 3 * size :].astype(low)
        return carry

    lax.fori_loop(0, 4, project, 0)
    for tile in range(4):
        at = pl.ds(tile * rows, rows)
        keys = (tile + 1) * rows
        scores = product(stacked(q_ref[at, :]), k_ref[:keys, :], 1, 1)
        scores = jnp.where(visible_keys(tile, rows, keys, length), scores, MASKED_SCORE)
        peak = jnp.max(scores, 1, keepdims=True)
        expo = jnp.exp(scores - peak)
        total = jnp.sum(expo, 1, keepdims=True)
        result = product((expo * (1.0 / total)).astype(low), v_ref[:keys, :], 1, 0)
        live = lax.broadcasted_iota(jnp.int32, (rows, 1), 0) + tile * rows < length
        lse = peak + jnp.log(total)
        for head in range(2):
            mine = slice(head * rows, (head + 1) * rows)
            heads_ref[at, head * size : (head + 1) * size] = jnp.where(live, result[mine], 0.0).astype(low)
            lse_ref[at, head : head + 1] = lse[mine]

    def out(tile, carry):
        at = tile_at(tile, rows)
        p_ref[at, :] = product(heads_ref[at, :], w_ref[:, 4 * size :], 1, 1).astype(low)
        return carry

    lax.fori_loop(0, 4, out, 0)


def attention(length, x, w, turns):
    tokens, width = x.shape
    size = w.shape[1] // 6
    low = jnp.bfloat16
    shapes = [(tokens, 2 * size), (tokens, size), (tokens, size), (tokens, 2 * size)]
    return pl.pallas_call(
        attention_kernel,
        out_shape=[jax.ShapeDtypeStruct(shape, low) for shape in shapes]
        + [jax.ShapeDtypeStruct((tokens, 128), jnp.float32), jax.ShapeDtypeStruct((tokens, width), low)],
        in_specs=[pl.BlockSpec(memory_space=pltpu.SMEM)] + [IN_VMEM] * 3,
        out_specs=[IN_VMEM] * 6,
        compiler_params=pltpu.CompilerParams(vmem_limit_bytes=VMEM_LIMIT),
        cost_estimate=pl.CostEstimate(flops=10_000_000_000, bytes_accessed=20_000_000, transcendentals=0),
    )(length, x, w, turns)


def attention_back_kernel(
    length_ref,
    q_ref,
    k_ref,
    v_ref,
    heads_ref,
    lse_ref,
    turn_ref,
    g_ref,
    y_ref,
    w_ref,
    x_ref,
    terms_ref,
    dx_ref,
    sum_ref,
    weights,
    tokens,
    dheads,
    dfused,
    dk,
    dv,
    mine,
    far,
    hop_x,
    hop_y,
    last_x,
    last_y,
    far_d,
    last_d,
    out_grad,
    qkv_grad,
    out_there,
    qkv_there,
    local_sems,
    send_sems,
    recv_sems,
):
    s, n, core, across, beside = places()
    other = (core + 2) % 4
    to_core, to_y, to_x = {"seq": core}, {"seq": across}, {"near": beside}
    rows = g_ref.shape[0]
    half = rows // 2
    size = k_ref.shape[1]
    low = jnp.bfloat16
    length = length_ref[0]
    far_size = terms_ref.shape[0]

    def local(source, target, at):
        copy = pltpu.make_async_copy(source, target, local_sems.at[at])
        copy.start()
        return copy

    def part(ref, p):
        return ref.at[pl.ds(p * half, half)]

    def token_rows(seq, p):
        return tokens.at[pl.ds(seq * rows + p * half, half)]

    def block(seq, near):
        return y_ref.at[pl.ds((seq * 2 + near) * rows, rows)]

    meet(to_core, to_y, to_x)
    copies, send = sender(send_sems, recv_sems)
    keep = local(g_ref, tokens.at[pl.ds(s * rows, rows)], 0)
    for p in range(2):
        send(("gy", p), part(g_ref, p), token_rows(s, p), to_y)
    for p in range(2):
        send(("gc", p), part(g_ref, p), token_rows(s, p), to_core)
    given = [block(other, beside), block(other, n), block(core, beside), block(core, n)]
    kept = [block(across, beside), block(across, n), block(s, beside), block(s, n)]
    loads = []
    for k in range(4):
        send(k, given[k], far.at[k], to_core)
        loads.append(local(kept[k], mine.at[k], 1 + k))
    load_w = local(w_ref, weights, 5)
    for k in range(3):
        loads[k].wait()
        copies[k].wait_recv()
        add_rows(mine.at[k], mine.at[k], far.at[k])
        if k == 0:
            send("hx", part(mine.at[0], 0), hop_x, to_x)
    send("x0", part(mine.at[2], 0), part(last_x, 0), to_x)
    for p in range(2):
        copies["gy", p].wait_recv()
        send(("gyc", p), token_rows(across, p), token_rows(across, p), to_core)
    send("hy", part(mine.at[0], 1), hop_y, to_y)
    send("y1", part(mine.at[1], 1), part(last_y, 1), to_y)
    loads[3].wait()
    copies[3].wait_recv()
    add_rows(sum_ref, mine.at[3], far.at[3])
    keep.wait()
    load_w.wait()
    for p in range(2):
        copies["gc", p].wait_recv()
        copies["gyc", p].wait_recv()

    def dheads_of(tile, carry):
        at = tile_at(tile, rows)
        live = lax.broadcasted_iota(jnp.int32, (rows, 1), 0) + tile * rows < length
        value = product(tokens[at, :], weights[:, 4 * size :], 1, 0)
        dheads[at, :] = jnp.where(live, value, 0.0).astype(low)
        return carry

    def by_rows(value):
        return value.astype(low).reshape(far_size, 2, -1, value.shape[1])

    width = tokens.shape[1]
    quarter = width // 4
    for q in range(4):
        out_grad[q] = by_rows(product(tokens[:, q * quarter : (q + 1) * quarter], heads_ref[...], 0, 0))
    send("out", out_grad.at[:, :, beside], out_there, to_x)
    lax.fori_loop(0, 4, dheads_of, 0)
    for copy in ("gyc", "gy", "gc"):
        for p in range(2):
            copies[copy, p].wait_send()
    load_x = local(x_ref, tokens, 0)
    copies["hx"].wait_recv()
    add_rows(part(mine.at[1], 0), part(mine.at[1], 0), hop_x)
    send("y0", part(mine.at[1], 0), part(last_y, 0), to_y)
    copies["hy"].wait_recv()
    add_rows(part(mine.at[2], 1), part(mine.at[2], 1), hop_y)
    send("x1", part(mine.at[2], 1), part(last_x, 1), to_x)

    dk[...] = jnp.zeros_like(dk)
    dv[...] = jnp.zeros_like(dv)
    for tile in range(4):
        at = pl.ds(tile * rows, rows)
        keys = (tile + 1) * rows
        query = stacked(q_ref[at, :])
        dhead = stacked(dheads[at, :])
        scores = product(query, k_ref[:keys, :], 1, 1)
        lse = jnp.concatenate([lse_ref[at, 0:1], lse_ref[at, 1:2]], 0)
        probs = jnp.where(visible_keys(tile, rows, keys, length), jnp.exp(scores - lse), 0.0)
        dprobs = product(dhead, v_ref[:keys, :], 1, 1)
        inner = jnp.sum(probs * dprobs, 1, keepdims=True)
        dscores = (probs * (dprobs - inner)).astype(low)
        dv[:keys, :] += product(probs.astype(low), dhead, 0, 0)
        dk[:keys, :] += product(dscores, query, 0, 0)
        dquery = product(dscores, k_ref[:keys, :], 1, 0) * size**-0.5
        cos, sin = turn_ref[at, : size // 2], turn_ref[at, size // 2 :]
        for head in range(2):
            rounded = dquery[head * rows : (head + 1) * rows].astype(low).astype(jnp.float32)
            first, second = turned(rounded, cos, -sin)
            dfused[at, head * size : head * size + size // 2] = first.astype(low)
            dfused[at, head * size + size // 2 : (head + 1) * size] = second.astype(low)
    first, second = turned(
        dk[...].astype(low).astype(jnp.float32), turn_ref[:, : size // 2], -turn_ref[:, size // 2 :]
    )
    dfused[:, 2 * size : 2 * size + size // 2] = first.astype(low)
    dfused[:, 2 * size + size // 2 : 3 * size] = second.astype(low)
    dfused[:, 3 * size :] = dv[...].astype(low)

    load_x.wait()
    for q in range(4):
        qkv_grad[q] = by_rows(product(tokens[:, q * quarter : (q + 1) * quarter], dfused[...], 0, 0))
        send(("qkv", q), qkv_grad.at[q, :, beside], qkv_there.at[q], to_x)

    for p, first, second in ((1, "y1", "x1"), (0, "x0", "y0")):
        copies[first].wait_recv()
        copies[second].wait_recv()
        add_rows(part(sum_ref, p), part(sum_ref, p), part(last_x, p), part(last_y, p))
    for key in ("hx", "hy", "y0", "y1", "x0", "x1"):
        copies[key].wait_send()

    def dx_of(k, tile):
        mine[k] = product(dfused[tile_at(tile, rows), :], weights[:, : 4 * size], 1, 1).astype(low)

    dx_of(0, other)
    send("d0", mine.at[0], far_d.at[0], to_core)
    dx_of(1, core)
    send("d1", mine.at[1], far_d.at[1], to_core)
    dx_of(2, across)
    copies["d0"].wait_recv()
    for p in range(2):
        add_rows(part(mine.at[2], p), part(mine.at[2], p), part(far_d.at[0], p))
        send(("dy", p), part(mine.at[2], p), part(last_d, p), to_y)
    dx_of(3, s)
    copies["d1"].wait_recv()
    add_rows(dx_ref, mine.at[3], far_d.at[1])
    outs = []
    copies["out"].wait_recv()
    for q in range(4):
        for f in range(far_size):
            out_there[q, f] = (
                out_there[q, f].astype(jnp.float32) + out_grad[q, f, n].astype(jnp.float32)
            ).astype(low)
    for p in range(2):
        copies["dy", p].wait_recv()
        add_rows(part(dx_ref, p), part(dx_ref, p), part(last_d, p))
    for q in range(4):
        copies["qkv", q].wait_recv()
        for f in range(far_size):
            qkv_there[q, f] = (
                qkv_there[q, f].astype(jnp.float32) + qkv_grad[q, f, n].astype(jnp.float32)
            ).astype(low)
        outs.append(local(out_there.at[q], terms_ref.at[:, q, :, 4 * size :], q))
        outs.append(local(qkv_there.at[q], terms_ref.at[:, q, :, : 4 * size], 4 + q))
    for copy in outs:
        copy.wait()
    waited = {"hx", "hy", "y0", "y1", "x0", "x1"}
    for key, copy in copies.items():
        if key not in waited and not (isinstance(key, tuple) and key[0] in ("gyc", "gy", "gc")):
            copy.wait_send()


def attention_back(length, saved, turns, g, y, w, x, collective_id):
    q, k, v, heads, lse = saved
    tokens, width = x.shape
    size = k.shape[1]
    rows = tokens // 4
    far_size = lax.axis_size("far")
    weight_rows = width // (8 * far_size)
    low = jnp.bfloat16
    block = pltpu.VMEM((rows, width), low)
    half_block = pltpu.VMEM((rows // 2, width), low)
    return pl.pallas_call(
        attention_back_kernel,
        out_shape=[
            jax.ShapeDtypeStruct((far_size, 4, weight_rows, 6 * size), low),
            jax.ShapeDtypeStruct((rows, width), jnp.float32),
            jax.ShapeDtypeStruct((rows, width), jnp.float32),
        ],
        in_specs=[pl.BlockSpec(memory_space=pltpu.SMEM)] + [IN_VMEM] * 6 + [ANYWHERE] * 4,
        out_specs=[ANYWHERE, IN_VMEM, IN_VMEM],
        scratch_shapes=[
            pltpu.VMEM(w.shape, low),
            pltpu.VMEM((tokens, width), low),
            pltpu.VMEM((tokens, 2 * size), low),
            pltpu.VMEM((tokens, 4 * size), low),
            pltpu.VMEM((tokens, size), jnp.float32),
            pltpu.VMEM((tokens, size), jnp.float32),
            pltpu.VMEM((4, rows, width), low),
            pltpu.VMEM((4, rows, width), low),
            half_block,
            half_block,
            block,
            block,
            pltpu.VMEM((2, rows, width), low),
            block,
            pltpu.VMEM((4, far_size, 2, weight_rows, 2 * size), low),
            pltpu.VMEM((4, far_size, 2, weight_rows, 4 * size), low),
            pltpu.VMEM((4, far_size, weight_rows, 2 * size), low),
            pltpu.VMEM((4, far_size, weight_rows, 4 * size), low),
            pltpu.SemaphoreType.DMA((8,)),
            pltpu.SemaphoreType.DMA((25,)),
            pltpu.SemaphoreType.DMA((25,)),
        ],
        compiler_params=pltpu.CompilerParams(
            collective_id=collective_id, has_side_effects=True, vmem_limit_bytes=VMEM_LIMIT
        ),
        cost_estimate=pl.CostEstimate(flops=20_000_000_000, bytes_accessed=40_000_000, transcendentals=0),
    )(length, q, k, v, heads, lse, turns, g, y, w, x)


def hidden_units(x, d, w, part):
    low = jnp.bfloat16
    gate = product(x, w[:, :part], 1, 0)
    upper = product(x, w[:, part : 2 * part], 1, 0)
    dact = product(d, w[:, 2 * part :], 1, 0)
    sig = 1.0 / (1.0 + jnp.exp(-gate))
    silu = gate * sig
    act = (silu * upper).astype(low)
    dgate = (dact * upper * (sig + silu * (1.0 - sig))).astype(low)
    dupper = (dact * silu).astype(low)
    return act, dgate, dupper


def load_weights(w_ref, weights, sems):
    loads = [
        pltpu.make_async_copy(w_ref.at[f], weights.at[:, f], sems.at[f]) for f in range(w_ref.shape[0])
    ]
    for load in loads:
        load.start()
    return loads


def feed_first_kernel(
    x_ref,
    d_ref,
    w_ref,
    all_ref,
    act_ref,
    dgu_ref,
    y_ref,
    dx_ref,
    weights,
    tokens,
    there,
    acts,
    dgus,
    ys,
    dxs,
    local_sems,
    d_sems,
    out_sems,
    send_sems,
    recv_sems,
):
    s, n, core, across, beside = places()
    other = (core + 2) % 4
    rows = x_ref.shape[0]
    half = rows // 2
    to_core, to_y, to_x = {"seq": core}, {"seq": across}, {"near": beside}
    part = weights.shape[3] // 3
    width = x_ref.shape[1]
    low = jnp.bfloat16

    def block(seq, near, p):
        return tokens.at[seq * 2 + near, pl.ds(p * half, half)]

    def own(p):
        return x_ref.at[pl.ds(p * half, half)]

    order = [
        s * 2 + n,
        core * 2 + n,
        across * 2 + n,
        other * 2 + n,
        s * 2 + beside,
        core * 2 + beside,
        across * 2 + beside,
        other * 2 + beside,
    ]

    def tile_of(step):
        tile = order[0]
        for k in range(1, 8):
            tile = jnp.where(step == k, order[k], tile)
        return tile

    def d_load(step):
        slot = step % 2
        at = tile_at(tile_of(step), rows)
        return pltpu.make_async_copy(d_ref.at[at], there.at[slot], d_sems.at[slot])

    def stores(step):
        slot = step % 2
        tile = tile_of(step)
        at = tile_at(tile, rows)
        pairs = (
            (tokens.at[tile], all_ref),
            (acts.at[slot], act_ref),
            (dgus.at[slot], dgu_ref),
            (ys.at[slot], y_ref),
            (dxs.at[slot], dx_ref),
        )
        return [
            pltpu.make_async_copy(source, target.at[at], out_sems.at[slot, k])
            for k, (source, target) in enumerate(pairs)
        ]

    def piece(seq, near, p, device):
        return block(seq, near, p), block(seq, near, p), device

    plan = {
        "y0": (own(0), block(s, n, 0), to_y),
        "x1": (own(1), block(s, n, 1), to_x),
        "y1": (own(1), block(s, n, 1), to_y),
        "x0": (own(0), block(s, n, 0), to_x),
        "c0": (own(0), block(s, n, 0), to_core),
        "c1": (own(1), block(s, n, 1), to_core),
        "yx": piece(across, n, 0, to_x),
        "yc0": piece(across, n, 0, to_core),
        "xy": piece(s, beside, 1, to_y),
        "xc1": piece(s, beside, 1, to_core),
        "yc1": piece(across, n, 1, to_core),
        "xc0": piece(s, beside, 0, to_core),
        "dc0": piece(across, beside, 0, to_core),
        "dc1": piece(across, beside, 1, to_core),
    }
    places_of = {key: at for at, key in enumerate(plan)}

    def copy_of(key):
        source, target, device = plan[key]
        at = places_of[key]
        return pltpu.make_async_remote_copy(
            src_ref=source,
            dst_ref=target,
            send_sem=send_sems.at[at],
            recv_sem=recv_sems.at[at],
            device_id=device,
            device_id_type=MESH_IDS,
        )

    def send(*keys):
        for key in keys:
            copy_of(key).start()

    def arrive(*keys):
        for key in keys:
            copy_of(key).wait_recv()

    meet(to_core, to_y, to_x)
    keep = pltpu.make_async_copy(x_ref, tokens.at[s * 2 + n], local_sems.at[0])
    keep.start()
    send("y0", "x1", "y1", "x0", "c0", "c1")
    loads = load_weights(w_ref, weights, local_sems.at[pl.ds(1, w_ref.shape[0])])
    d_load(0).start()
    keep.wait()
    for load in loads:
        load.wait()

    def before(step):
        if step == 1:
            arrive("c0", "c1")
        elif step == 2:
            arrive("y0")
            send("yx", "yc0")
            arrive("x1")
            send("xy", "xc1")
            arrive("y1")
            send("yc1")
            arrive("x0")
            send("xc0")
        elif step == 3:
            arrive("yc0", "yc1")
        elif step == 5:
            arrive("xc0", "xc1")
        elif step == 6:
            arrive("yx")
            send("dc0")
            arrive("xy")
            send("dc1")
        elif step == 7:
            arrive("dc0", "dc1")

    def step_of(step, carry):
        for k in (1, 2, 3, 5, 6, 7):

            @pl.when(step == k)
            def _():
                before(k)

        slot = step % 2

        @pl.when(step < 7)
        def _():
            d_load(step + 1).start()

        @pl.when(step >= 2)
        def _():
            for store in stores(step - 2):
                store.wait()

        d_load(step).wait()
        w = weights[...].reshape(width, 3 * part)
        act, dgate, dupper = hidden_units(tokens[tile_of(step)], there[slot], w, part)
        acts[slot] = act
        dgus[slot, :, :part] = dgate
        dgus[slot, :, part:] = dupper
        ys[slot] = product(act, w[:, 2 * part :], 1, 1).astype(low)
        dxs[slot] = product(dgus[slot], w[:, : 2 * part], 1, 1).astype(low)
        for store in stores(step):
            store.start()
        return carry

    lax.fori_loop(0, 8, step_of, 0)
    for step in (6, 7):
        for store in stores(step):
            store.wait()
    for key in plan:
        copy_of(key).wait_send()


def feed_first(x, d, w, collective_id):
    rows, width = x.shape
    part = w.shape[3] // 3
    tokens = 8 * rows
    low = jnp.bfloat16
    far, _, weight_rows, columns = w.shape
    sizes = (width, part, 2 * part, width, width)
    return pl.pallas_call(
        feed_first_kernel,
        out_shape=[jax.ShapeDtypeStruct((tokens, size), low) for size in sizes],
        in_specs=[ANYWHERE] * 3,
        out_specs=[ANYWHERE] * 5,
        scratch_shapes=[
            pltpu.VMEM((4, far, weight_rows, columns), low),
            pltpu.VMEM((8, rows, width), low),
            pltpu.VMEM((2, rows, width), low),
            pltpu.VMEM((2, rows, part), low),
            pltpu.VMEM((2, rows, 2 * part), low),
            pltpu.VMEM((2, rows, width), low),
            pltpu.VMEM((2, rows, width), low),
            pltpu.SemaphoreType.DMA((1 + far,)),
            pltpu.SemaphoreType.DMA((2,)),
            pltpu.SemaphoreType.DMA((2, 5)),
            pltpu.SemaphoreType.DMA((14,)),
            pltpu.SemaphoreType.DMA((14,)),
        ],
        compiler_params=pltpu.CompilerParams(
            collective_id=collective_id, has_side_effects=True, vmem_limit_bytes=VMEM_LIMIT
        ),
        cost_estimate=pl.CostEstimate(
            flops=12 * tokens * width * part, bytes_accessed=60_000_000, transcendentals=0
        ),
    )(x, d, w)


def feed_second_kernel(x_ref, d_ref, y0_ref, dx0_ref, w_ref, act_ref, dgu_ref, y_ref, dx_ref, weights, sems):
    part = weights.shape[3] // 3
    width = x_ref.shape[1]
    low = jnp.bfloat16

    @pl.when(pl.program_id(0) == 0)
    def _():
        for load in load_weights(w_ref, weights, sems):
            load.wait()

    w = weights[...].reshape(width, 3 * part)
    act, dgate, dupper = hidden_units(x_ref[...], d_ref[...], w, part)
    act_ref[...] = act
    dgu_ref[:, :part] = dgate
    dgu_ref[:, part:] = dupper
    y = product(act, w[:, 2 * part :], 1, 1) + y0_ref[...].astype(jnp.float32)
    y_ref[...] = y.astype(low)
    dx = product(dgu_ref[...], w[:, : 2 * part], 1, 1) + dx0_ref[...].astype(jnp.float32)
    dx_ref[...] = dx.astype(low)


def feed_second(x, d, y, dx, w, tile=512):
    tokens, width = x.shape
    part = w.shape[3] // 3
    low = jnp.bfloat16
    far, _, weight_rows, columns = w.shape

    def tokens_of(columns):
        return pl.BlockSpec((tile, columns), lambda t: (t, 0))

    sizes = (part, 2 * part, width, width)
    return pl.pallas_call(
        feed_second_kernel,
        grid=(tokens // tile,),
        out_shape=[jax.ShapeDtypeStruct((tokens, size), low) for size in sizes],
        in_specs=[tokens_of(width)] * 4 + [ANYWHERE],
        out_specs=[tokens_of(size) for size in sizes],
        scratch_shapes=[pltpu.VMEM((4, far, weight_rows, columns), low), pltpu.SemaphoreType.DMA((far,))],
        compiler_params=pltpu.CompilerParams(vmem_limit_bytes=VMEM_LIMIT),
        cost_estimate=pl.CostEstimate(
            flops=12 * tokens * width * part, bytes_accessed=60_000_000, transcendentals=0
        ),
    )(x, d, y, dx, w)


def feed_grads_kernel(x_ref, d_ref, dgu_ref, act_ref, o_ref):
    split = dgu_ref.shape[1]
    far, _, rows, columns = o_ref.shape
    gateup = product(x_ref[...], dgu_ref[...], 0, 0).astype(o_ref.dtype)
    o_ref[:, 0, :, :split] = gateup.reshape(far, rows, split)
    down = product(d_ref[...], act_ref[...], 0, 0).astype(o_ref.dtype)
    o_ref[:, 0, :, split:] = down.reshape(far, rows, columns - split)


def feed_grads(x, d, dgu, act, far):
    tokens, width = x.shape
    columns = dgu.shape[1] + act.shape[1]
    rows = width // (4 * far)
    some = pl.BlockSpec((tokens, width // 4), lambda t: (0, t))

    def whole(array):
        return pl.BlockSpec(array.shape, lambda t: (0, 0), pipeline_mode=pl.Buffered(1))

    return pl.pallas_call(
        feed_grads_kernel,
        grid=(4,),
        out_shape=jax.ShapeDtypeStruct((far, 4, rows, columns), x.dtype),
        in_specs=[some, some, whole(dgu), whole(act)],
        out_specs=pl.BlockSpec((far, 1, rows, columns), lambda t: (0, t, 0, 0)),
        compiler_params=pltpu.CompilerParams(vmem_limit_bytes=VMEM_LIMIT),
        cost_estimate=pl.CostEstimate(
            flops=2 * tokens * width * columns, bytes_accessed=40_000_000, transcendentals=0
        ),
    )(x, d, dgu, act)


def feed_back_kernel(
    hidden_ref,
    cotangent_ref,
    dgu_ref,
    act_ref,
    x_ref,
    d_ref,
    p_ref,
    terms_ref,
    dhidden_ref,
    low_ref,
    mine,
    far,
    hop_x,
    hop_y,
    last_x,
    last_y,
    xs,
    ds,
    outs,
    local_sems,
    x_sems,
    out_sems,
    send_sems,
    recv_sems,
):
    s, n, core, across, beside = places()
    other = (core + 2) % 4
    to_core, to_y, to_x = {"seq": core}, {"seq": across}, {"near": beside}
    rows, width = hidden_ref.shape
    half = rows // 2
    quarter = width // 4
    split = dgu_ref.shape[1]
    far_size, _, weight_rows, columns = terms_ref.shape

    def block(seq, near):
        return p_ref.at[pl.ds((seq * 2 + near) * rows, rows)]

    def part(ref, p):
        return ref.at[pl.ds(p * half, half)]

    def columns_in(q):
        slot = q % 2
        at = pl.ds(q * quarter, quarter)
        return (
            pltpu.make_async_copy(x_ref.at[:, at], xs.at[slot], x_sems.at[slot, 0]),
            pltpu.make_async_copy(d_ref.at[:, at], ds.at[slot], x_sems.at[slot, 1]),
        )

    def terms_out(q):
        return pltpu.make_async_copy(outs.at[q % 2], terms_ref.at[:, q], out_sems.at[q % 2])

    meet(to_core, to_y, to_x)
    copies, send = sender(send_sems, recv_sems)
    given = [block(other, beside), block(other, n), block(core, beside), block(core, n)]
    kept = [block(across, beside), block(across, n), block(s, beside), block(s, n)]
    loads = []
    for k in range(4):
        send(k, given[k], far.at[k], to_core)
        loads.append(pltpu.make_async_copy(kept[k], mine.at[k], local_sems.at[k]))
        loads[k].start()
    for q in range(2):
        for copy in columns_in(q):
            copy.start()

    def grads(q):
        slot = q % 2
        for copy in columns_in(q):
            copy.wait()
        if q >= 2:
            terms_out(q - 2).wait()
        gateup = product(xs[slot], dgu_ref[...], 0, 0).astype(jnp.bfloat16)
        outs[slot, :, :, :split] = gateup.reshape(far_size, weight_rows, split)
        down = product(ds[slot], act_ref[...], 0, 0).astype(jnp.bfloat16)
        outs[slot, :, :, split:] = down.reshape(far_size, weight_rows, columns - split)
        terms_out(q).start()
        if q < 2:
            for copy in columns_in(q + 2):
                copy.start()

    for k in range(3):
        loads[k].wait()
        copies[k].wait_recv()
        add_rows(mine.at[k], mine.at[k], far.at[k])
        if k == 0:
            send("hx", part(mine.at[0], 0), hop_x, to_x)
            send("hy", part(mine.at[0], 1), hop_y, to_y)
        elif k == 1:
            send("y1", part(mine.at[1], 1), part(last_y, 1), to_y)
        else:
            send("x0", part(mine.at[2], 0), part(last_x, 0), to_x)
    grads(0)
    grads(1)
    copies["hx"].wait_recv()
    add_rows(part(mine.at[1], 0), part(mine.at[1], 0), hop_x)
    send("y0", part(mine.at[1], 0), part(last_y, 0), to_y)
    copies["hy"].wait_recv()
    add_rows(part(mine.at[2], 1), part(mine.at[2], 1), hop_y)
    send("x1", part(mine.at[2], 1), part(last_x, 1), to_x)
    loads[3].wait()
    copies[3].wait_recv()
    add_rows(dhidden_ref, mine.at[3], far.at[3])
    grads(2)
    grads(3)
    for key in ("y1", "x0", "y0", "x1"):
        copies[key].wait_recv()
    step = 16

    def backward(i, carry):
        at = pl.ds(pl.multiple_of(i * step, step), step)
        dx = dhidden_ref[at, :] + last_x[at, :].astype(jnp.float32) + last_y[at, :].astype(jnp.float32)
        unit, scale = rms_normalize(hidden_ref[at, :])
        dhidden = cotangent_ref[at, :] + norm_backward(dx, unit, scale)
        dhidden_ref[at, :] = dhidden
        low_ref[at, :] = dhidden.astype(low_ref.dtype)
        return carry

    lax.fori_loop(0, rows // step, backward, 0)
    for q in (2, 3):
        terms_out(q).wait()
    for copy in copies.values():
        copy.wait_send()


def feed_back(hidden, cotangent, dgu, act, x, d, p, far, collective_id):
    rows, width = hidden.shape
    tokens, columns = x.shape[0], dgu.shape[1] + act.shape[1]
    weight_rows = width // (4 * far)
    low = jnp.bfloat16
    block = pltpu.VMEM((rows, width), low)
    half_block = pltpu.VMEM((rows // 2, width), low)
    return pl.pallas_call(
        feed_back_kernel,
        out_shape=[
            jax.ShapeDtypeStruct((far, 4, weight_rows, columns), low),
            jax.ShapeDtypeStruct((rows, width), jnp.float32),
            jax.ShapeDtypeStruct((rows, width), low),
        ],
        in_specs=[IN_VMEM] * 4 + [ANYWHERE] * 3,
        out_specs=[ANYWHERE, IN_VMEM, IN_VMEM],
        scratch_shapes=[
            pltpu.VMEM((4, rows, width), low),
            pltpu.VMEM((4, rows, width), low),
            half_block,
            half_block,
            block,
            block,
            pltpu.VMEM((2, tokens, width // 4), low),
            pltpu.VMEM((2, tokens, width // 4), low),
            pltpu.VMEM((2, far, weight_rows, columns), low),
            pltpu.SemaphoreType.DMA((4,)),
            pltpu.SemaphoreType.DMA((2, 2)),
            pltpu.SemaphoreType.DMA((2,)),
            pltpu.SemaphoreType.DMA((10,)),
            pltpu.SemaphoreType.DMA((10,)),
        ],
        compiler_params=pltpu.CompilerParams(
            collective_id=collective_id, has_side_effects=True, vmem_limit_bytes=VMEM_LIMIT
        ),
        cost_estimate=pl.CostEstimate(
            flops=2 * tokens * width * columns, bytes_accessed=60_000_000, transcendentals=0
        ),
    )(hidden, cotangent, dgu, act, x, d, p)


def rotary_tables(positions, width):
    half = width // 2
    freqs = jnp.exp(-(jnp.arange(half, dtype=jnp.float32) * 2.0 / width) * math.log(ROPE_BASE))
    angles = positions.astype(jnp.float32)[:, None] * freqs
    return jnp.concatenate([jnp.cos(angles), jnp.sin(angles)], -1)


def rms_normalize(value_rows):
    inverse_scale = lax.rsqrt(jnp.mean(value_rows * value_rows, -1, keepdims=True) + NORM_EPSILON)
    return (value_rows * inverse_scale, inverse_scale)


def norm_backward(unit_gradient, unit_input, inverse_scale):
    return inverse_scale * (
        unit_gradient - unit_input * jnp.mean(unit_gradient * unit_input, -1, keepdims=True)
    )


def adam_step(weight, grad, first, second, rate, decay):
    first_new = BETA_ONE * first + (1.0 - BETA_ONE) * grad
    second_new = BETA_TWO * second + (1.0 - BETA_TWO) * grad * grad
    corr_one = 1.0 - BETA_ONE**STEP
    corr_two = 1.0 - BETA_TWO**STEP
    update = (first_new * (1.0 / corr_one)) / (jnp.sqrt(second_new * (1.0 / corr_two)) + ADAM_EPSILON)
    return (weight - rate * (update + decay * weight), first_new, second_new)


def feed_pieces(part):
    gateup, down = [], []
    for half in range(2):
        for device in range(8):
            start = (half * 8 + device) * part
            gateup.append((half, device, 0, start))
            gateup.append((half, device, part, FEED_UNITS + start))
            down.append((half, device, 2 * part, start))
    return gateup, down


def head_pieces_of(columns):
    key = columns // 6
    query = 2 * key
    qkv, out = [], []
    for device in range(4):
        qkv.append((device, 0, device * query, query))
        qkv.append((device, query, 4 * query + device * key, key))
        qkv.append((device, query + key, 4 * (query + key) + device * key, key))
        out.append((device, query + 2 * key, device * query, query))
    return qkv, out


def norm_kernel(zero_ref, one_ref, gateup_ref, gains_ref, square_ref, terms_ref):
    halves = (zero_ref, one_ref)
    part = zero_ref.shape[2] // 3
    gateup, down = feed_pieces(part)
    two = gains_ref[...].astype(jnp.bfloat16).astype(jnp.float32)[:, 1:2]

    def over(x):
        return jnp.sum(x, 1, keepdims=True)

    two_squares = two_terms = down_squares = 0.0
    for half, device, at, column in gateup:
        grad = halves[half][device, :, at : at + part].astype(jnp.float32)
        weight = gateup_ref[:, column : column + part].astype(jnp.bfloat16).astype(jnp.float32)
        two_squares = two_squares + grad * grad
        two_terms = two_terms + grad * weight
    for half, device, at, column in down:
        grad = halves[half][device, :, at : at + part].astype(jnp.float32)
        down_squares = down_squares + grad * grad
    two_terms = over(two_terms)
    terms_ref[...] = two_terms
    total = jnp.sum(two * two * over(two_squares) + over(down_squares) + two_terms * two_terms)

    @pl.when(pl.program_id(0) == 0)
    def _():
        square_ref[0, 0] = total

    @pl.when(pl.program_id(0) > 0)
    def _():
        square_ref[0, 0] = square_ref[0, 0] + total


ROWS = 16


def rows_of(array):
    if array.ndim == 3:
        return pl.BlockSpec((array.shape[0], ROWS, array.shape[2]), lambda r: (0, r, 0))
    return pl.BlockSpec((ROWS, array.shape[1]), lambda r: (r, 0))


def feed_norm(zero, one, gateup, gains):
    arrays = (zero, one, gateup, gains)
    rows = gains.shape[0]
    terms = jax.ShapeDtypeStruct((rows, 1), jnp.float32)
    return pl.pallas_call(
        norm_kernel,
        grid=(rows // ROWS,),
        out_shape=[jax.ShapeDtypeStruct((1, 1), jnp.float32), terms],
        in_specs=[rows_of(x) for x in arrays],
        out_specs=[pl.BlockSpec(memory_space=pltpu.SMEM), rows_of(terms)],
        compiler_params=pltpu.CompilerParams(vmem_limit_bytes=VMEM_LIMIT),
        cost_estimate=pl.CostEstimate(flops=0, bytes_accessed=10_000_000, transcendentals=0),
    )(*arrays)


def settle_kernel(
    square_ref,
    terms_ref,
    qkv_ref,
    gains_ref,
    p_ref,
    head_ref,
    norm_ref,
    gain_grads_ref,
    mine,
    seq_parts,
    near_parts,
    far_parts,
    local_sem,
    send_sems,
    recv_sems,
    far_send_sems,
    far_recv_sems,
):
    s, n, core, across, beside = places()
    diagonal = (core + 2) % 4
    f = lax.axis_index("far")
    far_size = far_parts.shape[0]
    seqs = ({"seq": diagonal}, {"seq": across}, {"seq": core})
    fars = [{"far": (f + k) % far_size} for k in range(1, far_size)]
    meet(*seqs, {"near": beside}, *fars)
    copies, send = sender(send_sems, recv_sems)
    for k, seq in enumerate((diagonal, across, core)):
        send(("w", k), p_ref.at[seq], mine.at[s], seqs[k])
    keep = pltpu.make_async_copy(p_ref.at[s], mine.at[s], local_sem)
    keep.start()
    gains = gains_ref[...].astype(jnp.bfloat16).astype(jnp.float32)
    qkv, out = head_pieces_of(head_ref.shape[2])
    keep.wait()
    for k in range(3):
        copies["w", k].wait_recv()

    def over(x):
        return jnp.sum(x, 1, keepdims=True)

    one_squares = one_terms = out_squares = 0.0
    for device, at, column, size in qkv:
        grad = mine[device, :, at : at + size].astype(jnp.float32)
        weight = qkv_ref[:, column : column + size].astype(jnp.bfloat16).astype(jnp.float32)
        one_squares = one_squares + over(grad * grad)
        one_terms = one_terms + over(grad * weight)
    for device, at, column, size in out:
        grad = mine[device, :, at : at + size].astype(jnp.float32)
        out_squares = out_squares + over(grad * grad)
    one = gains[:, 0:1]
    rows = one * one * one_squares + out_squares + one_terms * one_terms
    gain_grads_ref[:, 0:1] = one_terms
    gain_grads_ref[:, 1:2] = terms_ref[...]
    total = jnp.sum(rows) + square_ref[0, 0]

    seq_parts[s] = jnp.full(seq_parts.shape[1:], total, jnp.float32)
    for k in range(3):
        send(("s", k), seq_parts.at[s], seq_parts.at[s], seqs[k])
    head_ref[...] = mine[...]
    for k in range(3):
        copies["s", k].wait_recv()
    near_parts[n] = (seq_parts[0] + seq_parts[1]) + (seq_parts[2] + seq_parts[3])
    send("n", near_parts.at[n], near_parts.at[n], {"near": beside})
    copies["n"].wait_recv()
    far_parts[f] = near_parts[0] + near_parts[1]
    far_copies = [
        pltpu.make_async_remote_copy(
            src_ref=far_parts.at[f],
            dst_ref=far_parts.at[f],
            send_sem=far_send_sems.at[k],
            recv_sem=far_recv_sems.at[k],
            device_id=far,
            device_id_type=MESH_IDS,
        )
        for k, far in enumerate(fars)
    ]
    for copy in far_copies:
        copy.start()
    for copy in far_copies:
        copy.wait_recv()
    everywhere = far_parts[0]
    for k in range(1, far_size):
        everywhere = everywhere + far_parts[k]
    norm_ref[...] = jnp.sqrt(everywhere)
    for copy in (*copies.values(), *far_copies):
        copy.wait_send()


def settle(square, terms, qkv, gains, p, collective_id):
    far = lax.axis_size("far")
    tile = (8, 128)
    return pl.pallas_call(
        settle_kernel,
        out_shape=[
            jax.ShapeDtypeStruct(p.shape, p.dtype),
            jax.ShapeDtypeStruct(tile, jnp.float32),
            jax.ShapeDtypeStruct(gains.shape, jnp.float32),
        ],
        in_specs=[pl.BlockSpec(memory_space=pltpu.SMEM)] + [IN_VMEM] * 3 + [ANYWHERE],
        out_specs=[IN_VMEM] * 3,
        scratch_shapes=[
            pltpu.VMEM(p.shape, p.dtype),
            pltpu.VMEM((4, *tile), jnp.float32),
            pltpu.VMEM((2, *tile), jnp.float32),
            pltpu.VMEM((far, *tile), jnp.float32),
            pltpu.SemaphoreType.DMA,
            pltpu.SemaphoreType.DMA((7,)),
            pltpu.SemaphoreType.DMA((7,)),
            pltpu.SemaphoreType.DMA((far - 1,)),
            pltpu.SemaphoreType.DMA((far - 1,)),
        ],
        compiler_params=pltpu.CompilerParams(
            collective_id=collective_id, has_side_effects=True, vmem_limit_bytes=VMEM_LIMIT
        ),
    )(square, terms, qkv, gains, p)


def adam_kernel(norm_ref, zero_ref, one_ref, head_ref, gain_grads_ref, *refs):
    weights, firsts, seconds = refs[0:5], refs[5:10], refs[10:15]
    weights_out, firsts_out, seconds_out = refs[15:20], refs[20:25], refs[25:30]
    halves = (zero_ref, one_ref)
    part = zero_ref.shape[2] // 3
    gateup, down = feed_pieces(part)
    qkv, out = head_pieces_of(head_ref.shape[2])
    clip = CLIP_NORM / jnp.maximum(norm_ref[0:1, 0:1], CLIP_NORM)
    gains = weights[4][...].astype(jnp.bfloat16).astype(jnp.float32) * clip
    one, two = gains[:, 0:1], gains[:, 1:2]

    def step(which, columns, grad, rate, decay):
        new = adam_step(
            weights[which][:, columns], grad, firsts[which][:, columns], seconds[which][:, columns], rate, decay
        )
        weights_out[which][:, columns] = new[0]
        firsts_out[which][:, columns] = new[1]
        seconds_out[which][:, columns] = new[2]

    for pieces, which, scale, rate in ((qkv, 0, one, RATE_MATRIX), (out, 1, clip, RATE_OUTPUT)):
        for device, at, column, size in pieces:
            grad = head_ref[device, :, at : at + size].astype(jnp.float32) * scale
            step(which, slice(column, column + size), grad, rate, DECAY_MATRIX)
    for pieces, which, scale in ((gateup, 2, two), (down, 3, clip)):
        for half, device, at, column in pieces:
            grad = halves[half][device, :, at : at + part].astype(jnp.float32) * scale
            step(which, slice(column, column + part), grad, RATE_MATRIX, DECAY_MATRIX)
    step(4, slice(0, 2), gain_grads_ref[...] * clip, RATE_GAIN, 0.0)


def adam(norm, zero, one, head, gain_grads, weights, firsts, seconds):
    state = (*weights, *firsts, *seconds)
    arrays = (zero, one, head, gain_grads, *state)
    return pl.pallas_call(
        adam_kernel,
        grid=(gain_grads.shape[0] // ROWS,),
        out_shape=[jax.ShapeDtypeStruct(x.shape, x.dtype) for x in state],
        in_specs=[pl.BlockSpec(norm.shape, lambda r: (0, 0))] + [rows_of(x) for x in arrays],
        out_specs=[rows_of(x) for x in state],
        compiler_params=pltpu.CompilerParams(vmem_limit_bytes=VMEM_LIMIT),
    )(norm, *arrays)


def product(left, right, left_dim, right_dim):
    return lax.dot_general(
        left, right, (((left_dim,), (right_dim,)), ((), ())), preferred_element_type=jnp.float32
    )


def shards(
    inputs,
    cotangent,
    lengths,
    positions,
    query_key_value_weight,
    out_weight,
    gateup_weight,
    down_weight,
    norm_gains,
    query_key_value_moment,
    output_weight_moment,
    gate_up_moment,
    down_weight_moment,
    norm_gains_moment,
    query_key_value_variance,
    out_second,
    gateup_second,
    down_second,
    gains_second,
):
    width = inputs.shape[2]
    seq = lax.axis_size("seq")
    far = lax.axis_size("far")
    group = seq * 2
    rows = out_weight.shape[0]
    query_width = QUERY_HEAD_COUNT * HEAD_SIZE
    key_width = KEY_VALUE_HEADS * HEAD_SIZE
    mine_q, mine_k = query_width // seq, key_width // seq
    units = FEED_UNITS // group
    part = units // 2
    low = jnp.bfloat16

    inputs = inputs[0]
    cotangent = cotangent[0]
    gains = norm_gains.astype(low).astype(jnp.float32)
    gain_one, gain_two = gains[:, :1], gains[:, 1:]

    def after(x, *others):
        return lax.optimization_barrier((x, *others))[0]

    def rounded(weight, gain=None):
        weight = weight.astype(low)
        return weight if gain is None else (weight.astype(jnp.float32) * gain).astype(low)

    by_far = (far, seq, 2 * rows, 3 * part)

    def feed_piece(half):
        start, size = half * FEED_UNITS // 2, FEED_UNITS // 2
        columns = [
            rounded(gateup_weight[:, start : start + size], gain_two),
            rounded(gateup_weight[:, FEED_UNITS + start : FEED_UNITS + start + size], gain_two),
            rounded(down_weight[:, start : start + size]),
        ]
        columns = [x.reshape(rows, group, part).transpose(1, 0, 2) for x in columns]
        return jnp.concatenate(columns, 2)

    (piece,) = exchange_plane([feed_piece(0).reshape(group * rows, 3 * part)], 1)
    feed_zero = lax.all_gather(piece, "far", axis=0, tiled=True).reshape(by_far)

    qkv_low = rounded(query_key_value_weight, gain_one)
    head_pieces = jnp.concatenate(
        [
            qkv_low[:, :query_width].reshape(rows, seq, mine_q),
            qkv_low[:, query_width : query_width + key_width].reshape(rows, seq, mine_k),
            qkv_low[:, query_width + key_width :].reshape(rows, seq, mine_k),
            rounded(out_weight).reshape(rows, seq, mine_q),
        ],
        2,
    ).transpose(1, 0, 2)
    unit_one, scale_one = rms_normalize(inputs)
    turns = rotary_tables(positions.reshape(-1), HEAD_SIZE)
    dout_here = cotangent.astype(low)
    head_pieces = after(head_pieces, piece)
    head_w, normed_one, all_turns, dout, piece = gather_heads(
        head_pieces, unit_one.astype(low), turns, dout_here, feed_piece(1), 2
    )
    feed_one = lax.all_gather(piece.reshape(group * rows, -1), "far", axis=0, tiled=True)
    feed_one = feed_one.reshape(by_far)
    all_turns = all_turns.reshape(-1, HEAD_SIZE)
    *saved, attended = attention(lengths, normed_one, head_w, all_turns)
    hidden = inputs + scatter_seq(attended, 3)
    unit_two, _ = rms_normalize(hidden)
    normed_two, act, dgateup, *sums = feed_first(unit_two.astype(low), dout, feed_zero, 4)
    terms = feed_grads(normed_two, dout, dgateup, act, far).reshape(width, 3 * part)
    grads_zero = lax.psum_scatter(terms, "far", scatter_dimension=0, tiled=True)
    act, dgateup, output_terms, dnormed_two = feed_second(
        normed_two, dout, *sums, after(feed_one, terms)
    )
    terms, dhidden, dattended = feed_back(
        hidden, cotangent, dgateup, act, normed_two, dout, dnormed_two, far, 5
    )
    terms = terms.reshape(width, 3 * part)
    grads_one = lax.psum_scatter(after(terms, grads_zero), "far", scatter_dimension=0, tiled=True)

    head_terms, dnormed_one, output_terms = attention_back(
        lengths, saved, all_turns, dattended, output_terms, head_w, normed_one, 6
    )
    head_terms = after(head_terms, grads_zero, grads_one)
    head_terms = lax.psum_scatter(
        head_terms.reshape(far * seq * rows, -1), "far", scatter_dimension=0, tiled=True
    )
    input_grad = dhidden + norm_backward(dnormed_one, unit_one, scale_one)
    layer_output = hidden + output_terms

    halves = [x.reshape(group, rows, 3 * part) for x in exchange_plane([grads_zero, grads_one], 7)]
    square, gain_terms = feed_norm(*halves, gateup_weight, norm_gains)
    head_terms = after(head_terms, square, input_grad, layer_output)
    head_grads, norm, gain_grads = settle(
        square, gain_terms, query_key_value_weight, norm_gains, head_terms.reshape(seq, rows, -1), 8
    )
    weights = (query_key_value_weight, out_weight, gateup_weight, down_weight, norm_gains)
    firsts = (query_key_value_moment, output_weight_moment, gate_up_moment, down_weight_moment, norm_gains_moment)
    seconds = (query_key_value_variance, out_second, gateup_second, down_second, gains_second)
    stepped = adam(norm, *halves, head_grads, gain_grads, weights, firsts, seconds)
    return (layer_output[None], input_grad[None], norm[0, 0], *stepped)


def solution(mesh):
    seq, fsdp = mesh.shape["seq"], mesh.shape["fsdp"]
    cut = Mesh(mesh.devices.reshape(seq, fsdp // 2, 2), EVERY)
    tokens = P(("far", "near"), "seq", None)
    matrix = P(EVERY, None)
    return jax.shard_map(
        shards,
        mesh=cut,
        in_specs=(tokens, tokens, P(("far", "near")), P(("far", "near"), "seq")) + (matrix,) * 15,
        out_specs=(tokens, tokens, P()) + (matrix,) * 15,
        check_vma=False,
    )
```

```python
import functools
import math

import jax
import jax.numpy as jnp
from jax import lax
from jax.experimental import pallas as pl
from jax.experimental.pallas import tpu as pltpu
from jax.sharding import Mesh, PartitionSpec as P

QUERY_HEAD_COUNT = 8
KEY_VALUE_HEADS = 4
HEAD_SIZE = 256
FEED_UNITS = 8192
STEP = 10

NORM_EPSILON = 1e-06
ROPE_BASE = 1000042.0
MASKED_SCORE = -1000000000.0
CLIP_NORM = 1.0
BETA_ONE = 0.9
BETA_TWO = 0.95
ADAM_EPSILON = 1e-08
DECAY_MATRIX = 0.1
RATE_MATRIX = 0.02
RATE_OUTPUT = 0.1
RATE_GAIN = 1.0

EVERY = ("seq", "far", "near")


MESH_IDS = pl.DeviceIdType.MESH
ANYWHERE = pl.BlockSpec(memory_space=pl.ANY)
IN_VMEM = pl.BlockSpec(memory_space=pltpu.VMEM)
VMEM_LIMIT = 60 * 1024 * 1024


def places():
    s, n = lax.axis_index("seq"), lax.axis_index("near")
    return s, n, s + 1 - 2 * (s % 2), (s + 2) % 4, 1 - n


def meet(*others):
    barrier = pltpu.get_barrier_semaphore()
    for other in others:
        pl.semaphore_signal(barrier, inc=1, device_id=other, device_id_type=MESH_IDS)
    pl.semaphore_wait(barrier, len(others))


def sender(send_sems, recv_sems):
    copies = {}

    def send(key, source, target, device):
        at = len(copies)
        copies[key] = pltpu.make_async_remote_copy(
            src_ref=source,
            dst_ref=target,
            send_sem=send_sems.at[at],
            recv_sem=recv_sems.at[at],
            device_id=device,
            device_id_type=MESH_IDS,
        )
        copies[key].start()

    return copies, send


def add_rows(target, first, second, third=None, step=64):
    rows = target.shape[0]

    def body(i, carry):
        at = pl.ds(pl.multiple_of(i * step, step), step)
        total = first[at, :].astype(jnp.float32) + second[at, :].astype(jnp.float32)
        if third is not None:
            total = total + third[at, :].astype(jnp.float32)
        target[at, :] = total.astype(target.dtype)
        return carry

    lax.fori_loop(0, rows // step, body, 0)


def exchange_plane_kernel(count, *refs):
    x_refs, o_refs = refs[:count], refs[count : 2 * count]
    local_sems, send_sems, recv_sems = refs[2 * count :]
    s, n, core, across, beside = places()
    diagonal = (core + 2) % 4
    mine = s * 2 + n
    others = [(seq, near) for near in (beside, n) for seq in (diagonal, across, core, s)][:-1]

    meet(*[{"seq": seq, "near": near} for seq, near in others])
    copies, send = sender(send_sems, recv_sems)
    locals_ = []
    for k, (x_ref, o_ref) in enumerate(zip(x_refs, o_refs)):
        rows = x_ref.shape[0] // 8

        def at(p):
            return pl.ds(p * rows, rows)

        for seq, near in others:
            target = {"seq": seq, "near": near}
            send(len(copies), x_ref.at[at(seq * 2 + near)], o_ref.at[at(mine)], target)
        locals_.append(pltpu.make_async_copy(x_ref.at[at(mine)], o_ref.at[at(mine)], local_sems.at[k]))
        locals_[k].start()
    for copy in copies.values():
        copy.wait_recv()
    for copy in copies.values():
        copy.wait_send()
    for copy in locals_:
        copy.wait()


def exchange_plane(arrays, collective_id):
    count = len(arrays)
    return pl.pallas_call(
        functools.partial(exchange_plane_kernel, count),
        out_shape=[jax.ShapeDtypeStruct(x.shape, x.dtype) for x in arrays],
        in_specs=[ANYWHERE] * count,
        out_specs=[ANYWHERE] * count,
        scratch_shapes=[
            pltpu.SemaphoreType.DMA((count,)),
            pltpu.SemaphoreType.DMA((7 * count,)),
            pltpu.SemaphoreType.DMA((7 * count,)),
        ],
        compiler_params=pltpu.CompilerParams(collective_id=collective_id, has_side_effects=True),
    )(*arrays)


def gather_heads_kernel(
    far_size,
    w_ref,
    x_ref,
    i_ref,
    d_ref,
    e_ref,
    o_ref,
    ox_ref,
    oi_ref,
    od_ref,
    oe_ref,
    local_sems,
    send_sems,
    recv_sems,
):
    s, n, core, across, beside = places()
    diagonal = (core + 2) % 4
    f = lax.axis_index("far")
    half = x_ref.shape[0] // 2
    to_core, to_y, to_x = {"seq": core}, {"seq": across}, {"near": beside}
    right, left = {"far": (f + 1) % far_size}, {"far": (f + far_size - 1) % far_size}

    others = [(seq, near) for near in (beside, n) for seq in (diagonal, across, core, s)][:-1]
    meet(*[{"seq": seq, "near": near} for seq, near in others], right, left)
    copies, send = sender(send_sems, recv_sems)
    keep = pltpu.make_async_copy(w_ref.at[s], o_ref.at[s, f, n], local_sems.at[0])
    keep.start()
    keep_x = pltpu.make_async_copy(x_ref, ox_ref.at[s], local_sems.at[1])
    keep_x.start()
    keep_i = pltpu.make_async_copy(i_ref, oi_ref.at[s], local_sems.at[2])
    keep_i.start()
    for k, seq in enumerate((diagonal, across, core)):
        send(("w", k), w_ref.at[seq], o_ref.at[s, f, n], {"seq": seq})
        send(("i", k), i_ref, oi_ref.at[s], {"seq": seq})
    for p in range(2):
        at = pl.ds(p * half, half)
        send(("y", p), x_ref.at[at], ox_ref.at[s, at], to_y)
        send(("c", p), x_ref.at[at], ox_ref.at[s, at], to_core)

    def block(seq, near, p):
        return od_ref.at[seq * 2 + near, pl.ds(p * half, half)]

    def own(p):
        return d_ref.at[pl.ds(p * half, half)]

    keep_d = pltpu.make_async_copy(d_ref, od_ref.at[s * 2 + n], local_sems.at[3])
    keep_d.start()
    send("y0", own(0), block(s, n, 0), to_y)
    send("x1", own(1), block(s, n, 1), to_x)
    send("y1", own(1), block(s, n, 1), to_y)
    send("x0", own(0), block(s, n, 0), to_x)
    send("c0", own(0), block(s, n, 0), to_core)
    send("c1", own(1), block(s, n, 1), to_core)
    keep_e = pltpu.make_async_copy(e_ref.at[s * 2 + n], oe_ref.at[s * 2 + n], local_sems.at[4])
    keep_e.start()
    for k, (seq, near) in enumerate(others):
        target = {"seq": seq, "near": near}
        send(("e", k), e_ref.at[seq * 2 + near], oe_ref.at[s * 2 + n], target)
    keep.wait()
    for k in range(3):
        copies["w", k].wait_recv()

    def along(far, p, device, sem):
        piece = o_ref.at[p, far, n]
        return pltpu.make_async_remote_copy(
            src_ref=piece,
            dst_ref=piece,
            send_sem=send_sems.at[base + 4 * sem + p],
            recv_sem=recv_sems.at[base + 4 * sem + p],
            device_id=device,
            device_id_type=MESH_IDS,
        )

    base = 33

    def to_right(k, p):
        return along((f + far_size - k) % far_size, p, right, k)

    def to_left(k, p):
        return along((f + k) % far_size, p, left, far_size + k)

    def x_from_left(k, p):
        return along((f + far_size - k) % far_size, p, to_x, 2 * far_size + k)

    def x_from_right(k, p):
        return along((f + k) % far_size, p, to_x, 3 * far_size + k)

    for k in range(far_size):
        for p in range(4):
            if k > 0:

                @pl.when(f >= k)
                def _():
                    to_right(k - 1, p).wait_recv()

            @pl.when((f >= k) & (f < far_size - 1))
            def _():
                to_right(k, p).start()

            if k > 0:

                @pl.when(f + k < far_size)
                def _():
                    to_left(k - 1, p).wait_recv()

            @pl.when((f + k < far_size) & (f > 0))
            def _():
                to_left(k, p).start()

            if k == 0:
                x_from_left(0, p).start()
            else:

                @pl.when(f >= k)
                def _():
                    x_from_left(k, p).start()

                @pl.when(f + k < far_size)
                def _():
                    x_from_right(k, p).start()

        if k == min(1, far_size - 1):
            for p in range(2):
                at = pl.ds(p * half, half)
                copies["y", p].wait_recv()
                send(("yc", p), ox_ref.at[across, at], ox_ref.at[across, at], to_core)
        if k == max(far_size - 2, 0):
            copies["y0"].wait_recv()
            send("yx", block(across, n, 0), block(across, n, 0), to_x)
            send("yc0", block(across, n, 0), block(across, n, 0), to_core)
            copies["x1"].wait_recv()
            send("xy", block(s, beside, 1), block(s, beside, 1), to_y)
            send("xc1", block(s, beside, 1), block(s, beside, 1), to_core)
            copies["y1"].wait_recv()
            send("yc1", block(across, n, 1), block(across, n, 1), to_core)
            copies["x0"].wait_recv()
            send("xc0", block(s, beside, 0), block(s, beside, 0), to_core)
    copies["yx"].wait_recv()
    send("dc0", block(across, beside, 0), block(across, beside, 0), to_core)
    copies["xy"].wait_recv()
    send("dc1", block(across, beside, 1), block(across, beside, 1), to_core)
    for key in ("c0", "c1", "yc0", "yc1", "xc0", "xc1", "dc0", "dc1"):
        copies[key].wait_recv()
    for p in range(2):
        copies["c", p].wait_recv()
        copies["yc", p].wait_recv()
    for k in range(3):
        copies["i", k].wait_recv()
    for k in range(7):
        copies["e", k].wait_recv()
    for k in range(far_size):
        for p in range(4):

            @pl.when((f >= k) & (f < far_size - 1))
            def _():
                to_right(k, p).wait_send()

            @pl.when((f + k < far_size) & (f > 0))
            def _():
                to_left(k, p).wait_send()

            @pl.when(f >= k)
            def _():
                x_from_left(k, p).wait_recv()
                x_from_left(k, p).wait_send()

            if k > 0:

                @pl.when(f + k < far_size)
                def _():
                    x_from_right(k, p).wait_recv()
                    x_from_right(k, p).wait_send()

    for copy in copies.values():
        copy.wait_send()
    keep_x.wait()
    keep_i.wait()
    keep_d.wait()
    keep_e.wait()


def gather_heads(w, x, i, d, e, collective_id):
    far_size = lax.axis_size("far")
    _, rows, columns = w.shape
    tokens, width = x.shape
    sems = 33 + 16 * far_size
    full, all_x, all_i, all_d, mine_e = pl.pallas_call(
        functools.partial(gather_heads_kernel, far_size),
        out_shape=[
            jax.ShapeDtypeStruct((4, far_size, 2, rows, columns), w.dtype),
            jax.ShapeDtypeStruct((4, tokens, width), x.dtype),
            jax.ShapeDtypeStruct((4, *i.shape), i.dtype),
            jax.ShapeDtypeStruct((8, *d.shape), d.dtype),
            jax.ShapeDtypeStruct(e.shape, e.dtype),
        ],
        in_specs=[ANYWHERE] * 5,
        out_specs=[ANYWHERE] * 5,
        scratch_shapes=[
            pltpu.SemaphoreType.DMA((5,)),
            pltpu.SemaphoreType.DMA((sems,)),
            pltpu.SemaphoreType.DMA((sems,)),
        ],
        compiler_params=pltpu.CompilerParams(collective_id=collective_id, has_side_effects=True),
    )(w, x, i, d, e)
    all_x, all_d = all_x.reshape(-1, width), all_d.reshape(-1, d.shape[1])
    return full.reshape(-1, columns), all_x, all_i, all_d, mine_e


def tile_at(tile, rows):
    return pl.ds(pl.multiple_of(tile * rows, rows), rows)


def stacked(pair):
    half = pair.shape[1] // 2
    return jnp.concatenate([pair[:, :half], pair[:, half:]], 0)


def turned(value, cos, sin):
    half = value.shape[1] // 2
    first, second = value[:, :half], value[:, half:]
    return first * cos - second * sin, second * cos + first * sin


def visible_keys(tile, rows, keys, length):
    shape = (2 * rows, keys)
    row = lax.broadcasted_iota(jnp.int32, shape, 0)
    row = jnp.where(row >= rows, row - rows, row) + tile * rows
    column = lax.broadcasted_iota(jnp.int32, shape, 1)
    return (column <= row) & (column < length)


def attention_kernel(
    length_ref,
    x_ref,
    w_ref,
    turn_ref,
    input_ref,
    q_ref,
    k_ref,
    v_ref,
    heads_ref,
    lse_ref,
    hidden_ref,
    unit_ref,
    terms,
    far,
    last,
    send_sems,
    recv_sems,
):
    s, _, core, across, _ = places()
    to_core, to_y = {"seq": core}, {"seq": across}
    rows = x_ref.shape[0] // 4
    half = rows // 2
    size = k_ref.shape[1]
    low = jnp.bfloat16
    length = length_ref[0]
    order = [(core + 2) % 4, across, core, s]

    def rotated(ref, at, column, value, scale):
        cos, sin = turn_ref[at, : size // 2], turn_ref[at, size // 2 :]
        first, second = turned(value, cos, sin)
        ref[at, column : column + size // 2] = (first * scale).astype(low)
        ref[at, column + size // 2 : column + size] = (second * scale).astype(low)

    def keys_of(tile, carry):
        at = tile_at(tile, rows)
        merged = product(x_ref[at, :], w_ref[:, 2 * size : 4 * size], 1, 0)
        rotated(k_ref, at, 0, merged[:, :size], 1.0)
        v_ref[at, :] = merged[:, size:].astype(low)
        return carry

    def part(ref, p):
        return ref.at[pl.ds(p * half, half)]

    meet(to_core, to_y)
    lax.fori_loop(0, 4, keys_of, 0)

    def attend(tile):
        at = pl.ds(tile * rows, rows)
        keys = (tile + 1) * rows
        scores = product(stacked(q_ref[at, :]), k_ref[:keys, :], 1, 1)
        scores = jnp.where(visible_keys(tile, rows, keys, length), scores, MASKED_SCORE)
        peak = jnp.max(scores, 1, keepdims=True)
        expo = jnp.exp(scores - peak)
        total = jnp.sum(expo, 1, keepdims=True)
        result = product((expo * (1.0 / total)).astype(low), v_ref[:keys, :], 1, 0)
        live = lax.broadcasted_iota(jnp.int32, (rows, 1), 0) + tile * rows < length
        lse = peak + jnp.log(total)
        for head in range(2):
            mine = slice(head * rows, (head + 1) * rows)
            heads_ref[at, head * size : (head + 1) * size] = jnp.where(live, result[mine], 0.0).astype(low)
            lse_ref[at, head : head + 1] = lse[mine]

    plan = [
        (terms.at[0], far.at[0], to_core),
        (terms.at[2], far.at[1], to_core),
        (part(terms.at[1], 0), part(last, 0), to_y),
        (part(terms.at[1], 1), part(last, 1), to_y),
    ]

    def copy_of(k):
        source, target, device = plan[k]
        return pltpu.make_async_remote_copy(
            src_ref=source,
            dst_ref=target,
            send_sem=send_sems.at[k],
            recv_sem=recv_sems.at[k],
            device_id=device,
            device_id_type=MESH_IDS,
        )

    def tile_step(step, carry):
        tile = order[0]
        for k in range(1, 4):
            tile = jnp.where(step == k, order[k], tile)
        at = tile_at(tile, rows)
        merged = product(x_ref[at, :], w_ref[:, : 2 * size], 1, 0)
        for head in range(2):
            rotated(q_ref, at, head * size, merged[:, head * size : (head + 1) * size], size**-0.5)
        for k in range(4):

            @pl.when(tile == k)
            def _():
                attend(k)

        terms[step] = product(heads_ref[at, :], w_ref[:, 4 * size :], 1, 1).astype(low)

        @pl.when(step == 0)
        def _():
            copy_of(0).start()

        @pl.when(step == 1)
        def _():
            copy_of(0).wait_recv()
            for p in range(2):
                add_rows(part(terms.at[1], p), part(terms.at[1], p), part(far.at[0], p))
                copy_of(2 + p).start()

        @pl.when(step == 2)
        def _():
            copy_of(1).start()

        return carry

    lax.fori_loop(0, 4, tile_step, 0)
    copy_of(1).wait_recv()
    add_rows(hidden_ref, terms.at[3], far.at[1])

    def finish(i, carry):
        at = pl.ds(pl.multiple_of(i * 16, 16), 16)
        hidden = input_ref[at, :] + (hidden_ref[at, :] + last[at, :].astype(jnp.float32))
        hidden_ref[at, :] = hidden
        unit_ref[at, :] = rms_normalize(hidden)[0].astype(low)
        return carry

    for p in range(2):
        copy_of(2 + p).wait_recv()
        lax.fori_loop(p * half // 16, (p + 1) * half // 16, finish, 0)
    for k in range(4):
        copy_of(k).wait_send()


def attention(length, x, w, turns, inputs, collective_id):
    tokens, width = x.shape
    size = w.shape[1] // 6
    rows = tokens // 4
    low = jnp.bfloat16
    results = [((tokens, 2 * size), low), ((tokens, size), low), ((tokens, size), low), ((tokens, 2 * size), low)]
    results += [((tokens, 128), jnp.float32), ((rows, width), jnp.float32), ((rows, width), low)]
    return pl.pallas_call(
        attention_kernel,
        out_shape=[jax.ShapeDtypeStruct(*result) for result in results],
        in_specs=[pl.BlockSpec(memory_space=pltpu.SMEM)] + [IN_VMEM] * 4,
        out_specs=[IN_VMEM] * 7,
        scratch_shapes=[
            pltpu.VMEM((4, rows, width), low),
            pltpu.VMEM((2, rows, width), low),
            pltpu.VMEM((rows, width), low),
            pltpu.SemaphoreType.DMA((4,)),
            pltpu.SemaphoreType.DMA((4,)),
        ],
        compiler_params=pltpu.CompilerParams(
            collective_id=collective_id, has_side_effects=True, vmem_limit_bytes=VMEM_LIMIT
        ),
        cost_estimate=pl.CostEstimate(flops=10_000_000_000, bytes_accessed=20_000_000, transcendentals=0),
    )(length, x, w, turns, inputs)


def attention_back_kernel(
    length_ref,
    q_ref,
    k_ref,
    v_ref,
    heads_ref,
    lse_ref,
    turn_ref,
    g_ref,
    y_ref,
    w_ref,
    x_ref,
    terms_ref,
    dx_ref,
    sum_ref,
    weights,
    tokens,
    dheads,
    dfused,
    dk,
    dv,
    mine,
    far,
    hop_x,
    hop_y,
    last_x,
    last_y,
    far_d,
    last_d,
    out_grad,
    qkv_grad,
    out_there,
    qkv_there,
    local_sems,
    send_sems,
    recv_sems,
):
    s, n, core, across, beside = places()
    other = (core + 2) % 4
    to_core, to_y, to_x = {"seq": core}, {"seq": across}, {"near": beside}
    rows = g_ref.shape[0]
    half = rows // 2
    size = k_ref.shape[1]
    low = jnp.bfloat16
    length = length_ref[0]
    far_size = terms_ref.shape[0]

    def local(source, target, at):
        copy = pltpu.make_async_copy(source, target, local_sems.at[at])
        copy.start()
        return copy

    def part(ref, p):
        return ref.at[pl.ds(p * half, half)]

    def token_rows(seq, p):
        return tokens.at[pl.ds(seq * rows + p * half, half)]

    def block(seq, near):
        return y_ref.at[pl.ds((seq * 2 + near) * rows, rows)]

    meet(to_core, to_y, to_x)
    copies, send = sender(send_sems, recv_sems)
    keep = local(g_ref, tokens.at[pl.ds(s * rows, rows)], 0)
    for p in range(2):
        send(("gy", p), part(g_ref, p), token_rows(s, p), to_y)
    for p in range(2):
        send(("gc", p), part(g_ref, p), token_rows(s, p), to_core)
    given = [block(other, beside), block(other, n), block(core, beside), block(core, n)]
    kept = [block(across, beside), block(across, n), block(s, beside), block(s, n)]
    loads = []
    for k in range(4):
        send(k, given[k], far.at[k], to_core)
        loads.append(local(kept[k], mine.at[k], 1 + k))
    load_w = local(w_ref, weights, 5)
    for k in range(3):
        loads[k].wait()
        copies[k].wait_recv()
        add_rows(mine.at[k], mine.at[k], far.at[k])
        if k == 0:
            send("hx", part(mine.at[0], 0), hop_x, to_x)
    send("x0", part(mine.at[2], 0), part(last_x, 0), to_x)
    for p in range(2):
        copies["gy", p].wait_recv()
        send(("gyc", p), token_rows(across, p), token_rows(across, p), to_core)
    send("hy", part(mine.at[0], 1), hop_y, to_y)
    send("y1", part(mine.at[1], 1), part(last_y, 1), to_y)
    loads[3].wait()
    copies[3].wait_recv()
    add_rows(sum_ref, mine.at[3], far.at[3])
    keep.wait()
    load_w.wait()
    for p in range(2):
        copies["gc", p].wait_recv()
        copies["gyc", p].wait_recv()

    def dheads_of(tile, carry):
        at = tile_at(tile, rows)
        live = lax.broadcasted_iota(jnp.int32, (rows, 1), 0) + tile * rows < length
        value = product(tokens[at, :], weights[:, 4 * size :], 1, 0)
        dheads[at, :] = jnp.where(live, value, 0.0).astype(low)
        return carry

    def by_rows(value):
        return value.astype(low).reshape(far_size, 2, -1, value.shape[1])

    width = tokens.shape[1]
    quarter = width // 4
    for q in range(4):
        out_grad[q] = by_rows(product(tokens[:, q * quarter : (q + 1) * quarter], heads_ref[...], 0, 0))
    send("out", out_grad.at[:, :, beside], out_there, to_x)
    lax.fori_loop(0, 4, dheads_of, 0)
    for copy in ("gyc", "gy", "gc"):
        for p in range(2):
            copies[copy, p].wait_send()
    load_x = local(x_ref, tokens, 0)
    copies["hx"].wait_recv()
    add_rows(part(mine.at[1], 0), part(mine.at[1], 0), hop_x)
    send("y0", part(mine.at[1], 0), part(last_y, 0), to_y)
    copies["hy"].wait_recv()
    add_rows(part(mine.at[2], 1), part(mine.at[2], 1), hop_y)
    send("x1", part(mine.at[2], 1), part(last_x, 1), to_x)

    dk[...] = jnp.zeros_like(dk)
    dv[...] = jnp.zeros_like(dv)
    for tile in range(4):
        at = pl.ds(tile * rows, rows)
        keys = (tile + 1) * rows
        query = stacked(q_ref[at, :])
        dhead = stacked(dheads[at, :])
        scores = product(query, k_ref[:keys, :], 1, 1)
        lse = jnp.concatenate([lse_ref[at, 0:1], lse_ref[at, 1:2]], 0)
        probs = jnp.where(visible_keys(tile, rows, keys, length), jnp.exp(scores - lse), 0.0)
        dprobs = product(dhead, v_ref[:keys, :], 1, 1)
        inner = jnp.sum(probs * dprobs, 1, keepdims=True)
        dscores = (probs * (dprobs - inner)).astype(low)
        dv[:keys, :] += product(probs.astype(low), dhead, 0, 0)
        dk[:keys, :] += product(dscores, query, 0, 0)
        dquery = product(dscores, k_ref[:keys, :], 1, 0) * size**-0.5
        cos, sin = turn_ref[at, : size // 2], turn_ref[at, size // 2 :]
        for head in range(2):
            rounded = dquery[head * rows : (head + 1) * rows].astype(low).astype(jnp.float32)
            first, second = turned(rounded, cos, -sin)
            dfused[at, head * size : head * size + size // 2] = first.astype(low)
            dfused[at, head * size + size // 2 : (head + 1) * size] = second.astype(low)
    first, second = turned(
        dk[...].astype(low).astype(jnp.float32), turn_ref[:, : size // 2], -turn_ref[:, size // 2 :]
    )
    dfused[:, 2 * size : 2 * size + size // 2] = first.astype(low)
    dfused[:, 2 * size + size // 2 : 3 * size] = second.astype(low)
    dfused[:, 3 * size :] = dv[...].astype(low)

    load_x.wait()
    for q in range(4):
        qkv_grad[q] = by_rows(product(tokens[:, q * quarter : (q + 1) * quarter], dfused[...], 0, 0))
        send(("qkv", q), qkv_grad.at[q, :, beside], qkv_there.at[q], to_x)

    for p, first, second in ((1, "y1", "x1"), (0, "x0", "y0")):
        copies[first].wait_recv()
        copies[second].wait_recv()
        add_rows(part(sum_ref, p), part(sum_ref, p), part(last_x, p), part(last_y, p))
    for key in ("hx", "hy", "y0", "y1", "x0", "x1"):
        copies[key].wait_send()

    def dx_of(k, tile):
        mine[k] = product(dfused[tile_at(tile, rows), :], weights[:, : 4 * size], 1, 1).astype(low)

    dx_of(0, other)
    send("d0", mine.at[0], far_d.at[0], to_core)
    dx_of(1, core)
    send("d1", mine.at[1], far_d.at[1], to_core)
    dx_of(2, across)
    copies["d0"].wait_recv()
    for p in range(2):
        add_rows(part(mine.at[2], p), part(mine.at[2], p), part(far_d.at[0], p))
        send(("dy", p), part(mine.at[2], p), part(last_d, p), to_y)
    dx_of(3, s)
    copies["d1"].wait_recv()
    add_rows(dx_ref, mine.at[3], far_d.at[1])
    outs = []
    copies["out"].wait_recv()
    for q in range(4):
        for f in range(far_size):
            out_there[q, f] = (
                out_there[q, f].astype(jnp.float32) + out_grad[q, f, n].astype(jnp.float32)
            ).astype(low)
    for p in range(2):
        copies["dy", p].wait_recv()
        add_rows(part(dx_ref, p), part(dx_ref, p), part(last_d, p))
    for q in range(4):
        copies["qkv", q].wait_recv()
        for f in range(far_size):
            qkv_there[q, f] = (
                qkv_there[q, f].astype(jnp.float32) + qkv_grad[q, f, n].astype(jnp.float32)
            ).astype(low)
        outs.append(local(out_there.at[q], terms_ref.at[:, q, :, 4 * size :], q))
        outs.append(local(qkv_there.at[q], terms_ref.at[:, q, :, : 4 * size], 4 + q))
    for copy in outs:
        copy.wait()
    waited = {"hx", "hy", "y0", "y1", "x0", "x1"}
    for key, copy in copies.items():
        if key not in waited and not (isinstance(key, tuple) and key[0] in ("gyc", "gy", "gc")):
            copy.wait_send()


def attention_back(length, saved, turns, g, y, w, x, collective_id):
    q, k, v, heads, lse = saved
    tokens, width = x.shape
    size = k.shape[1]
    rows = tokens // 4
    far_size = lax.axis_size("far")
    weight_rows = width // (8 * far_size)
    low = jnp.bfloat16
    block = pltpu.VMEM((rows, width), low)
    half_block = pltpu.VMEM((rows // 2, width), low)
    return pl.pallas_call(
        attention_back_kernel,
        out_shape=[
            jax.ShapeDtypeStruct((far_size, 4, weight_rows, 6 * size), low),
            jax.ShapeDtypeStruct((rows, width), jnp.float32),
            jax.ShapeDtypeStruct((rows, width), jnp.float32),
        ],
        in_specs=[pl.BlockSpec(memory_space=pltpu.SMEM)] + [IN_VMEM] * 6 + [ANYWHERE] * 4,
        out_specs=[ANYWHERE, IN_VMEM, IN_VMEM],
        scratch_shapes=[
            pltpu.VMEM(w.shape, low),
            pltpu.VMEM((tokens, width), low),
            pltpu.VMEM((tokens, 2 * size), low),
            pltpu.VMEM((tokens, 4 * size), low),
            pltpu.VMEM((tokens, size), jnp.float32),
            pltpu.VMEM((tokens, size), jnp.float32),
            pltpu.VMEM((4, rows, width), low),
            pltpu.VMEM((4, rows, width), low),
            half_block,
            half_block,
            block,
            block,
            pltpu.VMEM((2, rows, width), low),
            block,
            pltpu.VMEM((4, far_size, 2, weight_rows, 2 * size), low),
            pltpu.VMEM((4, far_size, 2, weight_rows, 4 * size), low),
            pltpu.VMEM((4, far_size, weight_rows, 2 * size), low),
            pltpu.VMEM((4, far_size, weight_rows, 4 * size), low),
            pltpu.SemaphoreType.DMA((8,)),
            pltpu.SemaphoreType.DMA((25,)),
            pltpu.SemaphoreType.DMA((25,)),
        ],
        compiler_params=pltpu.CompilerParams(
            collective_id=collective_id, has_side_effects=True, vmem_limit_bytes=VMEM_LIMIT
        ),
        cost_estimate=pl.CostEstimate(flops=20_000_000_000, bytes_accessed=40_000_000, transcendentals=0),
    )(length, q, k, v, heads, lse, turns, g, y, w, x)


def hidden_units(x, d, w, part):
    low = jnp.bfloat16
    gate = product(x, w[:, :part], 1, 0)
    upper = product(x, w[:, part : 2 * part], 1, 0)
    dact = product(d, w[:, 2 * part :], 1, 0)
    sig = 1.0 / (1.0 + jnp.exp(-gate))
    silu = gate * sig
    act = (silu * upper).astype(low)
    dgate = (dact * upper * (sig + silu * (1.0 - sig))).astype(low)
    dupper = (dact * silu).astype(low)
    return act, dgate, dupper


def load_weights(w_ref, weights, sems):
    loads = [
        pltpu.make_async_copy(w_ref.at[f], weights.at[:, f], sems.at[f]) for f in range(w_ref.shape[0])
    ]
    for load in loads:
        load.start()
    return loads


def feed_first_kernel(
    x_ref,
    d_ref,
    w_ref,
    all_ref,
    act_ref,
    dgu_ref,
    y_ref,
    dx_ref,
    weights,
    tokens,
    there,
    acts,
    dgus,
    ys,
    dxs,
    local_sems,
    d_sems,
    out_sems,
    send_sems,
    recv_sems,
):
    s, n, core, across, beside = places()
    other = (core + 2) % 4
    rows = x_ref.shape[0]
    half = rows // 2
    to_core, to_y, to_x = {"seq": core}, {"seq": across}, {"near": beside}
    part = weights.shape[3] // 3
    width = x_ref.shape[1]
    low = jnp.bfloat16

    def block(seq, near, p):
        return tokens.at[seq * 2 + near, pl.ds(p * half, half)]

    def own(p):
        return x_ref.at[pl.ds(p * half, half)]

    order = [
        s * 2 + n,
        core * 2 + n,
        across * 2 + n,
        other * 2 + n,
        s * 2 + beside,
        core * 2 + beside,
        across * 2 + beside,
        other * 2 + beside,
    ]

    def tile_of(step):
        tile = order[0]
        for k in range(1, 8):
            tile = jnp.where(step == k, order[k], tile)
        return tile

    def d_load(step):
        slot = step % 2
        at = tile_at(tile_of(step), rows)
        return pltpu.make_async_copy(d_ref.at[at], there.at[slot], d_sems.at[slot])

    def stores(step):
        slot = step % 2
        tile = tile_of(step)
        at = tile_at(tile, rows)
        pairs = (
            (tokens.at[tile], all_ref),
            (acts.at[slot], act_ref),
            (dgus.at[slot], dgu_ref),
            (ys.at[slot], y_ref),
            (dxs.at[slot], dx_ref),
        )
        return [
            pltpu.make_async_copy(source, target.at[at], out_sems.at[slot, k])
            for k, (source, target) in enumerate(pairs)
        ]

    def piece(seq, near, p, device):
        return block(seq, near, p), block(seq, near, p), device

    plan = {
        "y0": (own(0), block(s, n, 0), to_y),
        "x1": (own(1), block(s, n, 1), to_x),
        "y1": (own(1), block(s, n, 1), to_y),
        "x0": (own(0), block(s, n, 0), to_x),
        "c0": (own(0), block(s, n, 0), to_core),
        "c1": (own(1), block(s, n, 1), to_core),
        "yx": piece(across, n, 0, to_x),
        "yc0": piece(across, n, 0, to_core),
        "xy": piece(s, beside, 1, to_y),
        "xc1": piece(s, beside, 1, to_core),
        "yc1": piece(across, n, 1, to_core),
        "xc0": piece(s, beside, 0, to_core),
        "dc0": piece(across, beside, 0, to_core),
        "dc1": piece(across, beside, 1, to_core),
    }
    places_of = {key: at for at, key in enumerate(plan)}

    def copy_of(key):
        source, target, device = plan[key]
        at = places_of[key]
        return pltpu.make_async_remote_copy(
            src_ref=source,
            dst_ref=target,
            send_sem=send_sems.at[at],
            recv_sem=recv_sems.at[at],
            device_id=device,
            device_id_type=MESH_IDS,
        )

    def send(*keys):
        for key in keys:
            copy_of(key).start()

    def arrive(*keys):
        for key in keys:
            copy_of(key).wait_recv()

    meet(to_core, to_y, to_x)
    keep = pltpu.make_async_copy(x_ref, tokens.at[s * 2 + n], local_sems.at[0])
    keep.start()
    send("y0", "x1", "y1", "x0", "c0", "c1")
    loads = load_weights(w_ref, weights, local_sems.at[pl.ds(1, w_ref.shape[0])])
    d_load(0).start()
    keep.wait()
    for load in loads:
        load.wait()

    def before(step):
        if step == 1:
            arrive("c0", "c1")
        elif step == 2:
            arrive("y0")
            send("yx", "yc0")
            arrive("x1")
            send("xy", "xc1")
            arrive("y1")
            send("yc1")
            arrive("x0")
            send("xc0")
        elif step == 3:
            arrive("yc0", "yc1")
        elif step == 5:
            arrive("xc0", "xc1")
        elif step == 6:
            arrive("yx")
            send("dc0")
            arrive("xy")
            send("dc1")
        elif step == 7:
            arrive("dc0", "dc1")

    def step_of(step, carry):
        for k in (1, 2, 3, 5, 6, 7):

            @pl.when(step == k)
            def _():
                before(k)

        slot = step % 2

        @pl.when(step < 7)
        def _():
            d_load(step + 1).start()

        @pl.when(step >= 2)
        def _():
            for store in stores(step - 2):
                store.wait()

        d_load(step).wait()
        w = weights[...].reshape(width, 3 * part)
        act, dgate, dupper = hidden_units(tokens[tile_of(step)], there[slot], w, part)
        acts[slot] = act
        dgus[slot, :, :part] = dgate
        dgus[slot, :, part:] = dupper
        ys[slot] = product(act, w[:, 2 * part :], 1, 1).astype(low)
        dxs[slot] = product(dgus[slot], w[:, : 2 * part], 1, 1).astype(low)
        for store in stores(step):
            store.start()
        return carry

    lax.fori_loop(0, 8, step_of, 0)
    for step in (6, 7):
        for store in stores(step):
            store.wait()
    for key in plan:
        copy_of(key).wait_send()


def feed_first(x, d, w, collective_id):
    rows, width = x.shape
    part = w.shape[3] // 3
    tokens = 8 * rows
    low = jnp.bfloat16
    far, _, weight_rows, columns = w.shape
    sizes = (width, part, 2 * part, width, width)
    return pl.pallas_call(
        feed_first_kernel,
        out_shape=[jax.ShapeDtypeStruct((tokens, size), low) for size in sizes],
        in_specs=[ANYWHERE] * 3,
        out_specs=[ANYWHERE] * 5,
        scratch_shapes=[
            pltpu.VMEM((4, far, weight_rows, columns), low),
            pltpu.VMEM((8, rows, width), low),
            pltpu.VMEM((2, rows, width), low),
            pltpu.VMEM((2, rows, part), low),
            pltpu.VMEM((2, rows, 2 * part), low),
            pltpu.VMEM((2, rows, width), low),
            pltpu.VMEM((2, rows, width), low),
            pltpu.SemaphoreType.DMA((1 + far,)),
            pltpu.SemaphoreType.DMA((2,)),
            pltpu.SemaphoreType.DMA((2, 5)),
            pltpu.SemaphoreType.DMA((14,)),
            pltpu.SemaphoreType.DMA((14,)),
        ],
        compiler_params=pltpu.CompilerParams(
            collective_id=collective_id, has_side_effects=True, vmem_limit_bytes=VMEM_LIMIT
        ),
        cost_estimate=pl.CostEstimate(
            flops=12 * tokens * width * part, bytes_accessed=60_000_000, transcendentals=0
        ),
    )(x, d, w)


def feed_second_kernel(x_ref, d_ref, y0_ref, dx0_ref, w_ref, act_ref, dgu_ref, y_ref, dx_ref, weights, sems):
    part = weights.shape[3] // 3
    width = x_ref.shape[1]
    low = jnp.bfloat16

    @pl.when(pl.program_id(0) == 0)
    def _():
        for load in load_weights(w_ref, weights, sems):
            load.wait()

    w = weights[...].reshape(width, 3 * part)
    act, dgate, dupper = hidden_units(x_ref[...], d_ref[...], w, part)
    act_ref[...] = act
    dgu_ref[:, :part] = dgate
    dgu_ref[:, part:] = dupper
    y = product(act, w[:, 2 * part :], 1, 1) + y0_ref[...].astype(jnp.float32)
    y_ref[...] = y.astype(low)
    dx = product(dgu_ref[...], w[:, : 2 * part], 1, 1) + dx0_ref[...].astype(jnp.float32)
    dx_ref[...] = dx.astype(low)


def feed_second(x, d, y, dx, w, tile=512):
    tokens, width = x.shape
    part = w.shape[3] // 3
    low = jnp.bfloat16
    far, _, weight_rows, columns = w.shape

    def tokens_of(columns):
        return pl.BlockSpec((tile, columns), lambda t: (t, 0))

    sizes = (part, 2 * part, width, width)
    return pl.pallas_call(
        feed_second_kernel,
        grid=(tokens // tile,),
        out_shape=[jax.ShapeDtypeStruct((tokens, size), low) for size in sizes],
        in_specs=[tokens_of(width)] * 4 + [ANYWHERE],
        out_specs=[tokens_of(size) for size in sizes],
        scratch_shapes=[pltpu.VMEM((4, far, weight_rows, columns), low), pltpu.SemaphoreType.DMA((far,))],
        compiler_params=pltpu.CompilerParams(vmem_limit_bytes=VMEM_LIMIT),
        cost_estimate=pl.CostEstimate(
            flops=12 * tokens * width * part, bytes_accessed=60_000_000, transcendentals=0
        ),
    )(x, d, y, dx, w)


def feed_grads_kernel(x_ref, d_ref, dgu_ref, act_ref, o_ref):
    split = dgu_ref.shape[1]
    far, _, rows, columns = o_ref.shape
    gateup = product(x_ref[...], dgu_ref[...], 0, 0).astype(o_ref.dtype)
    o_ref[:, 0, :, :split] = gateup.reshape(far, rows, split)
    down = product(d_ref[...], act_ref[...], 0, 0).astype(o_ref.dtype)
    o_ref[:, 0, :, split:] = down.reshape(far, rows, columns - split)


def feed_grads(x, d, dgu, act, far):
    tokens, width = x.shape
    columns = dgu.shape[1] + act.shape[1]
    rows = width // (4 * far)
    some = pl.BlockSpec((tokens, width // 4), lambda t: (0, t))

    def whole(array):
        return pl.BlockSpec(array.shape, lambda t: (0, 0), pipeline_mode=pl.Buffered(1))

    return pl.pallas_call(
        feed_grads_kernel,
        grid=(4,),
        out_shape=jax.ShapeDtypeStruct((far, 4, rows, columns), x.dtype),
        in_specs=[some, some, whole(dgu), whole(act)],
        out_specs=pl.BlockSpec((far, 1, rows, columns), lambda t: (0, t, 0, 0)),
        compiler_params=pltpu.CompilerParams(vmem_limit_bytes=VMEM_LIMIT),
        cost_estimate=pl.CostEstimate(
            flops=2 * tokens * width * columns, bytes_accessed=40_000_000, transcendentals=0
        ),
    )(x, d, dgu, act)


def feed_back_kernel(
    hidden_ref,
    cotangent_ref,
    dgu_ref,
    act_ref,
    x_ref,
    d_ref,
    p_ref,
    terms_ref,
    dhidden_ref,
    low_ref,
    mine,
    far,
    hop_x,
    hop_y,
    last_x,
    last_y,
    xs,
    ds,
    outs,
    local_sems,
    x_sems,
    out_sems,
    send_sems,
    recv_sems,
):
    s, n, core, across, beside = places()
    other = (core + 2) % 4
    to_core, to_y, to_x = {"seq": core}, {"seq": across}, {"near": beside}
    rows, width = hidden_ref.shape
    half = rows // 2
    quarter = width // 4
    split = dgu_ref.shape[1]
    far_size, _, weight_rows, columns = terms_ref.shape

    def block(seq, near):
        return p_ref.at[pl.ds((seq * 2 + near) * rows, rows)]

    def part(ref, p):
        return ref.at[pl.ds(p * half, half)]

    def columns_in(q):
        slot = q % 2
        at = pl.ds(q * quarter, quarter)
        return (
            pltpu.make_async_copy(x_ref.at[:, at], xs.at[slot], x_sems.at[slot, 0]),
            pltpu.make_async_copy(d_ref.at[:, at], ds.at[slot], x_sems.at[slot, 1]),
        )

    def terms_out(q):
        return pltpu.make_async_copy(outs.at[q % 2], terms_ref.at[:, q], out_sems.at[q % 2])

    meet(to_core, to_y, to_x)
    copies, send = sender(send_sems, recv_sems)
    given = [block(other, beside), block(other, n), block(core, beside), block(core, n)]
    kept = [block(across, beside), block(across, n), block(s, beside), block(s, n)]
    loads = []
    for k in range(4):
        send(k, given[k], far.at[k], to_core)
        loads.append(pltpu.make_async_copy(kept[k], mine.at[k], local_sems.at[k]))
        loads[k].start()
    for q in range(2):
        for copy in columns_in(q):
            copy.start()

    def grads(q):
        slot = q % 2
        for copy in columns_in(q):
            copy.wait()
        if q >= 2:
            terms_out(q - 2).wait()
        gateup = product(xs[slot], dgu_ref[...], 0, 0).astype(jnp.bfloat16)
        outs[slot, :, :, :split] = gateup.reshape(far_size, weight_rows, split)
        down = product(ds[slot], act_ref[...], 0, 0).astype(jnp.bfloat16)
        outs[slot, :, :, split:] = down.reshape(far_size, weight_rows, columns - split)
        terms_out(q).start()
        if q < 2:
            for copy in columns_in(q + 2):
                copy.start()

    for k in range(3):
        loads[k].wait()
        copies[k].wait_recv()
        add_rows(mine.at[k], mine.at[k], far.at[k])
        if k == 0:
            send("hx", part(mine.at[0], 0), hop_x, to_x)
            send("hy", part(mine.at[0], 1), hop_y, to_y)
        elif k == 1:
            send("y1", part(mine.at[1], 1), part(last_y, 1), to_y)
        else:
            send("x0", part(mine.at[2], 0), part(last_x, 0), to_x)
    grads(0)
    grads(1)
    copies["hx"].wait_recv()
    add_rows(part(mine.at[1], 0), part(mine.at[1], 0), hop_x)
    send("y0", part(mine.at[1], 0), part(last_y, 0), to_y)
    copies["hy"].wait_recv()
    add_rows(part(mine.at[2], 1), part(mine.at[2], 1), hop_y)
    send("x1", part(mine.at[2], 1), part(last_x, 1), to_x)
    loads[3].wait()
    copies[3].wait_recv()
    add_rows(dhidden_ref, mine.at[3], far.at[3])
    grads(2)
    grads(3)
    for key in ("y1", "x0", "y0", "x1"):
        copies[key].wait_recv()
    step = 16

    def backward(i, carry):
        at = pl.ds(pl.multiple_of(i * step, step), step)
        dx = dhidden_ref[at, :] + last_x[at, :].astype(jnp.float32) + last_y[at, :].astype(jnp.float32)
        unit, scale = rms_normalize(hidden_ref[at, :])
        dhidden = cotangent_ref[at, :] + norm_backward(dx, unit, scale)
        dhidden_ref[at, :] = dhidden
        low_ref[at, :] = dhidden.astype(low_ref.dtype)
        return carry

    lax.fori_loop(0, rows // step, backward, 0)
    for q in (2, 3):
        terms_out(q).wait()
    for copy in copies.values():
        copy.wait_send()


def feed_back(hidden, cotangent, dgu, act, x, d, p, far, collective_id):
    rows, width = hidden.shape
    tokens, columns = x.shape[0], dgu.shape[1] + act.shape[1]
    weight_rows = width // (4 * far)
    low = jnp.bfloat16
    block = pltpu.VMEM((rows, width), low)
    half_block = pltpu.VMEM((rows // 2, width), low)
    return pl.pallas_call(
        feed_back_kernel,
        out_shape=[
            jax.ShapeDtypeStruct((far, 4, weight_rows, columns), low),
            jax.ShapeDtypeStruct((rows, width), jnp.float32),
            jax.ShapeDtypeStruct((rows, width), low),
        ],
        in_specs=[IN_VMEM] * 4 + [ANYWHERE] * 3,
        out_specs=[ANYWHERE, IN_VMEM, IN_VMEM],
        scratch_shapes=[
            pltpu.VMEM((4, rows, width), low),
            pltpu.VMEM((4, rows, width), low),
            half_block,
            half_block,
            block,
            block,
            pltpu.VMEM((2, tokens, width // 4), low),
            pltpu.VMEM((2, tokens, width // 4), low),
            pltpu.VMEM((2, far, weight_rows, columns), low),
            pltpu.SemaphoreType.DMA((4,)),
            pltpu.SemaphoreType.DMA((2, 2)),
            pltpu.SemaphoreType.DMA((2,)),
            pltpu.SemaphoreType.DMA((10,)),
            pltpu.SemaphoreType.DMA((10,)),
        ],
        compiler_params=pltpu.CompilerParams(
            collective_id=collective_id, has_side_effects=True, vmem_limit_bytes=VMEM_LIMIT
        ),
        cost_estimate=pl.CostEstimate(
            flops=2 * tokens * width * columns, bytes_accessed=60_000_000, transcendentals=0
        ),
    )(hidden, cotangent, dgu, act, x, d, p)


def rotary_tables(positions, width):
    half = width // 2
    freqs = jnp.exp(-(jnp.arange(half, dtype=jnp.float32) * 2.0 / width) * math.log(ROPE_BASE))
    angles = positions.astype(jnp.float32)[:, None] * freqs
    return jnp.concatenate([jnp.cos(angles), jnp.sin(angles)], -1)


def rms_normalize(value_rows):
    inverse_scale = lax.rsqrt(jnp.mean(value_rows * value_rows, -1, keepdims=True) + NORM_EPSILON)
    return (value_rows * inverse_scale, inverse_scale)


def norm_backward(unit_gradient, unit_input, inverse_scale):
    return inverse_scale * (
        unit_gradient - unit_input * jnp.mean(unit_gradient * unit_input, -1, keepdims=True)
    )


def adam_step(weight, grad, first, second, rate, decay):
    first_new = BETA_ONE * first + (1.0 - BETA_ONE) * grad
    second_new = BETA_TWO * second + (1.0 - BETA_TWO) * grad * grad
    corr_one = 1.0 - BETA_ONE**STEP
    corr_two = 1.0 - BETA_TWO**STEP
    update = (first_new * (1.0 / corr_one)) / (jnp.sqrt(second_new * (1.0 / corr_two)) + ADAM_EPSILON)
    return (weight - rate * (update + decay * weight), first_new, second_new)


def feed_pieces(part):
    gateup, down = [], []
    for half in range(2):
        for device in range(8):
            start = (half * 8 + device) * part
            gateup.append((half, device, 0, start))
            gateup.append((half, device, part, FEED_UNITS + start))
            down.append((half, device, 2 * part, start))
    return gateup, down


def head_pieces_of(columns):
    key = columns // 6
    query = 2 * key
    qkv, out = [], []
    for device in range(4):
        qkv.append((device, 0, device * query, query))
        qkv.append((device, query, 4 * query + device * key, key))
        qkv.append((device, query + key, 4 * (query + key) + device * key, key))
        out.append((device, query + 2 * key, device * query, query))
    return qkv, out


def norm_kernel(zero_ref, one_ref, gateup_ref, gains_ref, square_ref, terms_ref):
    halves = (zero_ref, one_ref)
    part = zero_ref.shape[2] // 3
    gateup, down = feed_pieces(part)
    two = gains_ref[...].astype(jnp.bfloat16).astype(jnp.float32)[:, 1:2]

    def over(x):
        return jnp.sum(x, 1, keepdims=True)

    two_squares = two_terms = down_squares = 0.0
    for half, device, at, column in gateup:
        grad = halves[half][device, :, at : at + part].astype(jnp.float32)
        weight = gateup_ref[:, column : column + part].astype(jnp.bfloat16).astype(jnp.float32)
        two_squares = two_squares + grad * grad
        two_terms = two_terms + grad * weight
    for half, device, at, column in down:
        grad = halves[half][device, :, at : at + part].astype(jnp.float32)
        down_squares = down_squares + grad * grad
    two_terms = over(two_terms)
    terms_ref[...] = two_terms
    total = jnp.sum(two * two * over(two_squares) + over(down_squares) + two_terms * two_terms)

    @pl.when(pl.program_id(0) == 0)
    def _():
        square_ref[0, 0] = total

    @pl.when(pl.program_id(0) > 0)
    def _():
        square_ref[0, 0] = square_ref[0, 0] + total


ROWS = 16


def rows_of(array):
    if array.ndim == 3:
        return pl.BlockSpec((array.shape[0], ROWS, array.shape[2]), lambda r: (0, r, 0))
    return pl.BlockSpec((ROWS, array.shape[1]), lambda r: (r, 0))


def feed_norm(zero, one, gateup, gains):
    arrays = (zero, one, gateup, gains)
    rows = gains.shape[0]
    terms = jax.ShapeDtypeStruct((rows, 1), jnp.float32)
    return pl.pallas_call(
        norm_kernel,
        grid=(rows // ROWS,),
        out_shape=[jax.ShapeDtypeStruct((1, 1), jnp.float32), terms],
        in_specs=[rows_of(x) for x in arrays],
        out_specs=[pl.BlockSpec(memory_space=pltpu.SMEM), rows_of(terms)],
        compiler_params=pltpu.CompilerParams(vmem_limit_bytes=VMEM_LIMIT),
        cost_estimate=pl.CostEstimate(flops=0, bytes_accessed=10_000_000, transcendentals=0),
    )(*arrays)


def settle_kernel(
    square_ref,
    terms_ref,
    qkv_ref,
    gains_ref,
    p_ref,
    head_ref,
    norm_ref,
    gain_grads_ref,
    mine,
    plane_parts,
    far_parts,
    local_sem,
    send_sems,
    recv_sems,
    far_send_sems,
    far_recv_sems,
):
    s, n, core, across, beside = places()
    diagonal = (core + 2) % 4
    f = lax.axis_index("far")
    far_size = far_parts.shape[0]
    seqs = ({"seq": diagonal}, {"seq": across}, {"seq": core})
    fars = [{"far": (f + k) % far_size} for k in range(1, far_size)]
    plane = [
        {"seq": seq, "near": near} for near in (beside, n) for seq in (diagonal, across, core, s)
    ][:-1]
    meet(*plane, *fars)
    copies, send = sender(send_sems, recv_sems)
    for k, seq in enumerate((diagonal, across, core)):
        send(("w", k), p_ref.at[seq], mine.at[s], seqs[k])
    keep = pltpu.make_async_copy(p_ref.at[s], mine.at[s], local_sem)
    keep.start()
    gains = gains_ref[...].astype(jnp.bfloat16).astype(jnp.float32)
    qkv, out = head_pieces_of(head_ref.shape[2])
    keep.wait()
    for k in range(3):
        copies["w", k].wait_recv()

    def over(x):
        return jnp.sum(x, 1, keepdims=True)

    one_squares = one_terms = out_squares = 0.0
    for device, at, column, size in qkv:
        grad = mine[device, :, at : at + size].astype(jnp.float32)
        weight = qkv_ref[:, column : column + size].astype(jnp.bfloat16).astype(jnp.float32)
        one_squares = one_squares + over(grad * grad)
        one_terms = one_terms + over(grad * weight)
    for device, at, column, size in out:
        grad = mine[device, :, at : at + size].astype(jnp.float32)
        out_squares = out_squares + over(grad * grad)
    one = gains[:, 0:1]
    rows = one * one * one_squares + out_squares + one_terms * one_terms
    gain_grads_ref[:, 0:1] = one_terms
    gain_grads_ref[:, 1:2] = terms_ref[...]
    total = jnp.sum(rows) + square_ref[0, 0]

    plane_parts[s, n] = jnp.full(plane_parts.shape[2:], total, jnp.float32)
    for k, device in enumerate(plane):
        send(("s", k), plane_parts.at[s, n], plane_parts.at[s, n], device)
    head_ref[...] = mine[...]
    for k in range(7):
        copies["s", k].wait_recv()
    everywhere = 0.0
    for seq in range(4):
        everywhere = everywhere + (plane_parts[seq, 0] + plane_parts[seq, 1])
    far_parts[f] = everywhere
    far_copies = [
        pltpu.make_async_remote_copy(
            src_ref=far_parts.at[f],
            dst_ref=far_parts.at[f],
            send_sem=far_send_sems.at[k],
            recv_sem=far_recv_sems.at[k],
            device_id=far,
            device_id_type=MESH_IDS,
        )
        for k, far in enumerate(fars)
    ]
    for copy in far_copies:
        copy.start()
    for copy in far_copies:
        copy.wait_recv()
    everywhere = far_parts[0]
    for k in range(1, far_size):
        everywhere = everywhere + far_parts[k]
    norm_ref[...] = jnp.sqrt(everywhere)
    for copy in (*copies.values(), *far_copies):
        copy.wait_send()


def settle(square, terms, qkv, gains, p, collective_id):
    far = lax.axis_size("far")
    tile = (8, 128)
    return pl.pallas_call(
        settle_kernel,
        out_shape=[
            jax.ShapeDtypeStruct(p.shape, p.dtype),
            jax.ShapeDtypeStruct(tile, jnp.float32),
            jax.ShapeDtypeStruct(gains.shape, jnp.float32),
        ],
        in_specs=[pl.BlockSpec(memory_space=pltpu.SMEM)] + [IN_VMEM] * 3 + [ANYWHERE],
        out_specs=[IN_VMEM] * 3,
        scratch_shapes=[
            pltpu.VMEM(p.shape, p.dtype),
            pltpu.VMEM((4, 2, *tile), jnp.float32),
            pltpu.VMEM((far, *tile), jnp.float32),
            pltpu.SemaphoreType.DMA,
            pltpu.SemaphoreType.DMA((10,)),
            pltpu.SemaphoreType.DMA((10,)),
            pltpu.SemaphoreType.DMA((far - 1,)),
            pltpu.SemaphoreType.DMA((far - 1,)),
        ],
        compiler_params=pltpu.CompilerParams(
            collective_id=collective_id, has_side_effects=True, vmem_limit_bytes=VMEM_LIMIT
        ),
    )(square, terms, qkv, gains, p)


def prepare_kernel(
    gains_ref,
    qkv_ref,
    out_ref,
    gateup_ref,
    down_ref,
    x_ref,
    d_ref,
    first_ref,
    second_ref,
    heads_ref,
    unit_ref,
    low_ref,
    gateup,
    down,
    qkv,
    out,
    x,
    d,
    first,
    second,
    heads,
    unit,
    low,
    load_sems,
    store_sems,
    send_sems,
    recv_sems,
):
    s, n, core, across, beside = places()
    mine = s * 2 + n
    others = [(seq, near) for near in (beside, n) for seq in ((core + 2) % 4, across, core, s)][:-1]
    rows = out.shape[0]
    part = first.shape[2] // 3
    units = 8 * part
    half = jnp.bfloat16

    def load(at, source, target):
        copy = pltpu.make_async_copy(source, target, load_sems.at[at])
        copy.start()
        return copy

    loads = []
    for c in range(2):
        for u in range(2):
            columns = pl.ds((2 * u + c) * units, units)
            loads.append(load(3 * c + u, gateup_ref.at[:, columns], gateup.at[:, columns]))
        columns = pl.ds(c * units, units)
        loads.append(load(3 * c + 2, down_ref.at[:, columns], down.at[:, columns]))
    loads.append(load(6, qkv_ref, qkv))
    loads.append(load(7, out_ref, out))
    loads.append(load(8, x_ref, x))
    loads.append(load(9, d_ref, d))
    gains = gains_ref[...].astype(half).astype(jnp.float32)
    one, two = gains[:, 0:1], gains[:, 1:2]

    def rounded(weight, gain=None):
        weight = weight.astype(half)
        return weight if gain is None else (weight.astype(jnp.float32) * gain).astype(half)

    def pieces(c, target):
        for copy in loads[3 * c : 3 * c + 3]:
            copy.wait()
        for p in range(8):
            start = c * units + p * part
            for u in range(2):
                at = slice(2 * u * units + start, 2 * u * units + start + part)
                target[p, :, u * part : (u + 1) * part] = rounded(gateup[:, at], two)
            target[p, :, 2 * part :] = rounded(down[:, start : start + part])

    def store(at, source, target):
        copy = pltpu.make_async_copy(source, target, store_sems.at[at])
        copy.start()
        return copy

    meet(*[{"seq": seq, "near": near} for seq, near in others])
    pieces(0, first)
    copies, send = sender(send_sems, recv_sems)
    for k, (seq, near) in enumerate(others):
        send(k, first.at[seq * 2 + near], first_ref.at[mine], {"seq": seq, "near": near})
    stores = [store(0, first.at[mine], first_ref.at[mine])]

    pieces(1, second)
    stores.append(store(1, second, second_ref))
    loads[6].wait()
    loads[7].wait()
    qkv_pieces, out_pieces = head_pieces_of(heads.shape[2])
    for p, at, column, size in qkv_pieces:
        heads[p, :, at : at + size] = rounded(qkv[:, column : column + size], one)
    for p, at, column, size in out_pieces:
        heads[p, :, at : at + size] = rounded(out[:, column : column + size])
    stores.append(store(2, heads, heads_ref))
    loads[8].wait()
    loads[9].wait()

    def tokens(i, carry):
        at = pl.ds(pl.multiple_of(i * 16, 16), 16)
        unit[at, :] = rms_normalize(x[at, :])[0].astype(half)
        low[at, :] = d[at, :].astype(half)
        return carry

    lax.fori_loop(0, x.shape[0] // 16, tokens, 0)
    stores.append(store(3, unit, unit_ref))
    stores.append(store(4, low, low_ref))
    for copy in stores:
        copy.wait()
    for copy in copies.values():
        copy.wait_recv()
    for copy in copies.values():
        copy.wait_send()


def prepare(gains, qkv, out, gateup, down, x, d, collective_id):
    rows = gains.shape[0]
    tokens, width = x.shape
    low = jnp.bfloat16
    part = FEED_UNITS // 16
    columns = (qkv.shape[1] + out.shape[1]) // 4
    f32 = [(gateup.shape, jnp.float32), (down.shape, jnp.float32), (qkv.shape, jnp.float32), (out.shape, jnp.float32)]
    f32 += [(x.shape, jnp.float32), (d.shape, jnp.float32)]
    results = [((8, rows, 3 * part), low)] * 2 + [((4, rows, columns), low)] + [((tokens, width), low)] * 2
    return pl.pallas_call(
        prepare_kernel,
        out_shape=[jax.ShapeDtypeStruct(*result) for result in results],
        in_specs=[IN_VMEM] + [ANYWHERE] * 6,
        out_specs=[ANYWHERE] * 5,
        scratch_shapes=[pltpu.VMEM(*array) for array in f32 + results]
        + [
            pltpu.SemaphoreType.DMA((10,)),
            pltpu.SemaphoreType.DMA((5,)),
            pltpu.SemaphoreType.DMA((7,)),
            pltpu.SemaphoreType.DMA((7,)),
        ],
        compiler_params=pltpu.CompilerParams(
            collective_id=collective_id, has_side_effects=True, vmem_limit_bytes=VMEM_LIMIT
        ),
    )(gains, qkv, out, gateup, down, x, d)


def adam_kernel(norm_ref, gains_ref, zero_ref, one_ref, head_ref, *refs):
    weights, firsts, seconds = refs[0:4], refs[4:8], refs[8:12]
    weights_out, firsts_out, seconds_out = refs[12:16], refs[16:20], refs[20:24]
    halves = (zero_ref, one_ref)
    part = zero_ref.shape[2] // 3
    gateup, down = feed_pieces(part)
    qkv, out = head_pieces_of(head_ref.shape[2])
    clip = CLIP_NORM / jnp.maximum(norm_ref[0:1, 0:1], CLIP_NORM)
    gains = gains_ref[...].astype(jnp.bfloat16).astype(jnp.float32) * clip
    one, two = gains[:, 0:1], gains[:, 1:2]

    def step(which, columns, grad, rate, decay):
        new = adam_step(
            weights[which][:, columns], grad, firsts[which][:, columns], seconds[which][:, columns], rate, decay
        )
        weights_out[which][:, columns] = new[0]
        firsts_out[which][:, columns] = new[1]
        seconds_out[which][:, columns] = new[2]

    for pieces, which, scale, rate in ((qkv, 0, one, RATE_MATRIX), (out, 1, clip, RATE_OUTPUT)):
        for device, at, column, size in pieces:
            grad = head_ref[device, :, at : at + size].astype(jnp.float32) * scale
            step(which, slice(column, column + size), grad, rate, DECAY_MATRIX)
    for pieces, which, scale in ((gateup, 2, two), (down, 3, clip)):
        for half, device, at, column in pieces:
            grad = halves[half][device, :, at : at + part].astype(jnp.float32) * scale
            step(which, slice(column, column + part), grad, RATE_MATRIX, DECAY_MATRIX)


def adam(norm, gains, zero, one, head, weights, firsts, seconds):
    state = (*weights, *firsts, *seconds)
    arrays = (gains, zero, one, head, *state)
    return pl.pallas_call(
        adam_kernel,
        grid=(gains.shape[0] // ROWS,),
        out_shape=[jax.ShapeDtypeStruct(x.shape, x.dtype) for x in state],
        in_specs=[pl.BlockSpec(norm.shape, lambda r: (0, 0))] + [rows_of(x) for x in arrays],
        out_specs=[rows_of(x) for x in state],
        compiler_params=pltpu.CompilerParams(vmem_limit_bytes=VMEM_LIMIT),
    )(norm, *arrays)


def product(left, right, left_dim, right_dim):
    return lax.dot_general(
        left, right, (((left_dim,), (right_dim,)), ((), ())), preferred_element_type=jnp.float32
    )


def shards(
    inputs,
    cotangent,
    lengths,
    positions,
    query_key_value_weight,
    out_weight,
    gateup_weight,
    down_weight,
    norm_gains,
    query_key_value_moment,
    output_weight_moment,
    gate_up_moment,
    down_weight_moment,
    norm_gains_moment,
    query_key_value_variance,
    out_second,
    gateup_second,
    down_second,
    gains_second,
):
    width = inputs.shape[2]
    seq = lax.axis_size("seq")
    far = lax.axis_size("far")
    group = seq * 2
    rows = out_weight.shape[0]
    units = FEED_UNITS // group
    part = units // 2

    inputs = inputs[0]
    cotangent = cotangent[0]

    def after(x, *others):
        return lax.optimization_barrier((x, *others))[0]

    by_far = (far, seq, 2 * rows, 3 * part)

    turns = rotary_tables(positions.reshape(-1), HEAD_SIZE)
    piece, second_pieces, head_pieces, unit_one, dout_here = prepare(
        norm_gains, query_key_value_weight, out_weight, gateup_weight, down_weight, inputs, cotangent, 1
    )
    feed_zero = lax.all_gather(piece.reshape(group * rows, -1), "far", axis=0, tiled=True)
    feed_zero = feed_zero.reshape(by_far)

    head_w, normed_one, all_turns, dout, piece = gather_heads(
        head_pieces, unit_one, turns, dout_here, second_pieces, 2
    )
    feed_one = lax.all_gather(piece.reshape(group * rows, -1), "far", axis=0, tiled=True)
    feed_one = feed_one.reshape(by_far)

    all_turns = all_turns.reshape(-1, HEAD_SIZE)
    *saved, hidden, unit_two = attention(lengths, normed_one, head_w, all_turns, inputs, 3)
    normed_two, act, dgateup, *sums = feed_first(unit_two, dout, feed_zero, 4)
    terms = feed_grads(normed_two, dout, dgateup, act, far).reshape(width, 3 * part)
    grads_zero = lax.psum_scatter(terms, "far", scatter_dimension=0, tiled=True)
    act, dgateup, output_terms, dnormed_two = feed_second(
        normed_two, dout, *sums, after(feed_one, terms)
    )
    terms, dhidden, dattended = feed_back(
        hidden, cotangent, dgateup, act, normed_two, dout, dnormed_two, far, 5
    )
    terms = terms.reshape(width, 3 * part)
    grads_one = lax.psum_scatter(after(terms, grads_zero), "far", scatter_dimension=0, tiled=True)

    head_terms, dnormed_one, output_terms = attention_back(
        lengths, saved, all_turns, dattended, output_terms, head_w, normed_one, 6
    )
    head_terms = after(head_terms, grads_zero, grads_one)
    head_terms = lax.psum_scatter(
        head_terms.reshape(far * seq * rows, -1), "far", scatter_dimension=0, tiled=True
    )
    input_grad = dhidden + norm_backward(dnormed_one, *rms_normalize(inputs))
    layer_output = hidden + output_terms

    halves = [x.reshape(group, rows, 3 * part) for x in exchange_plane([grads_zero, grads_one], 7)]
    square, gain_terms = feed_norm(*halves, gateup_weight, norm_gains)
    head_terms = after(head_terms, square, input_grad, layer_output)
    head_grads, norm, gain_grads = settle(
        square, gain_terms, query_key_value_weight, norm_gains, head_terms.reshape(seq, rows, -1), 8
    )
    weights = (query_key_value_weight, out_weight, gateup_weight, down_weight)
    firsts = (query_key_value_moment, output_weight_moment, gate_up_moment, down_weight_moment)
    seconds = (query_key_value_variance, out_second, gateup_second, down_second)
    stepped = adam(norm, norm_gains, *halves, head_grads, weights, firsts, seconds)
    grad_norm = norm[0, 0]
    gain_grads = gain_grads * (CLIP_NORM / jnp.maximum(grad_norm, CLIP_NORM))
    gains = adam_step(norm_gains, gain_grads, norm_gains_moment, gains_second, RATE_GAIN, 0.0)
    state = [x for k in range(3) for x in (*stepped[4 * k : 4 * k + 4], gains[k])]
    return (layer_output[None], input_grad[None], grad_norm, *state)


def solution(mesh):
    seq, fsdp = mesh.shape["seq"], mesh.shape["fsdp"]
    cut = Mesh(mesh.devices.reshape(seq, fsdp // 2, 2), EVERY)
    tokens = P(("far", "near"), "seq", None)
    matrix = P(EVERY, None)
    return jax.shard_map(
        shards,
        mesh=cut,
        in_specs=(tokens, tokens, P(("far", "near")), P(("far", "near"), "seq")) + (matrix,) * 15,
        out_specs=(tokens, tokens, P()) + (matrix,) * 15,
        check_vma=False,
    )
```

```python
import functools
import math

import jax
import jax.numpy as jnp
from jax import lax
from jax.experimental import pallas as pl
from jax.experimental.pallas import tpu as pltpu
from jax.sharding import Mesh, PartitionSpec as P

QUERY_HEAD_COUNT = 8
KEY_VALUE_HEADS = 4
HEAD_SIZE = 256
FEED_UNITS = 8192
STEP = 10

NORM_EPSILON = 1e-06
ROPE_BASE = 1000042.0
MASKED_SCORE = -1000000000.0
CLIP_NORM = 1.0
BETA_ONE = 0.9
BETA_TWO = 0.95
ADAM_EPSILON = 1e-08
DECAY_MATRIX = 0.1
RATE_MATRIX = 0.02
RATE_OUTPUT = 0.1
RATE_GAIN = 1.0

EVERY = ("seq", "far", "near")


MESH_IDS = pl.DeviceIdType.MESH
ANYWHERE = pl.BlockSpec(memory_space=pl.ANY)
IN_VMEM = pl.BlockSpec(memory_space=pltpu.VMEM)
VMEM_LIMIT = 60 * 1024 * 1024


def places():
    s, n = lax.axis_index("seq"), lax.axis_index("near")
    return s, n, s + 1 - 2 * (s % 2), (s + 2) % 4, 1 - n


def meet(*others):
    barrier = pltpu.get_barrier_semaphore()
    for other in others:
        pl.semaphore_signal(barrier, inc=1, device_id=other, device_id_type=MESH_IDS)
    pl.semaphore_wait(barrier, len(others))


def sender(send_sems, recv_sems):
    copies = {}

    def send(key, source, target, device):
        at = len(copies)
        copies[key] = pltpu.make_async_remote_copy(
            src_ref=source,
            dst_ref=target,
            send_sem=send_sems.at[at],
            recv_sem=recv_sems.at[at],
            device_id=device,
            device_id_type=MESH_IDS,
        )
        copies[key].start()

    return copies, send


def add_rows(target, first, second, third=None, step=64):
    rows = target.shape[0]

    def body(i, carry):
        at = pl.ds(pl.multiple_of(i * step, step), step)
        total = first[at, :].astype(jnp.float32) + second[at, :].astype(jnp.float32)
        if third is not None:
            total = total + third[at, :].astype(jnp.float32)
        target[at, :] = total.astype(target.dtype)
        return carry

    lax.fori_loop(0, rows // step, body, 0)


def exchange_plane_kernel(count, *refs):
    x_refs, o_refs = refs[:count], refs[count : 2 * count]
    local_sems, send_sems, recv_sems = refs[2 * count :]
    s, n, core, across, beside = places()
    diagonal = (core + 2) % 4
    mine = s * 2 + n
    others = [(seq, near) for near in (beside, n) for seq in (diagonal, across, core, s)][:-1]

    meet(*[{"seq": seq, "near": near} for seq, near in others])
    copies, send = sender(send_sems, recv_sems)
    locals_ = []
    for k, (x_ref, o_ref) in enumerate(zip(x_refs, o_refs)):
        rows = x_ref.shape[0] // 8

        def at(p):
            return pl.ds(p * rows, rows)

        for seq, near in others:
            target = {"seq": seq, "near": near}
            send(len(copies), x_ref.at[at(seq * 2 + near)], o_ref.at[at(mine)], target)
        locals_.append(pltpu.make_async_copy(x_ref.at[at(mine)], o_ref.at[at(mine)], local_sems.at[k]))
        locals_[k].start()
    for copy in copies.values():
        copy.wait_recv()
    for copy in copies.values():
        copy.wait_send()
    for copy in locals_:
        copy.wait()


def exchange_plane(arrays, collective_id):
    count = len(arrays)
    return pl.pallas_call(
        functools.partial(exchange_plane_kernel, count),
        out_shape=[jax.ShapeDtypeStruct(x.shape, x.dtype) for x in arrays],
        in_specs=[ANYWHERE] * count,
        out_specs=[ANYWHERE] * count,
        scratch_shapes=[
            pltpu.SemaphoreType.DMA((count,)),
            pltpu.SemaphoreType.DMA((7 * count,)),
            pltpu.SemaphoreType.DMA((7 * count,)),
        ],
        compiler_params=pltpu.CompilerParams(collective_id=collective_id, has_side_effects=True),
    )(*arrays)


def groups_of(w_ref, far_size, base, send_sems, recv_sems):
    _, n, _, _, beside = places()
    f = lax.axis_index("far")
    right, left = {"far": (f + 1) % far_size}, {"far": (f + far_size - 1) % far_size}
    to_x = {"near": beside}

    def along(far, p, device, sem):
        piece = w_ref.at[p, far, n]
        return pltpu.make_async_remote_copy(
            src_ref=piece,
            dst_ref=piece,
            send_sem=send_sems.at[base + 4 * sem + p],
            recv_sem=recv_sems.at[base + 4 * sem + p],
            device_id=device,
            device_id_type=MESH_IDS,
        )

    def to_right(k, p):
        return along((f + far_size - k) % far_size, p, right, k)

    def to_left(k, p):
        return along((f + k) % far_size, p, left, far_size + k)

    def x_from_left(k, p):
        return along((f + far_size - k) % far_size, p, to_x, 2 * far_size + k)

    def x_from_right(k, p):
        return along((f + k) % far_size, p, to_x, 3 * far_size + k)

    return to_right, to_left, x_from_left, x_from_right


NEAR_STEPS = 2


def gather_tokens_kernel(
    far_size,
    w_ref,
    x_ref,
    i_ref,
    d_ref,
    e_ref,
    o_ref,
    ox_ref,
    oi_ref,
    od_ref,
    oe_ref,
    local_sems,
    send_sems,
    recv_sems,
):
    s, n, core, across, beside = places()
    f = lax.axis_index("far")
    half = x_ref.shape[0] // 2
    to_core, to_y, to_x = {"seq": core}, {"seq": across}, {"near": beside}
    others = [(seq, near) for near in (beside, n) for seq in ((core + 2) % 4, across, core, s)][:-1]

    meet(*[{"seq": seq, "near": near} for seq, near in others])
    copies, send = sender(send_sems, recv_sems)

    def local(source, target, at):
        copy = pltpu.make_async_copy(source, target, local_sems.at[at])
        copy.start()
        return copy

    _, _, x_from_left, x_from_right = groups_of(o_ref, far_size, 30, send_sems, recv_sems)
    for k in range(NEAR_STEPS, far_size):
        for p in range(4):

            @pl.when(f >= k)
            def _():
                x_from_left(k, p).start()

            @pl.when(f + k < far_size)
            def _():
                x_from_right(k, p).start()

    keeps = [
        local(x_ref, ox_ref.at[s], 0),
        local(i_ref, oi_ref.at[s], 1),
        local(d_ref, od_ref.at[s * 2 + n], 2),
        local(e_ref.at[s * 2 + n], oe_ref.at[s * 2 + n], 3),
    ]
    for p in range(2):
        at = pl.ds(p * half, half)
        send(("y", p), x_ref.at[at], ox_ref.at[s, at], to_y)
        send(("c", p), x_ref.at[at], ox_ref.at[s, at], to_core)
    for k, seq in enumerate(((core + 2) % 4, across, core)):
        send(("i", k), i_ref, oi_ref.at[s], {"seq": seq})

    def block(seq, near, p):
        return od_ref.at[seq * 2 + near, pl.ds(p * half, half)]

    def own(p):
        return d_ref.at[pl.ds(p * half, half)]

    send("y0", own(0), block(s, n, 0), to_y)
    send("x1", own(1), block(s, n, 1), to_x)
    send("y1", own(1), block(s, n, 1), to_y)
    send("x0", own(0), block(s, n, 0), to_x)
    send("c0", own(0), block(s, n, 0), to_core)
    send("c1", own(1), block(s, n, 1), to_core)
    for k, (seq, near) in enumerate(others):
        send(("e", k), e_ref.at[seq * 2 + near], oe_ref.at[s * 2 + n], {"seq": seq, "near": near})
    for p in range(2):
        at = pl.ds(p * half, half)
        copies["y", p].wait_recv()
        send(("yc", p), ox_ref.at[across, at], ox_ref.at[across, at], to_core)
    copies["y0"].wait_recv()
    send("yx", block(across, n, 0), block(across, n, 0), to_x)
    send("yc0", block(across, n, 0), block(across, n, 0), to_core)
    copies["x1"].wait_recv()
    send("xy", block(s, beside, 1), block(s, beside, 1), to_y)
    send("xc1", block(s, beside, 1), block(s, beside, 1), to_core)
    copies["y1"].wait_recv()
    send("yc1", block(across, n, 1), block(across, n, 1), to_core)
    copies["x0"].wait_recv()
    send("xc0", block(s, beside, 0), block(s, beside, 0), to_core)
    copies["yx"].wait_recv()
    send("dc0", block(across, beside, 0), block(across, beside, 0), to_core)
    copies["xy"].wait_recv()
    send("dc1", block(across, beside, 1), block(across, beside, 1), to_core)
    for key in ("c0", "c1", "yc0", "yc1", "xc0", "xc1", "dc0", "dc1"):
        copies[key].wait_recv()
    for p in range(2):
        copies["c", p].wait_recv()
        copies["yc", p].wait_recv()
    for k in range(3):
        copies["i", k].wait_recv()
    for k in range(7):
        copies["e", k].wait_recv()
    for k in range(NEAR_STEPS, far_size):
        for p in range(4):

            @pl.when(f >= k)
            def _():
                x_from_left(k, p).wait_recv()
                x_from_left(k, p).wait_send()

            @pl.when(f + k < far_size)
            def _():
                x_from_right(k, p).wait_recv()
                x_from_right(k, p).wait_send()

    for copy in copies.values():
        copy.wait_send()
    for copy in keeps:
        copy.wait()


def gather_tokens(w, x, i, d, e, collective_id):
    far_size = w.shape[1]
    results = [w.shape, (4, *x.shape), (4, *i.shape), (8, *d.shape), e.shape]
    arrays = (w, x, i, d, e)
    sems = 30 + 16 * far_size
    all_w, all_x, all_i, all_d, mine_e = pl.pallas_call(
        functools.partial(gather_tokens_kernel, far_size),
        out_shape=[jax.ShapeDtypeStruct(shape, a.dtype) for shape, a in zip(results, arrays)],
        in_specs=[ANYWHERE] * 5,
        out_specs=[ANYWHERE] * 5,
        input_output_aliases={0: 0},
        scratch_shapes=[
            pltpu.SemaphoreType.DMA((4,)),
            pltpu.SemaphoreType.DMA((sems,)),
            pltpu.SemaphoreType.DMA((sems,)),
        ],
        compiler_params=pltpu.CompilerParams(collective_id=collective_id, has_side_effects=True),
    )(*arrays)
    all_x, all_d = all_x.reshape(-1, x.shape[1]), all_d.reshape(-1, d.shape[1])
    return all_w.reshape(-1, w.shape[-1]), all_x, all_i, all_d, mine_e


def tile_at(tile, rows):
    return pl.ds(pl.multiple_of(tile * rows, rows), rows)


def stacked(pair):
    half = pair.shape[1] // 2
    return jnp.concatenate([pair[:, :half], pair[:, half:]], 0)


def turned(value, cos, sin):
    half = value.shape[1] // 2
    first, second = value[:, :half], value[:, half:]
    return first * cos - second * sin, second * cos + first * sin


def visible_keys(tile, rows, keys, length):
    shape = (2 * rows, keys)
    row = lax.broadcasted_iota(jnp.int32, shape, 0)
    row = jnp.where(row >= rows, row - rows, row) + tile * rows
    column = lax.broadcasted_iota(jnp.int32, shape, 1)
    return (column <= row) & (column < length)


def attention_kernel(
    length_ref,
    x_ref,
    w_ref,
    turn_ref,
    input_ref,
    q_ref,
    k_ref,
    v_ref,
    heads_ref,
    lse_ref,
    hidden_ref,
    unit_ref,
    terms,
    far,
    last,
    send_sems,
    recv_sems,
):
    s, _, core, across, _ = places()
    to_core, to_y = {"seq": core}, {"seq": across}
    rows = x_ref.shape[0] // 4
    half = rows // 2
    size = k_ref.shape[1]
    low = jnp.bfloat16
    length = length_ref[0]
    order = [(core + 2) % 4, across, core, s]

    def rotated(ref, at, column, value, scale):
        cos, sin = turn_ref[at, : size // 2], turn_ref[at, size // 2 :]
        first, second = turned(value, cos, sin)
        ref[at, column : column + size // 2] = (first * scale).astype(low)
        ref[at, column + size // 2 : column + size] = (second * scale).astype(low)

    def keys_of(tile, carry):
        at = tile_at(tile, rows)
        merged = product(x_ref[at, :], w_ref[:, 2 * size : 4 * size], 1, 0)
        rotated(k_ref, at, 0, merged[:, :size], 1.0)
        v_ref[at, :] = merged[:, size:].astype(low)
        return carry

    def part(ref, p):
        return ref.at[pl.ds(p * half, half)]

    meet(to_core, to_y)
    lax.fori_loop(0, 4, keys_of, 0)

    def attend(tile):
        at = pl.ds(tile * rows, rows)
        keys = (tile + 1) * rows
        scores = product(stacked(q_ref[at, :]), k_ref[:keys, :], 1, 1)
        scores = jnp.where(visible_keys(tile, rows, keys, length), scores, MASKED_SCORE)
        peak = jnp.max(scores, 1, keepdims=True)
        expo = jnp.exp(scores - peak)
        total = jnp.sum(expo, 1, keepdims=True)
        result = product((expo * (1.0 / total)).astype(low), v_ref[:keys, :], 1, 0)
        live = lax.broadcasted_iota(jnp.int32, (rows, 1), 0) + tile * rows < length
        lse = peak + jnp.log(total)
        for head in range(2):
            mine = slice(head * rows, (head + 1) * rows)
            heads_ref[at, head * size : (head + 1) * size] = jnp.where(live, result[mine], 0.0).astype(low)
            lse_ref[at, head : head + 1] = lse[mine]

    plan = [
        (terms.at[0], far.at[0], to_core),
        (terms.at[2], far.at[1], to_core),
        (part(terms.at[1], 0), part(last, 0), to_y),
        (part(terms.at[1], 1), part(last, 1), to_y),
    ]

    def copy_of(k):
        source, target, device = plan[k]
        return pltpu.make_async_remote_copy(
            src_ref=source,
            dst_ref=target,
            send_sem=send_sems.at[k],
            recv_sem=recv_sems.at[k],
            device_id=device,
            device_id_type=MESH_IDS,
        )

    def tile_step(step, carry):
        tile = order[0]
        for k in range(1, 4):
            tile = jnp.where(step == k, order[k], tile)
        at = tile_at(tile, rows)
        merged = product(x_ref[at, :], w_ref[:, : 2 * size], 1, 0)
        for head in range(2):
            rotated(q_ref, at, head * size, merged[:, head * size : (head + 1) * size], size**-0.5)
        for k in range(4):

            @pl.when(tile == k)
            def _():
                attend(k)

        terms[step] = product(heads_ref[at, :], w_ref[:, 4 * size :], 1, 1).astype(low)

        @pl.when(step == 0)
        def _():
            copy_of(0).start()

        @pl.when(step == 1)
        def _():
            copy_of(0).wait_recv()
            for p in range(2):
                add_rows(part(terms.at[1], p), part(terms.at[1], p), part(far.at[0], p))
                copy_of(2 + p).start()

        @pl.when(step == 2)
        def _():
            copy_of(1).start()

        return carry

    lax.fori_loop(0, 4, tile_step, 0)
    copy_of(1).wait_recv()
    add_rows(hidden_ref, terms.at[3], far.at[1])

    def finish(i, carry):
        at = pl.ds(pl.multiple_of(i * 16, 16), 16)
        hidden = input_ref[at, :] + (hidden_ref[at, :] + last[at, :].astype(jnp.float32))
        hidden_ref[at, :] = hidden
        unit_ref[at, :] = rms_normalize(hidden)[0].astype(low)
        return carry

    for p in range(2):
        copy_of(2 + p).wait_recv()
        lax.fori_loop(p * half // 16, (p + 1) * half // 16, finish, 0)
    for k in range(4):
        copy_of(k).wait_send()


def attention(length, x, w, turns, inputs, collective_id):
    tokens, width = x.shape
    size = w.shape[1] // 6
    rows = tokens // 4
    low = jnp.bfloat16
    results = [((tokens, 2 * size), low), ((tokens, size), low), ((tokens, size), low), ((tokens, 2 * size), low)]
    results += [((tokens, 128), jnp.float32), ((rows, width), jnp.float32), ((rows, width), low)]
    return pl.pallas_call(
        attention_kernel,
        out_shape=[jax.ShapeDtypeStruct(*result) for result in results],
        in_specs=[pl.BlockSpec(memory_space=pltpu.SMEM)] + [IN_VMEM] * 4,
        out_specs=[IN_VMEM] * 7,
        scratch_shapes=[
            pltpu.VMEM((4, rows, width), low),
            pltpu.VMEM((2, rows, width), low),
            pltpu.VMEM((rows, width), low),
            pltpu.SemaphoreType.DMA((4,)),
            pltpu.SemaphoreType.DMA((4,)),
        ],
        compiler_params=pltpu.CompilerParams(
            collective_id=collective_id, has_side_effects=True, vmem_limit_bytes=VMEM_LIMIT
        ),
        cost_estimate=pl.CostEstimate(flops=10_000_000_000, bytes_accessed=20_000_000, transcendentals=0),
    )(length, x, w, turns, inputs)


def attention_back_kernel(
    length_ref,
    q_ref,
    k_ref,
    v_ref,
    heads_ref,
    lse_ref,
    turn_ref,
    g_ref,
    y_ref,
    w_ref,
    x_ref,
    terms_ref,
    dx_ref,
    sum_ref,
    weights,
    tokens,
    dheads,
    dfused,
    dk,
    dv,
    mine,
    far,
    hop_x,
    hop_y,
    last_x,
    last_y,
    far_d,
    last_d,
    out_grad,
    qkv_grad,
    out_there,
    qkv_there,
    local_sems,
    send_sems,
    recv_sems,
):
    s, n, core, across, beside = places()
    other = (core + 2) % 4
    to_core, to_y, to_x = {"seq": core}, {"seq": across}, {"near": beside}
    rows = g_ref.shape[0]
    half = rows // 2
    size = k_ref.shape[1]
    low = jnp.bfloat16
    length = length_ref[0]
    far_size = terms_ref.shape[0]

    def local(source, target, at):
        copy = pltpu.make_async_copy(source, target, local_sems.at[at])
        copy.start()
        return copy

    def part(ref, p):
        return ref.at[pl.ds(p * half, half)]

    def token_rows(seq, p):
        return tokens.at[pl.ds(seq * rows + p * half, half)]

    def block(seq, near):
        return y_ref.at[pl.ds((seq * 2 + near) * rows, rows)]

    meet(to_core, to_y, to_x)
    copies, send = sender(send_sems, recv_sems)
    keep = local(g_ref, tokens.at[pl.ds(s * rows, rows)], 0)
    for p in range(2):
        send(("gy", p), part(g_ref, p), token_rows(s, p), to_y)
    for p in range(2):
        send(("gc", p), part(g_ref, p), token_rows(s, p), to_core)
    given = [block(other, beside), block(other, n), block(core, beside), block(core, n)]
    kept = [block(across, beside), block(across, n), block(s, beside), block(s, n)]
    loads = []
    for k in range(4):
        send(k, given[k], far.at[k], to_core)
        loads.append(local(kept[k], mine.at[k], 1 + k))
    load_w = local(w_ref, weights, 5)
    for k in range(3):
        loads[k].wait()
        copies[k].wait_recv()
        add_rows(mine.at[k], mine.at[k], far.at[k])
        if k == 0:
            send("hx", part(mine.at[0], 0), hop_x, to_x)
    send("x0", part(mine.at[2], 0), part(last_x, 0), to_x)
    for p in range(2):
        copies["gy", p].wait_recv()
        send(("gyc", p), token_rows(across, p), token_rows(across, p), to_core)
    send("hy", part(mine.at[0], 1), hop_y, to_y)
    send("y1", part(mine.at[1], 1), part(last_y, 1), to_y)
    loads[3].wait()
    copies[3].wait_recv()
    add_rows(sum_ref, mine.at[3], far.at[3])
    keep.wait()
    load_w.wait()
    for p in range(2):
        copies["gc", p].wait_recv()
        copies["gyc", p].wait_recv()

    def dheads_of(tile, carry):
        at = tile_at(tile, rows)
        live = lax.broadcasted_iota(jnp.int32, (rows, 1), 0) + tile * rows < length
        value = product(tokens[at, :], weights[:, 4 * size :], 1, 0)
        dheads[at, :] = jnp.where(live, value, 0.0).astype(low)
        return carry

    def by_rows(value):
        return value.astype(low).reshape(far_size, 2, -1, value.shape[1])

    width = tokens.shape[1]
    quarter = width // 4
    for q in range(4):
        out_grad[q] = by_rows(product(tokens[:, q * quarter : (q + 1) * quarter], heads_ref[...], 0, 0))
    send("out", out_grad.at[:, :, beside], out_there, to_x)
    lax.fori_loop(0, 4, dheads_of, 0)
    for copy in ("gyc", "gy", "gc"):
        for p in range(2):
            copies[copy, p].wait_send()
    load_x = local(x_ref, tokens, 0)
    copies["hx"].wait_recv()
    add_rows(part(mine.at[1], 0), part(mine.at[1], 0), hop_x)
    send("y0", part(mine.at[1], 0), part(last_y, 0), to_y)
    copies["hy"].wait_recv()
    add_rows(part(mine.at[2], 1), part(mine.at[2], 1), hop_y)
    send("x1", part(mine.at[2], 1), part(last_x, 1), to_x)

    dk[...] = jnp.zeros_like(dk)
    dv[...] = jnp.zeros_like(dv)
    for tile in range(4):
        at = pl.ds(tile * rows, rows)
        keys = (tile + 1) * rows
        query = stacked(q_ref[at, :])
        dhead = stacked(dheads[at, :])
        scores = product(query, k_ref[:keys, :], 1, 1)
        lse = jnp.concatenate([lse_ref[at, 0:1], lse_ref[at, 1:2]], 0)
        probs = jnp.where(visible_keys(tile, rows, keys, length), jnp.exp(scores - lse), 0.0)
        dprobs = product(dhead, v_ref[:keys, :], 1, 1)
        inner = jnp.sum(probs * dprobs, 1, keepdims=True)
        dscores = (probs * (dprobs - inner)).astype(low)
        dv[:keys, :] += product(probs.astype(low), dhead, 0, 0)
        dk[:keys, :] += product(dscores, query, 0, 0)
        dquery = product(dscores, k_ref[:keys, :], 1, 0) * size**-0.5
        cos, sin = turn_ref[at, : size // 2], turn_ref[at, size // 2 :]
        for head in range(2):
            rounded = dquery[head * rows : (head + 1) * rows].astype(low).astype(jnp.float32)
            first, second = turned(rounded, cos, -sin)
            dfused[at, head * size : head * size + size // 2] = first.astype(low)
            dfused[at, head * size + size // 2 : (head + 1) * size] = second.astype(low)
    first, second = turned(
        dk[...].astype(low).astype(jnp.float32), turn_ref[:, : size // 2], -turn_ref[:, size // 2 :]
    )
    dfused[:, 2 * size : 2 * size + size // 2] = first.astype(low)
    dfused[:, 2 * size + size // 2 : 3 * size] = second.astype(low)
    dfused[:, 3 * size :] = dv[...].astype(low)

    load_x.wait()
    for q in range(4):
        qkv_grad[q] = by_rows(product(tokens[:, q * quarter : (q + 1) * quarter], dfused[...], 0, 0))
        send(("qkv", q), qkv_grad.at[q, :, beside], qkv_there.at[q], to_x)

    for p, first, second in ((1, "y1", "x1"), (0, "x0", "y0")):
        copies[first].wait_recv()
        copies[second].wait_recv()
        add_rows(part(sum_ref, p), part(sum_ref, p), part(last_x, p), part(last_y, p))
    for key in ("hx", "hy", "y0", "y1", "x0", "x1"):
        copies[key].wait_send()

    def dx_of(k, tile):
        mine[k] = product(dfused[tile_at(tile, rows), :], weights[:, : 4 * size], 1, 1).astype(low)

    dx_of(0, other)
    send("d0", mine.at[0], far_d.at[0], to_core)
    dx_of(1, core)
    send("d1", mine.at[1], far_d.at[1], to_core)
    dx_of(2, across)
    copies["d0"].wait_recv()
    for p in range(2):
        add_rows(part(mine.at[2], p), part(mine.at[2], p), part(far_d.at[0], p))
        send(("dy", p), part(mine.at[2], p), part(last_d, p), to_y)
    dx_of(3, s)
    copies["d1"].wait_recv()
    add_rows(dx_ref, mine.at[3], far_d.at[1])
    outs = []
    copies["out"].wait_recv()
    for q in range(4):
        for f in range(far_size):
            out_there[q, f] = (
                out_there[q, f].astype(jnp.float32) + out_grad[q, f, n].astype(jnp.float32)
            ).astype(low)
    for p in range(2):
        copies["dy", p].wait_recv()
        add_rows(part(dx_ref, p), part(dx_ref, p), part(last_d, p))
    for q in range(4):
        copies["qkv", q].wait_recv()
        for f in range(far_size):
            qkv_there[q, f] = (
                qkv_there[q, f].astype(jnp.float32) + qkv_grad[q, f, n].astype(jnp.float32)
            ).astype(low)
        outs.append(local(out_there.at[q], terms_ref.at[:, q, :, 4 * size :], q))
        outs.append(local(qkv_there.at[q], terms_ref.at[:, q, :, : 4 * size], 4 + q))
    for copy in outs:
        copy.wait()
    waited = {"hx", "hy", "y0", "y1", "x0", "x1"}
    for key, copy in copies.items():
        if key not in waited and not (isinstance(key, tuple) and key[0] in ("gyc", "gy", "gc")):
            copy.wait_send()


def attention_back(length, saved, turns, g, y, w, x, collective_id):
    q, k, v, heads, lse = saved
    tokens, width = x.shape
    size = k.shape[1]
    rows = tokens // 4
    far_size = lax.axis_size("far")
    weight_rows = width // (8 * far_size)
    low = jnp.bfloat16
    block = pltpu.VMEM((rows, width), low)
    half_block = pltpu.VMEM((rows // 2, width), low)
    return pl.pallas_call(
        attention_back_kernel,
        out_shape=[
            jax.ShapeDtypeStruct((far_size, 4, weight_rows, 6 * size), low),
            jax.ShapeDtypeStruct((rows, width), jnp.float32),
            jax.ShapeDtypeStruct((rows, width), jnp.float32),
        ],
        in_specs=[pl.BlockSpec(memory_space=pltpu.SMEM)] + [IN_VMEM] * 6 + [ANYWHERE] * 4,
        out_specs=[ANYWHERE, IN_VMEM, IN_VMEM],
        scratch_shapes=[
            pltpu.VMEM(w.shape, low),
            pltpu.VMEM((tokens, width), low),
            pltpu.VMEM((tokens, 2 * size), low),
            pltpu.VMEM((tokens, 4 * size), low),
            pltpu.VMEM((tokens, size), jnp.float32),
            pltpu.VMEM((tokens, size), jnp.float32),
            pltpu.VMEM((4, rows, width), low),
            pltpu.VMEM((4, rows, width), low),
            half_block,
            half_block,
            block,
            block,
            pltpu.VMEM((2, rows, width), low),
            block,
            pltpu.VMEM((4, far_size, 2, weight_rows, 2 * size), low),
            pltpu.VMEM((4, far_size, 2, weight_rows, 4 * size), low),
            pltpu.VMEM((4, far_size, weight_rows, 2 * size), low),
            pltpu.VMEM((4, far_size, weight_rows, 4 * size), low),
            pltpu.SemaphoreType.DMA((8,)),
            pltpu.SemaphoreType.DMA((25,)),
            pltpu.SemaphoreType.DMA((25,)),
        ],
        compiler_params=pltpu.CompilerParams(
            collective_id=collective_id, has_side_effects=True, vmem_limit_bytes=VMEM_LIMIT
        ),
        cost_estimate=pl.CostEstimate(flops=20_000_000_000, bytes_accessed=40_000_000, transcendentals=0),
    )(length, q, k, v, heads, lse, turns, g, y, w, x)


def hidden_units(x, d, w, part):
    low = jnp.bfloat16
    gate = product(x, w[:, :part], 1, 0)
    upper = product(x, w[:, part : 2 * part], 1, 0)
    dact = product(d, w[:, 2 * part :], 1, 0)
    sig = 1.0 / (1.0 + jnp.exp(-gate))
    silu = gate * sig
    act = (silu * upper).astype(low)
    dgate = (dact * upper * (sig + silu * (1.0 - sig))).astype(low)
    dupper = (dact * silu).astype(low)
    return act, dgate, dupper


def load_weights(w_ref, weights, sems):
    loads = [
        pltpu.make_async_copy(w_ref.at[f], weights.at[:, f], sems.at[f]) for f in range(w_ref.shape[0])
    ]
    for load in loads:
        load.start()
    return loads


def feed_first_kernel(
    x_ref,
    d_ref,
    w_ref,
    all_ref,
    act_ref,
    dgu_ref,
    y_ref,
    dx_ref,
    weights,
    tokens,
    there,
    acts,
    dgus,
    ys,
    dxs,
    local_sems,
    d_sems,
    out_sems,
    send_sems,
    recv_sems,
):
    s, n, core, across, beside = places()
    other = (core + 2) % 4
    rows = x_ref.shape[0]
    half = rows // 2
    to_core, to_y, to_x = {"seq": core}, {"seq": across}, {"near": beside}
    part = weights.shape[3] // 3
    width = x_ref.shape[1]
    low = jnp.bfloat16

    def block(seq, near, p):
        return tokens.at[seq * 2 + near, pl.ds(p * half, half)]

    def own(p):
        return x_ref.at[pl.ds(p * half, half)]

    order = [
        s * 2 + n,
        core * 2 + n,
        across * 2 + n,
        other * 2 + n,
        s * 2 + beside,
        core * 2 + beside,
        across * 2 + beside,
        other * 2 + beside,
    ]

    def tile_of(step):
        tile = order[0]
        for k in range(1, 8):
            tile = jnp.where(step == k, order[k], tile)
        return tile

    def d_load(step):
        slot = step % 2
        at = tile_at(tile_of(step), rows)
        return pltpu.make_async_copy(d_ref.at[at], there.at[slot], d_sems.at[slot])

    def stores(step):
        slot = step % 2
        tile = tile_of(step)
        at = tile_at(tile, rows)
        pairs = (
            (tokens.at[tile], all_ref),
            (acts.at[slot], act_ref),
            (dgus.at[slot], dgu_ref),
            (ys.at[slot], y_ref),
            (dxs.at[slot], dx_ref),
        )
        return [
            pltpu.make_async_copy(source, target.at[at], out_sems.at[slot, k])
            for k, (source, target) in enumerate(pairs)
        ]

    def piece(seq, near, p, device):
        return block(seq, near, p), block(seq, near, p), device

    plan = {
        "y0": (own(0), block(s, n, 0), to_y),
        "x1": (own(1), block(s, n, 1), to_x),
        "y1": (own(1), block(s, n, 1), to_y),
        "x0": (own(0), block(s, n, 0), to_x),
        "c0": (own(0), block(s, n, 0), to_core),
        "c1": (own(1), block(s, n, 1), to_core),
        "yx": piece(across, n, 0, to_x),
        "yc0": piece(across, n, 0, to_core),
        "xy": piece(s, beside, 1, to_y),
        "xc1": piece(s, beside, 1, to_core),
        "yc1": piece(across, n, 1, to_core),
        "xc0": piece(s, beside, 0, to_core),
        "dc0": piece(across, beside, 0, to_core),
        "dc1": piece(across, beside, 1, to_core),
    }
    places_of = {key: at for at, key in enumerate(plan)}

    def copy_of(key):
        source, target, device = plan[key]
        at = places_of[key]
        return pltpu.make_async_remote_copy(
            src_ref=source,
            dst_ref=target,
            send_sem=send_sems.at[at],
            recv_sem=recv_sems.at[at],
            device_id=device,
            device_id_type=MESH_IDS,
        )

    def send(*keys):
        for key in keys:
            copy_of(key).start()

    def arrive(*keys):
        for key in keys:
            copy_of(key).wait_recv()

    meet(to_core, to_y, to_x)
    keep = pltpu.make_async_copy(x_ref, tokens.at[s * 2 + n], local_sems.at[0])
    keep.start()
    send("y0", "x1", "y1", "x0", "c0", "c1")
    loads = load_weights(w_ref, weights, local_sems.at[pl.ds(1, w_ref.shape[0])])
    d_load(0).start()
    keep.wait()
    for load in loads:
        load.wait()

    def before(step):
        if step == 1:
            arrive("c0", "c1")
        elif step == 2:
            arrive("y0")
            send("yx", "yc0")
            arrive("x1")
            send("xy", "xc1")
            arrive("y1")
            send("yc1")
            arrive("x0")
            send("xc0")
        elif step == 3:
            arrive("yc0", "yc1")
        elif step == 5:
            arrive("xc0", "xc1")
        elif step == 6:
            arrive("yx")
            send("dc0")
            arrive("xy")
            send("dc1")
        elif step == 7:
            arrive("dc0", "dc1")

    def step_of(step, carry):
        for k in (1, 2, 3, 5, 6, 7):

            @pl.when(step == k)
            def _():
                before(k)

        slot = step % 2

        @pl.when(step < 7)
        def _():
            d_load(step + 1).start()

        @pl.when(step >= 2)
        def _():
            for store in stores(step - 2):
                store.wait()

        d_load(step).wait()
        w = weights[...].reshape(width, 3 * part)
        act, dgate, dupper = hidden_units(tokens[tile_of(step)], there[slot], w, part)
        acts[slot] = act
        dgus[slot, :, :part] = dgate
        dgus[slot, :, part:] = dupper
        ys[slot] = product(act, w[:, 2 * part :], 1, 1).astype(low)
        dxs[slot] = product(dgus[slot], w[:, : 2 * part], 1, 1).astype(low)
        for store in stores(step):
            store.start()
        return carry

    lax.fori_loop(0, 8, step_of, 0)
    for step in (6, 7):
        for store in stores(step):
            store.wait()
    for key in plan:
        copy_of(key).wait_send()


def feed_first(x, d, w, collective_id):
    rows, width = x.shape
    part = w.shape[3] // 3
    tokens = 8 * rows
    low = jnp.bfloat16
    far, _, weight_rows, columns = w.shape
    sizes = (width, part, 2 * part, width, width)
    return pl.pallas_call(
        feed_first_kernel,
        out_shape=[jax.ShapeDtypeStruct((tokens, size), low) for size in sizes],
        in_specs=[ANYWHERE] * 3,
        out_specs=[ANYWHERE] * 5,
        scratch_shapes=[
            pltpu.VMEM((4, far, weight_rows, columns), low),
            pltpu.VMEM((8, rows, width), low),
            pltpu.VMEM((2, rows, width), low),
            pltpu.VMEM((2, rows, part), low),
            pltpu.VMEM((2, rows, 2 * part), low),
            pltpu.VMEM((2, rows, width), low),
            pltpu.VMEM((2, rows, width), low),
            pltpu.SemaphoreType.DMA((1 + far,)),
            pltpu.SemaphoreType.DMA((2,)),
            pltpu.SemaphoreType.DMA((2, 5)),
            pltpu.SemaphoreType.DMA((14,)),
            pltpu.SemaphoreType.DMA((14,)),
        ],
        compiler_params=pltpu.CompilerParams(
            collective_id=collective_id, has_side_effects=True, vmem_limit_bytes=VMEM_LIMIT
        ),
        cost_estimate=pl.CostEstimate(
            flops=12 * tokens * width * part, bytes_accessed=60_000_000, transcendentals=0
        ),
    )(x, d, w)


def feed_second_kernel(x_ref, d_ref, y0_ref, dx0_ref, w_ref, act_ref, dgu_ref, y_ref, dx_ref, weights, sems):
    part = weights.shape[3] // 3
    width = x_ref.shape[1]
    low = jnp.bfloat16

    @pl.when(pl.program_id(0) == 0)
    def _():
        for load in load_weights(w_ref, weights, sems):
            load.wait()

    w = weights[...].reshape(width, 3 * part)
    act, dgate, dupper = hidden_units(x_ref[...], d_ref[...], w, part)
    act_ref[...] = act
    dgu_ref[:, :part] = dgate
    dgu_ref[:, part:] = dupper
    y = product(act, w[:, 2 * part :], 1, 1) + y0_ref[...].astype(jnp.float32)
    y_ref[...] = y.astype(low)
    dx = product(dgu_ref[...], w[:, : 2 * part], 1, 1) + dx0_ref[...].astype(jnp.float32)
    dx_ref[...] = dx.astype(low)


def feed_second(x, d, y, dx, w, tile=512):
    tokens, width = x.shape
    part = w.shape[3] // 3
    low = jnp.bfloat16
    far, _, weight_rows, columns = w.shape

    def tokens_of(columns):
        return pl.BlockSpec((tile, columns), lambda t: (t, 0))

    sizes = (part, 2 * part, width, width)
    return pl.pallas_call(
        feed_second_kernel,
        grid=(tokens // tile,),
        out_shape=[jax.ShapeDtypeStruct((tokens, size), low) for size in sizes],
        in_specs=[tokens_of(width)] * 4 + [ANYWHERE],
        out_specs=[tokens_of(size) for size in sizes],
        scratch_shapes=[pltpu.VMEM((4, far, weight_rows, columns), low), pltpu.SemaphoreType.DMA((far,))],
        compiler_params=pltpu.CompilerParams(vmem_limit_bytes=VMEM_LIMIT),
        cost_estimate=pl.CostEstimate(
            flops=12 * tokens * width * part, bytes_accessed=60_000_000, transcendentals=0
        ),
    )(x, d, y, dx, w)


def feed_grads_kernel(x_ref, d_ref, dgu_ref, act_ref, o_ref):
    split = dgu_ref.shape[1]
    far, _, rows, columns = o_ref.shape
    gateup = product(x_ref[...], dgu_ref[...], 0, 0).astype(o_ref.dtype)
    o_ref[:, 0, :, :split] = gateup.reshape(far, rows, split)
    down = product(d_ref[...], act_ref[...], 0, 0).astype(o_ref.dtype)
    o_ref[:, 0, :, split:] = down.reshape(far, rows, columns - split)


def feed_grads(x, d, dgu, act, far):
    tokens, width = x.shape
    columns = dgu.shape[1] + act.shape[1]
    rows = width // (4 * far)
    some = pl.BlockSpec((tokens, width // 4), lambda t: (0, t))

    def whole(array):
        return pl.BlockSpec(array.shape, lambda t: (0, 0), pipeline_mode=pl.Buffered(1))

    return pl.pallas_call(
        feed_grads_kernel,
        grid=(4,),
        out_shape=jax.ShapeDtypeStruct((far, 4, rows, columns), x.dtype),
        in_specs=[some, some, whole(dgu), whole(act)],
        out_specs=pl.BlockSpec((far, 1, rows, columns), lambda t: (0, t, 0, 0)),
        compiler_params=pltpu.CompilerParams(vmem_limit_bytes=VMEM_LIMIT),
        cost_estimate=pl.CostEstimate(
            flops=2 * tokens * width * columns, bytes_accessed=40_000_000, transcendentals=0
        ),
    )(x, d, dgu, act)


def feed_back_kernel(
    hidden_ref,
    cotangent_ref,
    dgu_ref,
    act_ref,
    x_ref,
    d_ref,
    p_ref,
    terms_ref,
    dhidden_ref,
    low_ref,
    mine,
    far,
    hop_x,
    hop_y,
    last_x,
    last_y,
    xs,
    ds,
    outs,
    local_sems,
    x_sems,
    out_sems,
    send_sems,
    recv_sems,
):
    s, n, core, across, beside = places()
    other = (core + 2) % 4
    to_core, to_y, to_x = {"seq": core}, {"seq": across}, {"near": beside}
    rows, width = hidden_ref.shape
    half = rows // 2
    quarter = width // 4
    split = dgu_ref.shape[1]
    far_size, _, weight_rows, columns = terms_ref.shape

    def block(seq, near):
        return p_ref.at[pl.ds((seq * 2 + near) * rows, rows)]

    def part(ref, p):
        return ref.at[pl.ds(p * half, half)]

    def columns_in(q):
        slot = q % 2
        at = pl.ds(q * quarter, quarter)
        return (
            pltpu.make_async_copy(x_ref.at[:, at], xs.at[slot], x_sems.at[slot, 0]),
            pltpu.make_async_copy(d_ref.at[:, at], ds.at[slot], x_sems.at[slot, 1]),
        )

    def terms_out(q):
        return pltpu.make_async_copy(outs.at[q % 2], terms_ref.at[:, q], out_sems.at[q % 2])

    meet(to_core, to_y, to_x)
    copies, send = sender(send_sems, recv_sems)
    given = [block(other, beside), block(other, n), block(core, beside), block(core, n)]
    kept = [block(across, beside), block(across, n), block(s, beside), block(s, n)]
    loads = []
    for k in range(4):
        send(k, given[k], far.at[k], to_core)
        loads.append(pltpu.make_async_copy(kept[k], mine.at[k], local_sems.at[k]))
        loads[k].start()
    for q in range(2):
        for copy in columns_in(q):
            copy.start()

    def grads(q):
        slot = q % 2
        for copy in columns_in(q):
            copy.wait()
        if q >= 2:
            terms_out(q - 2).wait()
        gateup = product(xs[slot], dgu_ref[...], 0, 0).astype(jnp.bfloat16)
        outs[slot, :, :, :split] = gateup.reshape(far_size, weight_rows, split)
        down = product(ds[slot], act_ref[...], 0, 0).astype(jnp.bfloat16)
        outs[slot, :, :, split:] = down.reshape(far_size, weight_rows, columns - split)
        terms_out(q).start()
        if q < 2:
            for copy in columns_in(q + 2):
                copy.start()

    for k in range(3):
        loads[k].wait()
        copies[k].wait_recv()
        add_rows(mine.at[k], mine.at[k], far.at[k])
        if k == 0:
            send("hx", part(mine.at[0], 0), hop_x, to_x)
            send("hy", part(mine.at[0], 1), hop_y, to_y)
        elif k == 1:
            send("y1", part(mine.at[1], 1), part(last_y, 1), to_y)
        else:
            send("x0", part(mine.at[2], 0), part(last_x, 0), to_x)
    grads(0)
    grads(1)
    copies["hx"].wait_recv()
    add_rows(part(mine.at[1], 0), part(mine.at[1], 0), hop_x)
    send("y0", part(mine.at[1], 0), part(last_y, 0), to_y)
    copies["hy"].wait_recv()
    add_rows(part(mine.at[2], 1), part(mine.at[2], 1), hop_y)
    send("x1", part(mine.at[2], 1), part(last_x, 1), to_x)
    loads[3].wait()
    copies[3].wait_recv()
    add_rows(dhidden_ref, mine.at[3], far.at[3])
    grads(2)
    grads(3)
    for key in ("y1", "x0", "y0", "x1"):
        copies[key].wait_recv()
    step = 16

    def backward(i, carry):
        at = pl.ds(pl.multiple_of(i * step, step), step)
        dx = dhidden_ref[at, :] + last_x[at, :].astype(jnp.float32) + last_y[at, :].astype(jnp.float32)
        unit, scale = rms_normalize(hidden_ref[at, :])
        dhidden = cotangent_ref[at, :] + norm_backward(dx, unit, scale)
        dhidden_ref[at, :] = dhidden
        low_ref[at, :] = dhidden.astype(low_ref.dtype)
        return carry

    lax.fori_loop(0, rows // step, backward, 0)
    for q in (2, 3):
        terms_out(q).wait()
    for copy in copies.values():
        copy.wait_send()


def feed_back(hidden, cotangent, dgu, act, x, d, p, far, collective_id):
    rows, width = hidden.shape
    tokens, columns = x.shape[0], dgu.shape[1] + act.shape[1]
    weight_rows = width // (4 * far)
    low = jnp.bfloat16
    block = pltpu.VMEM((rows, width), low)
    half_block = pltpu.VMEM((rows // 2, width), low)
    return pl.pallas_call(
        feed_back_kernel,
        out_shape=[
            jax.ShapeDtypeStruct((far, 4, weight_rows, columns), low),
            jax.ShapeDtypeStruct((rows, width), jnp.float32),
            jax.ShapeDtypeStruct((rows, width), low),
        ],
        in_specs=[IN_VMEM] * 4 + [ANYWHERE] * 3,
        out_specs=[ANYWHERE, IN_VMEM, IN_VMEM],
        scratch_shapes=[
            pltpu.VMEM((4, rows, width), low),
            pltpu.VMEM((4, rows, width), low),
            half_block,
            half_block,
            block,
            block,
            pltpu.VMEM((2, tokens, width // 4), low),
            pltpu.VMEM((2, tokens, width // 4), low),
            pltpu.VMEM((2, far, weight_rows, columns), low),
            pltpu.SemaphoreType.DMA((4,)),
            pltpu.SemaphoreType.DMA((2, 2)),
            pltpu.SemaphoreType.DMA((2,)),
            pltpu.SemaphoreType.DMA((10,)),
            pltpu.SemaphoreType.DMA((10,)),
        ],
        compiler_params=pltpu.CompilerParams(
            collective_id=collective_id, has_side_effects=True, vmem_limit_bytes=VMEM_LIMIT
        ),
        cost_estimate=pl.CostEstimate(
            flops=2 * tokens * width * columns, bytes_accessed=60_000_000, transcendentals=0
        ),
    )(hidden, cotangent, dgu, act, x, d, p)


def rotary_tables(positions, width):
    half = width // 2
    freqs = jnp.exp(-(jnp.arange(half, dtype=jnp.float32) * 2.0 / width) * math.log(ROPE_BASE))
    angles = positions.astype(jnp.float32)[:, None] * freqs
    return jnp.concatenate([jnp.cos(angles), jnp.sin(angles)], -1)


def rms_normalize(value_rows):
    inverse_scale = lax.rsqrt(jnp.mean(value_rows * value_rows, -1, keepdims=True) + NORM_EPSILON)
    return (value_rows * inverse_scale, inverse_scale)


def norm_backward(unit_gradient, unit_input, inverse_scale):
    return inverse_scale * (
        unit_gradient - unit_input * jnp.mean(unit_gradient * unit_input, -1, keepdims=True)
    )


def adam_step(weight, grad, first, second, rate, decay):
    first_new = BETA_ONE * first + (1.0 - BETA_ONE) * grad
    second_new = BETA_TWO * second + (1.0 - BETA_TWO) * grad * grad
    corr_one = 1.0 - BETA_ONE**STEP
    corr_two = 1.0 - BETA_TWO**STEP
    update = (first_new * (1.0 / corr_one)) / (jnp.sqrt(second_new * (1.0 / corr_two)) + ADAM_EPSILON)
    return (weight - rate * (update + decay * weight), first_new, second_new)


def feed_pieces(part):
    gateup, down = [], []
    for half in range(2):
        for device in range(8):
            start = (half * 8 + device) * part
            gateup.append((half, device, 0, start))
            gateup.append((half, device, part, FEED_UNITS + start))
            down.append((half, device, 2 * part, start))
    return gateup, down


def head_pieces_of(columns):
    key = columns // 6
    query = 2 * key
    qkv, out = [], []
    for device in range(4):
        qkv.append((device, 0, device * query, query))
        qkv.append((device, query, 4 * query + device * key, key))
        qkv.append((device, query + key, 4 * (query + key) + device * key, key))
        out.append((device, query + 2 * key, device * query, query))
    return qkv, out


def norm_kernel(zero_ref, one_ref, gateup_ref, gains_ref, square_ref, terms_ref):
    halves = (zero_ref, one_ref)
    part = zero_ref.shape[2] // 3
    gateup, down = feed_pieces(part)
    two = gains_ref[...].astype(jnp.bfloat16).astype(jnp.float32)[:, 1:2]

    def over(x):
        return jnp.sum(x, 1, keepdims=True)

    two_squares = two_terms = down_squares = 0.0
    for half, device, at, column in gateup:
        grad = halves[half][device, :, at : at + part].astype(jnp.float32)
        weight = gateup_ref[:, column : column + part].astype(jnp.bfloat16).astype(jnp.float32)
        two_squares = two_squares + grad * grad
        two_terms = two_terms + grad * weight
    for half, device, at, column in down:
        grad = halves[half][device, :, at : at + part].astype(jnp.float32)
        down_squares = down_squares + grad * grad
    two_terms = over(two_terms)
    terms_ref[...] = two_terms
    total = jnp.sum(two * two * over(two_squares) + over(down_squares) + two_terms * two_terms)

    @pl.when(pl.program_id(0) == 0)
    def _():
        square_ref[0, 0] = total

    @pl.when(pl.program_id(0) > 0)
    def _():
        square_ref[0, 0] = square_ref[0, 0] + total


ROWS = 16


def rows_of(array):
    if array.ndim == 3:
        return pl.BlockSpec((array.shape[0], ROWS, array.shape[2]), lambda r: (0, r, 0))
    return pl.BlockSpec((ROWS, array.shape[1]), lambda r: (r, 0))


def feed_norm(zero, one, gateup, gains):
    arrays = (zero, one, gateup, gains)
    rows = gains.shape[0]
    terms = jax.ShapeDtypeStruct((rows, 1), jnp.float32)
    return pl.pallas_call(
        norm_kernel,
        grid=(rows // ROWS,),
        out_shape=[jax.ShapeDtypeStruct((1, 1), jnp.float32), terms],
        in_specs=[rows_of(x) for x in arrays],
        out_specs=[pl.BlockSpec(memory_space=pltpu.SMEM), rows_of(terms)],
        compiler_params=pltpu.CompilerParams(vmem_limit_bytes=VMEM_LIMIT),
        cost_estimate=pl.CostEstimate(flops=0, bytes_accessed=10_000_000, transcendentals=0),
    )(*arrays)


def settle_kernel(
    square_ref,
    terms_ref,
    qkv_ref,
    gains_ref,
    p_ref,
    head_ref,
    norm_ref,
    gain_grads_ref,
    mine,
    plane_parts,
    far_parts,
    local_sem,
    send_sems,
    recv_sems,
    far_send_sems,
    far_recv_sems,
):
    s, n, core, across, beside = places()
    diagonal = (core + 2) % 4
    f = lax.axis_index("far")
    far_size = far_parts.shape[0]
    seqs = ({"seq": diagonal}, {"seq": across}, {"seq": core})
    fars = [{"far": (f + k) % far_size} for k in range(1, far_size)]
    plane = [
        {"seq": seq, "near": near} for near in (beside, n) for seq in (diagonal, across, core, s)
    ][:-1]
    meet(*plane, *fars)
    copies, send = sender(send_sems, recv_sems)
    for k, seq in enumerate((diagonal, across, core)):
        send(("w", k), p_ref.at[seq], mine.at[s], seqs[k])
    keep = pltpu.make_async_copy(p_ref.at[s], mine.at[s], local_sem)
    keep.start()
    gains = gains_ref[...].astype(jnp.bfloat16).astype(jnp.float32)
    qkv, out = head_pieces_of(head_ref.shape[2])
    keep.wait()
    for k in range(3):
        copies["w", k].wait_recv()

    def over(x):
        return jnp.sum(x, 1, keepdims=True)

    one_squares = one_terms = out_squares = 0.0
    for device, at, column, size in qkv:
        grad = mine[device, :, at : at + size].astype(jnp.float32)
        weight = qkv_ref[:, column : column + size].astype(jnp.bfloat16).astype(jnp.float32)
        one_squares = one_squares + over(grad * grad)
        one_terms = one_terms + over(grad * weight)
    for device, at, column, size in out:
        grad = mine[device, :, at : at + size].astype(jnp.float32)
        out_squares = out_squares + over(grad * grad)
    one = gains[:, 0:1]
    rows = one * one * one_squares + out_squares + one_terms * one_terms
    gain_grads_ref[:, 0:1] = one_terms
    gain_grads_ref[:, 1:2] = terms_ref[...]
    total = jnp.sum(rows) + square_ref[0, 0]

    plane_parts[s, n] = jnp.full(plane_parts.shape[2:], total, jnp.float32)
    for k, device in enumerate(plane):
        send(("s", k), plane_parts.at[s, n], plane_parts.at[s, n], device)
    head_ref[...] = mine[...]
    for k in range(7):
        copies["s", k].wait_recv()
    everywhere = 0.0
    for seq in range(4):
        everywhere = everywhere + (plane_parts[seq, 0] + plane_parts[seq, 1])
    far_parts[f] = everywhere
    far_copies = [
        pltpu.make_async_remote_copy(
            src_ref=far_parts.at[f],
            dst_ref=far_parts.at[f],
            send_sem=far_send_sems.at[k],
            recv_sem=far_recv_sems.at[k],
            device_id=far,
            device_id_type=MESH_IDS,
        )
        for k, far in enumerate(fars)
    ]
    for copy in far_copies:
        copy.start()
    for copy in far_copies:
        copy.wait_recv()
    everywhere = far_parts[0]
    for k in range(1, far_size):
        everywhere = everywhere + far_parts[k]
    norm_ref[...] = jnp.sqrt(everywhere)
    for copy in (*copies.values(), *far_copies):
        copy.wait_send()


def settle(square, terms, qkv, gains, p, collective_id):
    far = lax.axis_size("far")
    tile = (8, 128)
    return pl.pallas_call(
        settle_kernel,
        out_shape=[
            jax.ShapeDtypeStruct(p.shape, p.dtype),
            jax.ShapeDtypeStruct(tile, jnp.float32),
            jax.ShapeDtypeStruct(gains.shape, jnp.float32),
        ],
        in_specs=[pl.BlockSpec(memory_space=pltpu.SMEM)] + [IN_VMEM] * 3 + [ANYWHERE],
        out_specs=[IN_VMEM] * 3,
        scratch_shapes=[
            pltpu.VMEM(p.shape, p.dtype),
            pltpu.VMEM((4, 2, *tile), jnp.float32),
            pltpu.VMEM((far, *tile), jnp.float32),
            pltpu.SemaphoreType.DMA,
            pltpu.SemaphoreType.DMA((10,)),
            pltpu.SemaphoreType.DMA((10,)),
            pltpu.SemaphoreType.DMA((far - 1,)),
            pltpu.SemaphoreType.DMA((far - 1,)),
        ],
        compiler_params=pltpu.CompilerParams(
            collective_id=collective_id, has_side_effects=True, vmem_limit_bytes=VMEM_LIMIT
        ),
    )(square, terms, qkv, gains, p)


def prepare_kernel(
    gains_ref,
    qkv_ref,
    out_ref,
    gateup_ref,
    down_ref,
    x_ref,
    d_ref,
    first_ref,
    second_ref,
    heads_ref,
    unit_ref,
    low_ref,
    gateup,
    down,
    qkv,
    out,
    x,
    d,
    first,
    second,
    heads,
    unit,
    low,
    load_sems,
    store_sems,
    send_sems,
    recv_sems,
):
    s, n, core, across, beside = places()
    f = lax.axis_index("far")
    far_size = heads_ref.shape[1]
    ends = [{"far": (f + 1) % far_size}, {"far": (f + far_size - 1) % far_size}]
    mine = s * 2 + n
    others = [(seq, near) for near in (beside, n) for seq in ((core + 2) % 4, across, core, s)][:-1]
    rows = out.shape[0]
    part = first.shape[2] // 3
    units = 8 * part
    half = jnp.bfloat16

    def load(at, source, target):
        copy = pltpu.make_async_copy(source, target, load_sems.at[at])
        copy.start()
        return copy

    loads = []
    load_heads = [load(6, qkv_ref, qkv), load(7, out_ref, out)]
    for c in range(2):
        for u in range(2):
            columns = pl.ds((2 * u + c) * units, units)
            loads.append(load(3 * c + u, gateup_ref.at[:, columns], gateup.at[:, columns]))
        columns = pl.ds(c * units, units)
        loads.append(load(3 * c + 2, down_ref.at[:, columns], down.at[:, columns]))
    load_tokens = [load(8, x_ref, x), load(9, d_ref, d)]
    gains = gains_ref[...].astype(half).astype(jnp.float32)
    one, two = gains[:, 0:1], gains[:, 1:2]

    def rounded(weight, gain=None):
        weight = weight.astype(half)
        return weight if gain is None else (weight.astype(jnp.float32) * gain).astype(half)

    def pieces(c, target):
        for copy in loads[3 * c : 3 * c + 3]:
            copy.wait()
        for p in range(8):
            start = c * units + p * part
            for u in range(2):
                at = slice(2 * u * units + start, 2 * u * units + start + part)
                target[p, :, u * part : (u + 1) * part] = rounded(gateup[:, at], two)
            target[p, :, 2 * part :] = rounded(down[:, start : start + part])

    def store(at, source, target):
        copy = pltpu.make_async_copy(source, target, store_sems.at[at])
        copy.start()
        return copy

    meet(*[{"seq": seq, "near": near} for seq, near in others], *ends)
    for copy in load_heads:
        copy.wait()
    qkv_pieces, out_pieces = head_pieces_of(heads.shape[2])
    for p, at, column, size in qkv_pieces:
        heads[p, :, at : at + size] = rounded(qkv[:, column : column + size], one)
    for p, at, column, size in out_pieces:
        heads[p, :, at : at + size] = rounded(out[:, column : column + size])
    copies, send = sender(send_sems, recv_sems)
    keep = store(2, heads.at[s], heads_ref.at[s, f, n])
    for seq in (core, across, (core + 2) % 4):
        send(("w", len(copies)), heads.at[seq], heads_ref.at[s, f, n], {"seq": seq})
    to_right, to_left, x_from_left, x_from_right = groups_of(heads_ref, far_size, 10, send_sems, recv_sems)
    order = (s, core, across, (core + 2) % 4)

    def onward(k):
        for at, p in enumerate(order):
            if k == 0 and at == 0:
                keep.wait()
            elif k == 0:
                copies["w", at - 1].wait_recv()
            else:

                @pl.when(f >= k)
                def _():
                    to_right(k - 1, p).wait_recv()

            @pl.when((f >= k) & (f < far_size - 1))
            def _():
                to_right(k, p).start()

            if k > 0:

                @pl.when(f + k < far_size)
                def _():
                    to_left(k - 1, p).wait_recv()

            @pl.when((f + k < far_size) & (f > 0))
            def _():
                to_left(k, p).start()

            if k < NEAR_STEPS:

                @pl.when(f >= k)
                def _():
                    x_from_left(k, p).start()

                if k > 0:

                    @pl.when(f + k < far_size)
                    def _():
                        x_from_right(k, p).start()

    onward(0)
    pieces(0, first)
    for k, (seq, near) in enumerate(others):
        send(k, first.at[seq * 2 + near], first_ref.at[mine], {"seq": seq, "near": near})
    stores = [store(0, first.at[mine], first_ref.at[mine])]
    for k in range(1, min(2, far_size)):
        onward(k)
    pieces(1, second)
    stores.append(store(1, second, second_ref))
    for copy in load_tokens:
        copy.wait()

    def tokens(i, carry):
        at = pl.ds(pl.multiple_of(i * 16, 16), 16)
        unit[at, :] = rms_normalize(x[at, :])[0].astype(half)
        low[at, :] = d[at, :].astype(half)
        return carry

    lax.fori_loop(0, x.shape[0] // 16, tokens, 0)
    stores.append(store(3, unit, unit_ref))
    stores.append(store(4, low, low_ref))
    for k in range(2, far_size):
        onward(k)
    for copy in stores:
        copy.wait()
    for k in range(7):
        copies[k].wait_recv()
    for copy in copies.values():
        copy.wait_send()
    for k in range(far_size):
        for p in range(4):

            @pl.when((f >= k) & (f < far_size - 1))
            def _():
                to_right(k, p).wait_send()

            @pl.when((f + k < far_size) & (f > 0))
            def _():
                to_left(k, p).wait_send()

            if k < NEAR_STEPS:

                @pl.when(f >= k)
                def _():
                    x_from_left(k, p).wait_recv()
                    x_from_left(k, p).wait_send()

                if k > 0:

                    @pl.when(f + k < far_size)
                    def _():
                        x_from_right(k, p).wait_recv()
                        x_from_right(k, p).wait_send()


def prepare(gains, qkv, out, gateup, down, x, d, collective_id):
    rows = gains.shape[0]
    tokens, width = x.shape
    low = jnp.bfloat16
    part = FEED_UNITS // 16
    columns = (qkv.shape[1] + out.shape[1]) // 4
    f32 = [(gateup.shape, jnp.float32), (down.shape, jnp.float32), (qkv.shape, jnp.float32), (out.shape, jnp.float32)]
    f32 += [(x.shape, jnp.float32), (d.shape, jnp.float32)]
    results = [((8, rows, 3 * part), low)] * 2 + [((4, rows, columns), low)] + [((tokens, width), low)] * 2
    far = lax.axis_size("far")
    outs = results[:2] + [((4, far, 2, rows, columns), low)] + results[3:]
    return pl.pallas_call(
        prepare_kernel,
        out_shape=[jax.ShapeDtypeStruct(*result) for result in outs],
        in_specs=[IN_VMEM] + [ANYWHERE] * 6,
        out_specs=[ANYWHERE] * 5,
        scratch_shapes=[pltpu.VMEM(*array) for array in f32 + results]
        + [
            pltpu.SemaphoreType.DMA((10,)),
            pltpu.SemaphoreType.DMA((5,)),
            pltpu.SemaphoreType.DMA((10 + 16 * far,)),
            pltpu.SemaphoreType.DMA((10 + 16 * far,)),
        ],
        compiler_params=pltpu.CompilerParams(
            collective_id=collective_id, has_side_effects=True, vmem_limit_bytes=VMEM_LIMIT
        ),
    )(gains, qkv, out, gateup, down, x, d)


def adam_kernel(norm_ref, gains_ref, zero_ref, one_ref, head_ref, *refs):
    weights, firsts, seconds = refs[0:4], refs[4:8], refs[8:12]
    weights_out, firsts_out, seconds_out = refs[12:16], refs[16:20], refs[20:24]
    halves = (zero_ref, one_ref)
    part = zero_ref.shape[2] // 3
    gateup, down = feed_pieces(part)
    qkv, out = head_pieces_of(head_ref.shape[2])
    clip = CLIP_NORM / jnp.maximum(norm_ref[0:1, 0:1], CLIP_NORM)
    gains = gains_ref[...].astype(jnp.bfloat16).astype(jnp.float32) * clip
    one, two = gains[:, 0:1], gains[:, 1:2]

    def step(which, columns, grad, rate, decay):
        new = adam_step(
            weights[which][:, columns], grad, firsts[which][:, columns], seconds[which][:, columns], rate, decay
        )
        weights_out[which][:, columns] = new[0]
        firsts_out[which][:, columns] = new[1]
        seconds_out[which][:, columns] = new[2]

    for pieces, which, scale, rate in ((qkv, 0, one, RATE_MATRIX), (out, 1, clip, RATE_OUTPUT)):
        for device, at, column, size in pieces:
            grad = head_ref[device, :, at : at + size].astype(jnp.float32) * scale
            step(which, slice(column, column + size), grad, rate, DECAY_MATRIX)
    for pieces, which, scale in ((gateup, 2, two), (down, 3, clip)):
        for half, device, at, column in pieces:
            grad = halves[half][device, :, at : at + part].astype(jnp.float32) * scale
            step(which, slice(column, column + part), grad, RATE_MATRIX, DECAY_MATRIX)


def adam(norm, gains, zero, one, head, weights, firsts, seconds):
    state = (*weights, *firsts, *seconds)
    arrays = (gains, zero, one, head, *state)
    return pl.pallas_call(
        adam_kernel,
        grid=(gains.shape[0] // ROWS,),
        out_shape=[jax.ShapeDtypeStruct(x.shape, x.dtype) for x in state],
        in_specs=[pl.BlockSpec(norm.shape, lambda r: (0, 0))] + [rows_of(x) for x in arrays],
        out_specs=[rows_of(x) for x in state],
        compiler_params=pltpu.CompilerParams(vmem_limit_bytes=VMEM_LIMIT),
    )(norm, *arrays)


def product(left, right, left_dim, right_dim):
    return lax.dot_general(
        left, right, (((left_dim,), (right_dim,)), ((), ())), preferred_element_type=jnp.float32
    )


def shards(
    inputs,
    cotangent,
    lengths,
    positions,
    query_key_value_weight,
    out_weight,
    gateup_weight,
    down_weight,
    norm_gains,
    query_key_value_moment,
    output_weight_moment,
    gate_up_moment,
    down_weight_moment,
    norm_gains_moment,
    query_key_value_variance,
    out_second,
    gateup_second,
    down_second,
    gains_second,
):
    width = inputs.shape[2]
    seq = lax.axis_size("seq")
    far = lax.axis_size("far")
    group = seq * 2
    rows = out_weight.shape[0]
    units = FEED_UNITS // group
    part = units // 2

    inputs = inputs[0]
    cotangent = cotangent[0]

    def after(x, *others):
        return lax.optimization_barrier((x, *others))[0]

    by_far = (far, seq, 2 * rows, 3 * part)

    turns = rotary_tables(positions.reshape(-1), HEAD_SIZE)
    piece, second_pieces, head_w, unit_one, dout_here = prepare(
        norm_gains, query_key_value_weight, out_weight, gateup_weight, down_weight, inputs, cotangent, 1
    )
    feed_zero = lax.all_gather(piece.reshape(group * rows, -1), "far", axis=0, tiled=True)
    feed_zero = feed_zero.reshape(by_far)

    head_w, normed_one, all_turns, dout, piece = gather_tokens(
        head_w, unit_one, turns, dout_here, second_pieces, 2
    )
    feed_one = lax.all_gather(piece.reshape(group * rows, -1), "far", axis=0, tiled=True)
    feed_one = feed_one.reshape(by_far)

    all_turns = all_turns.reshape(-1, HEAD_SIZE)
    *saved, hidden, unit_two = attention(lengths, normed_one, head_w, all_turns, inputs, 3)
    normed_two, act, dgateup, *sums = feed_first(unit_two, dout, feed_zero, 4)
    terms = feed_grads(normed_two, dout, dgateup, act, far).reshape(width, 3 * part)
    grads_zero = lax.psum_scatter(terms, "far", scatter_dimension=0, tiled=True)
    act, dgateup, output_terms, dnormed_two = feed_second(
        normed_two, dout, *sums, after(feed_one, terms)
    )
    terms, dhidden, dattended = feed_back(
        hidden, cotangent, dgateup, act, normed_two, dout, dnormed_two, far, 5
    )
    terms = terms.reshape(width, 3 * part)
    grads_one = lax.psum_scatter(after(terms, grads_zero), "far", scatter_dimension=0, tiled=True)

    head_terms, dnormed_one, output_terms = attention_back(
        lengths, saved, all_turns, dattended, output_terms, head_w, normed_one, 6
    )
    head_terms = after(head_terms, grads_zero, grads_one)
    head_terms = lax.psum_scatter(
        head_terms.reshape(far * seq * rows, -1), "far", scatter_dimension=0, tiled=True
    )
    input_grad = dhidden + norm_backward(dnormed_one, *rms_normalize(inputs))
    layer_output = hidden + output_terms

    halves = [x.reshape(group, rows, 3 * part) for x in exchange_plane([grads_zero, grads_one], 7)]
    square, gain_terms = feed_norm(*halves, gateup_weight, norm_gains)
    head_terms = after(head_terms, square, input_grad, layer_output)
    head_grads, norm, gain_grads = settle(
        square, gain_terms, query_key_value_weight, norm_gains, head_terms.reshape(seq, rows, -1), 8
    )
    weights = (query_key_value_weight, out_weight, gateup_weight, down_weight)
    firsts = (query_key_value_moment, output_weight_moment, gate_up_moment, down_weight_moment)
    seconds = (query_key_value_variance, out_second, gateup_second, down_second)
    stepped = adam(norm, norm_gains, *halves, head_grads, weights, firsts, seconds)
    grad_norm = norm[0, 0]
    gain_grads = gain_grads * (CLIP_NORM / jnp.maximum(grad_norm, CLIP_NORM))
    gains = adam_step(norm_gains, gain_grads, norm_gains_moment, gains_second, RATE_GAIN, 0.0)
    state = [x for k in range(3) for x in (*stepped[4 * k : 4 * k + 4], gains[k])]
    return (layer_output[None], input_grad[None], grad_norm, *state)


def solution(mesh):
    seq, fsdp = mesh.shape["seq"], mesh.shape["fsdp"]
    cut = Mesh(mesh.devices.reshape(seq, fsdp // 2, 2), EVERY)
    tokens = P(("far", "near"), "seq", None)
    matrix = P(EVERY, None)
    return jax.shard_map(
        shards,
        mesh=cut,
        in_specs=(tokens, tokens, P(("far", "near")), P(("far", "near"), "seq")) + (matrix,) * 15,
        out_specs=(tokens, tokens, P()) + (matrix,) * 15,
        check_vma=False,
    )
```

```python
import functools
import math

import jax
import jax.numpy as jnp
from jax import lax
from jax.experimental import pallas as pl
from jax.experimental.pallas import tpu as pltpu
from jax.sharding import Mesh, PartitionSpec as P

QUERY_HEAD_COUNT = 8
KEY_VALUE_HEADS = 4
HEAD_SIZE = 256
FEED_UNITS = 8192
STEP = 10

NORM_EPSILON = 1e-06
ROPE_BASE = 1000042.0
MASKED_SCORE = -1000000000.0
CLIP_NORM = 1.0
BETA_ONE = 0.9
BETA_TWO = 0.95
ADAM_EPSILON = 1e-08
DECAY_MATRIX = 0.1
RATE_MATRIX = 0.02
RATE_OUTPUT = 0.1
RATE_GAIN = 1.0

EVERY = ("seq", "far", "near")


MESH_IDS = pl.DeviceIdType.MESH
ANYWHERE = pl.BlockSpec(memory_space=pl.ANY)
IN_VMEM = pl.BlockSpec(memory_space=pltpu.VMEM)
VMEM_LIMIT = 60 * 1024 * 1024


def places():
    s, n = lax.axis_index("seq"), lax.axis_index("near")
    return s, n, s + 1 - 2 * (s % 2), (s + 2) % 4, 1 - n


def meet(*others):
    barrier = pltpu.get_barrier_semaphore()
    for other in others:
        pl.semaphore_signal(barrier, inc=1, device_id=other, device_id_type=MESH_IDS)
    pl.semaphore_wait(barrier, len(others))


def sender(send_sems, recv_sems):
    copies = {}

    def send(key, source, target, device):
        at = len(copies)
        copies[key] = pltpu.make_async_remote_copy(
            src_ref=source,
            dst_ref=target,
            send_sem=send_sems.at[at],
            recv_sem=recv_sems.at[at],
            device_id=device,
            device_id_type=MESH_IDS,
        )
        copies[key].start()

    return copies, send


def add_rows(target, first, second, third=None, step=64):
    rows = target.shape[0]

    def body(i, carry):
        at = pl.ds(pl.multiple_of(i * step, step), step)
        total = first[at, :].astype(jnp.float32) + second[at, :].astype(jnp.float32)
        if third is not None:
            total = total + third[at, :].astype(jnp.float32)
        target[at, :] = total.astype(target.dtype)
        return carry

    lax.fori_loop(0, rows // step, body, 0)


def exchange_plane_kernel(count, *refs):
    x_refs, o_refs = refs[:count], refs[count : 2 * count]
    local_sems, send_sems, recv_sems = refs[2 * count :]
    s, n, core, across, beside = places()
    diagonal = (core + 2) % 4
    mine = s * 2 + n
    others = [(seq, near) for near in (beside, n) for seq in (diagonal, across, core, s)][:-1]

    meet(*[{"seq": seq, "near": near} for seq, near in others])
    copies, send = sender(send_sems, recv_sems)
    locals_ = []
    for k, (x_ref, o_ref) in enumerate(zip(x_refs, o_refs)):
        rows = x_ref.shape[0] // 8

        def at(p):
            return pl.ds(p * rows, rows)

        for seq, near in others:
            target = {"seq": seq, "near": near}
            send(len(copies), x_ref.at[at(seq * 2 + near)], o_ref.at[at(mine)], target)
        locals_.append(pltpu.make_async_copy(x_ref.at[at(mine)], o_ref.at[at(mine)], local_sems.at[k]))
        locals_[k].start()
    for copy in copies.values():
        copy.wait_recv()
    for copy in copies.values():
        copy.wait_send()
    for copy in locals_:
        copy.wait()


def exchange_plane(arrays, collective_id):
    count = len(arrays)
    return pl.pallas_call(
        functools.partial(exchange_plane_kernel, count),
        out_shape=[jax.ShapeDtypeStruct(x.shape, x.dtype) for x in arrays],
        in_specs=[ANYWHERE] * count,
        out_specs=[ANYWHERE] * count,
        scratch_shapes=[
            pltpu.SemaphoreType.DMA((count,)),
            pltpu.SemaphoreType.DMA((7 * count,)),
            pltpu.SemaphoreType.DMA((7 * count,)),
        ],
        compiler_params=pltpu.CompilerParams(collective_id=collective_id, has_side_effects=True),
    )(*arrays)


def groups_of(w_ref, far_size, base, send_sems, recv_sems):
    _, n, _, _, beside = places()
    f = lax.axis_index("far")
    right, left = {"far": (f + 1) % far_size}, {"far": (f + far_size - 1) % far_size}
    to_x = {"near": beside}

    def along(far, p, device, sem):
        piece = w_ref.at[p, far, n]
        return pltpu.make_async_remote_copy(
            src_ref=piece,
            dst_ref=piece,
            send_sem=send_sems.at[base + 4 * sem + p],
            recv_sem=recv_sems.at[base + 4 * sem + p],
            device_id=device,
            device_id_type=MESH_IDS,
        )

    def to_right(k, p):
        return along((f + far_size - k) % far_size, p, right, k)

    def to_left(k, p):
        return along((f + k) % far_size, p, left, far_size + k)

    def x_from_left(k, p):
        return along((f + far_size - k) % far_size, p, to_x, 2 * far_size + k)

    def x_from_right(k, p):
        return along((f + k) % far_size, p, to_x, 3 * far_size + k)

    return to_right, to_left, x_from_left, x_from_right


FIRST_STEPS = 1


def gather_tokens_kernel(
    far_size,
    w_ref,
    x_ref,
    i_ref,
    d_ref,
    e_ref,
    o_ref,
    ox_ref,
    oi_ref,
    od_ref,
    oe_ref,
    local_sems,
    send_sems,
    recv_sems,
):
    s, n, core, across, beside = places()
    f = lax.axis_index("far")
    half = x_ref.shape[0] // 2
    to_core, to_y, to_x = {"seq": core}, {"seq": across}, {"near": beside}
    others = [(seq, near) for near in (beside, n) for seq in ((core + 2) % 4, across, core, s)][:-1]

    ends = [{"far": (f + 1) % far_size}, {"far": (f + far_size - 1) % far_size}]
    meet(*[{"seq": seq, "near": near} for seq, near in others], *ends)
    copies, send = sender(send_sems, recv_sems)

    def local(source, target, at):
        copy = pltpu.make_async_copy(source, target, local_sems.at[at])
        copy.start()
        return copy

    to_right, to_left, x_from_left, x_from_right = groups_of(o_ref, far_size, 30, send_sems, recv_sems)

    def onward(k):
        for p in range(4):

            @pl.when(f >= k)
            def _():
                if k > FIRST_STEPS:
                    to_right(k - 1, p).wait_recv()
                x_from_left(k, p).start()

            @pl.when((f >= k) & (f < far_size - 1))
            def _():
                to_right(k, p).start()

            @pl.when(f + k < far_size)
            def _():
                if k > FIRST_STEPS:
                    to_left(k - 1, p).wait_recv()
                x_from_right(k, p).start()

            @pl.when((f + k < far_size) & (f > 0))
            def _():
                to_left(k, p).start()

    if FIRST_STEPS < far_size:
        onward(FIRST_STEPS)
    for k in range(FIRST_STEPS):
        for p in range(4):

            @pl.when(f >= k)
            def _():
                x_from_left(k, p).start()

            if k > 0:

                @pl.when(f + k < far_size)
                def _():
                    x_from_right(k, p).start()

    keeps = [
        local(x_ref, ox_ref.at[s], 0),
        local(i_ref, oi_ref.at[s], 1),
        local(d_ref, od_ref.at[s * 2 + n], 2),
        local(e_ref.at[s * 2 + n], oe_ref.at[s * 2 + n], 3),
    ]
    for p in range(2):
        at = pl.ds(p * half, half)
        send(("y", p), x_ref.at[at], ox_ref.at[s, at], to_y)
        send(("c", p), x_ref.at[at], ox_ref.at[s, at], to_core)
    for k, seq in enumerate(((core + 2) % 4, across, core)):
        send(("i", k), i_ref, oi_ref.at[s], {"seq": seq})

    def block(seq, near, p):
        return od_ref.at[seq * 2 + near, pl.ds(p * half, half)]

    def own(p):
        return d_ref.at[pl.ds(p * half, half)]

    send("y0", own(0), block(s, n, 0), to_y)
    send("x1", own(1), block(s, n, 1), to_x)
    send("y1", own(1), block(s, n, 1), to_y)
    send("x0", own(0), block(s, n, 0), to_x)
    send("c0", own(0), block(s, n, 0), to_core)
    send("c1", own(1), block(s, n, 1), to_core)
    for k, (seq, near) in enumerate(others):
        send(("e", k), e_ref.at[seq * 2 + near], oe_ref.at[s * 2 + n], {"seq": seq, "near": near})
    for k in range(FIRST_STEPS + 1, far_size):
        onward(k)
    for p in range(2):
        at = pl.ds(p * half, half)
        copies["y", p].wait_recv()
        send(("yc", p), ox_ref.at[across, at], ox_ref.at[across, at], to_core)
    copies["y0"].wait_recv()
    send("yx", block(across, n, 0), block(across, n, 0), to_x)
    send("yc0", block(across, n, 0), block(across, n, 0), to_core)
    copies["x1"].wait_recv()
    send("xy", block(s, beside, 1), block(s, beside, 1), to_y)
    send("xc1", block(s, beside, 1), block(s, beside, 1), to_core)
    copies["y1"].wait_recv()
    send("yc1", block(across, n, 1), block(across, n, 1), to_core)
    copies["x0"].wait_recv()
    send("xc0", block(s, beside, 0), block(s, beside, 0), to_core)
    copies["yx"].wait_recv()
    send("dc0", block(across, beside, 0), block(across, beside, 0), to_core)
    copies["xy"].wait_recv()
    send("dc1", block(across, beside, 1), block(across, beside, 1), to_core)
    for key in ("c0", "c1", "yc0", "yc1", "xc0", "xc1", "dc0", "dc1"):
        copies[key].wait_recv()
    for p in range(2):
        copies["c", p].wait_recv()
        copies["yc", p].wait_recv()
    for k in range(3):
        copies["i", k].wait_recv()
    for k in range(7):
        copies["e", k].wait_recv()
    for k in range(far_size):
        for p in range(4):
            if k >= FIRST_STEPS:

                @pl.when((f >= k) & (f < far_size - 1))
                def _():
                    to_right(k, p).wait_send()

                @pl.when((f + k < far_size) & (f > 0))
                def _():
                    to_left(k, p).wait_send()

            @pl.when(f >= k)
            def _():
                x_from_left(k, p).wait_recv()
                x_from_left(k, p).wait_send()

            if k > 0:

                @pl.when(f + k < far_size)
                def _():
                    x_from_right(k, p).wait_recv()
                    x_from_right(k, p).wait_send()

    for copy in copies.values():
        copy.wait_send()
    for copy in keeps:
        copy.wait()


def gather_tokens(w, x, i, d, e, collective_id):
    far_size = w.shape[1]
    results = [w.shape, (4, *x.shape), (4, *i.shape), (8, *d.shape), e.shape]
    arrays = (w, x, i, d, e)
    sems = 30 + 16 * far_size
    all_w, all_x, all_i, all_d, mine_e = pl.pallas_call(
        functools.partial(gather_tokens_kernel, far_size),
        out_shape=[jax.ShapeDtypeStruct(shape, a.dtype) for shape, a in zip(results, arrays)],
        in_specs=[ANYWHERE] * 5,
        out_specs=[ANYWHERE] * 5,
        input_output_aliases={0: 0},
        scratch_shapes=[
            pltpu.SemaphoreType.DMA((4,)),
            pltpu.SemaphoreType.DMA((sems,)),
            pltpu.SemaphoreType.DMA((sems,)),
        ],
        compiler_params=pltpu.CompilerParams(collective_id=collective_id, has_side_effects=True),
    )(*arrays)
    all_x, all_d = all_x.reshape(-1, x.shape[1]), all_d.reshape(-1, d.shape[1])
    return all_w.reshape(-1, w.shape[-1]), all_x, all_i, all_d, mine_e


def tile_at(tile, rows):
    return pl.ds(pl.multiple_of(tile * rows, rows), rows)


def stacked(pair):
    half = pair.shape[1] // 2
    return jnp.concatenate([pair[:, :half], pair[:, half:]], 0)


def turned(value, cos, sin):
    half = value.shape[1] // 2
    first, second = value[:, :half], value[:, half:]
    return first * cos - second * sin, second * cos + first * sin


def visible_keys(tile, rows, keys, length):
    shape = (2 * rows, keys)
    row = lax.broadcasted_iota(jnp.int32, shape, 0)
    row = jnp.where(row >= rows, row - rows, row) + tile * rows
    column = lax.broadcasted_iota(jnp.int32, shape, 1)
    return (column <= row) & (column < length)


def attention_kernel(
    length_ref,
    x_ref,
    w_ref,
    turn_ref,
    input_ref,
    q_ref,
    k_ref,
    v_ref,
    heads_ref,
    lse_ref,
    hidden_ref,
    unit_ref,
    terms,
    far,
    last,
    send_sems,
    recv_sems,
):
    s, _, core, across, _ = places()
    to_core, to_y = {"seq": core}, {"seq": across}
    rows = x_ref.shape[0] // 4
    half = rows // 2
    size = k_ref.shape[1]
    low = jnp.bfloat16
    length = length_ref[0]
    order = [(core + 2) % 4, across, core, s]

    def rotated(ref, at, column, value, scale):
        cos, sin = turn_ref[at, : size // 2], turn_ref[at, size // 2 :]
        first, second = turned(value, cos, sin)
        ref[at, column : column + size // 2] = (first * scale).astype(low)
        ref[at, column + size // 2 : column + size] = (second * scale).astype(low)

    def keys_of(tile, carry):
        at = tile_at(tile, rows)
        merged = product(x_ref[at, :], w_ref[:, 2 * size : 4 * size], 1, 0)
        rotated(k_ref, at, 0, merged[:, :size], 1.0)
        v_ref[at, :] = merged[:, size:].astype(low)
        return carry

    def part(ref, p):
        return ref.at[pl.ds(p * half, half)]

    meet(to_core, to_y)
    lax.fori_loop(0, 4, keys_of, 0)

    def attend(tile):
        at = pl.ds(tile * rows, rows)
        keys = (tile + 1) * rows
        scores = product(stacked(q_ref[at, :]), k_ref[:keys, :], 1, 1)
        scores = jnp.where(visible_keys(tile, rows, keys, length), scores, MASKED_SCORE)
        peak = jnp.max(scores, 1, keepdims=True)
        expo = jnp.exp(scores - peak)
        total = jnp.sum(expo, 1, keepdims=True)
        result = product((expo * (1.0 / total)).astype(low), v_ref[:keys, :], 1, 0)
        live = lax.broadcasted_iota(jnp.int32, (rows, 1), 0) + tile * rows < length
        lse = peak + jnp.log(total)
        for head in range(2):
            mine = slice(head * rows, (head + 1) * rows)
            heads_ref[at, head * size : (head + 1) * size] = jnp.where(live, result[mine], 0.0).astype(low)
            lse_ref[at, head : head + 1] = lse[mine]

    plan = [
        (terms.at[0], far.at[0], to_core),
        (terms.at[2], far.at[1], to_core),
        (part(terms.at[1], 0), part(last, 0), to_y),
        (part(terms.at[1], 1), part(last, 1), to_y),
    ]

    def copy_of(k):
        source, target, device = plan[k]
        return pltpu.make_async_remote_copy(
            src_ref=source,
            dst_ref=target,
            send_sem=send_sems.at[k],
            recv_sem=recv_sems.at[k],
            device_id=device,
            device_id_type=MESH_IDS,
        )

    def tile_step(step, carry):
        tile = order[0]
        for k in range(1, 4):
            tile = jnp.where(step == k, order[k], tile)
        at = tile_at(tile, rows)
        merged = product(x_ref[at, :], w_ref[:, : 2 * size], 1, 0)
        for head in range(2):
            rotated(q_ref, at, head * size, merged[:, head * size : (head + 1) * size], size**-0.5)
        for k in range(4):

            @pl.when(tile == k)
            def _():
                attend(k)

        terms[step] = product(heads_ref[at, :], w_ref[:, 4 * size :], 1, 1).astype(low)

        @pl.when(step == 0)
        def _():
            copy_of(0).start()

        @pl.when(step == 1)
        def _():
            copy_of(0).wait_recv()
            for p in range(2):
                add_rows(part(terms.at[1], p), part(terms.at[1], p), part(far.at[0], p))
                copy_of(2 + p).start()

        @pl.when(step == 2)
        def _():
            copy_of(1).start()

        return carry

    lax.fori_loop(0, 4, tile_step, 0)
    copy_of(1).wait_recv()
    add_rows(hidden_ref, terms.at[3], far.at[1])

    def finish(i, carry):
        at = pl.ds(pl.multiple_of(i * 16, 16), 16)
        hidden = input_ref[at, :] + (hidden_ref[at, :] + last[at, :].astype(jnp.float32))
        hidden_ref[at, :] = hidden
        unit_ref[at, :] = rms_normalize(hidden)[0].astype(low)
        return carry

    for p in range(2):
        copy_of(2 + p).wait_recv()
        lax.fori_loop(p * half // 16, (p + 1) * half // 16, finish, 0)
    for k in range(4):
        copy_of(k).wait_send()


def attention(length, x, w, turns, inputs, collective_id):
    tokens, width = x.shape
    size = w.shape[1] // 6
    rows = tokens // 4
    low = jnp.bfloat16
    results = [((tokens, 2 * size), low), ((tokens, size), low), ((tokens, size), low), ((tokens, 2 * size), low)]
    results += [((tokens, 128), jnp.float32), ((rows, width), jnp.float32), ((rows, width), low)]
    return pl.pallas_call(
        attention_kernel,
        out_shape=[jax.ShapeDtypeStruct(*result) for result in results],
        in_specs=[pl.BlockSpec(memory_space=pltpu.SMEM)] + [IN_VMEM] * 4,
        out_specs=[IN_VMEM] * 7,
        scratch_shapes=[
            pltpu.VMEM((4, rows, width), low),
            pltpu.VMEM((2, rows, width), low),
            pltpu.VMEM((rows, width), low),
            pltpu.SemaphoreType.DMA((4,)),
            pltpu.SemaphoreType.DMA((4,)),
        ],
        compiler_params=pltpu.CompilerParams(
            collective_id=collective_id, has_side_effects=True, vmem_limit_bytes=VMEM_LIMIT
        ),
        cost_estimate=pl.CostEstimate(flops=10_000_000_000, bytes_accessed=20_000_000, transcendentals=0),
    )(length, x, w, turns, inputs)


def attention_back_kernel(
    length_ref,
    q_ref,
    k_ref,
    v_ref,
    heads_ref,
    lse_ref,
    turn_ref,
    g_ref,
    y_ref,
    w_ref,
    x_ref,
    terms_ref,
    dx_ref,
    sum_ref,
    weights,
    tokens,
    dheads,
    dfused,
    dk,
    dv,
    mine,
    far,
    hop_x,
    hop_y,
    last_x,
    last_y,
    far_d,
    last_d,
    out_grad,
    qkv_grad,
    out_there,
    qkv_there,
    local_sems,
    send_sems,
    recv_sems,
):
    s, n, core, across, beside = places()
    other = (core + 2) % 4
    to_core, to_y, to_x = {"seq": core}, {"seq": across}, {"near": beside}
    rows = g_ref.shape[0]
    half = rows // 2
    size = k_ref.shape[1]
    low = jnp.bfloat16
    length = length_ref[0]
    far_size = terms_ref.shape[0]

    def local(source, target, at):
        copy = pltpu.make_async_copy(source, target, local_sems.at[at])
        copy.start()
        return copy

    def part(ref, p):
        return ref.at[pl.ds(p * half, half)]

    def token_rows(seq, p):
        return tokens.at[pl.ds(seq * rows + p * half, half)]

    def block(seq, near):
        return y_ref.at[pl.ds((seq * 2 + near) * rows, rows)]

    meet(to_core, to_y, to_x)
    copies, send = sender(send_sems, recv_sems)
    keep = local(g_ref, tokens.at[pl.ds(s * rows, rows)], 0)
    for p in range(2):
        send(("gy", p), part(g_ref, p), token_rows(s, p), to_y)
    for p in range(2):
        send(("gc", p), part(g_ref, p), token_rows(s, p), to_core)
    given = [block(other, beside), block(other, n), block(core, beside), block(core, n)]
    kept = [block(across, beside), block(across, n), block(s, beside), block(s, n)]
    loads = []
    for k in range(4):
        send(k, given[k], far.at[k], to_core)
        loads.append(local(kept[k], mine.at[k], 1 + k))
    load_w = local(w_ref, weights, 5)
    for k in range(3):
        loads[k].wait()
        copies[k].wait_recv()
        add_rows(mine.at[k], mine.at[k], far.at[k])
        if k == 0:
            send("hx", part(mine.at[0], 0), hop_x, to_x)
    send("x0", part(mine.at[2], 0), part(last_x, 0), to_x)
    for p in range(2):
        copies["gy", p].wait_recv()
        send(("gyc", p), token_rows(across, p), token_rows(across, p), to_core)
    send("hy", part(mine.at[0], 1), hop_y, to_y)
    send("y1", part(mine.at[1], 1), part(last_y, 1), to_y)
    loads[3].wait()
    copies[3].wait_recv()
    add_rows(sum_ref, mine.at[3], far.at[3])
    keep.wait()
    load_w.wait()
    for p in range(2):
        copies["gc", p].wait_recv()
        copies["gyc", p].wait_recv()

    def dheads_of(tile, carry):
        at = tile_at(tile, rows)
        live = lax.broadcasted_iota(jnp.int32, (rows, 1), 0) + tile * rows < length
        value = product(tokens[at, :], weights[:, 4 * size :], 1, 0)
        dheads[at, :] = jnp.where(live, value, 0.0).astype(low)
        return carry

    def by_rows(value):
        return value.astype(low).reshape(far_size, 2, -1, value.shape[1])

    width = tokens.shape[1]
    quarter = width // 4
    for q in range(4):
        out_grad[q] = by_rows(product(tokens[:, q * quarter : (q + 1) * quarter], heads_ref[...], 0, 0))
    send("out", out_grad.at[:, :, beside], out_there, to_x)
    lax.fori_loop(0, 4, dheads_of, 0)
    for copy in ("gyc", "gy", "gc"):
        for p in range(2):
            copies[copy, p].wait_send()
    load_x = local(x_ref, tokens, 0)
    copies["hx"].wait_recv()
    add_rows(part(mine.at[1], 0), part(mine.at[1], 0), hop_x)
    send("y0", part(mine.at[1], 0), part(last_y, 0), to_y)
    copies["hy"].wait_recv()
    add_rows(part(mine.at[2], 1), part(mine.at[2], 1), hop_y)
    send("x1", part(mine.at[2], 1), part(last_x, 1), to_x)

    dk[...] = jnp.zeros_like(dk)
    dv[...] = jnp.zeros_like(dv)
    for tile in range(4):
        at = pl.ds(tile * rows, rows)
        keys = (tile + 1) * rows
        query = stacked(q_ref[at, :])
        dhead = stacked(dheads[at, :])
        scores = product(query, k_ref[:keys, :], 1, 1)
        lse = jnp.concatenate([lse_ref[at, 0:1], lse_ref[at, 1:2]], 0)
        probs = jnp.where(visible_keys(tile, rows, keys, length), jnp.exp(scores - lse), 0.0)
        dprobs = product(dhead, v_ref[:keys, :], 1, 1)
        inner = jnp.sum(probs * dprobs, 1, keepdims=True)
        dscores = (probs * (dprobs - inner)).astype(low)
        dv[:keys, :] += product(probs.astype(low), dhead, 0, 0)
        dk[:keys, :] += product(dscores, query, 0, 0)
        dquery = product(dscores, k_ref[:keys, :], 1, 0) * size**-0.5
        cos, sin = turn_ref[at, : size // 2], turn_ref[at, size // 2 :]
        for head in range(2):
            rounded = dquery[head * rows : (head + 1) * rows].astype(low).astype(jnp.float32)
            first, second = turned(rounded, cos, -sin)
            dfused[at, head * size : head * size + size // 2] = first.astype(low)
            dfused[at, head * size + size // 2 : (head + 1) * size] = second.astype(low)
    first, second = turned(
        dk[...].astype(low).astype(jnp.float32), turn_ref[:, : size // 2], -turn_ref[:, size // 2 :]
    )
    dfused[:, 2 * size : 2 * size + size // 2] = first.astype(low)
    dfused[:, 2 * size + size // 2 : 3 * size] = second.astype(low)
    dfused[:, 3 * size :] = dv[...].astype(low)

    load_x.wait()
    for q in range(4):
        qkv_grad[q] = by_rows(product(tokens[:, q * quarter : (q + 1) * quarter], dfused[...], 0, 0))
        send(("qkv", q), qkv_grad.at[q, :, beside], qkv_there.at[q], to_x)

    for p, first, second in ((1, "y1", "x1"), (0, "x0", "y0")):
        copies[first].wait_recv()
        copies[second].wait_recv()
        add_rows(part(sum_ref, p), part(sum_ref, p), part(last_x, p), part(last_y, p))
    for key in ("hx", "hy", "y0", "y1", "x0", "x1"):
        copies[key].wait_send()

    def dx_of(k, tile):
        mine[k] = product(dfused[tile_at(tile, rows), :], weights[:, : 4 * size], 1, 1).astype(low)

    dx_of(0, other)
    send("d0", mine.at[0], far_d.at[0], to_core)
    dx_of(1, core)
    send("d1", mine.at[1], far_d.at[1], to_core)
    dx_of(2, across)
    copies["d0"].wait_recv()
    for p in range(2):
        add_rows(part(mine.at[2], p), part(mine.at[2], p), part(far_d.at[0], p))
        send(("dy", p), part(mine.at[2], p), part(last_d, p), to_y)
    dx_of(3, s)
    copies["d1"].wait_recv()
    add_rows(dx_ref, mine.at[3], far_d.at[1])
    outs = []
    copies["out"].wait_recv()
    for q in range(4):
        for f in range(far_size):
            out_there[q, f] = (
                out_there[q, f].astype(jnp.float32) + out_grad[q, f, n].astype(jnp.float32)
            ).astype(low)
    for p in range(2):
        copies["dy", p].wait_recv()
        add_rows(part(dx_ref, p), part(dx_ref, p), part(last_d, p))
    for q in range(4):
        copies["qkv", q].wait_recv()
        for f in range(far_size):
            qkv_there[q, f] = (
                qkv_there[q, f].astype(jnp.float32) + qkv_grad[q, f, n].astype(jnp.float32)
            ).astype(low)
        outs.append(local(out_there.at[q], terms_ref.at[:, q, :, 4 * size :], q))
        outs.append(local(qkv_there.at[q], terms_ref.at[:, q, :, : 4 * size], 4 + q))
    for copy in outs:
        copy.wait()
    waited = {"hx", "hy", "y0", "y1", "x0", "x1"}
    for key, copy in copies.items():
        if key not in waited and not (isinstance(key, tuple) and key[0] in ("gyc", "gy", "gc")):
            copy.wait_send()


def attention_back(length, saved, turns, g, y, w, x, collective_id):
    q, k, v, heads, lse = saved
    tokens, width = x.shape
    size = k.shape[1]
    rows = tokens // 4
    far_size = lax.axis_size("far")
    weight_rows = width // (8 * far_size)
    low = jnp.bfloat16
    block = pltpu.VMEM((rows, width), low)
    half_block = pltpu.VMEM((rows // 2, width), low)
    return pl.pallas_call(
        attention_back_kernel,
        out_shape=[
            jax.ShapeDtypeStruct((far_size, 4, weight_rows, 6 * size), low),
            jax.ShapeDtypeStruct((rows, width), jnp.float32),
            jax.ShapeDtypeStruct((rows, width), jnp.float32),
        ],
        in_specs=[pl.BlockSpec(memory_space=pltpu.SMEM)] + [IN_VMEM] * 6 + [ANYWHERE] * 4,
        out_specs=[ANYWHERE, IN_VMEM, IN_VMEM],
        scratch_shapes=[
            pltpu.VMEM(w.shape, low),
            pltpu.VMEM((tokens, width), low),
            pltpu.VMEM((tokens, 2 * size), low),
            pltpu.VMEM((tokens, 4 * size), low),
            pltpu.VMEM((tokens, size), jnp.float32),
            pltpu.VMEM((tokens, size), jnp.float32),
            pltpu.VMEM((4, rows, width), low),
            pltpu.VMEM((4, rows, width), low),
            half_block,
            half_block,
            block,
            block,
            pltpu.VMEM((2, rows, width), low),
            block,
            pltpu.VMEM((4, far_size, 2, weight_rows, 2 * size), low),
            pltpu.VMEM((4, far_size, 2, weight_rows, 4 * size), low),
            pltpu.VMEM((4, far_size, weight_rows, 2 * size), low),
            pltpu.VMEM((4, far_size, weight_rows, 4 * size), low),
            pltpu.SemaphoreType.DMA((8,)),
            pltpu.SemaphoreType.DMA((25,)),
            pltpu.SemaphoreType.DMA((25,)),
        ],
        compiler_params=pltpu.CompilerParams(
            collective_id=collective_id, has_side_effects=True, vmem_limit_bytes=VMEM_LIMIT
        ),
        cost_estimate=pl.CostEstimate(flops=20_000_000_000, bytes_accessed=40_000_000, transcendentals=0),
    )(length, q, k, v, heads, lse, turns, g, y, w, x)


def hidden_units(x, d, w, part):
    low = jnp.bfloat16
    gate = product(x, w[:, :part], 1, 0)
    upper = product(x, w[:, part : 2 * part], 1, 0)
    dact = product(d, w[:, 2 * part :], 1, 0)
    sig = 1.0 / (1.0 + jnp.exp(-gate))
    silu = gate * sig
    act = (silu * upper).astype(low)
    dgate = (dact * upper * (sig + silu * (1.0 - sig))).astype(low)
    dupper = (dact * silu).astype(low)
    return act, dgate, dupper


def load_weights(w_ref, weights, sems):
    loads = [
        pltpu.make_async_copy(w_ref.at[f], weights.at[:, f], sems.at[f]) for f in range(w_ref.shape[0])
    ]
    for load in loads:
        load.start()
    return loads


def feed_first_kernel(
    x_ref,
    d_ref,
    w_ref,
    all_ref,
    act_ref,
    dgu_ref,
    y_ref,
    dx_ref,
    weights,
    tokens,
    there,
    acts,
    dgus,
    ys,
    dxs,
    local_sems,
    d_sems,
    out_sems,
    send_sems,
    recv_sems,
):
    s, n, core, across, beside = places()
    other = (core + 2) % 4
    rows = x_ref.shape[0]
    half = rows // 2
    to_core, to_y, to_x = {"seq": core}, {"seq": across}, {"near": beside}
    part = weights.shape[3] // 3
    width = x_ref.shape[1]
    low = jnp.bfloat16

    def block(seq, near, p):
        return tokens.at[seq * 2 + near, pl.ds(p * half, half)]

    def own(p):
        return x_ref.at[pl.ds(p * half, half)]

    order = [
        s * 2 + n,
        core * 2 + n,
        across * 2 + n,
        other * 2 + n,
        s * 2 + beside,
        core * 2 + beside,
        across * 2 + beside,
        other * 2 + beside,
    ]

    def tile_of(step):
        tile = order[0]
        for k in range(1, 8):
            tile = jnp.where(step == k, order[k], tile)
        return tile

    def d_load(step):
        slot = step % 2
        at = tile_at(tile_of(step), rows)
        return pltpu.make_async_copy(d_ref.at[at], there.at[slot], d_sems.at[slot])

    def stores(step):
        slot = step % 2
        tile = tile_of(step)
        at = tile_at(tile, rows)
        pairs = (
            (tokens.at[tile], all_ref),
            (acts.at[slot], act_ref),
            (dgus.at[slot], dgu_ref),
            (ys.at[slot], y_ref),
            (dxs.at[slot], dx_ref),
        )
        return [
            pltpu.make_async_copy(source, target.at[at], out_sems.at[slot, k])
            for k, (source, target) in enumerate(pairs)
        ]

    def piece(seq, near, p, device):
        return block(seq, near, p), block(seq, near, p), device

    plan = {
        "y0": (own(0), block(s, n, 0), to_y),
        "x1": (own(1), block(s, n, 1), to_x),
        "y1": (own(1), block(s, n, 1), to_y),
        "x0": (own(0), block(s, n, 0), to_x),
        "c0": (own(0), block(s, n, 0), to_core),
        "c1": (own(1), block(s, n, 1), to_core),
        "yx": piece(across, n, 0, to_x),
        "yc0": piece(across, n, 0, to_core),
        "xy": piece(s, beside, 1, to_y),
        "xc1": piece(s, beside, 1, to_core),
        "yc1": piece(across, n, 1, to_core),
        "xc0": piece(s, beside, 0, to_core),
        "dc0": piece(across, beside, 0, to_core),
        "dc1": piece(across, beside, 1, to_core),
    }
    places_of = {key: at for at, key in enumerate(plan)}

    def copy_of(key):
        source, target, device = plan[key]
        at = places_of[key]
        return pltpu.make_async_remote_copy(
            src_ref=source,
            dst_ref=target,
            send_sem=send_sems.at[at],
            recv_sem=recv_sems.at[at],
            device_id=device,
            device_id_type=MESH_IDS,
        )

    def send(*keys):
        for key in keys:
            copy_of(key).start()

    def arrive(*keys):
        for key in keys:
            copy_of(key).wait_recv()

    meet(to_core, to_y, to_x)
    keep = pltpu.make_async_copy(x_ref, tokens.at[s * 2 + n], local_sems.at[0])
    keep.start()
    send("y0", "x1", "y1", "x0", "c0", "c1")
    loads = load_weights(w_ref, weights, local_sems.at[pl.ds(1, w_ref.shape[0])])
    d_load(0).start()
    keep.wait()
    for load in loads:
        load.wait()

    def before(step):
        if step == 1:
            arrive("c0", "c1")
        elif step == 2:
            arrive("y0")
            send("yx", "yc0")
            arrive("x1")
            send("xy", "xc1")
            arrive("y1")
            send("yc1")
            arrive("x0")
            send("xc0")
        elif step == 3:
            arrive("yc0", "yc1")
        elif step == 5:
            arrive("xc0", "xc1")
        elif step == 6:
            arrive("yx")
            send("dc0")
            arrive("xy")
            send("dc1")
        elif step == 7:
            arrive("dc0", "dc1")

    def step_of(step, carry):
        for k in (1, 2, 3, 5, 6, 7):

            @pl.when(step == k)
            def _():
                before(k)

        slot = step % 2

        @pl.when(step < 7)
        def _():
            d_load(step + 1).start()

        @pl.when(step >= 2)
        def _():
            for store in stores(step - 2):
                store.wait()

        d_load(step).wait()
        w = weights[...].reshape(width, 3 * part)
        act, dgate, dupper = hidden_units(tokens[tile_of(step)], there[slot], w, part)
        acts[slot] = act
        dgus[slot, :, :part] = dgate
        dgus[slot, :, part:] = dupper
        ys[slot] = product(act, w[:, 2 * part :], 1, 1).astype(low)
        dxs[slot] = product(dgus[slot], w[:, : 2 * part], 1, 1).astype(low)
        for store in stores(step):
            store.start()
        return carry

    lax.fori_loop(0, 8, step_of, 0)
    for step in (6, 7):
        for store in stores(step):
            store.wait()
    for key in plan:
        copy_of(key).wait_send()


def feed_first(x, d, w, collective_id):
    rows, width = x.shape
    part = w.shape[3] // 3
    tokens = 8 * rows
    low = jnp.bfloat16
    far, _, weight_rows, columns = w.shape
    sizes = (width, part, 2 * part, width, width)
    return pl.pallas_call(
        feed_first_kernel,
        out_shape=[jax.ShapeDtypeStruct((tokens, size), low) for size in sizes],
        in_specs=[ANYWHERE] * 3,
        out_specs=[ANYWHERE] * 5,
        scratch_shapes=[
            pltpu.VMEM((4, far, weight_rows, columns), low),
            pltpu.VMEM((8, rows, width), low),
            pltpu.VMEM((2, rows, width), low),
            pltpu.VMEM((2, rows, part), low),
            pltpu.VMEM((2, rows, 2 * part), low),
            pltpu.VMEM((2, rows, width), low),
            pltpu.VMEM((2, rows, width), low),
            pltpu.SemaphoreType.DMA((1 + far,)),
            pltpu.SemaphoreType.DMA((2,)),
            pltpu.SemaphoreType.DMA((2, 5)),
            pltpu.SemaphoreType.DMA((14,)),
            pltpu.SemaphoreType.DMA((14,)),
        ],
        compiler_params=pltpu.CompilerParams(
            collective_id=collective_id, has_side_effects=True, vmem_limit_bytes=VMEM_LIMIT
        ),
        cost_estimate=pl.CostEstimate(
            flops=12 * tokens * width * part, bytes_accessed=60_000_000, transcendentals=0
        ),
    )(x, d, w)


def feed_second_kernel(x_ref, d_ref, y0_ref, dx0_ref, w_ref, act_ref, dgu_ref, y_ref, dx_ref, weights, sems):
    part = weights.shape[3] // 3
    width = x_ref.shape[1]
    low = jnp.bfloat16

    @pl.when(pl.program_id(0) == 0)
    def _():
        for load in load_weights(w_ref, weights, sems):
            load.wait()

    w = weights[...].reshape(width, 3 * part)
    act, dgate, dupper = hidden_units(x_ref[...], d_ref[...], w, part)
    act_ref[...] = act
    dgu_ref[:, :part] = dgate
    dgu_ref[:, part:] = dupper
    y = product(act, w[:, 2 * part :], 1, 1) + y0_ref[...].astype(jnp.float32)
    y_ref[...] = y.astype(low)
    dx = product(dgu_ref[...], w[:, : 2 * part], 1, 1) + dx0_ref[...].astype(jnp.float32)
    dx_ref[...] = dx.astype(low)


def feed_second(x, d, y, dx, w, tile=512):
    tokens, width = x.shape
    part = w.shape[3] // 3
    low = jnp.bfloat16
    far, _, weight_rows, columns = w.shape

    def tokens_of(columns):
        return pl.BlockSpec((tile, columns), lambda t: (t, 0))

    sizes = (part, 2 * part, width, width)
    return pl.pallas_call(
        feed_second_kernel,
        grid=(tokens // tile,),
        out_shape=[jax.ShapeDtypeStruct((tokens, size), low) for size in sizes],
        in_specs=[tokens_of(width)] * 4 + [ANYWHERE],
        out_specs=[tokens_of(size) for size in sizes],
        scratch_shapes=[pltpu.VMEM((4, far, weight_rows, columns), low), pltpu.SemaphoreType.DMA((far,))],
        compiler_params=pltpu.CompilerParams(vmem_limit_bytes=VMEM_LIMIT),
        cost_estimate=pl.CostEstimate(
            flops=12 * tokens * width * part, bytes_accessed=60_000_000, transcendentals=0
        ),
    )(x, d, y, dx, w)


def feed_grads_kernel(x_ref, d_ref, dgu_ref, act_ref, o_ref):
    split = dgu_ref.shape[1]
    far, _, rows, columns = o_ref.shape
    gateup = product(x_ref[...], dgu_ref[...], 0, 0).astype(o_ref.dtype)
    o_ref[:, 0, :, :split] = gateup.reshape(far, rows, split)
    down = product(d_ref[...], act_ref[...], 0, 0).astype(o_ref.dtype)
    o_ref[:, 0, :, split:] = down.reshape(far, rows, columns - split)


def feed_grads(x, d, dgu, act, far):
    tokens, width = x.shape
    columns = dgu.shape[1] + act.shape[1]
    rows = width // (4 * far)
    some = pl.BlockSpec((tokens, width // 4), lambda t: (0, t))

    def whole(array):
        return pl.BlockSpec(array.shape, lambda t: (0, 0), pipeline_mode=pl.Buffered(1))

    return pl.pallas_call(
        feed_grads_kernel,
        grid=(4,),
        out_shape=jax.ShapeDtypeStruct((far, 4, rows, columns), x.dtype),
        in_specs=[some, some, whole(dgu), whole(act)],
        out_specs=pl.BlockSpec((far, 1, rows, columns), lambda t: (0, t, 0, 0)),
        compiler_params=pltpu.CompilerParams(vmem_limit_bytes=VMEM_LIMIT),
        cost_estimate=pl.CostEstimate(
            flops=2 * tokens * width * columns, bytes_accessed=40_000_000, transcendentals=0
        ),
    )(x, d, dgu, act)


def feed_back_kernel(
    hidden_ref,
    cotangent_ref,
    dgu_ref,
    act_ref,
    x_ref,
    d_ref,
    p_ref,
    terms_ref,
    dhidden_ref,
    low_ref,
    mine,
    far,
    hop_x,
    hop_y,
    last_x,
    last_y,
    xs,
    ds,
    outs,
    local_sems,
    x_sems,
    out_sems,
    send_sems,
    recv_sems,
):
    s, n, core, across, beside = places()
    other = (core + 2) % 4
    to_core, to_y, to_x = {"seq": core}, {"seq": across}, {"near": beside}
    rows, width = hidden_ref.shape
    half = rows // 2
    quarter = width // 4
    split = dgu_ref.shape[1]
    far_size, _, weight_rows, columns = terms_ref.shape

    def block(seq, near):
        return p_ref.at[pl.ds((seq * 2 + near) * rows, rows)]

    def part(ref, p):
        return ref.at[pl.ds(p * half, half)]

    def columns_in(q):
        slot = q % 2
        at = pl.ds(q * quarter, quarter)
        return (
            pltpu.make_async_copy(x_ref.at[:, at], xs.at[slot], x_sems.at[slot, 0]),
            pltpu.make_async_copy(d_ref.at[:, at], ds.at[slot], x_sems.at[slot, 1]),
        )

    def terms_out(q):
        return pltpu.make_async_copy(outs.at[q % 2], terms_ref.at[:, q], out_sems.at[q % 2])

    meet(to_core, to_y, to_x)
    copies, send = sender(send_sems, recv_sems)
    given = [block(other, beside), block(other, n), block(core, beside), block(core, n)]
    kept = [block(across, beside), block(across, n), block(s, beside), block(s, n)]
    loads = []
    for k in range(4):
        send(k, given[k], far.at[k], to_core)
        loads.append(pltpu.make_async_copy(kept[k], mine.at[k], local_sems.at[k]))
        loads[k].start()
    for q in range(2):
        for copy in columns_in(q):
            copy.start()

    def grads(q):
        slot = q % 2
        for copy in columns_in(q):
            copy.wait()
        if q >= 2:
            terms_out(q - 2).wait()
        gateup = product(xs[slot], dgu_ref[...], 0, 0).astype(jnp.bfloat16)
        outs[slot, :, :, :split] = gateup.reshape(far_size, weight_rows, split)
        down = product(ds[slot], act_ref[...], 0, 0).astype(jnp.bfloat16)
        outs[slot, :, :, split:] = down.reshape(far_size, weight_rows, columns - split)
        terms_out(q).start()
        if q < 2:
            for copy in columns_in(q + 2):
                copy.start()

    for k in range(3):
        loads[k].wait()
        copies[k].wait_recv()
        add_rows(mine.at[k], mine.at[k], far.at[k])
        if k == 0:
            send("hx", part(mine.at[0], 0), hop_x, to_x)
            send("hy", part(mine.at[0], 1), hop_y, to_y)
        elif k == 1:
            send("y1", part(mine.at[1], 1), part(last_y, 1), to_y)
        else:
            send("x0", part(mine.at[2], 0), part(last_x, 0), to_x)
    grads(0)
    grads(1)
    copies["hx"].wait_recv()
    add_rows(part(mine.at[1], 0), part(mine.at[1], 0), hop_x)
    send("y0", part(mine.at[1], 0), part(last_y, 0), to_y)
    copies["hy"].wait_recv()
    add_rows(part(mine.at[2], 1), part(mine.at[2], 1), hop_y)
    send("x1", part(mine.at[2], 1), part(last_x, 1), to_x)
    loads[3].wait()
    copies[3].wait_recv()
    add_rows(dhidden_ref, mine.at[3], far.at[3])
    grads(2)
    grads(3)
    for key in ("y1", "x0", "y0", "x1"):
        copies[key].wait_recv()
    step = 16

    def backward(i, carry):
        at = pl.ds(pl.multiple_of(i * step, step), step)
        dx = dhidden_ref[at, :] + last_x[at, :].astype(jnp.float32) + last_y[at, :].astype(jnp.float32)
        unit, scale = rms_normalize(hidden_ref[at, :])
        dhidden = cotangent_ref[at, :] + norm_backward(dx, unit, scale)
        dhidden_ref[at, :] = dhidden
        low_ref[at, :] = dhidden.astype(low_ref.dtype)
        return carry

    lax.fori_loop(0, rows // step, backward, 0)
    for q in (2, 3):
        terms_out(q).wait()
    for copy in copies.values():
        copy.wait_send()


def feed_back(hidden, cotangent, dgu, act, x, d, p, far, collective_id):
    rows, width = hidden.shape
    tokens, columns = x.shape[0], dgu.shape[1] + act.shape[1]
    weight_rows = width // (4 * far)
    low = jnp.bfloat16
    block = pltpu.VMEM((rows, width), low)
    half_block = pltpu.VMEM((rows // 2, width), low)
    return pl.pallas_call(
        feed_back_kernel,
        out_shape=[
            jax.ShapeDtypeStruct((far, 4, weight_rows, columns), low),
            jax.ShapeDtypeStruct((rows, width), jnp.float32),
            jax.ShapeDtypeStruct((rows, width), low),
        ],
        in_specs=[IN_VMEM] * 4 + [ANYWHERE] * 3,
        out_specs=[ANYWHERE, IN_VMEM, IN_VMEM],
        scratch_shapes=[
            pltpu.VMEM((4, rows, width), low),
            pltpu.VMEM((4, rows, width), low),
            half_block,
            half_block,
            block,
            block,
            pltpu.VMEM((2, tokens, width // 4), low),
            pltpu.VMEM((2, tokens, width // 4), low),
            pltpu.VMEM((2, far, weight_rows, columns), low),
            pltpu.SemaphoreType.DMA((4,)),
            pltpu.SemaphoreType.DMA((2, 2)),
            pltpu.SemaphoreType.DMA((2,)),
            pltpu.SemaphoreType.DMA((10,)),
            pltpu.SemaphoreType.DMA((10,)),
        ],
        compiler_params=pltpu.CompilerParams(
            collective_id=collective_id, has_side_effects=True, vmem_limit_bytes=VMEM_LIMIT
        ),
        cost_estimate=pl.CostEstimate(
            flops=2 * tokens * width * columns, bytes_accessed=60_000_000, transcendentals=0
        ),
    )(hidden, cotangent, dgu, act, x, d, p)


def rotary_tables(positions, width):
    half = width // 2
    freqs = jnp.exp(-(jnp.arange(half, dtype=jnp.float32) * 2.0 / width) * math.log(ROPE_BASE))
    angles = positions.astype(jnp.float32)[:, None] * freqs
    return jnp.concatenate([jnp.cos(angles), jnp.sin(angles)], -1)


def rms_normalize(value_rows):
    inverse_scale = lax.rsqrt(jnp.mean(value_rows * value_rows, -1, keepdims=True) + NORM_EPSILON)
    return (value_rows * inverse_scale, inverse_scale)


def norm_backward(unit_gradient, unit_input, inverse_scale):
    return inverse_scale * (
        unit_gradient - unit_input * jnp.mean(unit_gradient * unit_input, -1, keepdims=True)
    )


def adam_step(weight, grad, first, second, rate, decay):
    first_new = BETA_ONE * first + (1.0 - BETA_ONE) * grad
    second_new = BETA_TWO * second + (1.0 - BETA_TWO) * grad * grad
    corr_one = 1.0 - BETA_ONE**STEP
    corr_two = 1.0 - BETA_TWO**STEP
    update = (first_new * (1.0 / corr_one)) / (jnp.sqrt(second_new * (1.0 / corr_two)) + ADAM_EPSILON)
    return (weight - rate * (update + decay * weight), first_new, second_new)


def feed_pieces(part):
    gateup, down = [], []
    for half in range(2):
        for device in range(8):
            start = (half * 8 + device) * part
            gateup.append((half, device, 0, start))
            gateup.append((half, device, part, FEED_UNITS + start))
            down.append((half, device, 2 * part, start))
    return gateup, down


def head_pieces_of(columns):
    key = columns // 6
    query = 2 * key
    qkv, out = [], []
    for device in range(4):
        qkv.append((device, 0, device * query, query))
        qkv.append((device, query, 4 * query + device * key, key))
        qkv.append((device, query + key, 4 * (query + key) + device * key, key))
        out.append((device, query + 2 * key, device * query, query))
    return qkv, out


def norm_kernel(zero_ref, one_ref, gateup_ref, gains_ref, square_ref, terms_ref):
    halves = (zero_ref, one_ref)
    part = zero_ref.shape[2] // 3
    gateup, down = feed_pieces(part)
    two = gains_ref[...].astype(jnp.bfloat16).astype(jnp.float32)[:, 1:2]

    def over(x):
        return jnp.sum(x, 1, keepdims=True)

    two_squares = two_terms = down_squares = 0.0
    for half, device, at, column in gateup:
        grad = halves[half][device, :, at : at + part].astype(jnp.float32)
        weight = gateup_ref[:, column : column + part].astype(jnp.bfloat16).astype(jnp.float32)
        two_squares = two_squares + grad * grad
        two_terms = two_terms + grad * weight
    for half, device, at, column in down:
        grad = halves[half][device, :, at : at + part].astype(jnp.float32)
        down_squares = down_squares + grad * grad
    two_terms = over(two_terms)
    terms_ref[...] = two_terms
    total = jnp.sum(two * two * over(two_squares) + over(down_squares) + two_terms * two_terms)

    @pl.when(pl.program_id(0) == 0)
    def _():
        square_ref[0, 0] = total

    @pl.when(pl.program_id(0) > 0)
    def _():
        square_ref[0, 0] = square_ref[0, 0] + total


ROWS = 16


def rows_of(array):
    if array.ndim == 3:
        return pl.BlockSpec((array.shape[0], ROWS, array.shape[2]), lambda r: (0, r, 0))
    return pl.BlockSpec((ROWS, array.shape[1]), lambda r: (r, 0))


def feed_norm(zero, one, gateup, gains):
    arrays = (zero, one, gateup, gains)
    rows = gains.shape[0]
    terms = jax.ShapeDtypeStruct((rows, 1), jnp.float32)
    return pl.pallas_call(
        norm_kernel,
        grid=(rows // ROWS,),
        out_shape=[jax.ShapeDtypeStruct((1, 1), jnp.float32), terms],
        in_specs=[rows_of(x) for x in arrays],
        out_specs=[pl.BlockSpec(memory_space=pltpu.SMEM), rows_of(terms)],
        compiler_params=pltpu.CompilerParams(vmem_limit_bytes=VMEM_LIMIT),
        cost_estimate=pl.CostEstimate(flops=0, bytes_accessed=10_000_000, transcendentals=0),
    )(*arrays)


def settle_kernel(
    square_ref,
    terms_ref,
    qkv_ref,
    gains_ref,
    p_ref,
    head_ref,
    norm_ref,
    gain_grads_ref,
    mine,
    plane_parts,
    far_parts,
    local_sem,
    send_sems,
    recv_sems,
    far_send_sems,
    far_recv_sems,
):
    s, n, core, across, beside = places()
    diagonal = (core + 2) % 4
    f = lax.axis_index("far")
    far_size = far_parts.shape[0]
    seqs = ({"seq": diagonal}, {"seq": across}, {"seq": core})
    fars = [{"far": (f + k) % far_size} for k in range(1, far_size)]
    plane = [
        {"seq": seq, "near": near} for near in (beside, n) for seq in (diagonal, across, core, s)
    ][:-1]
    meet(*plane, *fars)
    copies, send = sender(send_sems, recv_sems)
    for k, seq in enumerate((diagonal, across, core)):
        send(("w", k), p_ref.at[seq], mine.at[s], seqs[k])
    keep = pltpu.make_async_copy(p_ref.at[s], mine.at[s], local_sem)
    keep.start()
    gains = gains_ref[...].astype(jnp.bfloat16).astype(jnp.float32)
    qkv, out = head_pieces_of(head_ref.shape[2])
    keep.wait()
    for k in range(3):
        copies["w", k].wait_recv()

    def over(x):
        return jnp.sum(x, 1, keepdims=True)

    one_squares = one_terms = out_squares = 0.0
    for device, at, column, size in qkv:
        grad = mine[device, :, at : at + size].astype(jnp.float32)
        weight = qkv_ref[:, column : column + size].astype(jnp.bfloat16).astype(jnp.float32)
        one_squares = one_squares + over(grad * grad)
        one_terms = one_terms + over(grad * weight)
    for device, at, column, size in out:
        grad = mine[device, :, at : at + size].astype(jnp.float32)
        out_squares = out_squares + over(grad * grad)
    one = gains[:, 0:1]
    rows = one * one * one_squares + out_squares + one_terms * one_terms
    gain_grads_ref[:, 0:1] = one_terms
    gain_grads_ref[:, 1:2] = terms_ref[...]
    total = jnp.sum(rows) + square_ref[0, 0]

    plane_parts[s, n] = jnp.full(plane_parts.shape[2:], total, jnp.float32)
    for k, device in enumerate(plane):
        send(("s", k), plane_parts.at[s, n], plane_parts.at[s, n], device)
    head_ref[...] = mine[...]
    for k in range(7):
        copies["s", k].wait_recv()
    everywhere = 0.0
    for seq in range(4):
        everywhere = everywhere + (plane_parts[seq, 0] + plane_parts[seq, 1])
    far_parts[f] = everywhere
    far_copies = [
        pltpu.make_async_remote_copy(
            src_ref=far_parts.at[f],
            dst_ref=far_parts.at[f],
            send_sem=far_send_sems.at[k],
            recv_sem=far_recv_sems.at[k],
            device_id=far,
            device_id_type=MESH_IDS,
        )
        for k, far in enumerate(fars)
    ]
    for copy in far_copies:
        copy.start()
    for copy in far_copies:
        copy.wait_recv()
    everywhere = far_parts[0]
    for k in range(1, far_size):
        everywhere = everywhere + far_parts[k]
    norm_ref[...] = jnp.sqrt(everywhere)
    for copy in (*copies.values(), *far_copies):
        copy.wait_send()


def settle(square, terms, qkv, gains, p, collective_id):
    far = lax.axis_size("far")
    tile = (8, 128)
    return pl.pallas_call(
        settle_kernel,
        out_shape=[
            jax.ShapeDtypeStruct(p.shape, p.dtype),
            jax.ShapeDtypeStruct(tile, jnp.float32),
            jax.ShapeDtypeStruct(gains.shape, jnp.float32),
        ],
        in_specs=[pl.BlockSpec(memory_space=pltpu.SMEM)] + [IN_VMEM] * 3 + [ANYWHERE],
        out_specs=[IN_VMEM] * 3,
        scratch_shapes=[
            pltpu.VMEM(p.shape, p.dtype),
            pltpu.VMEM((4, 2, *tile), jnp.float32),
            pltpu.VMEM((far, *tile), jnp.float32),
            pltpu.SemaphoreType.DMA,
            pltpu.SemaphoreType.DMA((10,)),
            pltpu.SemaphoreType.DMA((10,)),
            pltpu.SemaphoreType.DMA((far - 1,)),
            pltpu.SemaphoreType.DMA((far - 1,)),
        ],
        compiler_params=pltpu.CompilerParams(
            collective_id=collective_id, has_side_effects=True, vmem_limit_bytes=VMEM_LIMIT
        ),
    )(square, terms, qkv, gains, p)


def prepare_kernel(
    gains_ref,
    qkv_ref,
    out_ref,
    gateup_ref,
    down_ref,
    x_ref,
    d_ref,
    first_ref,
    second_ref,
    heads_ref,
    unit_ref,
    low_ref,
    gateup,
    down,
    qkv,
    out,
    x,
    d,
    first,
    second,
    heads,
    unit,
    low,
    load_sems,
    store_sems,
    send_sems,
    recv_sems,
):
    s, n, core, across, beside = places()
    f = lax.axis_index("far")
    far_size = heads_ref.shape[1]
    ends = [{"far": (f + 1) % far_size}, {"far": (f + far_size - 1) % far_size}]
    mine = s * 2 + n
    others = [(seq, near) for near in (beside, n) for seq in ((core + 2) % 4, across, core, s)][:-1]
    rows = out.shape[0]
    part = first.shape[2] // 3
    units = 8 * part
    half = jnp.bfloat16

    def load(at, source, target):
        copy = pltpu.make_async_copy(source, target, load_sems.at[at])
        copy.start()
        return copy

    loads = []
    load_heads = [load(6, qkv_ref, qkv), load(7, out_ref, out)]
    for c in range(2):
        for u in range(2):
            columns = pl.ds((2 * u + c) * units, units)
            loads.append(load(3 * c + u, gateup_ref.at[:, columns], gateup.at[:, columns]))
        columns = pl.ds(c * units, units)
        loads.append(load(3 * c + 2, down_ref.at[:, columns], down.at[:, columns]))
    load_tokens = [load(8, x_ref, x), load(9, d_ref, d)]
    gains = gains_ref[...].astype(half).astype(jnp.float32)
    one, two = gains[:, 0:1], gains[:, 1:2]

    def rounded(weight, gain=None):
        weight = weight.astype(half)
        return weight if gain is None else (weight.astype(jnp.float32) * gain).astype(half)

    def pieces(c, target):
        for copy in loads[3 * c : 3 * c + 3]:
            copy.wait()
        for p in range(8):
            start = c * units + p * part
            for u in range(2):
                at = slice(2 * u * units + start, 2 * u * units + start + part)
                target[p, :, u * part : (u + 1) * part] = rounded(gateup[:, at], two)
            target[p, :, 2 * part :] = rounded(down[:, start : start + part])

    def store(at, source, target):
        copy = pltpu.make_async_copy(source, target, store_sems.at[at])
        copy.start()
        return copy

    meet(*[{"seq": seq, "near": near} for seq, near in others], *ends)
    for copy in load_heads:
        copy.wait()
    qkv_pieces, out_pieces = head_pieces_of(heads.shape[2])
    for p, at, column, size in qkv_pieces:
        heads[p, :, at : at + size] = rounded(qkv[:, column : column + size], one)
    for p, at, column, size in out_pieces:
        heads[p, :, at : at + size] = rounded(out[:, column : column + size])
    copies, send = sender(send_sems, recv_sems)
    keep = store(2, heads.at[s], heads_ref.at[s, f, n])
    for seq in (core, across, (core + 2) % 4):
        send(("w", len(copies)), heads.at[seq], heads_ref.at[s, f, n], {"seq": seq})
    to_right, to_left, _, _ = groups_of(heads_ref, far_size, 10, send_sems, recv_sems)
    order = (s, core, across, (core + 2) % 4)

    def onward(k):
        for at, p in enumerate(order):
            if k == 0 and at == 0:
                keep.wait()
            elif k == 0:
                copies["w", at - 1].wait_recv()
            else:

                @pl.when(f >= k)
                def _():
                    to_right(k - 1, p).wait_recv()

            @pl.when((f >= k) & (f < far_size - 1))
            def _():
                to_right(k, p).start()

            if k > 0:

                @pl.when(f + k < far_size)
                def _():
                    to_left(k - 1, p).wait_recv()

            @pl.when((f + k < far_size) & (f > 0))
            def _():
                to_left(k, p).start()

    onward(0)
    pieces(0, first)
    for k, (seq, near) in enumerate(others):
        send(k, first.at[seq * 2 + near], first_ref.at[mine], {"seq": seq, "near": near})
    stores = [store(0, first.at[mine], first_ref.at[mine])]
    for k in range(1, FIRST_STEPS):
        onward(k)
    pieces(1, second)
    stores.append(store(1, second, second_ref))
    for copy in load_tokens:
        copy.wait()

    def tokens(i, carry):
        at = pl.ds(pl.multiple_of(i * 16, 16), 16)
        unit[at, :] = rms_normalize(x[at, :])[0].astype(half)
        low[at, :] = d[at, :].astype(half)
        return carry

    lax.fori_loop(0, x.shape[0] // 16, tokens, 0)
    stores.append(store(3, unit, unit_ref))
    stores.append(store(4, low, low_ref))
    for p in order:

        @pl.when(f >= FIRST_STEPS)
        def _():
            to_right(FIRST_STEPS - 1, p).wait_recv()

        @pl.when(f + FIRST_STEPS < far_size)
        def _():
            to_left(FIRST_STEPS - 1, p).wait_recv()

    for copy in stores:
        copy.wait()
    for k in range(7):
        copies[k].wait_recv()
    for copy in copies.values():
        copy.wait_send()
    for k in range(FIRST_STEPS):
        for p in range(4):

            @pl.when((f >= k) & (f < far_size - 1))
            def _():
                to_right(k, p).wait_send()

            @pl.when((f + k < far_size) & (f > 0))
            def _():
                to_left(k, p).wait_send()


def prepare(gains, qkv, out, gateup, down, x, d, collective_id):
    rows = gains.shape[0]
    tokens, width = x.shape
    low = jnp.bfloat16
    part = FEED_UNITS // 16
    columns = (qkv.shape[1] + out.shape[1]) // 4
    f32 = [(gateup.shape, jnp.float32), (down.shape, jnp.float32), (qkv.shape, jnp.float32), (out.shape, jnp.float32)]
    f32 += [(x.shape, jnp.float32), (d.shape, jnp.float32)]
    results = [((8, rows, 3 * part), low)] * 2 + [((4, rows, columns), low)] + [((tokens, width), low)] * 2
    far = lax.axis_size("far")
    outs = results[:2] + [((4, far, 2, rows, columns), low)] + results[3:]
    return pl.pallas_call(
        prepare_kernel,
        out_shape=[jax.ShapeDtypeStruct(*result) for result in outs],
        in_specs=[IN_VMEM] + [ANYWHERE] * 6,
        out_specs=[ANYWHERE] * 5,
        scratch_shapes=[pltpu.VMEM(*array) for array in f32 + results]
        + [
            pltpu.SemaphoreType.DMA((10,)),
            pltpu.SemaphoreType.DMA((5,)),
            pltpu.SemaphoreType.DMA((10 + 16 * far,)),
            pltpu.SemaphoreType.DMA((10 + 16 * far,)),
        ],
        compiler_params=pltpu.CompilerParams(
            collective_id=collective_id, has_side_effects=True, vmem_limit_bytes=VMEM_LIMIT
        ),
    )(gains, qkv, out, gateup, down, x, d)


def adam_kernel(norm_ref, gains_ref, zero_ref, one_ref, head_ref, *refs):
    weights, firsts, seconds = refs[0:4], refs[4:8], refs[8:12]
    weights_out, firsts_out, seconds_out = refs[12:16], refs[16:20], refs[20:24]
    halves = (zero_ref, one_ref)
    part = zero_ref.shape[2] // 3
    gateup, down = feed_pieces(part)
    qkv, out = head_pieces_of(head_ref.shape[2])
    clip = CLIP_NORM / jnp.maximum(norm_ref[0:1, 0:1], CLIP_NORM)
    gains = gains_ref[...].astype(jnp.bfloat16).astype(jnp.float32) * clip
    one, two = gains[:, 0:1], gains[:, 1:2]

    def step(which, columns, grad, rate, decay):
        new = adam_step(
            weights[which][:, columns], grad, firsts[which][:, columns], seconds[which][:, columns], rate, decay
        )
        weights_out[which][:, columns] = new[0]
        firsts_out[which][:, columns] = new[1]
        seconds_out[which][:, columns] = new[2]

    for pieces, which, scale, rate in ((qkv, 0, one, RATE_MATRIX), (out, 1, clip, RATE_OUTPUT)):
        for device, at, column, size in pieces:
            grad = head_ref[device, :, at : at + size].astype(jnp.float32) * scale
            step(which, slice(column, column + size), grad, rate, DECAY_MATRIX)
    for pieces, which, scale in ((gateup, 2, two), (down, 3, clip)):
        for half, device, at, column in pieces:
            grad = halves[half][device, :, at : at + part].astype(jnp.float32) * scale
            step(which, slice(column, column + part), grad, RATE_MATRIX, DECAY_MATRIX)


def adam(norm, gains, zero, one, head, weights, firsts, seconds):
    state = (*weights, *firsts, *seconds)
    arrays = (gains, zero, one, head, *state)
    return pl.pallas_call(
        adam_kernel,
        grid=(gains.shape[0] // ROWS,),
        out_shape=[jax.ShapeDtypeStruct(x.shape, x.dtype) for x in state],
        in_specs=[pl.BlockSpec(norm.shape, lambda r: (0, 0))] + [rows_of(x) for x in arrays],
        out_specs=[rows_of(x) for x in state],
        compiler_params=pltpu.CompilerParams(vmem_limit_bytes=VMEM_LIMIT),
    )(norm, *arrays)


def product(left, right, left_dim, right_dim):
    return lax.dot_general(
        left, right, (((left_dim,), (right_dim,)), ((), ())), preferred_element_type=jnp.float32
    )


def shards(
    inputs,
    cotangent,
    lengths,
    positions,
    query_key_value_weight,
    out_weight,
    gateup_weight,
    down_weight,
    norm_gains,
    query_key_value_moment,
    output_weight_moment,
    gate_up_moment,
    down_weight_moment,
    norm_gains_moment,
    query_key_value_variance,
    out_second,
    gateup_second,
    down_second,
    gains_second,
):
    width = inputs.shape[2]
    seq = lax.axis_size("seq")
    far = lax.axis_size("far")
    group = seq * 2
    rows = out_weight.shape[0]
    units = FEED_UNITS // group
    part = units // 2

    inputs = inputs[0]
    cotangent = cotangent[0]

    def after(x, *others):
        return lax.optimization_barrier((x, *others))[0]

    by_far = (far, seq, 2 * rows, 3 * part)

    turns = rotary_tables(positions.reshape(-1), HEAD_SIZE)
    piece, second_pieces, head_w, unit_one, dout_here = prepare(
        norm_gains, query_key_value_weight, out_weight, gateup_weight, down_weight, inputs, cotangent, 1
    )
    feed_zero = lax.all_gather(piece.reshape(group * rows, -1), "far", axis=0, tiled=True)
    feed_zero = feed_zero.reshape(by_far)

    head_w, normed_one, all_turns, dout, piece = gather_tokens(
        head_w, unit_one, turns, dout_here, second_pieces, 2
    )
    feed_one = lax.all_gather(piece.reshape(group * rows, -1), "far", axis=0, tiled=True)
    feed_one = feed_one.reshape(by_far)

    all_turns = all_turns.reshape(-1, HEAD_SIZE)
    *saved, hidden, unit_two = attention(lengths, normed_one, head_w, all_turns, inputs, 3)
    normed_two, act, dgateup, *sums = feed_first(unit_two, dout, feed_zero, 4)
    terms = feed_grads(normed_two, dout, dgateup, act, far).reshape(width, 3 * part)
    grads_zero = lax.psum_scatter(terms, "far", scatter_dimension=0, tiled=True)
    act, dgateup, output_terms, dnormed_two = feed_second(
        normed_two, dout, *sums, after(feed_one, terms)
    )
    terms, dhidden, dattended = feed_back(
        hidden, cotangent, dgateup, act, normed_two, dout, dnormed_two, far, 5
    )
    terms = terms.reshape(width, 3 * part)
    grads_one = lax.psum_scatter(after(terms, grads_zero), "far", scatter_dimension=0, tiled=True)

    head_terms, dnormed_one, output_terms = attention_back(
        lengths, saved, all_turns, dattended, output_terms, head_w, normed_one, 6
    )
    head_terms = after(head_terms, grads_zero, grads_one)
    head_terms = lax.psum_scatter(
        head_terms.reshape(far * seq * rows, -1), "far", scatter_dimension=0, tiled=True
    )
    input_grad = dhidden + norm_backward(dnormed_one, *rms_normalize(inputs))
    layer_output = hidden + output_terms

    halves = [x.reshape(group, rows, 3 * part) for x in exchange_plane([grads_zero, grads_one], 7)]
    square, gain_terms = feed_norm(*halves, gateup_weight, norm_gains)
    head_terms = after(head_terms, square, input_grad, layer_output)
    head_grads, norm, gain_grads = settle(
        square, gain_terms, query_key_value_weight, norm_gains, head_terms.reshape(seq, rows, -1), 8
    )
    weights = (query_key_value_weight, out_weight, gateup_weight, down_weight)
    firsts = (query_key_value_moment, output_weight_moment, gate_up_moment, down_weight_moment)
    seconds = (query_key_value_variance, out_second, gateup_second, down_second)
    stepped = adam(norm, norm_gains, *halves, head_grads, weights, firsts, seconds)
    grad_norm = norm[0, 0]
    gain_grads = gain_grads * (CLIP_NORM / jnp.maximum(grad_norm, CLIP_NORM))
    gains = adam_step(norm_gains, gain_grads, norm_gains_moment, gains_second, RATE_GAIN, 0.0)
    state = [x for k in range(3) for x in (*stepped[4 * k : 4 * k + 4], gains[k])]
    return (layer_output[None], input_grad[None], grad_norm, *state)


def solution(mesh):
    seq, fsdp = mesh.shape["seq"], mesh.shape["fsdp"]
    cut = Mesh(mesh.devices.reshape(seq, fsdp // 2, 2), EVERY)
    tokens = P(("far", "near"), "seq", None)
    matrix = P(EVERY, None)
    return jax.shard_map(
        shards,
        mesh=cut,
        in_specs=(tokens, tokens, P(("far", "near")), P(("far", "near"), "seq")) + (matrix,) * 15,
        out_specs=(tokens, tokens, P()) + (matrix,) * 15,
        check_vma=False,
    )
```

```python
import functools
import math

import jax
import jax.numpy as jnp
from jax import lax
from jax.experimental import pallas as pl
from jax.experimental.pallas import tpu as pltpu
from jax.sharding import Mesh, PartitionSpec as P

QUERY_HEAD_COUNT = 8
KEY_VALUE_HEADS = 4
HEAD_SIZE = 256
FEED_UNITS = 8192
STEP = 10

NORM_EPSILON = 1e-06
ROPE_BASE = 1000042.0
MASKED_SCORE = -1000000000.0
CLIP_NORM = 1.0
BETA_ONE = 0.9
BETA_TWO = 0.95
ADAM_EPSILON = 1e-08
DECAY_MATRIX = 0.1
RATE_MATRIX = 0.02
RATE_OUTPUT = 0.1
RATE_GAIN = 1.0

EVERY = ("seq", "far", "near")


MESH_IDS = pl.DeviceIdType.MESH
ANYWHERE = pl.BlockSpec(memory_space=pl.ANY)
IN_VMEM = pl.BlockSpec(memory_space=pltpu.VMEM)
VMEM_LIMIT = 60 * 1024 * 1024


def places():
    s, n = lax.axis_index("seq"), lax.axis_index("near")
    return s, n, s + 1 - 2 * (s % 2), (s + 2) % 4, 1 - n


def meet(*others):
    barrier = pltpu.get_barrier_semaphore()
    for other in others:
        pl.semaphore_signal(barrier, inc=1, device_id=other, device_id_type=MESH_IDS)
    pl.semaphore_wait(barrier, len(others))


def sender(send_sems, recv_sems):
    copies = {}

    def send(key, source, target, device):
        at = len(copies)
        copies[key] = pltpu.make_async_remote_copy(
            src_ref=source,
            dst_ref=target,
            send_sem=send_sems.at[at],
            recv_sem=recv_sems.at[at],
            device_id=device,
            device_id_type=MESH_IDS,
        )
        copies[key].start()

    return copies, send


def add_rows(target, first, second, third=None, step=64):
    rows = target.shape[0]

    def body(i, carry):
        at = pl.ds(pl.multiple_of(i * step, step), step)
        total = first[at, :].astype(jnp.float32) + second[at, :].astype(jnp.float32)
        if third is not None:
            total = total + third[at, :].astype(jnp.float32)
        target[at, :] = total.astype(target.dtype)
        return carry

    lax.fori_loop(0, rows // step, body, 0)


def exchange_plane_kernel(count, *refs):
    x_refs, o_refs = refs[:count], refs[count : 2 * count]
    local_sems, send_sems, recv_sems = refs[2 * count :]
    s, n, core, across, beside = places()
    diagonal = (core + 2) % 4
    mine = s * 2 + n
    others = [(seq, near) for near in (beside, n) for seq in (diagonal, across, core, s)][:-1]

    meet(*[{"seq": seq, "near": near} for seq, near in others])
    copies, send = sender(send_sems, recv_sems)
    locals_ = []
    for k, (x_ref, o_ref) in enumerate(zip(x_refs, o_refs)):
        rows = x_ref.shape[0] // 8

        def at(p):
            return pl.ds(p * rows, rows)

        for seq, near in others:
            target = {"seq": seq, "near": near}
            send(len(copies), x_ref.at[at(seq * 2 + near)], o_ref.at[at(mine)], target)
        locals_.append(pltpu.make_async_copy(x_ref.at[at(mine)], o_ref.at[at(mine)], local_sems.at[k]))
        locals_[k].start()
    for copy in copies.values():
        copy.wait_recv()
    for copy in copies.values():
        copy.wait_send()
    for copy in locals_:
        copy.wait()


def exchange_plane(arrays, collective_id):
    count = len(arrays)
    return pl.pallas_call(
        functools.partial(exchange_plane_kernel, count),
        out_shape=[jax.ShapeDtypeStruct(x.shape, x.dtype) for x in arrays],
        in_specs=[ANYWHERE] * count,
        out_specs=[ANYWHERE] * count,
        scratch_shapes=[
            pltpu.SemaphoreType.DMA((count,)),
            pltpu.SemaphoreType.DMA((7 * count,)),
            pltpu.SemaphoreType.DMA((7 * count,)),
        ],
        compiler_params=pltpu.CompilerParams(collective_id=collective_id, has_side_effects=True),
    )(*arrays)


def groups_of(w_ref, far_size, base, send_sems, recv_sems):
    _, n, _, _, beside = places()
    f = lax.axis_index("far")
    right, left = {"far": (f + 1) % far_size}, {"far": (f + far_size - 1) % far_size}
    to_x = {"near": beside}

    def along(far, p, device, sem):
        piece = w_ref.at[p, far, n]
        return pltpu.make_async_remote_copy(
            src_ref=piece,
            dst_ref=piece,
            send_sem=send_sems.at[base + 4 * sem + p],
            recv_sem=recv_sems.at[base + 4 * sem + p],
            device_id=device,
            device_id_type=MESH_IDS,
        )

    def to_right(k, p):
        return along((f + far_size - k) % far_size, p, right, k)

    def to_left(k, p):
        return along((f + k) % far_size, p, left, far_size + k)

    def x_from_left(k, p):
        return along((f + far_size - k) % far_size, p, to_x, 2 * far_size + k)

    def x_from_right(k, p):
        return along((f + k) % far_size, p, to_x, 3 * far_size + k)

    return to_right, to_left, x_from_left, x_from_right


FIRST_STEPS = 1


def gather_tokens_kernel(
    far_size,
    w_ref,
    x_ref,
    i_ref,
    d_ref,
    e_ref,
    o_ref,
    ox_ref,
    oi_ref,
    od_ref,
    oe_ref,
    local_sems,
    send_sems,
    recv_sems,
):
    s, n, core, across, beside = places()
    f = lax.axis_index("far")
    half = x_ref.shape[0] // 2
    to_core, to_y, to_x = {"seq": core}, {"seq": across}, {"near": beside}
    others = [(seq, near) for near in (beside, n) for seq in ((core + 2) % 4, across, core, s)][:-1]

    ends = [{"far": (f + 1) % far_size}, {"far": (f + far_size - 1) % far_size}]
    meet(*[{"seq": seq, "near": near} for seq, near in others], *ends)
    copies, send = sender(send_sems, recv_sems)

    def local(source, target, at):
        copy = pltpu.make_async_copy(source, target, local_sems.at[at])
        copy.start()
        return copy

    to_right, to_left, x_from_left, x_from_right = groups_of(o_ref, far_size, 30, send_sems, recv_sems)

    def onward(k):
        for p in range(4):

            @pl.when(f >= k)
            def _():
                if k > FIRST_STEPS:
                    to_right(k - 1, p).wait_recv()
                x_from_left(k, p).start()

            @pl.when((f >= k) & (f < far_size - 1))
            def _():
                to_right(k, p).start()

            @pl.when(f + k < far_size)
            def _():
                if k > FIRST_STEPS:
                    to_left(k - 1, p).wait_recv()
                x_from_right(k, p).start()

            @pl.when((f + k < far_size) & (f > 0))
            def _():
                to_left(k, p).start()

    if FIRST_STEPS < far_size:
        onward(FIRST_STEPS)
    for k in range(FIRST_STEPS):
        for p in range(4):

            @pl.when(f >= k)
            def _():
                x_from_left(k, p).start()

            if k > 0:

                @pl.when(f + k < far_size)
                def _():
                    x_from_right(k, p).start()

    keeps = [
        local(x_ref, ox_ref.at[s], 0),
        local(i_ref, oi_ref.at[s], 1),
        local(d_ref, od_ref.at[s * 2 + n], 2),
        local(e_ref.at[s * 2 + n], oe_ref.at[s * 2 + n], 3),
    ]
    for p in range(2):
        at = pl.ds(p * half, half)
        send(("y", p), x_ref.at[at], ox_ref.at[s, at], to_y)
        send(("c", p), x_ref.at[at], ox_ref.at[s, at], to_core)
    for k, seq in enumerate(((core + 2) % 4, across, core)):
        send(("i", k), i_ref, oi_ref.at[s], {"seq": seq})

    def block(seq, near, p):
        return od_ref.at[seq * 2 + near, pl.ds(p * half, half)]

    def own(p):
        return d_ref.at[pl.ds(p * half, half)]

    send("y0", own(0), block(s, n, 0), to_y)
    send("x1", own(1), block(s, n, 1), to_x)
    send("y1", own(1), block(s, n, 1), to_y)
    send("x0", own(0), block(s, n, 0), to_x)
    send("c0", own(0), block(s, n, 0), to_core)
    send("c1", own(1), block(s, n, 1), to_core)
    for k, (seq, near) in enumerate(others):
        send(("e", k), e_ref.at[seq * 2 + near], oe_ref.at[s * 2 + n], {"seq": seq, "near": near})
    for k in range(FIRST_STEPS + 1, far_size):
        onward(k)
    for p in range(2):
        at = pl.ds(p * half, half)
        copies["y", p].wait_recv()
        send(("yc", p), ox_ref.at[across, at], ox_ref.at[across, at], to_core)
    copies["y0"].wait_recv()
    send("yx", block(across, n, 0), block(across, n, 0), to_x)
    send("yc0", block(across, n, 0), block(across, n, 0), to_core)
    copies["x1"].wait_recv()
    send("xy", block(s, beside, 1), block(s, beside, 1), to_y)
    send("xc1", block(s, beside, 1), block(s, beside, 1), to_core)
    copies["y1"].wait_recv()
    send("yc1", block(across, n, 1), block(across, n, 1), to_core)
    copies["x0"].wait_recv()
    send("xc0", block(s, beside, 0), block(s, beside, 0), to_core)
    copies["yx"].wait_recv()
    send("dc0", block(across, beside, 0), block(across, beside, 0), to_core)
    copies["xy"].wait_recv()
    send("dc1", block(across, beside, 1), block(across, beside, 1), to_core)
    for key in ("c0", "c1", "yc0", "yc1", "xc0", "xc1", "dc0", "dc1"):
        copies[key].wait_recv()
    for p in range(2):
        copies["c", p].wait_recv()
        copies["yc", p].wait_recv()
    for k in range(3):
        copies["i", k].wait_recv()
    for k in range(7):
        copies["e", k].wait_recv()
    for k in range(far_size):
        for p in range(4):
            if k >= FIRST_STEPS:

                @pl.when((f >= k) & (f < far_size - 1))
                def _():
                    to_right(k, p).wait_send()

                @pl.when((f + k < far_size) & (f > 0))
                def _():
                    to_left(k, p).wait_send()

            @pl.when(f >= k)
            def _():
                x_from_left(k, p).wait_recv()
                x_from_left(k, p).wait_send()

            if k > 0:

                @pl.when(f + k < far_size)
                def _():
                    x_from_right(k, p).wait_recv()
                    x_from_right(k, p).wait_send()

    for copy in copies.values():
        copy.wait_send()
    for copy in keeps:
        copy.wait()


def gather_tokens(w, x, i, d, e, collective_id):
    far_size = w.shape[1]
    results = [w.shape, (4, *x.shape), (4, *i.shape), (8, *d.shape), e.shape]
    arrays = (w, x, i, d, e)
    sems = 30 + 16 * far_size
    all_w, all_x, all_i, all_d, mine_e = pl.pallas_call(
        functools.partial(gather_tokens_kernel, far_size),
        out_shape=[jax.ShapeDtypeStruct(shape, a.dtype) for shape, a in zip(results, arrays)],
        in_specs=[ANYWHERE] * 5,
        out_specs=[ANYWHERE] * 5,
        input_output_aliases={0: 0},
        scratch_shapes=[
            pltpu.SemaphoreType.DMA((4,)),
            pltpu.SemaphoreType.DMA((sems,)),
            pltpu.SemaphoreType.DMA((sems,)),
        ],
        compiler_params=pltpu.CompilerParams(collective_id=collective_id, has_side_effects=True),
    )(*arrays)
    all_x, all_d = all_x.reshape(-1, x.shape[1]), all_d.reshape(-1, d.shape[1])
    return all_w.reshape(-1, w.shape[-1]), all_x, all_i, all_d, mine_e


def tile_at(tile, rows):
    return pl.ds(pl.multiple_of(tile * rows, rows), rows)


def stacked(pair):
    half = pair.shape[1] // 2
    return jnp.concatenate([pair[:, :half], pair[:, half:]], 0)


def turned(value, cos, sin):
    half = value.shape[1] // 2
    first, second = value[:, :half], value[:, half:]
    return first * cos - second * sin, second * cos + first * sin


def visible_keys(tile, rows, keys, length):
    shape = (2 * rows, keys)
    row = lax.broadcasted_iota(jnp.int32, shape, 0)
    row = jnp.where(row >= rows, row - rows, row) + tile * rows
    column = lax.broadcasted_iota(jnp.int32, shape, 1)
    return (column <= row) & (column < length)


def attention_kernel(
    length_ref,
    x_ref,
    w_ref,
    turn_ref,
    input_ref,
    q_ref,
    k_ref,
    v_ref,
    heads_ref,
    lse_ref,
    hidden_ref,
    unit_ref,
    terms,
    far,
    last,
    send_sems,
    recv_sems,
):
    s, _, core, across, _ = places()
    to_core, to_y = {"seq": core}, {"seq": across}
    rows = x_ref.shape[0] // 4
    half = rows // 2
    size = k_ref.shape[1]
    low = jnp.bfloat16
    length = length_ref[0]
    order = [(core + 2) % 4, across, core, s]

    def rotated(ref, at, column, value, scale):
        cos, sin = turn_ref[at, : size // 2], turn_ref[at, size // 2 :]
        first, second = turned(value, cos, sin)
        ref[at, column : column + size // 2] = (first * scale).astype(low)
        ref[at, column + size // 2 : column + size] = (second * scale).astype(low)

    def keys_of(tile, carry):
        at = tile_at(tile, rows)
        merged = product(x_ref[at, :], w_ref[:, 2 * size : 4 * size], 1, 0)
        rotated(k_ref, at, 0, merged[:, :size], 1.0)
        v_ref[at, :] = merged[:, size:].astype(low)
        return carry

    def part(ref, p):
        return ref.at[pl.ds(p * half, half)]

    meet(to_core, to_y)
    lax.fori_loop(0, 4, keys_of, 0)

    def attend(tile):
        at = pl.ds(tile * rows, rows)
        keys = (tile + 1) * rows
        scores = product(stacked(q_ref[at, :]), k_ref[:keys, :], 1, 1)
        scores = jnp.where(visible_keys(tile, rows, keys, length), scores, MASKED_SCORE)
        peak = jnp.max(scores, 1, keepdims=True)
        expo = jnp.exp(scores - peak)
        total = jnp.sum(expo, 1, keepdims=True)
        result = product((expo * (1.0 / total)).astype(low), v_ref[:keys, :], 1, 0)
        live = lax.broadcasted_iota(jnp.int32, (rows, 1), 0) + tile * rows < length
        lse = peak + jnp.log(total)
        for head in range(2):
            mine = slice(head * rows, (head + 1) * rows)
            heads_ref[at, head * size : (head + 1) * size] = jnp.where(live, result[mine], 0.0).astype(low)
            lse_ref[at, head : head + 1] = lse[mine]

    plan = [
        (terms.at[0], far.at[0], to_core),
        (terms.at[2], far.at[1], to_core),
        (part(terms.at[1], 0), part(last, 0), to_y),
        (part(terms.at[1], 1), part(last, 1), to_y),
    ]

    def copy_of(k):
        source, target, device = plan[k]
        return pltpu.make_async_remote_copy(
            src_ref=source,
            dst_ref=target,
            send_sem=send_sems.at[k],
            recv_sem=recv_sems.at[k],
            device_id=device,
            device_id_type=MESH_IDS,
        )

    def tile_step(step, carry):
        tile = order[0]
        for k in range(1, 4):
            tile = jnp.where(step == k, order[k], tile)
        at = tile_at(tile, rows)
        merged = product(x_ref[at, :], w_ref[:, : 2 * size], 1, 0)
        for head in range(2):
            rotated(q_ref, at, head * size, merged[:, head * size : (head + 1) * size], size**-0.5)
        for k in range(4):

            @pl.when(tile == k)
            def _():
                attend(k)

        terms[step] = product(heads_ref[at, :], w_ref[:, 4 * size :], 1, 1).astype(low)

        @pl.when(step == 0)
        def _():
            copy_of(0).start()

        @pl.when(step == 1)
        def _():
            copy_of(0).wait_recv()
            for p in range(2):
                add_rows(part(terms.at[1], p), part(terms.at[1], p), part(far.at[0], p))
                copy_of(2 + p).start()

        @pl.when(step == 2)
        def _():
            copy_of(1).start()

        return carry

    lax.fori_loop(0, 4, tile_step, 0)
    copy_of(1).wait_recv()
    add_rows(hidden_ref, terms.at[3], far.at[1])

    def finish(i, carry):
        at = pl.ds(pl.multiple_of(i * 16, 16), 16)
        hidden = input_ref[at, :] + (hidden_ref[at, :] + last[at, :].astype(jnp.float32))
        hidden_ref[at, :] = hidden
        unit_ref[at, :] = rms_normalize(hidden)[0].astype(low)
        return carry

    for p in range(2):
        copy_of(2 + p).wait_recv()
        lax.fori_loop(p * half // 16, (p + 1) * half // 16, finish, 0)
    for k in range(4):
        copy_of(k).wait_send()


def attention(length, x, w, turns, inputs, collective_id):
    tokens, width = x.shape
    size = w.shape[1] // 6
    rows = tokens // 4
    low = jnp.bfloat16
    results = [((tokens, 2 * size), low), ((tokens, size), low), ((tokens, size), low), ((tokens, 2 * size), low)]
    results += [((tokens, 128), jnp.float32), ((rows, width), jnp.float32), ((rows, width), low)]
    return pl.pallas_call(
        attention_kernel,
        out_shape=[jax.ShapeDtypeStruct(*result) for result in results],
        in_specs=[pl.BlockSpec(memory_space=pltpu.SMEM)] + [IN_VMEM] * 4,
        out_specs=[IN_VMEM] * 7,
        scratch_shapes=[
            pltpu.VMEM((4, rows, width), low),
            pltpu.VMEM((2, rows, width), low),
            pltpu.VMEM((rows, width), low),
            pltpu.SemaphoreType.DMA((4,)),
            pltpu.SemaphoreType.DMA((4,)),
        ],
        compiler_params=pltpu.CompilerParams(
            collective_id=collective_id, has_side_effects=True, vmem_limit_bytes=VMEM_LIMIT
        ),
        cost_estimate=pl.CostEstimate(flops=10_000_000_000, bytes_accessed=20_000_000, transcendentals=0),
    )(length, x, w, turns, inputs)


def attention_back_kernel(
    length_ref,
    q_ref,
    k_ref,
    v_ref,
    heads_ref,
    lse_ref,
    turn_ref,
    g_ref,
    y_ref,
    w_ref,
    x_ref,
    terms_ref,
    dx_ref,
    sum_ref,
    weights,
    tokens,
    dheads,
    dfused,
    dk,
    dv,
    mine,
    far,
    hop_x,
    hop_y,
    last_x,
    last_y,
    far_d,
    last_d,
    out_grad,
    qkv_grad,
    out_there,
    qkv_there,
    local_sems,
    send_sems,
    recv_sems,
):
    s, n, core, across, beside = places()
    other = (core + 2) % 4
    to_core, to_y, to_x = {"seq": core}, {"seq": across}, {"near": beside}
    rows = g_ref.shape[0]
    half = rows // 2
    size = k_ref.shape[1]
    low = jnp.bfloat16
    length = length_ref[0]
    far_size = terms_ref.shape[0]

    def local(source, target, at):
        copy = pltpu.make_async_copy(source, target, local_sems.at[at])
        copy.start()
        return copy

    def part(ref, p):
        return ref.at[pl.ds(p * half, half)]

    def token_rows(seq, p):
        return tokens.at[pl.ds(seq * rows + p * half, half)]

    def block(seq, near):
        return y_ref.at[pl.ds((seq * 2 + near) * rows, rows)]

    meet(to_core, to_y, to_x)
    copies, send = sender(send_sems, recv_sems)
    keep = local(g_ref, tokens.at[pl.ds(s * rows, rows)], 0)
    for p in range(2):
        send(("gy", p), part(g_ref, p), token_rows(s, p), to_y)
    for p in range(2):
        send(("gc", p), part(g_ref, p), token_rows(s, p), to_core)
    given = [block(other, beside), block(other, n), block(core, beside), block(core, n)]
    kept = [block(across, beside), block(across, n), block(s, beside), block(s, n)]
    loads = []
    for k in range(4):
        send(k, given[k], far.at[k], to_core)
        loads.append(local(kept[k], mine.at[k], 1 + k))
    load_w = local(w_ref, weights, 5)
    for k in range(3):
        loads[k].wait()
        copies[k].wait_recv()
        add_rows(mine.at[k], mine.at[k], far.at[k])
        if k == 0:
            send("hx", part(mine.at[0], 0), hop_x, to_x)
    send("x0", part(mine.at[2], 0), part(last_x, 0), to_x)
    for p in range(2):
        copies["gy", p].wait_recv()
        send(("gyc", p), token_rows(across, p), token_rows(across, p), to_core)
    send("hy", part(mine.at[0], 1), hop_y, to_y)
    send("y1", part(mine.at[1], 1), part(last_y, 1), to_y)
    loads[3].wait()
    copies[3].wait_recv()
    add_rows(sum_ref, mine.at[3], far.at[3])
    keep.wait()
    load_w.wait()
    for p in range(2):
        copies["gc", p].wait_recv()
        copies["gyc", p].wait_recv()

    def dheads_of(tile, carry):
        at = tile_at(tile, rows)
        live = lax.broadcasted_iota(jnp.int32, (rows, 1), 0) + tile * rows < length
        value = product(tokens[at, :], weights[:, 4 * size :], 1, 0)
        dheads[at, :] = jnp.where(live, value, 0.0).astype(low)
        return carry

    def by_rows(value):
        return value.astype(low).reshape(far_size, 2, -1, value.shape[1])

    width = tokens.shape[1]
    quarter = width // 4
    for q in range(4):
        out_grad[q] = by_rows(product(tokens[:, q * quarter : (q + 1) * quarter], heads_ref[...], 0, 0))
    send("out", out_grad.at[:, :, beside], out_there, to_x)
    lax.fori_loop(0, 4, dheads_of, 0)
    for copy in ("gyc", "gy", "gc"):
        for p in range(2):
            copies[copy, p].wait_send()
    load_x = local(x_ref, tokens, 0)
    copies["hx"].wait_recv()
    add_rows(part(mine.at[1], 0), part(mine.at[1], 0), hop_x)
    send("y0", part(mine.at[1], 0), part(last_y, 0), to_y)
    copies["hy"].wait_recv()
    add_rows(part(mine.at[2], 1), part(mine.at[2], 1), hop_y)
    send("x1", part(mine.at[2], 1), part(last_x, 1), to_x)

    dk[...] = jnp.zeros_like(dk)
    dv[...] = jnp.zeros_like(dv)
    for tile in range(4):
        at = pl.ds(tile * rows, rows)
        keys = (tile + 1) * rows
        query = stacked(q_ref[at, :])
        dhead = stacked(dheads[at, :])
        scores = product(query, k_ref[:keys, :], 1, 1)
        lse = jnp.concatenate([lse_ref[at, 0:1], lse_ref[at, 1:2]], 0)
        probs = jnp.where(visible_keys(tile, rows, keys, length), jnp.exp(scores - lse), 0.0)
        dprobs = product(dhead, v_ref[:keys, :], 1, 1)
        inner = jnp.sum(probs * dprobs, 1, keepdims=True)
        dscores = (probs * (dprobs - inner)).astype(low)
        dv[:keys, :] += product(probs.astype(low), dhead, 0, 0)
        dk[:keys, :] += product(dscores, query, 0, 0)
        dquery = product(dscores, k_ref[:keys, :], 1, 0) * size**-0.5
        cos, sin = turn_ref[at, : size // 2], turn_ref[at, size // 2 :]
        for head in range(2):
            rounded = dquery[head * rows : (head + 1) * rows].astype(low).astype(jnp.float32)
            first, second = turned(rounded, cos, -sin)
            dfused[at, head * size : head * size + size // 2] = first.astype(low)
            dfused[at, head * size + size // 2 : (head + 1) * size] = second.astype(low)
    first, second = turned(
        dk[...].astype(low).astype(jnp.float32), turn_ref[:, : size // 2], -turn_ref[:, size // 2 :]
    )
    dfused[:, 2 * size : 2 * size + size // 2] = first.astype(low)
    dfused[:, 2 * size + size // 2 : 3 * size] = second.astype(low)
    dfused[:, 3 * size :] = dv[...].astype(low)

    load_x.wait()
    for q in range(4):
        qkv_grad[q] = by_rows(product(tokens[:, q * quarter : (q + 1) * quarter], dfused[...], 0, 0))
        send(("qkv", q), qkv_grad.at[q, :, beside], qkv_there.at[q], to_x)

    for p, first, second in ((1, "y1", "x1"), (0, "x0", "y0")):
        copies[first].wait_recv()
        copies[second].wait_recv()
        add_rows(part(sum_ref, p), part(sum_ref, p), part(last_x, p), part(last_y, p))
    for key in ("hx", "hy", "y0", "y1", "x0", "x1"):
        copies[key].wait_send()

    def dx_of(k, tile):
        mine[k] = product(dfused[tile_at(tile, rows), :], weights[:, : 4 * size], 1, 1).astype(low)

    dx_of(0, other)
    send("d0", mine.at[0], far_d.at[0], to_core)
    dx_of(1, core)
    send("d1", mine.at[1], far_d.at[1], to_core)
    dx_of(2, across)
    copies["d0"].wait_recv()
    for p in range(2):
        add_rows(part(mine.at[2], p), part(mine.at[2], p), part(far_d.at[0], p))
        send(("dy", p), part(mine.at[2], p), part(last_d, p), to_y)
    dx_of(3, s)
    copies["d1"].wait_recv()
    add_rows(dx_ref, mine.at[3], far_d.at[1])
    outs = []
    copies["out"].wait_recv()
    for q in range(4):
        for f in range(far_size):
            out_there[q, f] = (
                out_there[q, f].astype(jnp.float32) + out_grad[q, f, n].astype(jnp.float32)
            ).astype(low)
    for p in range(2):
        copies["dy", p].wait_recv()
        add_rows(part(dx_ref, p), part(dx_ref, p), part(last_d, p))
    for q in range(4):
        copies["qkv", q].wait_recv()
        for f in range(far_size):
            qkv_there[q, f] = (
                qkv_there[q, f].astype(jnp.float32) + qkv_grad[q, f, n].astype(jnp.float32)
            ).astype(low)
        outs.append(local(out_there.at[q], terms_ref.at[:, q, :, 4 * size :], q))
        outs.append(local(qkv_there.at[q], terms_ref.at[:, q, :, : 4 * size], 4 + q))
    for copy in outs:
        copy.wait()
    waited = {"hx", "hy", "y0", "y1", "x0", "x1"}
    for key, copy in copies.items():
        if key not in waited and not (isinstance(key, tuple) and key[0] in ("gyc", "gy", "gc")):
            copy.wait_send()


def attention_back(length, saved, turns, g, y, w, x, collective_id):
    q, k, v, heads, lse = saved
    tokens, width = x.shape
    size = k.shape[1]
    rows = tokens // 4
    far_size = lax.axis_size("far")
    weight_rows = width // (8 * far_size)
    low = jnp.bfloat16
    block = pltpu.VMEM((rows, width), low)
    half_block = pltpu.VMEM((rows // 2, width), low)
    return pl.pallas_call(
        attention_back_kernel,
        out_shape=[
            jax.ShapeDtypeStruct((far_size, 4, weight_rows, 6 * size), low),
            jax.ShapeDtypeStruct((rows, width), jnp.float32),
            jax.ShapeDtypeStruct((rows, width), jnp.float32),
        ],
        in_specs=[pl.BlockSpec(memory_space=pltpu.SMEM)] + [IN_VMEM] * 6 + [ANYWHERE] * 4,
        out_specs=[ANYWHERE, IN_VMEM, IN_VMEM],
        scratch_shapes=[
            pltpu.VMEM(w.shape, low),
            pltpu.VMEM((tokens, width), low),
            pltpu.VMEM((tokens, 2 * size), low),
            pltpu.VMEM((tokens, 4 * size), low),
            pltpu.VMEM((tokens, size), jnp.float32),
            pltpu.VMEM((tokens, size), jnp.float32),
            pltpu.VMEM((4, rows, width), low),
            pltpu.VMEM((4, rows, width), low),
            half_block,
            half_block,
            block,
            block,
            pltpu.VMEM((2, rows, width), low),
            block,
            pltpu.VMEM((4, far_size, 2, weight_rows, 2 * size), low),
            pltpu.VMEM((4, far_size, 2, weight_rows, 4 * size), low),
            pltpu.VMEM((4, far_size, weight_rows, 2 * size), low),
            pltpu.VMEM((4, far_size, weight_rows, 4 * size), low),
            pltpu.SemaphoreType.DMA((8,)),
            pltpu.SemaphoreType.DMA((25,)),
            pltpu.SemaphoreType.DMA((25,)),
        ],
        compiler_params=pltpu.CompilerParams(
            collective_id=collective_id, has_side_effects=True, vmem_limit_bytes=VMEM_LIMIT
        ),
        cost_estimate=pl.CostEstimate(flops=20_000_000_000, bytes_accessed=40_000_000, transcendentals=0),
    )(length, q, k, v, heads, lse, turns, g, y, w, x)


def hidden_units(x, d, w, part):
    low = jnp.bfloat16
    gate = product(x, w[:, :part], 1, 0)
    upper = product(x, w[:, part : 2 * part], 1, 0)
    dact = product(d, w[:, 2 * part :], 1, 0)
    sig = 1.0 / (1.0 + jnp.exp(-gate))
    silu = gate * sig
    act = (silu * upper).astype(low)
    dgate = (dact * upper * (sig + silu * (1.0 - sig))).astype(low)
    dupper = (dact * silu).astype(low)
    return act, dgate, dupper


def load_weights(w_ref, weights, sems):
    loads = [
        pltpu.make_async_copy(w_ref.at[f], weights.at[:, f], sems.at[f]) for f in range(w_ref.shape[0])
    ]
    for load in loads:
        load.start()
    return loads


def feed_first_kernel(
    x_ref,
    d_ref,
    w_ref,
    all_ref,
    act_ref,
    dgu_ref,
    y_ref,
    dx_ref,
    weights,
    tokens,
    there,
    acts,
    dgus,
    ys,
    dxs,
    local_sems,
    d_sems,
    out_sems,
    send_sems,
    recv_sems,
):
    s, n, core, across, beside = places()
    other = (core + 2) % 4
    rows = x_ref.shape[0]
    half = rows // 2
    to_core, to_y, to_x = {"seq": core}, {"seq": across}, {"near": beside}
    part = weights.shape[3] // 3
    width = x_ref.shape[1]
    low = jnp.bfloat16

    def block(seq, near, p):
        return tokens.at[seq * 2 + near, pl.ds(p * half, half)]

    def own(p):
        return x_ref.at[pl.ds(p * half, half)]

    order = [
        s * 2 + n,
        core * 2 + n,
        across * 2 + n,
        other * 2 + n,
        s * 2 + beside,
        core * 2 + beside,
        across * 2 + beside,
        other * 2 + beside,
    ]

    def tile_of(step):
        tile = order[0]
        for k in range(1, 8):
            tile = jnp.where(step == k, order[k], tile)
        return tile

    def d_load(step):
        slot = step % 2
        at = tile_at(tile_of(step), rows)
        return pltpu.make_async_copy(d_ref.at[at], there.at[slot], d_sems.at[slot])

    def stores(step):
        slot = step % 2
        tile = tile_of(step)
        at = tile_at(tile, rows)
        pairs = (
            (tokens.at[tile], all_ref),
            (acts.at[slot], act_ref),
            (dgus.at[slot], dgu_ref),
            (ys.at[slot], y_ref),
            (dxs.at[slot], dx_ref),
        )
        return [
            pltpu.make_async_copy(source, target.at[at], out_sems.at[slot, k])
            for k, (source, target) in enumerate(pairs)
        ]

    def piece(seq, near, p, device):
        return block(seq, near, p), block(seq, near, p), device

    plan = {
        "y0": (own(0), block(s, n, 0), to_y),
        "x1": (own(1), block(s, n, 1), to_x),
        "y1": (own(1), block(s, n, 1), to_y),
        "x0": (own(0), block(s, n, 0), to_x),
        "c0": (own(0), block(s, n, 0), to_core),
        "c1": (own(1), block(s, n, 1), to_core),
        "yx": piece(across, n, 0, to_x),
        "yc0": piece(across, n, 0, to_core),
        "xy": piece(s, beside, 1, to_y),
        "xc1": piece(s, beside, 1, to_core),
        "yc1": piece(across, n, 1, to_core),
        "xc0": piece(s, beside, 0, to_core),
        "dc0": piece(across, beside, 0, to_core),
        "dc1": piece(across, beside, 1, to_core),
    }
    places_of = {key: at for at, key in enumerate(plan)}

    def copy_of(key):
        source, target, device = plan[key]
        at = places_of[key]
        return pltpu.make_async_remote_copy(
            src_ref=source,
            dst_ref=target,
            send_sem=send_sems.at[at],
            recv_sem=recv_sems.at[at],
            device_id=device,
            device_id_type=MESH_IDS,
        )

    def send(*keys):
        for key in keys:
            copy_of(key).start()

    def arrive(*keys):
        for key in keys:
            copy_of(key).wait_recv()

    meet(to_core, to_y, to_x)
    keep = pltpu.make_async_copy(x_ref, tokens.at[s * 2 + n], local_sems.at[0])
    keep.start()
    send("y0", "x1", "y1", "x0", "c0", "c1")
    loads = load_weights(w_ref, weights, local_sems.at[pl.ds(1, w_ref.shape[0])])
    d_load(0).start()
    keep.wait()
    for load in loads:
        load.wait()

    def before(step):
        if step == 1:
            arrive("c0", "c1")
        elif step == 2:
            arrive("y0")
            send("yx", "yc0")
            arrive("x1")
            send("xy", "xc1")
            arrive("y1")
            send("yc1")
            arrive("x0")
            send("xc0")
        elif step == 3:
            arrive("yc0", "yc1")
        elif step == 5:
            arrive("xc0", "xc1")
        elif step == 6:
            arrive("yx")
            send("dc0")
            arrive("xy")
            send("dc1")
        elif step == 7:
            arrive("dc0", "dc1")

    def step_of(step, carry):
        for k in (1, 2, 3, 5, 6, 7):

            @pl.when(step == k)
            def _():
                before(k)

        slot = step % 2

        @pl.when(step < 7)
        def _():
            d_load(step + 1).start()

        @pl.when(step >= 2)
        def _():
            for store in stores(step - 2):
                store.wait()

        d_load(step).wait()
        w = weights[...].reshape(width, 3 * part)
        act, dgate, dupper = hidden_units(tokens[tile_of(step)], there[slot], w, part)
        acts[slot] = act
        dgus[slot, :, :part] = dgate
        dgus[slot, :, part:] = dupper
        ys[slot] = product(act, w[:, 2 * part :], 1, 1).astype(low)
        dxs[slot] = product(dgus[slot], w[:, : 2 * part], 1, 1).astype(low)
        for store in stores(step):
            store.start()
        return carry

    lax.fori_loop(0, 8, step_of, 0)
    for step in (6, 7):
        for store in stores(step):
            store.wait()
    for key in plan:
        copy_of(key).wait_send()


def feed_first(x, d, w, collective_id):
    rows, width = x.shape
    part = w.shape[3] // 3
    tokens = 8 * rows
    low = jnp.bfloat16
    far, _, weight_rows, columns = w.shape
    sizes = (width, part, 2 * part, width, width)
    return pl.pallas_call(
        feed_first_kernel,
        out_shape=[jax.ShapeDtypeStruct((tokens, size), low) for size in sizes],
        in_specs=[ANYWHERE] * 3,
        out_specs=[ANYWHERE] * 5,
        scratch_shapes=[
            pltpu.VMEM((4, far, weight_rows, columns), low),
            pltpu.VMEM((8, rows, width), low),
            pltpu.VMEM((2, rows, width), low),
            pltpu.VMEM((2, rows, part), low),
            pltpu.VMEM((2, rows, 2 * part), low),
            pltpu.VMEM((2, rows, width), low),
            pltpu.VMEM((2, rows, width), low),
            pltpu.SemaphoreType.DMA((1 + far,)),
            pltpu.SemaphoreType.DMA((2,)),
            pltpu.SemaphoreType.DMA((2, 5)),
            pltpu.SemaphoreType.DMA((14,)),
            pltpu.SemaphoreType.DMA((14,)),
        ],
        compiler_params=pltpu.CompilerParams(
            collective_id=collective_id, has_side_effects=True, vmem_limit_bytes=VMEM_LIMIT
        ),
        cost_estimate=pl.CostEstimate(
            flops=12 * tokens * width * part, bytes_accessed=60_000_000, transcendentals=0
        ),
    )(x, d, w)


def feed_second_kernel(x_ref, d_ref, y0_ref, dx0_ref, w_ref, act_ref, dgu_ref, y_ref, dx_ref, weights, sems):
    part = weights.shape[3] // 3
    width = x_ref.shape[1]
    low = jnp.bfloat16

    @pl.when(pl.program_id(0) == 0)
    def _():
        for load in load_weights(w_ref, weights, sems):
            load.wait()

    w = weights[...].reshape(width, 3 * part)
    act, dgate, dupper = hidden_units(x_ref[...], d_ref[...], w, part)
    act_ref[...] = act
    dgu_ref[:, :part] = dgate
    dgu_ref[:, part:] = dupper
    y = product(act, w[:, 2 * part :], 1, 1) + y0_ref[...].astype(jnp.float32)
    y_ref[...] = y.astype(low)
    dx = product(dgu_ref[...], w[:, : 2 * part], 1, 1) + dx0_ref[...].astype(jnp.float32)
    dx_ref[...] = dx.astype(low)


def feed_second(x, d, y, dx, w, tile=512):
    tokens, width = x.shape
    part = w.shape[3] // 3
    low = jnp.bfloat16
    far, _, weight_rows, columns = w.shape

    def tokens_of(columns):
        return pl.BlockSpec((tile, columns), lambda t: (t, 0))

    sizes = (part, 2 * part, width, width)
    return pl.pallas_call(
        feed_second_kernel,
        grid=(tokens // tile,),
        out_shape=[jax.ShapeDtypeStruct((tokens, size), low) for size in sizes],
        in_specs=[tokens_of(width)] * 4 + [ANYWHERE],
        out_specs=[tokens_of(size) for size in sizes],
        scratch_shapes=[pltpu.VMEM((4, far, weight_rows, columns), low), pltpu.SemaphoreType.DMA((far,))],
        compiler_params=pltpu.CompilerParams(vmem_limit_bytes=VMEM_LIMIT),
        cost_estimate=pl.CostEstimate(
            flops=12 * tokens * width * part, bytes_accessed=60_000_000, transcendentals=0
        ),
    )(x, d, y, dx, w)


def feed_grads_kernel(x_ref, d_ref, dgu_ref, act_ref, o_ref):
    split = dgu_ref.shape[1]
    far, _, rows, columns = o_ref.shape
    gateup = product(x_ref[...], dgu_ref[...], 0, 0).astype(o_ref.dtype)
    o_ref[:, 0, :, :split] = gateup.reshape(far, rows, split)
    down = product(d_ref[...], act_ref[...], 0, 0).astype(o_ref.dtype)
    o_ref[:, 0, :, split:] = down.reshape(far, rows, columns - split)


def feed_grads(x, d, dgu, act, far):
    tokens, width = x.shape
    columns = dgu.shape[1] + act.shape[1]
    rows = width // (4 * far)
    some = pl.BlockSpec((tokens, width // 4), lambda t: (0, t))

    def whole(array):
        return pl.BlockSpec(array.shape, lambda t: (0, 0), pipeline_mode=pl.Buffered(1))

    return pl.pallas_call(
        feed_grads_kernel,
        grid=(4,),
        out_shape=jax.ShapeDtypeStruct((far, 4, rows, columns), x.dtype),
        in_specs=[some, some, whole(dgu), whole(act)],
        out_specs=pl.BlockSpec((far, 1, rows, columns), lambda t: (0, t, 0, 0)),
        compiler_params=pltpu.CompilerParams(vmem_limit_bytes=VMEM_LIMIT),
        cost_estimate=pl.CostEstimate(
            flops=2 * tokens * width * columns, bytes_accessed=40_000_000, transcendentals=0
        ),
    )(x, d, dgu, act)


def feed_back_kernel(
    hidden_ref,
    cotangent_ref,
    dgu_ref,
    act_ref,
    x_ref,
    d_ref,
    p_ref,
    terms_ref,
    dhidden_ref,
    low_ref,
    mine,
    far,
    hop_x,
    hop_y,
    last_x,
    last_y,
    xs,
    ds,
    outs,
    local_sems,
    x_sems,
    out_sems,
    send_sems,
    recv_sems,
):
    s, n, core, across, beside = places()
    other = (core + 2) % 4
    to_core, to_y, to_x = {"seq": core}, {"seq": across}, {"near": beside}
    rows, width = hidden_ref.shape
    half = rows // 2
    quarter = width // 4
    split = dgu_ref.shape[1]
    far_size, _, weight_rows, columns = terms_ref.shape

    def block(seq, near):
        return p_ref.at[pl.ds((seq * 2 + near) * rows, rows)]

    def part(ref, p):
        return ref.at[pl.ds(p * half, half)]

    def columns_in(q):
        slot = q % 2
        at = pl.ds(q * quarter, quarter)
        return (
            pltpu.make_async_copy(x_ref.at[:, at], xs.at[slot], x_sems.at[slot, 0]),
            pltpu.make_async_copy(d_ref.at[:, at], ds.at[slot], x_sems.at[slot, 1]),
        )

    def terms_out(q):
        return pltpu.make_async_copy(outs.at[q % 2], terms_ref.at[:, q], out_sems.at[q % 2])

    meet(to_core, to_y, to_x)
    copies, send = sender(send_sems, recv_sems)
    given = [block(other, beside), block(other, n), block(core, beside), block(core, n)]
    kept = [block(across, beside), block(across, n), block(s, beside), block(s, n)]
    loads = []
    for k in range(4):
        send(k, given[k], far.at[k], to_core)
        loads.append(pltpu.make_async_copy(kept[k], mine.at[k], local_sems.at[k]))
        loads[k].start()
    for q in range(2):
        for copy in columns_in(q):
            copy.start()

    def grads(q):
        slot = q % 2
        for copy in columns_in(q):
            copy.wait()
        if q >= 2:
            terms_out(q - 2).wait()
        gateup = product(xs[slot], dgu_ref[...], 0, 0).astype(jnp.bfloat16)
        outs[slot, :, :, :split] = gateup.reshape(far_size, weight_rows, split)
        down = product(ds[slot], act_ref[...], 0, 0).astype(jnp.bfloat16)
        outs[slot, :, :, split:] = down.reshape(far_size, weight_rows, columns - split)
        terms_out(q).start()
        if q < 2:
            for copy in columns_in(q + 2):
                copy.start()

    for k in range(3):
        loads[k].wait()
        copies[k].wait_recv()
        add_rows(mine.at[k], mine.at[k], far.at[k])
        if k == 0:
            send("hx", part(mine.at[0], 0), hop_x, to_x)
            send("hy", part(mine.at[0], 1), hop_y, to_y)
        elif k == 1:
            send("y1", part(mine.at[1], 1), part(last_y, 1), to_y)
        else:
            send("x0", part(mine.at[2], 0), part(last_x, 0), to_x)
    grads(0)
    grads(1)
    copies["hx"].wait_recv()
    add_rows(part(mine.at[1], 0), part(mine.at[1], 0), hop_x)
    send("y0", part(mine.at[1], 0), part(last_y, 0), to_y)
    copies["hy"].wait_recv()
    add_rows(part(mine.at[2], 1), part(mine.at[2], 1), hop_y)
    send("x1", part(mine.at[2], 1), part(last_x, 1), to_x)
    loads[3].wait()
    copies[3].wait_recv()
    add_rows(dhidden_ref, mine.at[3], far.at[3])
    grads(2)
    grads(3)
    for key in ("y1", "x0", "y0", "x1"):
        copies[key].wait_recv()
    step = 16

    def backward(i, carry):
        at = pl.ds(pl.multiple_of(i * step, step), step)
        dx = dhidden_ref[at, :] + last_x[at, :].astype(jnp.float32) + last_y[at, :].astype(jnp.float32)
        unit, scale = rms_normalize(hidden_ref[at, :])
        dhidden = cotangent_ref[at, :] + norm_backward(dx, unit, scale)
        dhidden_ref[at, :] = dhidden
        low_ref[at, :] = dhidden.astype(low_ref.dtype)
        return carry

    lax.fori_loop(0, rows // step, backward, 0)
    for q in (2, 3):
        terms_out(q).wait()
    for copy in copies.values():
        copy.wait_send()


def feed_back(hidden, cotangent, dgu, act, x, d, p, far, collective_id):
    rows, width = hidden.shape
    tokens, columns = x.shape[0], dgu.shape[1] + act.shape[1]
    weight_rows = width // (4 * far)
    low = jnp.bfloat16
    block = pltpu.VMEM((rows, width), low)
    half_block = pltpu.VMEM((rows // 2, width), low)
    return pl.pallas_call(
        feed_back_kernel,
        out_shape=[
            jax.ShapeDtypeStruct((far, 4, weight_rows, columns), low),
            jax.ShapeDtypeStruct((rows, width), jnp.float32),
            jax.ShapeDtypeStruct((rows, width), low),
        ],
        in_specs=[IN_VMEM] * 4 + [ANYWHERE] * 3,
        out_specs=[ANYWHERE, IN_VMEM, IN_VMEM],
        scratch_shapes=[
            pltpu.VMEM((4, rows, width), low),
            pltpu.VMEM((4, rows, width), low),
            half_block,
            half_block,
            block,
            block,
            pltpu.VMEM((2, tokens, width // 4), low),
            pltpu.VMEM((2, tokens, width // 4), low),
            pltpu.VMEM((2, far, weight_rows, columns), low),
            pltpu.SemaphoreType.DMA((4,)),
            pltpu.SemaphoreType.DMA((2, 2)),
            pltpu.SemaphoreType.DMA((2,)),
            pltpu.SemaphoreType.DMA((10,)),
            pltpu.SemaphoreType.DMA((10,)),
        ],
        compiler_params=pltpu.CompilerParams(
            collective_id=collective_id, has_side_effects=True, vmem_limit_bytes=VMEM_LIMIT
        ),
        cost_estimate=pl.CostEstimate(
            flops=2 * tokens * width * columns, bytes_accessed=60_000_000, transcendentals=0
        ),
    )(hidden, cotangent, dgu, act, x, d, p)


def rotary_tables(positions, width):
    half = width // 2
    freqs = jnp.exp(-(jnp.arange(half, dtype=jnp.float32) * 2.0 / width) * math.log(ROPE_BASE))
    angles = positions.astype(jnp.float32)[:, None] * freqs
    return jnp.concatenate([jnp.cos(angles), jnp.sin(angles)], -1)


def rms_normalize(value_rows):
    inverse_scale = lax.rsqrt(jnp.mean(value_rows * value_rows, -1, keepdims=True) + NORM_EPSILON)
    return (value_rows * inverse_scale, inverse_scale)


def norm_backward(unit_gradient, unit_input, inverse_scale):
    return inverse_scale * (
        unit_gradient - unit_input * jnp.mean(unit_gradient * unit_input, -1, keepdims=True)
    )


def adam_step(weight, grad, first, second, rate, decay):
    first_new = BETA_ONE * first + (1.0 - BETA_ONE) * grad
    second_new = BETA_TWO * second + (1.0 - BETA_TWO) * grad * grad
    corr_one = 1.0 - BETA_ONE**STEP
    corr_two = 1.0 - BETA_TWO**STEP
    update = (first_new * (1.0 / corr_one)) / (jnp.sqrt(second_new * (1.0 / corr_two)) + ADAM_EPSILON)
    return (weight - rate * (update + decay * weight), first_new, second_new)


def feed_pieces(part):
    gateup, down = [], []
    for half in range(2):
        for device in range(8):
            start = (half * 8 + device) * part
            gateup.append((half, device, 0, start))
            gateup.append((half, device, part, FEED_UNITS + start))
            down.append((half, device, 2 * part, start))
    return gateup, down


def head_pieces_of(columns):
    key = columns // 6
    query = 2 * key
    qkv, out = [], []
    for device in range(4):
        qkv.append((device, 0, device * query, query))
        qkv.append((device, query, 4 * query + device * key, key))
        qkv.append((device, query + key, 4 * (query + key) + device * key, key))
        out.append((device, query + 2 * key, device * query, query))
    return qkv, out


def norm_kernel(zero_ref, one_ref, gateup_ref, gains_ref, square_ref, terms_ref):
    halves = (zero_ref, one_ref)
    part = zero_ref.shape[2] // 3
    gateup, down = feed_pieces(part)
    two = gains_ref[...].astype(jnp.bfloat16).astype(jnp.float32)[:, 1:2]

    def over(x):
        return jnp.sum(x, 1, keepdims=True)

    two_squares = two_terms = down_squares = 0.0
    for half, device, at, column in gateup:
        grad = halves[half][device, :, at : at + part].astype(jnp.float32)
        weight = gateup_ref[:, column : column + part].astype(jnp.bfloat16).astype(jnp.float32)
        two_squares = two_squares + grad * grad
        two_terms = two_terms + grad * weight
    for half, device, at, column in down:
        grad = halves[half][device, :, at : at + part].astype(jnp.float32)
        down_squares = down_squares + grad * grad
    two_terms = over(two_terms)
    terms_ref[...] = two_terms
    total = jnp.sum(two * two * over(two_squares) + over(down_squares) + two_terms * two_terms)

    @pl.when(pl.program_id(0) == 0)
    def _():
        square_ref[0, 0] = total

    @pl.when(pl.program_id(0) > 0)
    def _():
        square_ref[0, 0] = square_ref[0, 0] + total


ROWS = 16


def rows_of(array):
    if array.ndim == 3:
        return pl.BlockSpec((array.shape[0], ROWS, array.shape[2]), lambda r: (0, r, 0))
    return pl.BlockSpec((ROWS, array.shape[1]), lambda r: (r, 0))


def feed_norm(zero, one, gateup, gains):
    arrays = (zero, one, gateup, gains)
    rows = gains.shape[0]
    terms = jax.ShapeDtypeStruct((rows, 1), jnp.float32)
    return pl.pallas_call(
        norm_kernel,
        grid=(rows // ROWS,),
        out_shape=[jax.ShapeDtypeStruct((1, 1), jnp.float32), terms],
        in_specs=[rows_of(x) for x in arrays],
        out_specs=[pl.BlockSpec(memory_space=pltpu.SMEM), rows_of(terms)],
        compiler_params=pltpu.CompilerParams(vmem_limit_bytes=VMEM_LIMIT),
        cost_estimate=pl.CostEstimate(flops=0, bytes_accessed=10_000_000, transcendentals=0),
    )(*arrays)


def settle_kernel(
    square_ref,
    terms_ref,
    qkv_ref,
    gains_ref,
    p_ref,
    head_ref,
    norm_ref,
    gain_grads_ref,
    mine,
    plane_parts,
    far_parts,
    local_sem,
    send_sems,
    recv_sems,
    far_send_sems,
    far_recv_sems,
):
    s, n, core, across, beside = places()
    diagonal = (core + 2) % 4
    f = lax.axis_index("far")
    far_size = far_parts.shape[0]
    seqs = ({"seq": diagonal}, {"seq": across}, {"seq": core})
    fars = [{"far": (f + k) % far_size} for k in range(1, far_size)]
    plane = [
        {"seq": seq, "near": near} for near in (beside, n) for seq in (diagonal, across, core, s)
    ][:-1]
    meet(*plane, *fars)
    copies, send = sender(send_sems, recv_sems)
    for k, seq in enumerate((diagonal, across, core)):
        send(("w", k), p_ref.at[seq], mine.at[s], seqs[k])
    keep = pltpu.make_async_copy(p_ref.at[s], mine.at[s], local_sem)
    keep.start()
    one = as_column(gains_ref[0:1, :].astype(jnp.bfloat16).astype(jnp.float32))
    qkv, out = head_pieces_of(head_ref.shape[2])
    keep.wait()
    for k in range(3):
        copies["w", k].wait_recv()

    def over(x):
        return jnp.sum(x, 1, keepdims=True)

    one_squares = one_terms = out_squares = 0.0
    for device, at, column, size in qkv:
        grad = mine[device, :, at : at + size].astype(jnp.float32)
        weight = qkv_ref[:, column : column + size].astype(jnp.bfloat16).astype(jnp.float32)
        one_squares = one_squares + over(grad * grad)
        one_terms = one_terms + over(grad * weight)
    for device, at, column, size in out:
        grad = mine[device, :, at : at + size].astype(jnp.float32)
        out_squares = out_squares + over(grad * grad)
    rows = one * one * one_squares + out_squares + one_terms * one_terms
    gain_grads_ref[0:1, :] = as_row(one_terms)
    gain_grads_ref[1:2, :] = as_row(terms_ref[...])
    total = jnp.sum(rows) + square_ref[0, 0]

    plane_parts[s, n] = jnp.full(plane_parts.shape[2:], total, jnp.float32)
    for k, device in enumerate(plane):
        send(("s", k), plane_parts.at[s, n], plane_parts.at[s, n], device)
    head_ref[...] = mine[...]
    for k in range(7):
        copies["s", k].wait_recv()
    everywhere = 0.0
    for seq in range(4):
        everywhere = everywhere + (plane_parts[seq, 0] + plane_parts[seq, 1])
    far_parts[f] = everywhere
    far_copies = [
        pltpu.make_async_remote_copy(
            src_ref=far_parts.at[f],
            dst_ref=far_parts.at[f],
            send_sem=far_send_sems.at[k],
            recv_sem=far_recv_sems.at[k],
            device_id=far,
            device_id_type=MESH_IDS,
        )
        for k, far in enumerate(fars)
    ]
    for copy in far_copies:
        copy.start()
    for copy in far_copies:
        copy.wait_recv()
    everywhere = far_parts[0]
    for k in range(1, far_size):
        everywhere = everywhere + far_parts[k]
    norm_ref[0, 0] = jnp.max(jnp.sqrt(everywhere))
    for copy in (*copies.values(), *far_copies):
        copy.wait_send()


def settle(square, terms, qkv, gains, p, collective_id):
    far = lax.axis_size("far")
    tile = (8, 128)
    return pl.pallas_call(
        settle_kernel,
        out_shape=[
            jax.ShapeDtypeStruct(p.shape, p.dtype),
            jax.ShapeDtypeStruct((1, 1), jnp.float32),
            jax.ShapeDtypeStruct(gains.shape, jnp.float32),
        ],
        in_specs=[pl.BlockSpec(memory_space=pltpu.SMEM)] + [IN_VMEM] * 3 + [ANYWHERE],
        out_specs=[IN_VMEM, pl.BlockSpec(memory_space=pltpu.SMEM), IN_VMEM],
        scratch_shapes=[
            pltpu.VMEM(p.shape, p.dtype),
            pltpu.VMEM((4, 2, *tile), jnp.float32),
            pltpu.VMEM((far, *tile), jnp.float32),
            pltpu.SemaphoreType.DMA,
            pltpu.SemaphoreType.DMA((10,)),
            pltpu.SemaphoreType.DMA((10,)),
            pltpu.SemaphoreType.DMA((far - 1,)),
            pltpu.SemaphoreType.DMA((far - 1,)),
        ],
        compiler_params=pltpu.CompilerParams(
            collective_id=collective_id, has_side_effects=True, vmem_limit_bytes=VMEM_LIMIT
        ),
    )(square, terms, qkv, gains, p)


def diagonal_of(size):
    shape = (size, size)
    return lax.broadcasted_iota(jnp.int32, shape, 0) == lax.broadcasted_iota(jnp.int32, shape, 1)


def as_column(row):
    return jnp.sum(jnp.where(diagonal_of(row.shape[1]), row, 0.0), 1, keepdims=True)


def as_row(column):
    return jnp.sum(jnp.where(diagonal_of(column.shape[0]), column, 0.0), 0, keepdims=True)


def prepare_kernel(
    gains_ref,
    qkv_ref,
    out_ref,
    gateup_ref,
    down_ref,
    x_ref,
    d_ref,
    first_ref,
    second_ref,
    heads_ref,
    unit_ref,
    low_ref,
    gateup,
    down,
    qkv,
    out,
    x,
    d,
    first,
    second,
    heads,
    unit,
    low,
    load_sems,
    store_sems,
    send_sems,
    recv_sems,
):
    s, n, core, across, beside = places()
    f = lax.axis_index("far")
    far_size = heads_ref.shape[1]
    ends = [{"far": (f + 1) % far_size}, {"far": (f + far_size - 1) % far_size}]
    mine = s * 2 + n
    others = [(seq, near) for near in (beside, n) for seq in ((core + 2) % 4, across, core, s)][:-1]
    rows = out.shape[0]
    part = first.shape[2] // 3
    units = 8 * part
    half = jnp.bfloat16

    def load(at, source, target):
        copy = pltpu.make_async_copy(source, target, load_sems.at[at])
        copy.start()
        return copy

    loads = []
    load_heads = [load(6, qkv_ref, qkv), load(7, out_ref, out)]
    for c in range(2):
        for u in range(2):
            columns = pl.ds((2 * u + c) * units, units)
            loads.append(load(3 * c + u, gateup_ref.at[:, columns], gateup.at[:, columns]))
        columns = pl.ds(c * units, units)
        loads.append(load(3 * c + 2, down_ref.at[:, columns], down.at[:, columns]))
    load_tokens = [load(8, x_ref, x), load(9, d_ref, d)]
    gains = gains_ref[...].astype(half).astype(jnp.float32)
    one, two = as_column(gains[0:1, :]), as_column(gains[1:2, :])

    def rounded(weight, gain=None):
        weight = weight.astype(half)
        return weight if gain is None else (weight.astype(jnp.float32) * gain).astype(half)

    def pieces(c, target):
        for copy in loads[3 * c : 3 * c + 3]:
            copy.wait()
        for p in range(8):
            start = c * units + p * part
            for u in range(2):
                at = slice(2 * u * units + start, 2 * u * units + start + part)
                target[p, :, u * part : (u + 1) * part] = rounded(gateup[:, at], two)
            target[p, :, 2 * part :] = rounded(down[:, start : start + part])

    def store(at, source, target):
        copy = pltpu.make_async_copy(source, target, store_sems.at[at])
        copy.start()
        return copy

    meet(*[{"seq": seq, "near": near} for seq, near in others], *ends)
    for copy in load_heads:
        copy.wait()
    qkv_pieces, out_pieces = head_pieces_of(heads.shape[2])
    for p, at, column, size in qkv_pieces:
        heads[p, :, at : at + size] = rounded(qkv[:, column : column + size], one)
    for p, at, column, size in out_pieces:
        heads[p, :, at : at + size] = rounded(out[:, column : column + size])
    copies, send = sender(send_sems, recv_sems)
    keep = store(2, heads.at[s], heads_ref.at[s, f, n])
    for seq in (core, across, (core + 2) % 4):
        send(("w", len(copies)), heads.at[seq], heads_ref.at[s, f, n], {"seq": seq})
    to_right, to_left, _, _ = groups_of(heads_ref, far_size, 10, send_sems, recv_sems)
    order = (s, core, across, (core + 2) % 4)

    def onward(k):
        for at, p in enumerate(order):
            if k == 0 and at == 0:
                keep.wait()
            elif k == 0:
                copies["w", at - 1].wait_recv()
            else:

                @pl.when(f >= k)
                def _():
                    to_right(k - 1, p).wait_recv()

            @pl.when((f >= k) & (f < far_size - 1))
            def _():
                to_right(k, p).start()

            if k > 0:

                @pl.when(f + k < far_size)
                def _():
                    to_left(k - 1, p).wait_recv()

            @pl.when((f + k < far_size) & (f > 0))
            def _():
                to_left(k, p).start()

    onward(0)
    pieces(0, first)
    for k, (seq, near) in enumerate(others):
        send(k, first.at[seq * 2 + near], first_ref.at[mine], {"seq": seq, "near": near})
    stores = [store(0, first.at[mine], first_ref.at[mine])]
    for k in range(1, FIRST_STEPS):
        onward(k)
    pieces(1, second)
    stores.append(store(1, second, second_ref))
    for copy in load_tokens:
        copy.wait()

    def tokens(i, carry):
        at = pl.ds(pl.multiple_of(i * 16, 16), 16)
        unit[at, :] = rms_normalize(x[at, :])[0].astype(half)
        low[at, :] = d[at, :].astype(half)
        return carry

    lax.fori_loop(0, x.shape[0] // 16, tokens, 0)
    stores.append(store(3, unit, unit_ref))
    stores.append(store(4, low, low_ref))
    for p in order:

        @pl.when(f >= FIRST_STEPS)
        def _():
            to_right(FIRST_STEPS - 1, p).wait_recv()

        @pl.when(f + FIRST_STEPS < far_size)
        def _():
            to_left(FIRST_STEPS - 1, p).wait_recv()

    for copy in stores:
        copy.wait()
    for k in range(7):
        copies[k].wait_recv()
    for copy in copies.values():
        copy.wait_send()
    for k in range(FIRST_STEPS):
        for p in range(4):

            @pl.when((f >= k) & (f < far_size - 1))
            def _():
                to_right(k, p).wait_send()

            @pl.when((f + k < far_size) & (f > 0))
            def _():
                to_left(k, p).wait_send()


def prepare(gains, qkv, out, gateup, down, x, d, collective_id):
    rows = gains.shape[1]
    tokens, width = x.shape
    low = jnp.bfloat16
    part = FEED_UNITS // 16
    columns = (qkv.shape[1] + out.shape[1]) // 4
    f32 = [(gateup.shape, jnp.float32), (down.shape, jnp.float32), (qkv.shape, jnp.float32), (out.shape, jnp.float32)]
    f32 += [(x.shape, jnp.float32), (d.shape, jnp.float32)]
    results = [((8, rows, 3 * part), low)] * 2 + [((4, rows, columns), low)] + [((tokens, width), low)] * 2
    far = lax.axis_size("far")
    outs = results[:2] + [((4, far, 2, rows, columns), low)] + results[3:]
    return pl.pallas_call(
        prepare_kernel,
        out_shape=[jax.ShapeDtypeStruct(*result) for result in outs],
        in_specs=[IN_VMEM] + [ANYWHERE] * 6,
        out_specs=[ANYWHERE] * 5,
        scratch_shapes=[pltpu.VMEM(*array) for array in f32 + results]
        + [
            pltpu.SemaphoreType.DMA((10,)),
            pltpu.SemaphoreType.DMA((5,)),
            pltpu.SemaphoreType.DMA((10 + 16 * far,)),
            pltpu.SemaphoreType.DMA((10 + 16 * far,)),
        ],
        compiler_params=pltpu.CompilerParams(
            collective_id=collective_id, has_side_effects=True, vmem_limit_bytes=VMEM_LIMIT
        ),
    )(gains, qkv, out, gateup, down, x, d)


def adam_kernel(norm_ref, gains_ref, zero_ref, one_ref, head_ref, *refs):
    weights, firsts, seconds = refs[0:4], refs[4:8], refs[8:12]
    weights_out, firsts_out, seconds_out = refs[12:16], refs[16:20], refs[20:24]
    halves = (zero_ref, one_ref)
    part = zero_ref.shape[2] // 3
    gateup, down = feed_pieces(part)
    qkv, out = head_pieces_of(head_ref.shape[2])
    clip = CLIP_NORM / jnp.maximum(jnp.full((1, 1), norm_ref[0, 0], jnp.float32), CLIP_NORM)
    gains = gains_ref[...].astype(jnp.bfloat16).astype(jnp.float32) * clip
    one, two = gains[:, 0:1], gains[:, 1:2]

    def step(which, columns, grad, rate, decay):
        new = adam_step(
            weights[which][:, columns], grad, firsts[which][:, columns], seconds[which][:, columns], rate, decay
        )
        weights_out[which][:, columns] = new[0]
        firsts_out[which][:, columns] = new[1]
        seconds_out[which][:, columns] = new[2]

    for pieces, which, scale, rate in ((qkv, 0, one, RATE_MATRIX), (out, 1, clip, RATE_OUTPUT)):
        for device, at, column, size in pieces:
            grad = head_ref[device, :, at : at + size].astype(jnp.float32) * scale
            step(which, slice(column, column + size), grad, rate, DECAY_MATRIX)
    for pieces, which, scale in ((gateup, 2, two), (down, 3, clip)):
        for half, device, at, column in pieces:
            grad = halves[half][device, :, at : at + part].astype(jnp.float32) * scale
            step(which, slice(column, column + part), grad, RATE_MATRIX, DECAY_MATRIX)


def adam(norm, gains, zero, one, head, weights, firsts, seconds):
    state = (*weights, *firsts, *seconds)
    arrays = (gains, zero, one, head, *state)
    return pl.pallas_call(
        adam_kernel,
        grid=(gains.shape[0] // ROWS,),
        out_shape=[jax.ShapeDtypeStruct(x.shape, x.dtype) for x in state],
        in_specs=[pl.BlockSpec(memory_space=pltpu.SMEM)] + [rows_of(x) for x in arrays],
        out_specs=[rows_of(x) for x in state],
        compiler_params=pltpu.CompilerParams(vmem_limit_bytes=VMEM_LIMIT),
    )(norm, *arrays)


def product(left, right, left_dim, right_dim):
    return lax.dot_general(
        left, right, (((left_dim,), (right_dim,)), ((), ())), preferred_element_type=jnp.float32
    )


def shards(
    inputs,
    cotangent,
    lengths,
    positions,
    query_key_value_weight,
    out_weight,
    gateup_weight,
    down_weight,
    norm_gains,
    query_key_value_moment,
    output_weight_moment,
    gate_up_moment,
    down_weight_moment,
    norm_gains_moment,
    query_key_value_variance,
    out_second,
    gateup_second,
    down_second,
    gains_second,
):
    width = inputs.shape[2]
    seq = lax.axis_size("seq")
    far = lax.axis_size("far")
    group = seq * 2
    rows = out_weight.shape[0]
    units = FEED_UNITS // group
    part = units // 2

    inputs = inputs[0]
    cotangent = cotangent[0]

    def after(x, *others):
        return lax.optimization_barrier((x, *others))[0]

    by_far = (far, seq, 2 * rows, 3 * part)

    turns = rotary_tables(positions.reshape(-1), HEAD_SIZE)
    piece, second_pieces, head_w, unit_one, dout_here = prepare(
        norm_gains.T, query_key_value_weight, out_weight, gateup_weight, down_weight, inputs, cotangent, 1
    )
    feed_zero = lax.all_gather(piece.reshape(group * rows, -1), "far", axis=0, tiled=True)
    feed_zero = feed_zero.reshape(by_far)

    head_w, normed_one, all_turns, dout, piece = gather_tokens(
        head_w, unit_one, turns, dout_here, second_pieces, 2
    )
    feed_one = lax.all_gather(piece.reshape(group * rows, -1), "far", axis=0, tiled=True)
    feed_one = feed_one.reshape(by_far)

    all_turns = all_turns.reshape(-1, HEAD_SIZE)
    *saved, hidden, unit_two = attention(lengths, normed_one, head_w, all_turns, inputs, 3)
    normed_two, act, dgateup, *sums = feed_first(unit_two, dout, feed_zero, 4)
    terms = feed_grads(normed_two, dout, dgateup, act, far).reshape(width, 3 * part)
    grads_zero = lax.psum_scatter(terms, "far", scatter_dimension=0, tiled=True)
    act, dgateup, output_terms, dnormed_two = feed_second(
        normed_two, dout, *sums, after(feed_one, terms)
    )
    terms, dhidden, dattended = feed_back(
        hidden, cotangent, dgateup, act, normed_two, dout, dnormed_two, far, 5
    )
    terms = terms.reshape(width, 3 * part)
    grads_one = lax.psum_scatter(terms, "far", scatter_dimension=0, tiled=True)

    head_terms, dnormed_one, output_terms = attention_back(
        lengths, saved, all_turns, dattended, output_terms, head_w, normed_one, 6
    )
    zero = exchange_plane([grads_zero], 7)
    head_terms = after(head_terms, zero[0], grads_one)
    head_terms = lax.psum_scatter(
        head_terms.reshape(far * seq * rows, -1), "far", scatter_dimension=0, tiled=True
    )
    input_grad = dhidden + norm_backward(dnormed_one, *rms_normalize(inputs))
    layer_output = hidden + output_terms

    halves = [x.reshape(group, rows, 3 * part) for x in (*zero, *exchange_plane([grads_one], 7))]
    square, gain_terms = feed_norm(*halves, gateup_weight, norm_gains)
    head_terms = after(head_terms, square, input_grad, layer_output)
    head_grads, norm, gain_grads = settle(
        square, gain_terms, query_key_value_weight, norm_gains.T, head_terms.reshape(seq, rows, -1), 8
    )
    weights = (query_key_value_weight, out_weight, gateup_weight, down_weight)
    firsts = (query_key_value_moment, output_weight_moment, gate_up_moment, down_weight_moment)
    seconds = (query_key_value_variance, out_second, gateup_second, down_second)
    stepped = adam(norm, norm_gains, *halves, head_grads, weights, firsts, seconds)
    grad_norm = norm[0, 0]
    gain_grads = gain_grads.T * (CLIP_NORM / jnp.maximum(grad_norm, CLIP_NORM))
    gains = adam_step(norm_gains, gain_grads, norm_gains_moment, gains_second, RATE_GAIN, 0.0)
    state = [x for k in range(3) for x in (*stepped[4 * k : 4 * k + 4], gains[k])]
    return (layer_output[None], input_grad[None], grad_norm, *state)


def solution(mesh):
    seq, fsdp = mesh.shape["seq"], mesh.shape["fsdp"]
    cut = Mesh(mesh.devices.reshape(seq, fsdp // 2, 2), EVERY)
    tokens = P(("far", "near"), "seq", None)
    matrix = P(EVERY, None)
    return jax.shard_map(
        shards,
        mesh=cut,
        in_specs=(tokens, tokens, P(("far", "near")), P(("far", "near"), "seq")) + (matrix,) * 15,
        out_specs=(tokens, tokens, P()) + (matrix,) * 15,
        check_vma=False,
    )
```
